32 devices in a mesh: dp: 16 (over z, x, core), tensor: 2 (over y).
Axes of the slice: x: 2, y: 2, z: 4, core: 2. Of those that a mesh axis runs over, the one named last changes fastest.
Arguments:
- tokens: bfloat16 [4096, 2048], P('dp'), may hold values from -6 to 6
- lengths: int32 [16, 4], P('dp'), may hold values from 1 to 128, 256 in all within a row
- routes: int32 [4096, 6], P('dp'), may hold values from 0 to 15, all different within a row; in each aligned block of 256 rows (0 to 255, 256 to 511, ...) at most 128 rows name the same one
- grad_out: bfloat16 [4096, 2048], P('dp'), may hold values from -6 to 6
- g_attn: float32 [2048], replicated, may hold values from 0.5 to 1.5
- w_query: bfloat16 [2048, 3072], P(None, 'tensor')
- key_value_down_weight: bfloat16 [2048, 576], replicated, may hold values from -0.125 to 0.125
- latent_norm_gain: float32 [512], replicated, may hold values from 0.5 to 1.5
- key_value_up_weight: bfloat16 [512, 4096], P(None, 'tensor'), may hold values from -0.25 to 0.25
- w_out: bfloat16 [2048, 2048], P(None, 'tensor'), may hold values from -1 to 1
- g_ffn: float32 [2048], replicated, may hold values from 0.5 to 1.5
- router: float32 [2048, 16], replicated
- shared_gate: bfloat16 [2048, 2816], P(None, 'tensor'), may hold values from -0.125 to 0.125
- shared_up: bfloat16 [2048, 2816], P(None, 'tensor'), may hold values from -0.125 to 0.125
- shared_down: bfloat16 [2048, 2816], P(None, 'tensor'), may hold values from -0.109375 to 0.109375
- expert_gate: bfloat16 [16, 2048, 1408], P('dp', None, 'tensor'), may hold values from -0.125 to 0.125
- expert_up: bfloat16 [16, 2048, 1408], P('dp', None, 'tensor'), may hold values from -0.125 to 0.125
- expert_down: bfloat16 [16, 2048, 1408], P('dp', None, 'tensor'), may hold values from -0.625 to 0.625
Outputs:
- output: bfloat16 [4096, 2048], P('dp')
- grad_tokens: float32 [4096, 2048], P('dp')
- grad_g_attn: float32 [2048], P('dp')
- grad_w_query: float32 [2048, 3072], P('dp', 'tensor')
- grad_w_kv_down: float32 [2048, 576], P('dp', 'tensor')
- grad_g_kv: float32 [512], P(('dp', 'tensor'))
- grad_w_kv_up: float32 [512, 4096], P('dp', 'tensor')
- grad_w_out: float32 [2048, 2048], P('dp', 'tensor')
- grad_g_ffn: float32 [2048], P('dp')
- grad_router: float32 [2048, 16], P(('dp', 'tensor'))
- grad_shared_gate: float32 [2048, 2816], P('dp', 'tensor')
- grad_shared_up: float32 [2048, 2816], P('dp', 'tensor')
- grad_shared_down: float32 [2048, 2816], P('dp', 'tensor')
- grad_expert_gate: float32 [16, 2048, 1408], P('dp', None, 'tensor')
- grad_expert_up: float32 [16, 2048, 1408], P('dp', None, 'tensor')
- grad_expert_down: float32 [16, 2048, 1408], P('dp', None, 'tensor')
The draws below stay inside these ranges and needn't reach their ends.
Inputs may be any that keep to these rules, and one draw needn't show every extreme that they name: `lengths`: each device's documents sum to 256 tokens and the longest is exactly 128. `routes`: a token names 6 different experts; among the tokens of one device no expert is named more than 128 times, a bound that some block reaches.
All inputs are finite; a program needn't handle non-finite values.
Results may differ from the reference program's by a relative error of at most 0.025.
Values may be sent and summed in bfloat16 or wider, within the bound.
A program may use at most 320 MiB of HBM per device.

```python
import math
import jax
import jax.numpy as jnp
import numpy as np
from jax import lax

MODEL_WIDTH = 2048
HEAD_COUNT = 16
PLAIN_HEAD_SIZE = 128
TURNED_HEAD_SIZE = 64
VALUE_HEAD_SIZE = 128
QK = 192
LATENT_RANK = 512
FF = 1408
SFF = 2816
TOPK = 6
DOCS = 4
TOK_DEV = 256
EXPERTS = 16
MAXLEN = 128
CAP = 128
TOKENS = 4096
N_DP = 16


def draw_w_query(key, part):
    key = jax.random.fold_in(key, 11)
    return (jax.random.normal(key, (MODEL_WIDTH, HEAD_COUNT * QK), jnp.float32) * MODEL_WIDTH ** (-0.5)).astype(jnp.bfloat16)


def draw_router(key, part):
    key = jax.random.fold_in(key, 23)
    return jax.random.normal(key, (MODEL_WIDTH, EXPERTS), jnp.float32) * (0.7 * MODEL_WIDTH ** (-0.5))


def block_scale(own_key, extent, split, least, top_value):
    def one(axis_at, shards_of):
        steps = jax.random.uniform(jax.random.fold_in(jax.random.fold_in(own_key, 6), axis_at), (shards_of,), jnp.float32, least / len(split), top_value / len(split))
        return jnp.repeat(jnp.exp(steps), extent[axis_at] // shards_of).reshape((-1,) + (1,) * (len(extent) - axis_at - 1))

    level = one(*split[0])
    for cut in split[1:]:
        level = level * one(*cut)
    return level


def profile(number_of, total, most, skew):
    loads = [(1 << 20) // math.isqrt(grade ** skew) + 1 for grade in range(2, number_of + 1)]
    rest, counts = total - most - (number_of - 1), [1] * (number_of - 1)
    while rest > 0:
        movable = [i for i in range(number_of - 1) if counts[i] < most]
        whole, budget = sum([loads[i] for i in movable]), rest
        for i in movable:
            more = min(most - counts[i], max(1, budget * loads[i] // whole), rest)
            counts[i] = counts[i] + more
            rest = rest - more
    return np.array([most] + counts)


def ragged_sizes(rng, amount, total, most, slope):
    if amount == 2:
        one = jax.random.randint(rng, (), max(1, total - most), min(most, total - 1) + 1)
        return jnp.stack([one, total - one])
    sizes = jnp.asarray(profile(amount, total, most, slope), jnp.int32)
    pairs = (amount - 1) // 2
    giver, receiver = sizes[1:1 + 2 * pairs:2], sizes[2:2 + 2 * pairs:2]
    margin = jnp.minimum(giver - 1, most - receiver)
    shifted = jax.random.randint(jax.random.fold_in(rng, 1), (pairs,), 0, 1 << 20) % (margin + 1)
    sizes = sizes.at[1:1 + 2 * pairs:2].set(giver - shifted).at[2:2 + 2 * pairs:2].set(receiver + shifted)
    return sizes[jax.random.permutation(jax.random.fold_in(rng, 2), amount)]


def deal_out(stream_key, own, number, rows, number_of, top, most, slope):
    order = jax.random.permutation(stream_key, number_of)
    heavy_load, ordinary = portions_of(number_of, rows * top, most, slope, True), portions_of(number_of, rows * top, most, slope, False)
    places = jnp.arange(number_of)

    def named(sizes, offset_by):
        used = int((sizes > 0).sum())
        fixed = max(1, used // 4)
        moved = fixed + (places - fixed + offset_by * (used - fixed)) % max(1, number_of - fixed)
        return jnp.zeros((number_of,), jnp.int32).at[order[jnp.where(places < fixed, places, moved)]].set(jnp.asarray(sizes, jnp.int32))

    sizes = jnp.where(number % 4 == 0, named(heavy_load, number // 4), named(ordinary, number - number // 4 - 1))
    mixed = jax.random.permutation(jax.random.fold_in(own, 3), number_of)
    giver, receiver = mixed[0:number_of // 2 * 2:2], mixed[1:number_of // 2 * 2:2]
    margin = jnp.minimum(sizes[giver] - 1, most - sizes[receiver]) // 2
    margin = jnp.where((giver == order[0]) | (receiver == order[0]) | (sizes[receiver] == 0), 0, jnp.maximum(margin, 0))
    moved = jax.random.randint(jax.random.fold_in(own, 4), (number_of // 2,), 0, 1 << 20) % (margin + 1)
    sizes = sizes.at[giver].add(-moved).at[receiver].add(moved)
    members = jnp.searchsorted(jnp.cumsum(sizes), jnp.arange(rows * top), side="right").astype(jnp.int32)
    table = members.reshape(top, rows).T
    table = table[jax.random.permutation(jax.random.fold_in(own, 1), rows)]
    offset_by = jax.random.randint(jax.random.fold_in(own, 2), (rows, 1), 0, top)
    return jnp.take_along_axis(table, (jnp.arange(top)[None, :] + offset_by) % top, axis=1)


def portions_of(number_of, total, most, skew, full):
    portions = [(1 << 20) // math.isqrt(standing ** skew) + 1 for standing in range(1, number_of + 1)]
    largest = most if full else min(most, max(-(-total // number_of), total * portions[0] // sum(portions)))
    least = 1 if total - largest >= number_of - 1 else 0
    counts, spare = [largest] + [least] * (number_of - 1), total - largest - least * (number_of - 1)
    while spare > 0:
        free = [i for i in range(1, number_of) if counts[i] < largest] or [i for i in range(1, number_of) if counts[i] < most]
        mass, left = sum([portions[i] for i in free]), spare
        for i in free:
            addition = min(most - counts[i], max(1, left * portions[i] // mass), spare)
            counts[i] = counts[i] + addition
            spare = spare - addition
    return np.array(counts)


def scatter_about(key, dims, deviation, most, cuts=(), kind=jnp.bfloat16):
    values = jax.random.normal(key, dims, jnp.float32) * deviation
    if len(cuts) > 0:
        values = block_scale(key, dims, cuts, -0.22, 0.18) * values
    return jnp.clip(values, min=-most, max=most).astype(kind)


def setup_inputs(seed: int = 0) -> dict:
    keys = jax.random.split(jax.random.key(seed), 19)
    tokens = scatter_about(keys[0], (TOKENS, MODEL_WIDTH), 1.0, 6.0, ((0, 16),))
    lengths = jax.vmap(lambda own: ragged_sizes(own, DOCS, TOK_DEV, MAXLEN, 2))(jax.random.split(keys[1], N_DP)).reshape((N_DP, DOCS)).astype(jnp.int32)
    routes_keys = jax.random.split(jax.random.fold_in(keys[2], 1), TOKENS // TOK_DEV)
    routes_turns = jax.random.permutation(jax.random.fold_in(keys[2], 3), TOKENS // TOK_DEV)
    routes = jax.vmap(lambda own, number: deal_out(jax.random.fold_in(keys[2], 2), own, number, TOK_DEV, EXPERTS, TOPK, CAP, 1))(routes_keys, routes_turns).reshape((TOKENS, TOPK))
    grad_out = scatter_about(keys[3], (TOKENS, MODEL_WIDTH), 1.0, 6.0, ((0, 16),))
    g_attn = jnp.clip(1.0 + 0.1 * jax.random.normal(keys[4], (MODEL_WIDTH,), jnp.float32), 0.5, 1.5)
    w_query = draw_w_query(jax.random.fold_in(keys[18], 71), 0)
    key_value_down_weight = scatter_about(keys[6], (MODEL_WIDTH, LATENT_RANK + TURNED_HEAD_SIZE), MODEL_WIDTH ** -0.5, 0.125)
    latent_norm_gain = jnp.clip(1.0 + 0.1 * jax.random.normal(keys[7], (LATENT_RANK,), jnp.float32), 0.5, 1.5)
    key_value_up_weight = scatter_about(keys[8], (LATENT_RANK, HEAD_COUNT * (PLAIN_HEAD_SIZE + VALUE_HEAD_SIZE)), LATENT_RANK ** -0.5, 0.25, ((1, 2),))
    w_out = scatter_about(keys[9], (MODEL_WIDTH, HEAD_COUNT * VALUE_HEAD_SIZE), (HEAD_COUNT * VALUE_HEAD_SIZE // 64) ** -0.5, 1.0, ((1, 2),))
    g_ffn = jnp.clip(1.0 + 0.1 * jax.random.normal(keys[10], (MODEL_WIDTH,), jnp.float32), 0.5, 1.5)
    router = draw_router(jax.random.fold_in(keys[18], 71), 0)
    shared_gate = scatter_about(keys[12], (MODEL_WIDTH, SFF), MODEL_WIDTH ** -0.5, 0.125, ((1, 2),))
    shared_up = scatter_about(keys[13], (MODEL_WIDTH, SFF), MODEL_WIDTH ** -0.5, 0.125, ((1, 2),))
    shared_down = scatter_about(keys[14], (MODEL_WIDTH, SFF), SFF ** -0.5, 0.109375, ((1, 2),))
    expert_gate = scatter_about(keys[15], (EXPERTS, MODEL_WIDTH, FF), MODEL_WIDTH ** -0.5, 0.125, ((0, 16), (2, 2)))
    expert_up = scatter_about(keys[16], (EXPERTS, MODEL_WIDTH, FF), MODEL_WIDTH ** -0.5, 0.125, ((0, 16), (2, 2)))
    expert_down = scatter_about(keys[17], (EXPERTS, MODEL_WIDTH, FF), (FF // 16) ** -0.5, 0.625, ((0, 16), (2, 2)))
    return dict(tokens=tokens, lengths=lengths, routes=routes, grad_out=grad_out, g_attn=g_attn, w_query=w_query, key_value_down_weight=key_value_down_weight, latent_norm_gain=latent_norm_gain, key_value_up_weight=key_value_up_weight, w_out=w_out, g_ffn=g_ffn, router=router, shared_gate=shared_gate, shared_up=shared_up, shared_down=shared_down, expert_gate=expert_gate, expert_up=expert_up, expert_down=expert_down)


@jax.custom_vjp
def low(v):
    return lax.optimization_barrier(v.astype(jnp.bfloat16)).astype(jnp.float32)

@jax.custom_vjp
def low_back(v):
    return v

def low_keep(v):
    return (low(v), None)

def low_pass(kept, grad):
    return (grad,)

def back_keep(v):
    return (v, None)

def back_low(kept, grad):
    return (low(grad),)
low.defvjp(low_keep, low_pass)
low_back.defvjp(back_keep, back_low)
epsilon = 1e-06

def product(left, right):
    return jnp.dot(left, right, precision=lax.Precision.HIGHEST, preferred_element_type=jnp.float32)

def rms_normalize(values, gain):
    return values * lax.rsqrt(lax.optimization_barrier(jnp.mean(values * values, axis=-1, keepdims=True)) + epsilon) * gain

def apply_rotation(values, token_position):
    half = values.shape[-1] // 2
    freqs = 10000.0 ** (-jnp.arange(half, dtype=jnp.float32) / half)
    angles = token_position.astype(jnp.float32)[:, None] * freqs[None, :]
    shape = (angles.shape[0],) + (1,) * (values.ndim - 2) + (half,)
    cosine = jnp.cos(angles).reshape(shape)
    sine = jnp.sin(angles).reshape(shape)
    first = values[..., :half]
    second = values[..., half:]
    return jnp.concatenate([first * cosine - second * sine, second * cosine + first * sine], axis=-1)

def doc_layout(lengths_row, rows_here):
    ends = jnp.cumsum(lengths_row).astype(jnp.int32)
    starts = ends - lengths_row
    places = jnp.arange(rows_here, dtype=jnp.int32)
    segment = lax.optimization_barrier(jnp.sum((places[:, None] >= ends[None, :]).astype(jnp.int32), axis=1))
    member = segment[:, None] == jnp.arange(lengths_row.shape[0], dtype=jnp.int32)[None, :]
    begins = lax.optimization_barrier(jnp.sum(jnp.where(member, starts[None, :], 0), axis=1))
    return (segment, places - begins)

def attend_block(query, key_nope, key_turned_part, value, segment):
    highest = lax.Precision.HIGHEST
    raw = jnp.einsum('thd,shd->hts', query[..., :PLAIN_HEAD_SIZE], key_nope, precision=highest)
    raw = raw + jnp.einsum('thd,sd->hts', query[..., PLAIN_HEAD_SIZE:], key_turned_part, precision=highest)
    scores = low_back(raw) * QK ** (-0.5)
    places = jnp.arange(segment.shape[0], dtype=jnp.int32)
    allowed = (segment[:, None] == segment[None, :]) & (places[None, :] <= places[:, None])
    scores = jnp.where(allowed[None], scores, -jnp.inf)
    weights = jax.nn.softmax(scores, axis=-1)
    context = jnp.einsum('hts,shd->thd', low(weights), value, precision=highest)
    return low(low_back(context))

def reference(tokens, lengths, routes, grad_out, g_attn, w_query, key_value_down_weight, latent_norm_gain, key_value_up_weight, w_out, g_ffn, router, shared_gate, shared_up, shared_down, expert_gate, expert_up, expert_down):
    segment_blocks, position_blocks = lax.map(lambda row: doc_layout(row, TOK_DEV), lengths)
    token_position = position_blocks.reshape(TOKENS)
    flat_routes = routes.reshape(N_DP, TOK_DEV * TOPK)
    onehot = (flat_routes[:, :, None] == jnp.arange(EXPERTS, dtype=jnp.int32)[None, None, :]).astype(jnp.int32)
    running = jnp.cumsum(onehot, axis=1)
    slot = lax.optimization_barrier(jnp.sum(running * onehot, axis=2)) - 1
    device = jnp.arange(N_DP, dtype=jnp.int32)[:, None]
    pair_place = (flat_routes * (N_DP * CAP) + device * CAP + slot).reshape(-1).astype(jnp.int32)
    pair_token = (device * TOK_DEV + jnp.arange(TOK_DEV * TOPK, dtype=jnp.int32)[None, :] // TOPK).reshape(-1).astype(jnp.int32)
    slot_token = jnp.zeros((EXPERTS * N_DP * CAP,), jnp.int32).at[pair_place].set(pair_token).reshape(EXPERTS, N_DP * CAP)
    slot_valid = jnp.zeros((EXPERTS * N_DP * CAP,), jnp.float32).at[pair_place].set(1.0).reshape(EXPERTS, N_DP * CAP)

    def forward(tokens_f, g_attn, w_query, key_value_down_weight, latent_norm_gain, key_value_up_weight, w_out, g_ffn, router, shared_gate, shared_up, shared_down, expert_gate, expert_up, expert_down):
        normed = low(rms_normalize(tokens_f, g_attn))
        query_full = low_back(product(normed, w_query)).reshape(TOKENS, HEAD_COUNT, QK)
        query = low(jnp.concatenate([query_full[..., :PLAIN_HEAD_SIZE], apply_rotation(query_full[..., PLAIN_HEAD_SIZE:], token_position)], axis=-1))
        latent_with_key = low_back(product(normed, key_value_down_weight))
        key_turned_part = low(apply_rotation(latent_with_key[:, LATENT_RANK:], token_position))
        latent_vector = low(rms_normalize(latent_with_key[:, :LATENT_RANK], latent_norm_gain))
        key_value = low(low_back(product(latent_vector, key_value_up_weight))).reshape(TOKENS, HEAD_COUNT, PLAIN_HEAD_SIZE + VALUE_HEAD_SIZE)
        packs = (query.reshape(N_DP, TOK_DEV, HEAD_COUNT, QK), key_value[..., :PLAIN_HEAD_SIZE].reshape(N_DP, TOK_DEV, HEAD_COUNT, PLAIN_HEAD_SIZE), key_turned_part.reshape(N_DP, TOK_DEV, TURNED_HEAD_SIZE), key_value[..., PLAIN_HEAD_SIZE:].reshape(N_DP, TOK_DEV, HEAD_COUNT, VALUE_HEAD_SIZE), segment_blocks)
        context = lax.map(jax.checkpoint(lambda pack: attend_block(*pack)), packs).reshape(TOKENS, HEAD_COUNT * VALUE_HEAD_SIZE)
        attn = low_back(product(context, w_out.T))
        hidden = tokens_f + attn
        ffn_in = rms_normalize(hidden, g_ffn)
        ffn_low = low(ffn_in)
        router_probs = jax.nn.softmax(product(ffn_in, router), axis=-1)
        gate_weights = jnp.take_along_axis(router_probs, routes, axis=1)

        def expert_apply(pack):
            w_gate, w_up, w_down, token_ids, valid = pack
            rows_in = jnp.take(ffn_low, token_ids, axis=0) * valid[:, None]
            gate_pre = low_back(product(rows_in, w_gate))
            up_pre = low_back(product(rows_in, w_up))
            inner = low(jax.nn.silu(gate_pre) * up_pre)
            return low_back(product(inner, w_down.T))
        expert_rows = lax.map(jax.checkpoint(expert_apply), (expert_gate, expert_up, expert_down, slot_token, slot_valid))
        pair_rows = jnp.take(expert_rows.reshape(-1, MODEL_WIDTH), pair_place, axis=0).reshape(TOKENS, TOPK, MODEL_WIDTH)
        routed = lax.optimization_barrier(jnp.sum(gate_weights[:, :, None] * pair_rows, axis=1))
        shared_pre_gate = low_back(product(ffn_low, shared_gate))
        shared_pre_up = low_back(product(ffn_low, shared_up))
        shared_inner = low(jax.nn.silu(shared_pre_gate) * shared_pre_up)
        shared_result = low_back(product(shared_inner, shared_down.T))
        return hidden + routed + shared_result
    floats = (tokens.astype(jnp.float32), g_attn, w_query.astype(jnp.float32), key_value_down_weight.astype(jnp.float32), latent_norm_gain, key_value_up_weight.astype(jnp.float32), w_out.astype(jnp.float32), g_ffn, router, shared_gate.astype(jnp.float32), shared_up.astype(jnp.float32), shared_down.astype(jnp.float32), expert_gate.astype(jnp.float32), expert_up.astype(jnp.float32), expert_down.astype(jnp.float32))
    result, pullback = jax.vjp(forward, *floats)
    grads = pullback(grad_out.astype(jnp.float32))
    return (result.astype(jnp.bfloat16), grads[0], grads[1], grads[2], grads[3], grads[4], grads[5], grads[6], grads[7], grads[8], grads[9], grads[10], grads[11], grads[12], grads[13], grads[14])
```

```python
import jax
import jax.numpy as jnp
from jax import lax
from jax.sharding import PartitionSpec as P

PLAIN_HEAD_SIZE = 128
VALUE_HEAD_SIZE = 128
QK = 192
LATENT_RANK = 512
TOPK = 6


epsilon = 1e-06


def rms_normalize_pieces(values, gain):
    factor = lax.rsqrt(jnp.mean(values * values, axis=-1, keepdims=True) + epsilon)
    unit = values * factor
    return (unit * gain, unit, factor)


def normalize_back(grad, unit, factor, gain):
    inner = grad * gain
    return factor * (inner - unit * jnp.mean(inner * unit, axis=-1, keepdims=True))


def apply_rotation(values, token_position):
    half = values.shape[-1] // 2
    freqs = 10000.0 ** (-jnp.arange(half, dtype=jnp.float32) / half)
    angles = token_position.astype(jnp.float32)[:, None] * freqs[None, :]
    shape = (angles.shape[0],) + (1,) * (values.ndim - 2) + (half,)
    cosine = jnp.cos(angles).reshape(shape)
    sine = jnp.sin(angles).reshape(shape)
    first = values[..., :half]
    second = values[..., half:]
    return jnp.concatenate(
        [first * cosine - second * sine, second * cosine + first * sine], axis=-1
    )


def doc_layout(lengths_row, rows_here):
    ends = jnp.cumsum(lengths_row)
    starts = ends - lengths_row
    places = jnp.arange(rows_here, dtype=jnp.int32)
    segment = jnp.sum((places[:, None] >= ends[None, :]).astype(jnp.int32), axis=1)
    member = segment[:, None] == jnp.arange(lengths_row.shape[0], dtype=jnp.int32)[None, :]
    begins = jnp.sum(jnp.where(member, starts[None, :], 0), axis=1)
    return (segment, places - begins)


def contract_last(left, right, precision=None):
    return lax.dot_general(
        left,
        right,
        (((1,), (1,)), ((), ())),
        precision=precision,
        preferred_element_type=jnp.float32,
    )


def contract_first(left, right, precision=None):
    return lax.dot_general(
        left,
        right,
        (((0,), (0,)), ((), ())),
        precision=precision,
        preferred_element_type=jnp.float32,
    )


def swish_parts(gate_pre):
    sigma = jax.nn.sigmoid(gate_pre)
    return (gate_pre * sigma, sigma * (1.0 + gate_pre * (1.0 - sigma)))


def shards(
    tokens,
    lengths,
    routes,
    grad_out,
    g_attn,
    w_query,
    key_value_down_weight,
    latent_norm_gain,
    key_value_up_weight,
    w_out,
    g_ffn,
    router,
    shared_gate,
    shared_up,
    shared_down,
    expert_gate,
    expert_up,
    expert_down,
):
    rows_here = tokens.shape[0]
    features = tokens.shape[1]
    heads_local = w_out.shape[1] // VALUE_HEAD_SIZE
    devices = lax.axis_size("dp")
    capacity = rows_here * TOPK * 4 // (3 * devices)
    experts = router.shape[1]
    highest = lax.Precision.HIGHEST
    softmax_scale = QK ** (-0.5)
    segment, token_position = doc_layout(lengths[0], rows_here)
    places = jnp.arange(rows_here, dtype=jnp.int32)
    allowed = (segment[:, None] == segment[None, :]) & (places[None, :] <= places[:, None])
    tokens_f = tokens.astype(jnp.float32)
    attn_normed, attn_unit, attn_factor = rms_normalize_pieces(tokens_f, g_attn)
    normed_bf = attn_normed.astype(jnp.bfloat16)
    query_full = jnp.dot(normed_bf, w_query, preferred_element_type=jnp.float32).reshape(
        rows_here, heads_local, QK
    )
    query_bf = jnp.concatenate(
        [
            query_full[..., :PLAIN_HEAD_SIZE],
            apply_rotation(query_full[..., PLAIN_HEAD_SIZE:], token_position),
        ],
        axis=-1,
    ).astype(jnp.bfloat16)
    latent_with_key = jnp.dot(normed_bf, key_value_down_weight, preferred_element_type=jnp.float32)
    key_turned_part = apply_rotation(latent_with_key[:, LATENT_RANK:], token_position).astype(
        jnp.bfloat16
    )
    latent_after_norm, latent_unit_scale, latent_norm_factor = rms_normalize_pieces(
        latent_with_key[:, :LATENT_RANK], latent_norm_gain
    )
    latent_bf = latent_after_norm.astype(jnp.bfloat16)
    key_value = (
        jnp.dot(latent_bf, key_value_up_weight, preferred_element_type=jnp.float32)
        .astype(jnp.bfloat16)
        .reshape(rows_here, heads_local, PLAIN_HEAD_SIZE + VALUE_HEAD_SIZE)
    )
    key_nope = key_value[..., :PLAIN_HEAD_SIZE]
    value = key_value[..., PLAIN_HEAD_SIZE:]

    def masked_scores():
        raw = jnp.einsum(
            "thd,shd->hts",
            query_bf[..., :PLAIN_HEAD_SIZE],
            key_nope,
            preferred_element_type=jnp.float32,
        )
        raw = raw + jnp.einsum(
            "thd,sd->hts",
            query_bf[..., PLAIN_HEAD_SIZE:],
            key_turned_part,
            preferred_element_type=jnp.float32,
        )
        return jnp.where(allowed[None], raw * softmax_scale, -jnp.inf)

    scores = masked_scores()
    top_score = jnp.max(scores, axis=-1, keepdims=True)
    expo = jnp.exp(scores - top_score)
    total = jnp.sum(expo, axis=-1, keepdims=True)
    log_total = top_score + jnp.log(total)
    attn_weights = (expo / total).astype(jnp.bfloat16)
    context = jnp.einsum("hts,shd->thd", attn_weights, value, preferred_element_type=jnp.float32)
    context = context.astype(jnp.bfloat16).reshape(rows_here, heads_local * VALUE_HEAD_SIZE)
    attn = lax.psum(contract_last(context, w_out).astype(jnp.bfloat16), "tensor").astype(
        jnp.float32
    )
    hidden = tokens_f + attn
    ffn_normed, ffn_unit, ffn_factor = rms_normalize_pieces(hidden, g_ffn)
    ffn_bf = ffn_normed.astype(jnp.bfloat16)
    router_probs = jax.nn.softmax(jnp.dot(ffn_normed, router, precision=highest), axis=-1)
    own = lax.axis_index("dp")

    everyone_grad = lax.all_gather(grad_out, "dp", tiled=True)
    everyone_routes = lax.all_gather(routes, "dp", tiled=True)
    everyone_ffn = lax.all_gather(ffn_bf, "dp", tiled=True)
    everyone_probs = lax.all_gather(router_probs, "dp", tiled=True)
    chooses = jnp.any(everyone_routes == own, axis=1).reshape(devices, rows_here)
    own_probs = lax.dynamic_slice_in_dim(everyone_probs, own, 1, 1).reshape(devices, rows_here)
    own_gates = jnp.where(chooses, own_probs, 0.0)
    upto = (places[:, None] <= places[None, :]).astype(jnp.bfloat16)
    slot = jnp.dot(chooses.astype(jnp.bfloat16), upto, preferred_element_type=jnp.float32) - 1.0
    slots = jnp.arange(capacity, dtype=jnp.float32)
    picked = chooses[:, None, :] & (slot[:, None, :] == slots[None, :, None])
    pick = picked.astype(jnp.bfloat16)
    slot_gates = jnp.sum(jnp.where(picked, own_gates[:, None, :], 0.0), axis=2).reshape(-1, 1)

    def pick_rows(values):
        blocks = values.reshape(devices, rows_here, features)
        return jnp.einsum(
            "jst,jtc->jsc", pick, blocks, preferred_element_type=jnp.float32
        ).astype(jnp.bfloat16).reshape(devices * capacity, features)

    def put_rows(values, hidden_parts, weights):
        blocks = values.astype(jnp.bfloat16).reshape(devices, capacity, features)
        left = jnp.concatenate(
            [pick.transpose(0, 2, 1)]
            + [h.reshape(devices, rows_here, h.shape[1]) for h in hidden_parts],
            axis=2,
        )
        right = jnp.concatenate(
            [blocks]
            + [
                jnp.broadcast_to(w.T[None], (devices, w.shape[1], features))
                for w in weights
            ],
            axis=1,
        )
        return (
            jnp.einsum("jtk,jkc->jtc", left, right, preferred_element_type=jnp.float32)
            .astype(jnp.bfloat16)
            .reshape(devices * rows_here, features)
        )

    expert_rows = pick_rows(everyone_ffn)
    grad_picked = pick_rows(everyone_grad)
    grad_rows = (slot_gates * grad_picked.astype(jnp.float32)).astype(jnp.bfloat16)

    gate_pre = jnp.dot(expert_rows, expert_gate[0], preferred_element_type=jnp.float32)
    up_pre = jnp.dot(expert_rows, expert_up[0], preferred_element_type=jnp.float32)
    gate_act, gate_slope = swish_parts(gate_pre)
    expert_hidden = (gate_act * up_pre).astype(jnp.bfloat16)
    expert_result = contract_last(expert_hidden, expert_down[0])
    slot_grads = jnp.sum(grad_picked.astype(jnp.float32) * expert_result, axis=1)
    grad_expert_down = contract_first(grad_rows, expert_hidden)[None]
    grad_expert_hidden = jnp.dot(grad_rows, expert_down[0], preferred_element_type=jnp.float32)
    grad_gate_pre = (grad_expert_hidden * up_pre * gate_slope).astype(jnp.bfloat16)
    grad_up_pre = (grad_expert_hidden * gate_act).astype(jnp.bfloat16)
    grad_expert_gate = contract_first(expert_rows, grad_gate_pre)[None]
    grad_expert_up = contract_first(expert_rows, grad_up_pre)[None]
    grad_rows_in = contract_last(grad_gate_pre, expert_gate[0]) + contract_last(
        grad_up_pre, expert_up[0]
    )

    part = shared_gate.shape[1] // devices
    part_gate = lax.dynamic_slice_in_dim(shared_gate, own * part, part, 1)
    part_up = lax.dynamic_slice_in_dim(shared_up, own * part, part, 1)
    part_down = lax.dynamic_slice_in_dim(shared_down, own * part, part, 1)
    shared_pre_gate = jnp.dot(everyone_ffn, part_gate, preferred_element_type=jnp.float32)
    shared_pre_up = jnp.dot(everyone_ffn, part_up, preferred_element_type=jnp.float32)
    shared_act, shared_slope = swish_parts(shared_pre_gate)
    shared_hidden = (shared_act * shared_pre_up).astype(jnp.bfloat16)
    grad_shared_hidden = jnp.dot(everyone_grad, part_down, preferred_element_type=jnp.float32)
    grad_shared_gate_pre = (grad_shared_hidden * shared_pre_up * shared_slope).astype(jnp.bfloat16)
    grad_shared_up_pre = (grad_shared_hidden * shared_act).astype(jnp.bfloat16)
    shared_grads = jnp.concatenate(
        [
            contract_first(everyone_ffn, grad_shared_gate_pre),
            contract_first(everyone_ffn, grad_shared_up_pre),
            contract_first(everyone_grad, shared_hidden),
        ],
        axis=1,
    ).astype(jnp.bfloat16)
    share_rows = features // devices
    shared_grads = lax.all_to_all(
        shared_grads.reshape(devices, share_rows, 3 * part), "dp", split_axis=0, concat_axis=0
    ).astype(jnp.float32)
    grad_shared_gate, grad_shared_up, grad_shared_down = (
        shared_grads[:, :, i * part : (i + 1) * part]
        .transpose(1, 0, 2)
        .reshape(share_rows, devices * part)
        for i in range(3)
    )

    grad_top = grad_out.astype(jnp.float32)
    ffn_part = put_rows(slot_gates * expert_result, [shared_hidden], [part_down])
    ffn_total = lax.psum_scatter(ffn_part, "dp", scatter_dimension=0, tiled=True)
    ffn_total = lax.psum(ffn_total, "tensor").astype(jnp.float32)
    output = (hidden + ffn_total).astype(jnp.bfloat16)
    pair_grads = jnp.sum(
        jnp.where(picked, slot_grads.reshape(devices, capacity, 1), 0.0), axis=1
    ).reshape(devices * rows_here, 1)
    pair_high = pair_grads.astype(jnp.bfloat16).astype(jnp.float32)
    column = jnp.arange(128, dtype=jnp.int32)[None, :]
    pair_columns = jnp.where(
        column == own,
        pair_high,
        jnp.where(column == own + experts, pair_grads - pair_high, 0.0),
    )
    grad_ffn_in = put_rows(
        grad_rows_in, [grad_shared_gate_pre, grad_shared_up_pre], [part_gate, part_up]
    )
    grad_ffn_sum = lax.psum_scatter(
        jnp.concatenate([grad_ffn_in, pair_columns.astype(jnp.bfloat16)], axis=1),
        "dp",
        scatter_dimension=0,
        tiled=True,
    )
    grad_ffn_sum = lax.psum(grad_ffn_sum.astype(jnp.float32), "tensor")
    dense_grad = (
        grad_ffn_sum[:, features : features + experts]
        + grad_ffn_sum[:, features + experts : features + 2 * experts]
    )
    grad_logits = router_probs * (
        dense_grad - jnp.sum(router_probs * dense_grad, axis=-1, keepdims=True)
    )
    grad_router_in = contract_last(grad_logits, router, highest)
    grad_router_part = contract_first(ffn_normed, grad_logits, highest) / lax.axis_size("tensor")
    grad_ffn_total = grad_ffn_sum[:, :features] + grad_router_in
    grad_g_ffn = jnp.sum(grad_ffn_total * ffn_unit, axis=0)
    grad_hidden = grad_top + normalize_back(grad_ffn_total, ffn_unit, ffn_factor, g_ffn)
    grad_hidden_bf = grad_hidden.astype(jnp.bfloat16)
    grad_w_out = contract_first(grad_hidden_bf, context)
    grad_context = jnp.dot(grad_hidden_bf, w_out, preferred_element_type=jnp.float32).astype(
        jnp.bfloat16
    )
    grad_context = grad_context.reshape(rows_here, heads_local, VALUE_HEAD_SIZE)
    redone = jnp.exp(masked_scores() - log_total)
    redone_bf = redone.astype(jnp.bfloat16)
    grad_weights = jnp.einsum(
        "thd,shd->hts", grad_context, value, preferred_element_type=jnp.float32
    )
    grad_value = jnp.einsum(
        "hts,thd->shd", redone_bf, grad_context, preferred_element_type=jnp.float32
    )
    row_inner = jnp.sum(redone * grad_weights, axis=-1, keepdims=True)
    grad_raw = (redone * (grad_weights - row_inner) * softmax_scale).astype(jnp.bfloat16)
    grad_query_nope = jnp.einsum(
        "hts,shd->thd", grad_raw, key_nope, preferred_element_type=jnp.float32
    )
    grad_query_rot = jnp.einsum(
        "hts,sd->thd", grad_raw, key_turned_part, preferred_element_type=jnp.float32
    )
    grad_key_nope = jnp.einsum(
        "hts,thd->shd",
        grad_raw,
        query_bf[..., :PLAIN_HEAD_SIZE],
        preferred_element_type=jnp.float32,
    )
    grad_key_rot = jnp.einsum(
        "hts,thd->sd", grad_raw, query_bf[..., PLAIN_HEAD_SIZE:], preferred_element_type=jnp.float32
    )
    grad_query = jnp.concatenate(
        [grad_query_nope, apply_rotation(grad_query_rot, -token_position)], axis=-1
    )
    grad_query = grad_query.reshape(rows_here, heads_local * QK).astype(jnp.bfloat16)
    grad_w_query = contract_first(normed_bf, grad_query)
    grad_in_query = contract_last(grad_query, w_query)
    grad_key_value = (
        jnp.concatenate([grad_key_nope, grad_value], axis=-1)
        .reshape(rows_here, heads_local * (PLAIN_HEAD_SIZE + VALUE_HEAD_SIZE))
        .astype(jnp.bfloat16)
    )
    grad_w_kv_up = contract_first(latent_bf, grad_key_value)
    grad_latent_normed = contract_last(grad_key_value, key_value_up_weight)
    grad_g_kv_part = jnp.sum(grad_latent_normed * latent_unit_scale, axis=0)
    grad_latent = normalize_back(
        grad_latent_normed, latent_unit_scale, latent_norm_factor, latent_norm_gain
    )
    grad_down_part = jnp.concatenate(
        [grad_latent, apply_rotation(grad_key_rot, -token_position)], axis=1
    )
    grad_in_summed, grad_down = (
        lax.psum(grad_in_query.astype(jnp.bfloat16), "tensor").astype(jnp.float32),
        lax.psum(grad_down_part.astype(jnp.bfloat16), "tensor").astype(jnp.float32),
    )
    grad_down_bf = grad_down.astype(jnp.bfloat16)
    share = grad_down.shape[1] // lax.axis_size("tensor")
    grad_columns = lax.dynamic_slice_in_dim(
        grad_down_bf, lax.axis_index("tensor") * share, share, 1
    )
    grad_w_kv_down = contract_first(normed_bf, grad_columns)
    grad_attn_in = grad_in_summed + contract_last(grad_down_bf, key_value_down_weight)
    grad_g_attn = jnp.sum(grad_attn_in * attn_unit, axis=0)
    grad_tokens = grad_hidden + normalize_back(grad_attn_in, attn_unit, attn_factor, g_attn)
    summed = (
        lax.psum_scatter(
            grad_w_query.astype(jnp.bfloat16), "dp", scatter_dimension=0, tiled=True
        ).astype(jnp.float32),
        lax.psum_scatter(
            grad_w_kv_down.astype(jnp.bfloat16), "dp", scatter_dimension=0, tiled=True
        ).astype(jnp.float32),
        lax.psum_scatter(
            grad_w_kv_up.astype(jnp.bfloat16), "dp", scatter_dimension=0, tiled=True
        ).astype(jnp.float32),
        lax.psum_scatter(
            grad_w_out.astype(jnp.bfloat16), "dp", scatter_dimension=0, tiled=True
        ).astype(jnp.float32),
        lax.psum_scatter(
            grad_g_attn.astype(jnp.bfloat16), "dp", scatter_dimension=0, tiled=True
        ).astype(jnp.float32),
        lax.psum_scatter(
            grad_g_ffn.astype(jnp.bfloat16), "dp", scatter_dimension=0, tiled=True
        ).astype(jnp.float32),
    )
    everywhere = (
        lax.psum_scatter(grad_router_part, ("dp", "tensor"), scatter_dimension=0, tiled=True),
        lax.psum_scatter(grad_g_kv_part, ("dp", "tensor"), scatter_dimension=0, tiled=True),
    )
    return (
        output,
        grad_tokens,
        summed[4],
        summed[0],
        summed[1],
        everywhere[1],
        summed[2],
        summed[3],
        summed[5],
        everywhere[0],
        grad_shared_gate,
        grad_shared_up,
        grad_shared_down,
        grad_expert_gate,
        grad_expert_up,
        grad_expert_down,
    )


def solution(mesh):
    in_specs = (
        P("dp", None),
        P("dp", None),
        P("dp", None),
        P("dp", None),
        P(),
        P(None, "tensor"),
        P(),
        P(),
        P(None, "tensor"),
        P(None, "tensor"),
        P(),
        P(),
        P(None, "tensor"),
        P(None, "tensor"),
        P(None, "tensor"),
        P("dp", None, "tensor"),
        P("dp", None, "tensor"),
        P("dp", None, "tensor"),
    )
    out_specs = (
        P("dp", None),
        P("dp", None),
        P("dp"),
        P("dp", "tensor"),
        P("dp", "tensor"),
        P(("dp", "tensor")),
        P("dp", "tensor"),
        P("dp", "tensor"),
        P("dp"),
        P(("dp", "tensor"), None),
        P("dp", "tensor"),
        P("dp", "tensor"),
        P("dp", "tensor"),
        P("dp", None, "tensor"),
        P("dp", None, "tensor"),
        P("dp", None, "tensor"),
    )
    return jax.shard_map(shards, mesh=mesh, in_specs=in_specs, out_specs=out_specs, check_vma=False)
```

```python
import functools

import jax
import jax.numpy as jnp
from jax import lax
from jax.experimental import pallas as pl
from jax.experimental.pallas import tpu as pltpu
from jax.sharding import PartitionSpec as P

PLAIN_HEAD_SIZE = 128
VALUE_HEAD_SIZE = 128
QK = 192
LATENT_RANK = 512
TOPK = 6


epsilon = 1e-06


def rms_normalize_pieces(values, gain):
    factor = lax.rsqrt(jnp.mean(values * values, axis=-1, keepdims=True) + epsilon)
    unit = values * factor
    return (unit * gain, unit, factor)


def normalize_back(grad, unit, factor, gain):
    inner = grad * gain
    return factor * (inner - unit * jnp.mean(inner * unit, axis=-1, keepdims=True))


def apply_rotation(values, token_position):
    half = values.shape[-1] // 2
    freqs = 10000.0 ** (-jnp.arange(half, dtype=jnp.float32) / half)
    angles = token_position.astype(jnp.float32)[:, None] * freqs[None, :]
    shape = (angles.shape[0],) + (1,) * (values.ndim - 2) + (half,)
    cosine = jnp.cos(angles).reshape(shape)
    sine = jnp.sin(angles).reshape(shape)
    first = values[..., :half]
    second = values[..., half:]
    return jnp.concatenate(
        [first * cosine - second * sine, second * cosine + first * sine], axis=-1
    )


def doc_layout(lengths_row, rows_here):
    ends = jnp.cumsum(lengths_row)
    starts = ends - lengths_row
    places = jnp.arange(rows_here, dtype=jnp.int32)
    segment = jnp.sum((places[:, None] >= ends[None, :]).astype(jnp.int32), axis=1)
    member = segment[:, None] == jnp.arange(lengths_row.shape[0], dtype=jnp.int32)[None, :]
    begins = jnp.sum(jnp.where(member, starts[None, :], 0), axis=1)
    return (segment, places - begins)


def contract_last(left, right, precision=None):
    return lax.dot_general(
        left,
        right,
        (((1,), (1,)), ((), ())),
        precision=precision,
        preferred_element_type=jnp.float32,
    )


def contract_first(left, right, precision=None):
    return lax.dot_general(
        left,
        right,
        (((0,), (0,)), ((), ())),
        precision=precision,
        preferred_element_type=jnp.float32,
    )


def swish_parts(gate_pre):
    sigma = jax.nn.sigmoid(gate_pre)
    return (gate_pre * sigma, sigma * (1.0 + gate_pre * (1.0 - sigma)))


VMEM_LIMIT = 60 * 1024 * 1024


def place_of(x_size):
    me = lax.axis_index("dp")
    core = me % 2
    x = (me // 2) % x_size
    z = me // (2 * x_size)
    return z, x, core


def index_of(z, x, core, x_size):
    return (z * x_size + x) * 2 + core


def remote(src, dst, send_sem, recv_sem, target):
    return pltpu.make_async_remote_copy(
        src_ref=src,
        dst_ref=dst,
        send_sem=send_sem,
        recv_sem=recv_sem,
        device_id={"dp": target},
        device_id_type=pl.DeviceIdType.MESH,
    )


def greet(z, x, core, z_size, x_size, pair=False):
    barrier = pltpu.get_barrier_semaphore()

    def tell(target):
        pl.semaphore_signal(
            barrier, inc=1, device_id={"dp": target}, device_id_type=pl.DeviceIdType.MESH
        )

    tell(index_of(z, x, 1 - core, x_size))
    tell(index_of(z, 1 - x, core, x_size))

    @pl.when(z > 0)
    def _():
        tell(index_of(z - 1, x, core, x_size))

    @pl.when(z < z_size - 1)
    def _():
        tell(index_of(z + 1, x, core, x_size))

    inner = (z + z_size - 1) // z_size - z // (z_size - 1)
    if pair:
        pl.semaphore_signal(
            barrier,
            inc=1,
            device_id={"tensor": 1 - lax.axis_index("tensor")},
            device_id_type=pl.DeviceIdType.MESH,
        )
    pl.semaphore_wait(barrier, 3 + inner + (1 if pair else 0))


def gather_kernel(z_size, x_size, count, *refs):
    ins, outs = refs[:count], refs[count : 2 * count]
    own_sem, up_s, up_r, dn_s, dn_r, x_s, x_r, c_s, c_r = refs[2 * count :]
    z, x, core = place_of(x_size)
    greet(z, x, core, z_size, x_size)
    at = functools.partial(index_of, x_size=x_size)
    keep = [
        pltpu.make_async_copy(ins[a], outs[a].at[at(z, x, core)], own_sem.at[a])
        for a in range(count)
    ]
    for copy in keep:
        copy.start()

    def up(a, d):
        block = outs[a].at[at(z - d, x, core)]
        src = ins[a] if d == 0 else block
        return remote(src, block, up_s.at[a, d], up_r.at[a, d], at(z + 1, x, core))

    def down(a, d):
        block = outs[a].at[at(z + d, x, core)]
        src = ins[a] if d == 0 else block
        return remote(src, block, dn_s.at[a, d], dn_r.at[a, d], at(z - 1, x, core))

    def across(a, w, own=False):
        block = outs[a].at[at(w, x, core)]
        return remote(ins[a] if own else block, block, x_s.at[a, w], x_r.at[a, w], at(z, 1 - x, core))

    def beside(a, w, v, own=False):
        block = outs[a].at[at(w, v, core)]
        return remote(
            ins[a] if own else block, block, c_s.at[a, w, v], c_r.at[a, w, v], at(z, x, 1 - core)
        )

    def each(do):
        for a in range(count):
            do(a)

    def from_across(w):
        def do(a):
            across(a, w).wait_recv()
            beside(a, w, 1 - x).start()

        each(do)

    def when_up(d, do):
        pl.when(z >= d)(lambda: each(do))

    def when_down(d, do):
        pl.when(z + d < z_size)(lambda: each(do))

    def first(a):
        across(a, z, True).start()
        pl.when(z < z_size - 1)(lambda: up(a, 0).start())
        pl.when(z > 0)(lambda: down(a, 0).start())
        beside(a, z, x, True).start()

    each(first)
    for d in range(1, z_size):

        def passed_up(a):
            up(a, d - 1).wait_recv()
            pl.when(z < z_size - 1)(lambda: up(a, d).start())
            across(a, z - d).start()
            beside(a, z - d, x).start()

        def passed_down(a):
            down(a, d - 1).wait_recv()
            pl.when(z > 0)(lambda: down(a, d).start())
            across(a, z + d).start()
            beside(a, z + d, x).start()

        when_up(d, passed_up)
        when_down(d, passed_down)
        if d == 1:
            from_across(z)
        else:
            pl.when(z >= d - 1)(lambda: from_across(z - (d - 1)))
            pl.when(z + d - 1 < z_size)(lambda: from_across(z + (d - 1)))
    pl.when(z >= z_size - 1)(lambda: from_across(z - (z_size - 1)))
    pl.when(z < 1)(lambda: from_across(z + (z_size - 1)))
    for a in range(count):
        for w in range(z_size):
            for v in range(x_size):
                beside(a, w, v).wait()
            across(a, w).wait_send()
    for d in range(z_size):
        pl.when((z >= d) & (z < z_size - 1))(lambda: each(lambda a: up(a, d).wait_send()))
        pl.when((z + d < z_size) & (z > 0))(lambda: each(lambda a: down(a, d).wait_send()))
    for copy in keep:
        copy.wait()


def gather_rows(arrays, z_size, x_size, collective_id):
    count = len(arrays)
    n = 2 * z_size * x_size
    dma = pltpu.SemaphoreType.DMA
    outs = pl.pallas_call(
        functools.partial(gather_kernel, z_size, x_size, count),
        out_shape=[jax.ShapeDtypeStruct((n,) + a.shape, a.dtype) for a in arrays],
        in_specs=[pl.BlockSpec(memory_space=pl.ANY)] * count,
        out_specs=[pl.BlockSpec(memory_space=pl.ANY)] * count,
        scratch_shapes=[dma((count,))]
        + [dma((count, z_size))] * 6
        + [dma((count, z_size, x_size))] * 2,
        compiler_params=pltpu.CompilerParams(
            collective_id=collective_id, has_side_effects=True, vmem_limit_bytes=VMEM_LIMIT
        ),
        name="gather_rows",
    )(*arrays)
    return outs


def add_into(dst, *srcs):
    rows = dst.shape[0]
    step = 32 if rows % 32 == 0 else 16

    def body(i, _):
        here = pl.ds(pl.multiple_of(i * step, step), step)
        total = dst[here, :].astype(jnp.float32)
        for src in srcs:
            total = total + src[here, :].astype(jnp.float32)
        dst[here, :] = total.astype(dst.dtype)
        return 0

    lax.fori_loop(0, rows // step, body, 0)


def scatter_kernel(x_size, parts, pair, *refs):
    z_size = 4
    ins, outs, refs = refs[:parts], refs[parts : 2 * parts], refs[2 * parts :]
    own, c_buf, x_buf, z_buf = (refs[i * parts : (i + 1) * parts] for i in range(4))
    refs = refs[4 * parts :]
    y_buf = None
    if pair:
        y_buf, y_s, y_r, refs = refs[:parts], refs[parts], refs[parts + 1], refs[parts + 2 :]
    l_sem, c_s, c_r, x_s, x_r, z_s, z_r = refs
    z, x, core = place_of(x_size)
    at = functools.partial(index_of, x_size=x_size)
    half = z // 2
    inner = ((z + 3) // 4) * ((6 - z) // 4)
    order = [3 - 3 * half, 2 - half, 1 - z + 4 * half, z]
    load = lambda p, w, v: pltpu.make_async_copy(
        ins[p].at[at(w, v, core)], own[p].at[w, v], l_sem.at[p, w, v]
    )
    beside = lambda p, w, v: remote(
        ins[p].at[at(w, v, 1 - core)],
        c_buf[p].at[w, v],
        c_s.at[p, w, v],
        c_r.at[p, w, v],
        at(z, x, 1 - core),
    )
    across = lambda p, w: remote(
        c_buf[p].at[w, 1 - x], x_buf[p].at[w], x_s.at[p, w], x_r.at[p, w], at(z, 1 - x, core)
    )

    def along(p, w, slot, target):
        return remote(
            c_buf[p].at[w, x], z_buf[p].at[slot], z_s.at[p, w], z_r.at[p, slot], at(target, x, core)
        )

    twin = lambda p: pltpu.make_async_remote_copy(
        src_ref=c_buf[p].at[z, x],
        dst_ref=y_buf[p],
        send_sem=y_s.at[p],
        recv_sem=y_r.at[p],
        device_id={"tensor": 1 - lax.axis_index("tensor")},
        device_id_type=pl.DeviceIdType.MESH,
    )

    for v in (1 - x, x):
        for w in order:
            for p in range(parts):
                load(p, w, v).start()
    greet(z, x, core, z_size, x_size, pair)
    for v in (1 - x, x):
        for w in order:
            for p in range(parts):
                beside(p, w, v).start()
    for w in order:
        for p in range(parts):
            load(p, w, 1 - x).wait()
            beside(p, w, 1 - x).wait_recv()
            add_into(c_buf[p].at[w, 1 - x], own[p].at[w, 1 - x])
            across(p, w).start()
    for k, w in enumerate(order):
        for p in range(parts):
            load(p, w, x).wait()
            beside(p, w, x).wait_recv()
            add_into(c_buf[p].at[w, x], own[p].at[w, x])
            across(p, w).wait_recv()
            if k < 3:

                @pl.when(inner == 1)
                def _():
                    along(p, w, w, z).wait_recv()
                    add_into(c_buf[p].at[w, x], x_buf[p].at[w], z_buf[p].at[w])

                @pl.when(inner == 0)
                def _():
                    add_into(c_buf[p].at[w, x], x_buf[p].at[w])

                @pl.when(w > z)
                def _():
                    along(p, w, w, z + 1).start()

                @pl.when(w < z - 1)
                def _():
                    along(p, w, w, z - 1).start()

                @pl.when(w == z - 1)
                def _():
                    along(p, w, z_size, z - 1).start()

            else:
                add_into(c_buf[p].at[w, x], x_buf[p].at[w])

                @pl.when(z > 0)
                def _():
                    along(p, w, z, z).wait_recv()
                    add_into(c_buf[p].at[w, x], z_buf[p].at[z])

                @pl.when(z < z_size - 1)
                def _():
                    along(p, w, z_size, z).wait_recv()
                    add_into(c_buf[p].at[w, x], z_buf[p].at[z_size])

                if pair:
                    twin(p).start()
                else:
                    outs[p][...] = c_buf[p][z, x].astype(outs[p].dtype)
    if pair:
        for p in range(parts):
            twin(p).wait()
            outs[p][...] = (
                c_buf[p][z, x].astype(jnp.float32) + y_buf[p][...].astype(jnp.float32)
            ).astype(outs[p].dtype)
    for w in range(z_size):
        for p in range(parts):
            for v in range(x_size):
                beside(p, w, v).wait_send()
            across(p, w).wait_send()

            @pl.when(z != w)
            def _():
                along(p, w, w, z).wait_send()


def scatter_sums(arrays, x_size, collective_id, out_dtype, pair=False):
    parts = len(arrays)
    dma = pltpu.SemaphoreType.DMA
    blocks = [a.shape[1:] for a in arrays]
    return pl.pallas_call(
        functools.partial(scatter_kernel, x_size, parts, pair),
        out_shape=[jax.ShapeDtypeStruct(b, out_dtype) for b in blocks],
        in_specs=[pl.BlockSpec(memory_space=pl.ANY)] * parts,
        out_specs=[pl.BlockSpec(memory_space=pltpu.VMEM)] * parts,
        scratch_shapes=[pltpu.VMEM((4, x_size) + b, a.dtype) for a, b in zip(arrays, blocks)]
        + [pltpu.VMEM((4, x_size) + b, a.dtype) for a, b in zip(arrays, blocks)]
        + [pltpu.VMEM((4,) + b, a.dtype) for a, b in zip(arrays, blocks)]
        + [pltpu.VMEM((5,) + b, a.dtype) for a, b in zip(arrays, blocks)]
        + ([pltpu.VMEM(b, a.dtype) for a, b in zip(arrays, blocks)] + [dma((parts,))] * 2 if pair else [])
        + [dma((parts, 4, x_size))] * 3
        + [dma((parts, 4))] * 3
        + [dma((parts, 5))],
        compiler_params=pltpu.CompilerParams(
            collective_id=collective_id, has_side_effects=True, vmem_limit_bytes=VMEM_LIMIT
        ),
        name="scatter_sums",
    )(*arrays)


def pair_kernel(chunks, extras, left, right, *refs):
    ins, total, outs = refs[:extras], refs[extras], refs[extras + 1 : 2 * extras + 1]
    sent, got, refs = refs[2 * extras + 1], refs[2 * extras + 2], refs[2 * extras + 3 :]
    e_got, (s_sem, r_sem, es_sem, er_sem) = refs[:extras], refs[extras:]
    width = total.shape[1] // chunks
    other = {"tensor": 1 - lax.axis_index("tensor")}
    barrier = pltpu.get_barrier_semaphore()
    pl.semaphore_signal(barrier, inc=1, device_id=other, device_id_type=pl.DeviceIdType.MESH)
    pl.semaphore_wait(barrier, 1)

    def copy(src, dst, send_sem, recv_sem):
        return pltpu.make_async_remote_copy(
            src_ref=src,
            dst_ref=dst,
            send_sem=send_sem,
            recv_sem=recv_sem,
            device_id=other,
            device_id_type=pl.DeviceIdType.MESH,
        )

    chunk = lambda i: copy(sent.at[i], got.at[i], s_sem.at[i], r_sem.at[i])
    extra = lambda i: copy(ins[i], e_got[i], es_sem.at[i], er_sem.at[i])
    for i in range(extras):
        extra(i).start()
    for i in range(chunks):
        sent[i] = lax.dot_general(
            left[...],
            right[pl.ds(i * width, width), :],
            (((1,), (1,)), ((), ())),
            preferred_element_type=jnp.float32,
        ).astype(jnp.bfloat16)
        chunk(i).start()
    for i in range(extras):
        extra(i).wait()
        outs[i][...] = ins[i][...].astype(jnp.float32) + e_got[i][...].astype(jnp.float32)
    for i in range(chunks):
        chunk(i).wait()
        total[:, pl.ds(i * width, width)] = sent[i].astype(jnp.float32) + got[i].astype(
            jnp.float32
        )


def pair_product(left, right, extras, collective_id, chunks=8):
    rows, columns = left.shape[0], right.shape[0]
    dma = pltpu.SemaphoreType.DMA
    vmem = pl.BlockSpec(memory_space=pltpu.VMEM)
    block = pltpu.VMEM((chunks, rows, columns // chunks), jnp.bfloat16)
    return pl.pallas_call(
        functools.partial(pair_kernel, chunks, len(extras)),
        out_shape=[jax.ShapeDtypeStruct((rows, columns), jnp.float32)]
        + [jax.ShapeDtypeStruct(e.shape, jnp.float32) for e in extras],
        in_specs=[vmem] * (2 + len(extras)),
        out_specs=[vmem] * (1 + len(extras)),
        scratch_shapes=[block, block]
        + [pltpu.VMEM(e.shape, e.dtype) for e in extras]
        + [dma((chunks,))] * 2
        + [dma((max(1, len(extras)),))] * 2,
        compiler_params=pltpu.CompilerParams(
            collective_id=collective_id, has_side_effects=True, vmem_limit_bytes=VMEM_LIMIT
        ),
        name="pair_product",
    )(left, right, *extras)


def tuned():
    return lax.axis_size("dp") == 16 and lax.axis_size("tensor") == 2


def gather_all(arrays):
    if tuned():
        return gather_rows(arrays, 4, 2, 1)
    return [lax.all_gather(a, "dp") for a in arrays]


def sum_home(arrays, collective_id, pair=False):
    if tuned():
        return scatter_sums(arrays, 2, collective_id, jnp.float32, pair)
    sums = [lax.psum_scatter(a, "dp", scatter_dimension=0) for a in arrays]
    if pair:
        sums = [lax.psum(a.astype(jnp.float32), "tensor") for a in sums]
    return [a.astype(jnp.float32) for a in sums]


def product_sum(left, right, extras, collective_id):
    if tuned():
        return pair_product(left, right, extras, collective_id)
    product = contract_last(left, right).astype(jnp.bfloat16)
    return [lax.psum(a, "tensor").astype(jnp.float32) for a in [product] + extras]


def shards(
    tokens,
    lengths,
    routes,
    grad_out,
    g_attn,
    w_query,
    key_value_down_weight,
    latent_norm_gain,
    key_value_up_weight,
    w_out,
    g_ffn,
    router,
    shared_gate,
    shared_up,
    shared_down,
    expert_gate,
    expert_up,
    expert_down,
):
    rows_here = tokens.shape[0]
    features = tokens.shape[1]
    heads_local = w_out.shape[1] // VALUE_HEAD_SIZE
    devices = lax.axis_size("dp")
    capacity = rows_here * TOPK * 4 // (3 * devices)
    experts = router.shape[1]
    highest = lax.Precision.HIGHEST
    softmax_scale = QK ** (-0.5)
    segment, token_position = doc_layout(lengths[0], rows_here)
    places = jnp.arange(rows_here, dtype=jnp.int32)
    allowed = (segment[:, None] == segment[None, :]) & (places[None, :] <= places[:, None])
    tokens_f = tokens.astype(jnp.float32)
    attn_normed, attn_unit, attn_factor = rms_normalize_pieces(tokens_f, g_attn)
    normed_bf = attn_normed.astype(jnp.bfloat16)
    query_full = jnp.dot(normed_bf, w_query, preferred_element_type=jnp.float32).reshape(
        rows_here, heads_local, QK
    )
    query_bf = jnp.concatenate(
        [
            query_full[..., :PLAIN_HEAD_SIZE],
            apply_rotation(query_full[..., PLAIN_HEAD_SIZE:], token_position),
        ],
        axis=-1,
    ).astype(jnp.bfloat16)
    latent_with_key = jnp.dot(normed_bf, key_value_down_weight, preferred_element_type=jnp.float32)
    key_turned_part = apply_rotation(latent_with_key[:, LATENT_RANK:], token_position).astype(
        jnp.bfloat16
    )
    latent_after_norm, latent_unit_scale, latent_norm_factor = rms_normalize_pieces(
        latent_with_key[:, :LATENT_RANK], latent_norm_gain
    )
    latent_bf = latent_after_norm.astype(jnp.bfloat16)
    key_value = (
        jnp.dot(latent_bf, key_value_up_weight, preferred_element_type=jnp.float32)
        .astype(jnp.bfloat16)
        .reshape(rows_here, heads_local, PLAIN_HEAD_SIZE + VALUE_HEAD_SIZE)
    )
    key_nope = key_value[..., :PLAIN_HEAD_SIZE]
    value = key_value[..., PLAIN_HEAD_SIZE:]

    def masked_scores():
        raw = jnp.einsum(
            "thd,shd->hts",
            query_bf[..., :PLAIN_HEAD_SIZE],
            key_nope,
            preferred_element_type=jnp.float32,
        )
        raw = raw + jnp.einsum(
            "thd,sd->hts",
            query_bf[..., PLAIN_HEAD_SIZE:],
            key_turned_part,
            preferred_element_type=jnp.float32,
        )
        return jnp.where(allowed[None], raw * softmax_scale, -jnp.inf)

    scores = masked_scores()
    top_score = jnp.max(scores, axis=-1, keepdims=True)
    expo = jnp.exp(scores - top_score)
    total = jnp.sum(expo, axis=-1, keepdims=True)
    log_total = top_score + jnp.log(total)
    attn_weights = (expo / total).astype(jnp.bfloat16)
    context = jnp.einsum("hts,shd->thd", attn_weights, value, preferred_element_type=jnp.float32)
    context = context.astype(jnp.bfloat16).reshape(rows_here, heads_local * VALUE_HEAD_SIZE)
    (attn,) = product_sum(context, w_out, [], 2)
    hidden = tokens_f + attn
    ffn_normed, ffn_unit, ffn_factor = rms_normalize_pieces(hidden, g_ffn)
    ffn_bf = ffn_normed.astype(jnp.bfloat16)
    router_probs = jax.nn.softmax(jnp.dot(ffn_normed, router, precision=highest), axis=-1)
    own = lax.axis_index("dp")

    everyone_grad = lax.all_gather(grad_out, "dp", tiled=True)
    named = jnp.any(routes[:, :, None] == jnp.arange(128, dtype=jnp.int32)[None, None, :], axis=1)
    dense_gates = jnp.where(
        named, jnp.pad(router_probs, ((0, 0), (0, 128 - experts))), -1.0
    )
    everyone_ffn, everyone_gates = gather_all([ffn_bf, dense_gates])
    everyone_ffn = everyone_ffn.reshape(devices * rows_here, features)
    own_probs = lax.dynamic_slice_in_dim(everyone_gates, own, 1, 2).reshape(devices, rows_here)
    chooses = own_probs >= 0.0
    own_gates = jnp.where(chooses, own_probs, 0.0)
    upto = (places[:, None] <= places[None, :]).astype(jnp.bfloat16)
    slot = jnp.dot(chooses.astype(jnp.bfloat16), upto, preferred_element_type=jnp.float32) - 1.0
    slots = jnp.arange(capacity, dtype=jnp.float32)
    picked = chooses[:, None, :] & (slot[:, None, :] == slots[None, :, None])
    pick = picked.astype(jnp.bfloat16)
    slot_gates = jnp.sum(jnp.where(picked, own_gates[:, None, :], 0.0), axis=2).reshape(-1, 1)

    def pick_rows(values):
        blocks = values.reshape(devices, rows_here, features)
        return jnp.einsum(
            "jst,jtc->jsc", pick, blocks, preferred_element_type=jnp.float32
        ).astype(jnp.bfloat16).reshape(devices * capacity, features)

    def put_rows(values, hidden_parts, weights):
        blocks = values.astype(jnp.bfloat16).reshape(devices, capacity, features)
        left = jnp.concatenate(
            [pick.transpose(0, 2, 1)]
            + [h.reshape(devices, rows_here, h.shape[1]) for h in hidden_parts],
            axis=2,
        )
        right = jnp.concatenate(
            [blocks]
            + [
                jnp.broadcast_to(w.T[None], (devices, w.shape[1], features))
                for w in weights
            ],
            axis=1,
        )
        return (
            jnp.einsum("jtk,jkc->jtc", left, right, preferred_element_type=jnp.float32)
            .astype(jnp.bfloat16)
            .reshape(devices * rows_here, features)
        )

    expert_rows = pick_rows(everyone_ffn)
    grad_picked = pick_rows(everyone_grad)
    grad_rows = (slot_gates * grad_picked.astype(jnp.float32)).astype(jnp.bfloat16)

    gate_pre = jnp.dot(expert_rows, expert_gate[0], preferred_element_type=jnp.float32)
    up_pre = jnp.dot(expert_rows, expert_up[0], preferred_element_type=jnp.float32)
    gate_act, gate_slope = swish_parts(gate_pre)
    expert_hidden = (gate_act * up_pre).astype(jnp.bfloat16)
    expert_result = contract_last(expert_hidden, expert_down[0])
    slot_grads = jnp.sum(grad_picked.astype(jnp.float32) * expert_result, axis=1)
    grad_expert_down = contract_first(grad_rows, expert_hidden)[None]
    grad_expert_hidden = jnp.dot(grad_rows, expert_down[0], preferred_element_type=jnp.float32)
    grad_gate_pre = (grad_expert_hidden * up_pre * gate_slope).astype(jnp.bfloat16)
    grad_up_pre = (grad_expert_hidden * gate_act).astype(jnp.bfloat16)
    grad_expert_gate = contract_first(expert_rows, grad_gate_pre)[None]
    grad_expert_up = contract_first(expert_rows, grad_up_pre)[None]
    grad_rows_in = contract_last(grad_gate_pre, expert_gate[0]) + contract_last(
        grad_up_pre, expert_up[0]
    )

    part = shared_gate.shape[1] // devices
    part_gate = lax.dynamic_slice_in_dim(shared_gate, own * part, part, 1)
    part_up = lax.dynamic_slice_in_dim(shared_up, own * part, part, 1)
    part_down = lax.dynamic_slice_in_dim(shared_down, own * part, part, 1)
    shared_pre_gate = jnp.dot(everyone_ffn, part_gate, preferred_element_type=jnp.float32)
    shared_pre_up = jnp.dot(everyone_ffn, part_up, preferred_element_type=jnp.float32)
    shared_act, shared_slope = swish_parts(shared_pre_gate)
    shared_hidden = (shared_act * shared_pre_up).astype(jnp.bfloat16)
    grad_shared_hidden = jnp.dot(everyone_grad, part_down, preferred_element_type=jnp.float32)
    grad_shared_gate_pre = (grad_shared_hidden * shared_pre_up * shared_slope).astype(jnp.bfloat16)
    grad_shared_up_pre = (grad_shared_hidden * shared_act).astype(jnp.bfloat16)
    shared_grads = jnp.concatenate(
        [
            contract_first(everyone_ffn, grad_shared_gate_pre),
            contract_first(everyone_ffn, grad_shared_up_pre),
            contract_first(everyone_grad, shared_hidden),
        ],
        axis=1,
    ).astype(jnp.bfloat16)
    share_rows = features // devices
    shared_grads = lax.all_to_all(
        shared_grads.reshape(devices, share_rows, 3 * part), "dp", split_axis=0, concat_axis=0
    ).astype(jnp.float32)
    grad_shared_gate, grad_shared_up, grad_shared_down = (
        shared_grads[:, :, i * part : (i + 1) * part]
        .transpose(1, 0, 2)
        .reshape(share_rows, devices * part)
        for i in range(3)
    )

    grad_top = grad_out.astype(jnp.float32)
    ffn_part = put_rows(slot_gates * expert_result, [shared_hidden], [part_down])
    ffn_total = lax.psum_scatter(ffn_part, "dp", scatter_dimension=0, tiled=True)
    ffn_total = lax.psum(ffn_total, "tensor").astype(jnp.float32)
    output = (hidden + ffn_total).astype(jnp.bfloat16)
    pair_grads = jnp.sum(
        jnp.where(picked, slot_grads.reshape(devices, capacity, 1), 0.0), axis=1
    ).reshape(devices * rows_here, 1)
    pair_high = pair_grads.astype(jnp.bfloat16).astype(jnp.float32)
    column = jnp.arange(128, dtype=jnp.int32)[None, :]
    pair_columns = jnp.where(
        column == own,
        pair_high,
        jnp.where(column == own + experts, pair_grads - pair_high, 0.0),
    )
    grad_ffn_in = put_rows(
        grad_rows_in, [grad_shared_gate_pre, grad_shared_up_pre], [part_gate, part_up]
    )
    (grad_ffn_sum,) = sum_home(
        [
            jnp.concatenate([grad_ffn_in, pair_columns.astype(jnp.bfloat16)], axis=1).reshape(
                devices, rows_here, features + 128
            )
        ],
        3,
        True,
    )
    dense_grad = (
        grad_ffn_sum[:, features : features + experts]
        + grad_ffn_sum[:, features + experts : features + 2 * experts]
    )
    grad_logits = router_probs * (
        dense_grad - jnp.sum(router_probs * dense_grad, axis=-1, keepdims=True)
    )
    grad_router_in = contract_last(grad_logits, router, highest)
    grad_router_part = contract_first(ffn_normed, grad_logits, highest)
    grad_ffn_total = grad_ffn_sum[:, :features] + grad_router_in
    grad_g_ffn = jnp.sum(grad_ffn_total * ffn_unit, axis=0)
    grad_hidden = grad_top + normalize_back(grad_ffn_total, ffn_unit, ffn_factor, g_ffn)
    grad_hidden_bf = grad_hidden.astype(jnp.bfloat16)
    grad_w_out = contract_first(grad_hidden_bf, context)
    grad_context = jnp.dot(grad_hidden_bf, w_out, preferred_element_type=jnp.float32).astype(
        jnp.bfloat16
    )
    grad_context = grad_context.reshape(rows_here, heads_local, VALUE_HEAD_SIZE)
    redone = jnp.exp(masked_scores() - log_total)
    redone_bf = redone.astype(jnp.bfloat16)
    grad_weights = jnp.einsum(
        "thd,shd->hts", grad_context, value, preferred_element_type=jnp.float32
    )
    grad_value = jnp.einsum(
        "hts,thd->shd", redone_bf, grad_context, preferred_element_type=jnp.float32
    )
    row_inner = jnp.sum(redone * grad_weights, axis=-1, keepdims=True)
    grad_raw = (redone * (grad_weights - row_inner) * softmax_scale).astype(jnp.bfloat16)
    grad_query_nope = jnp.einsum(
        "hts,shd->thd", grad_raw, key_nope, preferred_element_type=jnp.float32
    )
    grad_query_rot = jnp.einsum(
        "hts,sd->thd", grad_raw, key_turned_part, preferred_element_type=jnp.float32
    )
    grad_key_nope = jnp.einsum(
        "hts,thd->shd",
        grad_raw,
        query_bf[..., :PLAIN_HEAD_SIZE],
        preferred_element_type=jnp.float32,
    )
    grad_key_rot = jnp.einsum(
        "hts,thd->sd", grad_raw, query_bf[..., PLAIN_HEAD_SIZE:], preferred_element_type=jnp.float32
    )
    grad_query = jnp.concatenate(
        [grad_query_nope, apply_rotation(grad_query_rot, -token_position)], axis=-1
    )
    grad_query = grad_query.reshape(rows_here, heads_local * QK).astype(jnp.bfloat16)
    grad_w_query = contract_first(normed_bf, grad_query)
    grad_key_value = (
        jnp.concatenate([grad_key_nope, grad_value], axis=-1)
        .reshape(rows_here, heads_local * (PLAIN_HEAD_SIZE + VALUE_HEAD_SIZE))
        .astype(jnp.bfloat16)
    )
    grad_w_kv_up = contract_first(latent_bf, grad_key_value)
    grad_latent_normed = contract_last(grad_key_value, key_value_up_weight)
    grad_latent_part = jnp.concatenate(
        [grad_latent_normed, apply_rotation(grad_key_rot, -token_position)], axis=1
    ).astype(jnp.bfloat16)
    grad_in_summed, grad_latent_sum = product_sum(grad_query, w_query, [grad_latent_part], 4)
    grad_latent_normed = grad_latent_sum[:, :LATENT_RANK]
    grad_g_kv = jnp.sum(grad_latent_normed * latent_unit_scale, axis=0)
    grad_latent = normalize_back(
        grad_latent_normed, latent_unit_scale, latent_norm_factor, latent_norm_gain
    )
    grad_down = jnp.concatenate([grad_latent, grad_latent_sum[:, LATENT_RANK:]], axis=1)
    grad_down_bf = grad_down.astype(jnp.bfloat16)
    share = grad_down.shape[1] // lax.axis_size("tensor")
    grad_columns = lax.dynamic_slice_in_dim(
        grad_down_bf, lax.axis_index("tensor") * share, share, 1
    )
    grad_w_kv_down = contract_first(normed_bf, grad_columns)
    grad_attn_in = grad_in_summed + contract_last(grad_down_bf, key_value_down_weight)
    grad_g_attn = jnp.sum(grad_attn_in * attn_unit, axis=0)
    grad_tokens = grad_hidden + normalize_back(grad_attn_in, attn_unit, attn_factor, g_attn)
    vectors = jnp.concatenate(
        [
            grad_router_part,
            grad_g_attn[:, None],
            grad_g_ffn[:, None],
            jnp.pad(
                grad_g_kv.reshape(devices, -1), ((0, 0), (0, share_rows - LATENT_RANK // devices))
            ).reshape(-1, 1),
            jnp.zeros((features, 128 - experts - 3), jnp.float32),
        ],
        axis=1,
    )
    blocks = [
        a.astype(jnp.bfloat16).reshape(devices, a.shape[0] // devices, a.shape[1])
        for a in (grad_w_query, grad_w_out, grad_w_kv_up, grad_w_kv_down)
    ]
    grad_w_query, grad_w_out, grad_w_kv_up, grad_w_kv_down, vectors = sum_home(
        blocks + [vectors.reshape(devices, share_rows, 128)], 5
    )
    rank, ranks = lax.axis_index("tensor"), lax.axis_size("tensor")
    router_rows = share_rows // ranks
    grad_router = lax.dynamic_slice_in_dim(vectors[:, :experts], rank * router_rows, router_rows, 0)
    latent_rows = LATENT_RANK // devices // ranks
    grad_g_kv = lax.dynamic_slice_in_dim(
        vectors[:, experts + 2], rank * latent_rows, latent_rows, 0
    )
    return (
        output,
        grad_tokens,
        vectors[:, experts],
        grad_w_query,
        grad_w_kv_down,
        grad_g_kv,
        grad_w_kv_up,
        grad_w_out,
        vectors[:, experts + 1],
        grad_router,
        grad_shared_gate,
        grad_shared_up,
        grad_shared_down,
        grad_expert_gate,
        grad_expert_up,
        grad_expert_down,
    )


def solution(mesh):
    in_specs = (
        P("dp", None),
        P("dp", None),
        P("dp", None),
        P("dp", None),
        P(),
        P(None, "tensor"),
        P(),
        P(),
        P(None, "tensor"),
        P(None, "tensor"),
        P(),
        P(),
        P(None, "tensor"),
        P(None, "tensor"),
        P(None, "tensor"),
        P("dp", None, "tensor"),
        P("dp", None, "tensor"),
        P("dp", None, "tensor"),
    )
    out_specs = (
        P("dp", None),
        P("dp", None),
        P("dp"),
        P("dp", "tensor"),
        P("dp", "tensor"),
        P(("dp", "tensor")),
        P("dp", "tensor"),
        P("dp", "tensor"),
        P("dp"),
        P(("dp", "tensor"), None),
        P("dp", "tensor"),
        P("dp", "tensor"),
        P("dp", "tensor"),
        P("dp", None, "tensor"),
        P("dp", None, "tensor"),
        P("dp", None, "tensor"),
    )
    return jax.shard_map(shards, mesh=mesh, in_specs=in_specs, out_specs=out_specs, check_vma=False)
```

```python
import functools

import jax
import jax.numpy as jnp
from jax import lax
from jax.experimental import pallas as pl
from jax.experimental.pallas import tpu as pltpu
from jax.sharding import PartitionSpec as P

PLAIN_HEAD_SIZE = 128
VALUE_HEAD_SIZE = 128
QK = 192
LATENT_RANK = 512
TOPK = 6


epsilon = 1e-06


def rms_normalize_pieces(values, gain):
    factor = lax.rsqrt(jnp.mean(values * values, axis=-1, keepdims=True) + epsilon)
    unit = values * factor
    return (unit * gain, unit, factor)


def normalize_back(grad, unit, factor, gain):
    inner = grad * gain
    return factor * (inner - unit * jnp.mean(inner * unit, axis=-1, keepdims=True))


def apply_rotation(values, token_position):
    half = values.shape[-1] // 2
    freqs = 10000.0 ** (-jnp.arange(half, dtype=jnp.float32) / half)
    angles = token_position.astype(jnp.float32)[:, None] * freqs[None, :]
    shape = (angles.shape[0],) + (1,) * (values.ndim - 2) + (half,)
    cosine = jnp.cos(angles).reshape(shape)
    sine = jnp.sin(angles).reshape(shape)
    first = values[..., :half]
    second = values[..., half:]
    return jnp.concatenate(
        [first * cosine - second * sine, second * cosine + first * sine], axis=-1
    )


def doc_layout(lengths_row, rows_here):
    ends = jnp.cumsum(lengths_row)
    starts = ends - lengths_row
    places = jnp.arange(rows_here, dtype=jnp.int32)
    segment = jnp.sum((places[:, None] >= ends[None, :]).astype(jnp.int32), axis=1)
    member = segment[:, None] == jnp.arange(lengths_row.shape[0], dtype=jnp.int32)[None, :]
    begins = jnp.sum(jnp.where(member, starts[None, :], 0), axis=1)
    return (segment, places - begins)


def contract_last(left, right, precision=None):
    return lax.dot_general(
        left,
        right,
        (((1,), (1,)), ((), ())),
        precision=precision,
        preferred_element_type=jnp.float32,
    )


def contract_first(left, right, precision=None):
    return lax.dot_general(
        left,
        right,
        (((0,), (0,)), ((), ())),
        precision=precision,
        preferred_element_type=jnp.float32,
    )


def swish_parts(gate_pre):
    sigma = jax.nn.sigmoid(gate_pre)
    return (gate_pre * sigma, sigma * (1.0 + gate_pre * (1.0 - sigma)))


VMEM_LIMIT = 60 * 1024 * 1024


def place_of(x_size):
    me = lax.axis_index("dp")
    core = me % 2
    x = (me // 2) % x_size
    z = me // (2 * x_size)
    return z, x, core


def index_of(z, x, core, x_size):
    return (z * x_size + x) * 2 + core


def remote(src, dst, send_sem, recv_sem, target):
    return pltpu.make_async_remote_copy(
        src_ref=src,
        dst_ref=dst,
        send_sem=send_sem,
        recv_sem=recv_sem,
        device_id={"dp": target},
        device_id_type=pl.DeviceIdType.MESH,
    )


def greet(z, x, core, z_size, x_size, pair=False):
    barrier = pltpu.get_barrier_semaphore()

    def tell(target):
        pl.semaphore_signal(
            barrier, inc=1, device_id={"dp": target}, device_id_type=pl.DeviceIdType.MESH
        )

    tell(index_of(z, x, 1 - core, x_size))
    tell(index_of(z, 1 - x, core, x_size))

    @pl.when(z > 0)
    def _():
        tell(index_of(z - 1, x, core, x_size))

    @pl.when(z < z_size - 1)
    def _():
        tell(index_of(z + 1, x, core, x_size))

    inner = (z + z_size - 1) // z_size - z // (z_size - 1)
    if pair:
        pl.semaphore_signal(
            barrier,
            inc=1,
            device_id={"tensor": 1 - lax.axis_index("tensor")},
            device_id_type=pl.DeviceIdType.MESH,
        )
    pl.semaphore_wait(barrier, 3 + inner + (1 if pair else 0))


def add_into(dst, *srcs):
    rows = dst.shape[0]
    step = 32 if rows % 32 == 0 else 16

    def body(i, _):
        here = pl.ds(pl.multiple_of(i * step, step), step)
        total = dst[here, :].astype(jnp.float32)
        for src in srcs:
            total = total + src[here, :].astype(jnp.float32)
        dst[here, :] = total.astype(dst.dtype)
        return 0

    lax.fori_loop(0, rows // step, body, 0)


def scatter_kernel(x_size, parts, pair, *refs):
    z_size = 4
    ins, outs, refs = refs[:parts], refs[parts : 2 * parts], refs[2 * parts :]
    own, c_buf, x_buf, z_buf = (refs[i * parts : (i + 1) * parts] for i in range(4))
    refs = refs[4 * parts :]
    y_buf = None
    if pair:
        y_buf, y_s, y_r, refs = refs[:parts], refs[parts], refs[parts + 1], refs[parts + 2 :]
    l_sem, c_s, c_r, x_s, x_r, z_s, z_r = refs
    z, x, core = place_of(x_size)
    at = functools.partial(index_of, x_size=x_size)
    half = z // 2
    inner = ((z + 3) // 4) * ((6 - z) // 4)
    order = [3 - 3 * half, 2 - half, 1 - z + 4 * half, z]
    load = lambda p, w, v: pltpu.make_async_copy(
        ins[p].at[at(w, v, core)], own[p].at[w, v], l_sem.at[p, w, v]
    )
    beside = lambda p, w, v: remote(
        ins[p].at[at(w, v, 1 - core)],
        c_buf[p].at[w, v],
        c_s.at[p, w, v],
        c_r.at[p, w, v],
        at(z, x, 1 - core),
    )
    across = lambda p, w: remote(
        c_buf[p].at[w, 1 - x], x_buf[p].at[w], x_s.at[p, w], x_r.at[p, w], at(z, 1 - x, core)
    )

    def along(p, w, slot, target):
        return remote(
            c_buf[p].at[w, x], z_buf[p].at[slot], z_s.at[p, w], z_r.at[p, slot], at(target, x, core)
        )

    twin = lambda p: pltpu.make_async_remote_copy(
        src_ref=c_buf[p].at[z, x],
        dst_ref=y_buf[p],
        send_sem=y_s.at[p],
        recv_sem=y_r.at[p],
        device_id={"tensor": 1 - lax.axis_index("tensor")},
        device_id_type=pl.DeviceIdType.MESH,
    )

    for v in (1 - x, x):
        for w in order:
            for p in range(parts):
                load(p, w, v).start()
    greet(z, x, core, z_size, x_size, pair)
    for v in (1 - x, x):
        for w in order:
            for p in range(parts):
                beside(p, w, v).start()
    for w in order:
        for p in range(parts):
            load(p, w, 1 - x).wait()
            beside(p, w, 1 - x).wait_recv()
            add_into(c_buf[p].at[w, 1 - x], own[p].at[w, 1 - x])
            across(p, w).start()
    for k, w in enumerate(order):
        for p in range(parts):
            load(p, w, x).wait()
            beside(p, w, x).wait_recv()
            add_into(c_buf[p].at[w, x], own[p].at[w, x])
            across(p, w).wait_recv()
            if k < 3:

                @pl.when(inner == 1)
                def _():
                    along(p, w, w, z).wait_recv()
                    add_into(c_buf[p].at[w, x], x_buf[p].at[w], z_buf[p].at[w])

                @pl.when(inner == 0)
                def _():
                    add_into(c_buf[p].at[w, x], x_buf[p].at[w])

                @pl.when(w > z)
                def _():
                    along(p, w, w, z + 1).start()

                @pl.when(w < z - 1)
                def _():
                    along(p, w, w, z - 1).start()

                @pl.when(w == z - 1)
                def _():
                    along(p, w, z_size, z - 1).start()

            else:
                add_into(c_buf[p].at[w, x], x_buf[p].at[w])

                @pl.when(z > 0)
                def _():
                    along(p, w, z, z).wait_recv()
                    add_into(c_buf[p].at[w, x], z_buf[p].at[z])

                @pl.when(z < z_size - 1)
                def _():
                    along(p, w, z_size, z).wait_recv()
                    add_into(c_buf[p].at[w, x], z_buf[p].at[z_size])

                if pair:
                    twin(p).start()
                else:
                    outs[p][...] = c_buf[p][z, x].astype(outs[p].dtype)
    if pair:
        for p in range(parts):
            twin(p).wait()
            outs[p][...] = (
                c_buf[p][z, x].astype(jnp.float32) + y_buf[p][...].astype(jnp.float32)
            ).astype(outs[p].dtype)
    for w in range(z_size):
        for p in range(parts):
            for v in range(x_size):
                beside(p, w, v).wait_send()
            across(p, w).wait_send()

            @pl.when(z != w)
            def _():
                along(p, w, w, z).wait_send()


def scatter_sums(arrays, x_size, collective_id, out_dtype, pair=False):
    parts = len(arrays)
    dma = pltpu.SemaphoreType.DMA
    blocks = [a.shape[1:] for a in arrays]
    return pl.pallas_call(
        functools.partial(scatter_kernel, x_size, parts, pair),
        out_shape=[jax.ShapeDtypeStruct(b, out_dtype) for b in blocks],
        in_specs=[pl.BlockSpec(memory_space=pl.ANY)] * parts,
        out_specs=[pl.BlockSpec(memory_space=pltpu.VMEM)] * parts,
        scratch_shapes=[pltpu.VMEM((4, x_size) + b, a.dtype) for a, b in zip(arrays, blocks)]
        + [pltpu.VMEM((4, x_size) + b, a.dtype) for a, b in zip(arrays, blocks)]
        + [pltpu.VMEM((4,) + b, a.dtype) for a, b in zip(arrays, blocks)]
        + [pltpu.VMEM((5,) + b, a.dtype) for a, b in zip(arrays, blocks)]
        + ([pltpu.VMEM(b, a.dtype) for a, b in zip(arrays, blocks)] + [dma((parts,))] * 2 if pair else [])
        + [dma((parts, 4, x_size))] * 3
        + [dma((parts, 4))] * 3
        + [dma((parts, 5))],
        compiler_params=pltpu.CompilerParams(
            collective_id=collective_id, has_side_effects=True, vmem_limit_bytes=VMEM_LIMIT
        ),
        name="scatter_sums",
    )(*arrays)


def pair_kernel(chunks, extras, left, right, *refs):
    ins, total, outs = refs[:extras], refs[extras], refs[extras + 1 : 2 * extras + 1]
    sent, got, refs = refs[2 * extras + 1], refs[2 * extras + 2], refs[2 * extras + 3 :]
    e_got, (s_sem, r_sem, es_sem, er_sem) = refs[:extras], refs[extras:]
    width = total.shape[1] // chunks
    other = {"tensor": 1 - lax.axis_index("tensor")}
    barrier = pltpu.get_barrier_semaphore()
    pl.semaphore_signal(barrier, inc=1, device_id=other, device_id_type=pl.DeviceIdType.MESH)
    pl.semaphore_wait(barrier, 1)

    def copy(src, dst, send_sem, recv_sem):
        return pltpu.make_async_remote_copy(
            src_ref=src,
            dst_ref=dst,
            send_sem=send_sem,
            recv_sem=recv_sem,
            device_id=other,
            device_id_type=pl.DeviceIdType.MESH,
        )

    chunk = lambda i: copy(sent.at[i], got.at[i], s_sem.at[i], r_sem.at[i])
    extra = lambda i: copy(ins[i], e_got[i], es_sem.at[i], er_sem.at[i])
    for i in range(extras):
        extra(i).start()
    for i in range(chunks):
        sent[i] = lax.dot_general(
            left[...],
            right[pl.ds(i * width, width), :],
            (((1,), (1,)), ((), ())),
            preferred_element_type=jnp.float32,
        ).astype(jnp.bfloat16)
        chunk(i).start()
    for i in range(extras):
        extra(i).wait()
        outs[i][...] = ins[i][...].astype(jnp.float32) + e_got[i][...].astype(jnp.float32)
    for i in range(chunks):
        chunk(i).wait()
        total[:, pl.ds(i * width, width)] = sent[i].astype(jnp.float32) + got[i].astype(
            jnp.float32
        )


def pair_product(left, right, extras, collective_id, chunks=8):
    rows, columns = left.shape[0], right.shape[0]
    dma = pltpu.SemaphoreType.DMA
    vmem = pl.BlockSpec(memory_space=pltpu.VMEM)
    block = pltpu.VMEM((chunks, rows, columns // chunks), jnp.bfloat16)
    return pl.pallas_call(
        functools.partial(pair_kernel, chunks, len(extras)),
        out_shape=[jax.ShapeDtypeStruct((rows, columns), jnp.float32)]
        + [jax.ShapeDtypeStruct(e.shape, jnp.float32) for e in extras],
        in_specs=[vmem] * (2 + len(extras)),
        out_specs=[vmem] * (1 + len(extras)),
        scratch_shapes=[block, block]
        + [pltpu.VMEM(e.shape, e.dtype) for e in extras]
        + [dma((chunks,))] * 2
        + [dma((max(1, len(extras)),))] * 2,
        compiler_params=pltpu.CompilerParams(
            collective_id=collective_id, has_side_effects=True, vmem_limit_bytes=VMEM_LIMIT
        ),
        name="pair_product",
    )(left, right, *extras)


def nn(left, right):
    return lax.dot_general(
        left, right, (((1,), (0,)), ((), ())), preferred_element_type=jnp.float32
    )


def is_at(j, where):
    low = (3 - j) // 3
    high = j // 3
    return (low, (4 - j) // 3 - low, (j + 1) // 3 - high, high)[where]


def ffn_kernel(
    x_size,
    own_ffn,
    own_gates,
    grad_all,
    gate_t,
    up_t,
    down_t,
    shared_in,
    shared_out,
    out_part,
    dx_part,
    rows_all,
    dy_all,
    he_all,
    dge_all,
    due_all,
    shared_grads,
    blk,
    gts,
    gate_v,
    up_v,
    down_v,
    s_in,
    s_out,
    g_buf,
    rows_b,
    grow_b,
    dy_b,
    he_b,
    dge_b,
    due_b,
    out_r,
    dx_r,
    out_l,
    dx_l,
    out_st,
    dx_st,
    acc,
    gate_col,
    dgate_acc,
    own_sem,
    up_s,
    up_r,
    dn_s,
    dn_r,
    x_s,
    x_r,
    c_s,
    c_r,
    w_sem,
    g_sem,
    st_sem,
):
    z_size, bf16, f32 = 4, jnp.bfloat16, jnp.float32
    hidden = gate_t.shape[0]
    rows_here, features = own_ffn.shape
    slots = rows_b.shape[0] // 2
    wide = 512
    z, x, core = place_of(x_size)
    own = lax.axis_index("dp")
    at = functools.partial(index_of, x_size=x_size)
    ins, outs = (own_ffn, own_gates), (blk, gts)
    half = z // 2
    order = [z, 1 - z + 4 * half, 2 - half, 3 - 3 * half]

    def place(j):
        return sum(is_at(j, i) * order[i] for i in range(4))

    weights = [
        pltpu.make_async_copy(gate_t, gate_v.at[pl.ds(0, hidden)], w_sem.at[0]),
        pltpu.make_async_copy(up_t, up_v.at[pl.ds(0, hidden)], w_sem.at[1]),
        pltpu.make_async_copy(down_t, down_v.at[pl.ds(0, hidden)], w_sem.at[2]),
        pltpu.make_async_copy(shared_in, s_in, w_sem.at[3]),
        pltpu.make_async_copy(shared_out, s_out, w_sem.at[4]),
    ]
    keep = [
        pltpu.make_async_copy(ins[a], outs[a].at[at(z, x, core)], own_sem.at[a]) for a in range(2)
    ]

    def grad_copy(k):
        w, v = place(k // 2), x + (k % 2) * (1 - 2 * x)
        return pltpu.make_async_copy(
            grad_all.at[pl.ds(2 * (w * x_size + v), 2)], g_buf.at[k % 2], g_sem.at[k % 2]
        )

    for copy in keep + weights:
        copy.start()
    grad_copy(0).start()
    greet(z, x, core, z_size, x_size)

    def up(a, d):
        block = outs[a].at[at(z - d, x, core)]
        src = ins[a] if d == 0 else block
        return remote(src, block, up_s.at[a, d], up_r.at[a, d], at(z + 1, x, core))

    def down(a, d):
        block = outs[a].at[at(z + d, x, core)]
        src = ins[a] if d == 0 else block
        return remote(src, block, dn_s.at[a, d], dn_r.at[a, d], at(z - 1, x, core))

    def across(a, w, first=False):
        block = outs[a].at[at(w, x, core)]
        src = ins[a] if first else block
        return remote(src, block, x_s.at[a, w], x_r.at[a, w], at(z, 1 - x, core))

    def beside(a, w, v, first=False):
        block = outs[a].at[at(w, v, core)]
        src = ins[a] if first else block
        return remote(src, block, c_s.at[a, w, v], c_r.at[a, w, v], at(z, x, 1 - core))

    for a in (1, 0):
        beside(a, z, x, True).start()
        across(a, z, True).start()
        pl.when(z < z_size - 1)(lambda: up(a, 0).start())
        pl.when(z > 0)(lambda: down(a, 0).start())

    def pass_on(d):
        for a in (1, 0):

            @pl.when(z >= d)
            def _():
                up(a, d - 1).wait_recv()
                pl.when(z < z_size - 1)(lambda: up(a, d).start())
                across(a, z - d).start()
                beside(a, z - d, x).start()

            @pl.when(z + d < z_size)
            def _():
                down(a, d - 1).wait_recv()
                pl.when(z > 0)(lambda: down(a, d).start())
                across(a, z + d).start()
                beside(a, z + d, x).start()

    def from_across(w):
        for a in (1, 0):
            across(a, w).wait_recv()
            beside(a, w, 1 - x).start()

    gate_v[pl.ds(hidden, gate_v.shape[0] - hidden), :] = jnp.zeros(
        (gate_v.shape[0] - hidden, features), bf16
    )
    up_v[pl.ds(hidden, up_v.shape[0] - hidden), :] = jnp.zeros(
        (up_v.shape[0] - hidden, features), bf16
    )
    down_v[pl.ds(hidden, down_v.shape[0] - hidden), :] = jnp.zeros(
        (down_v.shape[0] - hidden, features), bf16
    )
    acc[...] = jnp.zeros(acc.shape, f32)
    for copy in weights:
        copy.wait()
    for a in range(2):
        out_r[a, pl.ds(slots, 128), :] = s_out[...]
        dx_r[a, pl.ds(slots, 256), :] = s_in[...]
    for copy in keep:
        copy.wait()
    lane = lax.broadcasted_iota(jnp.int32, (rows_here, 128), 1)
    earlier = lax.broadcasted_iota(jnp.int32, (rows_here, rows_here), 1)
    later = lax.broadcasted_iota(jnp.int32, (rows_here, rows_here), 0)
    upto = (earlier <= later).astype(bf16)
    slot_lane = lax.broadcasted_iota(jnp.int32, (rows_here, slots), 1).astype(f32)

    def staged(pair):
        return [
            pltpu.make_async_copy(src, dst.at[pair], st_sem.at[i])
            for i, (src, dst) in enumerate(
                [
                    (rows_b, rows_all),
                    (dy_b, dy_all),
                    (he_b, he_all),
                    (dge_b, dge_all),
                    (due_b, due_all),
                    (out_st, out_part),
                    (dx_st, dx_part),
                ]
            )
        ]

    def body(k, _):
        w, v = place(k // 2), x + (k % 2) * (1 - 2 * x)
        pair = w * x_size + v
        block = 2 * pair
        here = k % 2
        for r in range(1, 5):

            @pl.when(k == 2 * r - 1)
            def _():
                if r < 4:
                    pass_on(r)
                from_across(order[r - 1])

        grad_copy(k).wait()
        pl.when(k < 7)(lambda: grad_copy(k + 1).start())
        for a in (1, 0):
            beside(a, w, v).wait_recv()

        @pl.when(k > 0)
        def _():
            for copy in staged(pair):
                copy.wait()

        for a in range(2):
            gates = gts[block + a]
            count = nn(upto, (gates >= 0.0).astype(bf16))
            gate = jnp.sum(jnp.where(lane == own, gates, 0.0), axis=1, keepdims=True)
            slot = jnp.sum(jnp.where(lane == own, count, 0.0), axis=1, keepdims=True) - 1.0
            pick = ((slot_lane == slot) & (gate >= 0.0)).astype(f32).astype(bf16)
            out_l[a, :, pl.ds(0, slots)] = pick
            dx_l[a, :, pl.ds(0, slots)] = pick
            high = gate.astype(bf16).astype(f32)
            middle = (gate - high).astype(bf16).astype(f32)
            low = gate - high - middle
            parts = jnp.where(
                lane == 0, high, jnp.where(lane == 1, middle, jnp.where(lane == 2, low, 0.0))
            ).astype(bf16)
            picked = jnp.sum(contract_first(pick, parts), axis=1, keepdims=True)
            gate_col[pl.ds(a * slots, slots), :] = jnp.broadcast_to(picked, (slots, 128))

        def pick_rows(n, _):
            cols = pl.ds(pl.multiple_of(n * wide, wide), wide)
            for a in range(2):
                mine = pl.ds(a * slots, slots)
                pick = out_l[a, :, pl.ds(0, slots)]
                rows_b[mine, cols] = contract_first(pick, blk[block + a, :, cols]).astype(bf16)
                grows = contract_first(pick, g_buf[here, a, :, cols])
                grow_b[mine, cols] = grows.astype(bf16)
                dy_b[mine, cols] = (gate_col[mine, pl.ds(0, 1)] * grows).astype(bf16)
            return 0

        lax.fori_loop(0, features // wide, pick_rows, 0)

        for a in range(2):
            pre = contract_last(blk[block + a], s_in[...])
            grad_hidden = contract_last(g_buf[here, a], s_out[...])
            act, slope = swish_parts(pre[:, :128])
            up_pre = pre[:, 128:]
            out_l[a, :, pl.ds(slots, 128)] = (act * up_pre).astype(bf16)
            dx_l[a, :, pl.ds(slots, 128)] = (grad_hidden * up_pre * slope).astype(bf16)
            dx_l[a, :, pl.ds(slots + 128, 128)] = (grad_hidden * act).astype(bf16)

        def shared_weights(n, _):
            cols = pl.ds(pl.multiple_of(n * wide, wide), wide)
            for a in range(2):
                acc[pl.ds(0, 256), cols] += contract_first(
                    dx_l[a, :, pl.ds(slots, 256)], blk[block + a, :, cols]
                )
                acc[pl.ds(256, 128), cols] += contract_first(
                    out_l[a, :, pl.ds(slots, 128)], g_buf[here, a, :, cols]
                )
            return 0

        lax.fori_loop(0, features // wide, shared_weights, 0)

        def hidden_units(n, _):
            units = pl.ds(pl.multiple_of(n * 256, 256), 256)
            gate_pre = contract_last(rows_b[...], gate_v[units, :])
            up_pre = contract_last(rows_b[...], up_v[units, :])
            grad_hidden = contract_last(dy_b[...], down_v[units, :])
            act, slope = swish_parts(gate_pre)
            he_b[:, units] = (act * up_pre).astype(bf16)
            dge_b[:, units] = (grad_hidden * up_pre * slope).astype(bf16)
            due_b[:, units] = (grad_hidden * act).astype(bf16)
            return 0

        lax.fori_loop(0, gate_v.shape[0] // 256, hidden_units, 0)
        dgate_acc[...] = jnp.zeros(dgate_acc.shape, f32)

        def back(n, _):
            cols = pl.ds(pl.multiple_of(n * wide, wide), wide)
            result = nn(he_b[...], down_v[:, cols])
            product = grow_b[:, cols].astype(f32) * result
            for i in range(wide // 128):
                dgate_acc[...] += product[:, i * 128 : (i + 1) * 128]
            result = (gate_col[:, pl.ds(0, 1)] * result).astype(bf16)
            grad_in = (nn(dge_b[...], gate_v[:, cols]) + nn(due_b[...], up_v[:, cols])).astype(bf16)
            for a in range(2):
                mine = slice(a * slots, (a + 1) * slots)
                out_r[a, pl.ds(0, slots), cols] = result[mine]
                dx_r[a, pl.ds(0, slots), cols] = grad_in[mine]
                out_st[a, :, cols] = nn(out_l[a], out_r[a, :, cols]).astype(bf16)
                dx_st[a, :, cols] = nn(dx_l[a], dx_r[a, :, cols]).astype(bf16)
            return 0

        lax.fori_loop(0, features // wide, back, 0)
        dgate = jnp.sum(dgate_acc[...], axis=1, keepdims=True)
        high = dgate.astype(bf16).astype(f32)
        spread = lax.broadcasted_iota(jnp.int32, (2 * slots, 128), 1)
        spread = jnp.where(
            spread == own, high, jnp.where(spread == own + 16, dgate - high, 0.0)
        ).astype(bf16)
        for a in range(2):
            dx_st[a, :, pl.ds(features, 128)] = nn(
                out_l[a, :, pl.ds(0, slots)], spread[a * slots : (a + 1) * slots]
            ).astype(bf16)
        for copy in staged(pair):
            copy.start()
        return 0

    lax.fori_loop(0, 8, body, 0)
    for copy in staged(0):
        copy.wait()
    shared_grads[...] = acc[...].astype(bf16)
    for a in range(2):
        for w in range(z_size):
            for v in range(x_size):
                beside(a, w, v).wait_send()
            across(a, w).wait_send()
    for d in range(z_size):
        for a in range(2):
            pl.when((z >= d) & (z < z_size - 1))(lambda: up(a, d).wait_send())
            pl.when((z + d < z_size) & (z > 0))(lambda: down(a, d).wait_send())


def ffn_tuned(own_ffn, own_gates, grad_all, gate_t, up_t, down_t, shared_in, shared_out, slots):
    rows, features = own_ffn.shape
    hidden = gate_t.shape[0]
    padded = -(-hidden // 256) * 256
    bf16, f32, dma = jnp.bfloat16, jnp.float32, pltpu.SemaphoreType.DMA
    anywhere = pl.BlockSpec(memory_space=pl.ANY)
    shape = jax.ShapeDtypeStruct
    return pl.pallas_call(
        functools.partial(ffn_kernel, 2),
        out_shape=[
            shape((8, 2, rows, features), bf16),
            shape((8, 2, rows, features + 128), bf16),
            shape((8, 2 * slots, features), bf16),
            shape((8, 2 * slots, features), bf16),
            shape((8, 2 * slots, padded), bf16),
            shape((8, 2 * slots, padded), bf16),
            shape((8, 2 * slots, padded), bf16),
            shape((384, features), bf16),
        ],
        in_specs=[anywhere] * 8,
        out_specs=[anywhere] * 7 + [pl.BlockSpec(memory_space=pltpu.VMEM)],
        scratch_shapes=[
            pltpu.VMEM((16, rows, features), bf16),
            pltpu.VMEM((16, rows, 128), f32),
            pltpu.VMEM((padded, features), bf16),
            pltpu.VMEM((padded, features), bf16),
            pltpu.VMEM((padded, features), bf16),
            pltpu.VMEM((256, features), bf16),
            pltpu.VMEM((128, features), bf16),
            pltpu.VMEM((2, 2, rows, features), bf16),
            pltpu.VMEM((2 * slots, features), bf16),
            pltpu.VMEM((2 * slots, features), bf16),
            pltpu.VMEM((2 * slots, features), bf16),
            pltpu.VMEM((2 * slots, padded), bf16),
            pltpu.VMEM((2 * slots, padded), bf16),
            pltpu.VMEM((2 * slots, padded), bf16),
            pltpu.VMEM((2, slots + 128, features), bf16),
            pltpu.VMEM((2, slots + 256, features), bf16),
            pltpu.VMEM((2, rows, slots + 128), bf16),
            pltpu.VMEM((2, rows, slots + 256), bf16),
            pltpu.VMEM((2, rows, features), bf16),
            pltpu.VMEM((2, rows, features + 128), bf16),
            pltpu.VMEM((384, features), f32),
            pltpu.VMEM((2 * slots, 128), f32),
            pltpu.VMEM((2 * slots, 128), f32),
            dma((2,)),
        ]
        + [dma((2, 4))] * 6
        + [dma((2, 4, 2))] * 2
        + [dma((5,)), dma((2,)), dma((7,))],
        compiler_params=pltpu.CompilerParams(
            collective_id=1, has_side_effects=True, vmem_limit_bytes=VMEM_LIMIT
        ),
        name="ffn",
    )(
        own_ffn,
        own_gates,
        grad_all.reshape(16, rows, features),
        gate_t,
        up_t,
        down_t,
        shared_in,
        shared_out,
    )


def tuned():
    return lax.axis_size("dp") == 16 and lax.axis_size("tensor") == 2


def sum_home(arrays, collective_id, pair=False):
    if tuned():
        return scatter_sums(arrays, 2, collective_id, jnp.float32, pair)
    sums = [lax.psum_scatter(a, "dp", scatter_dimension=0) for a in arrays]
    if pair:
        sums = [lax.psum(a.astype(jnp.float32), "tensor") for a in sums]
    return [a.astype(jnp.float32) for a in sums]


def product_sum(left, right, extras, collective_id):
    if tuned():
        return pair_product(left, right, extras, collective_id)
    product = contract_last(left, right).astype(jnp.bfloat16)
    return [lax.psum(a, "tensor").astype(jnp.float32) for a in [product] + extras]


def ffn_with_kernel(own_ffn, gates, everyone_grad, weights, shared, capacity, experts):
    part = shared[0].shape[1]
    hidden, features = weights[0].shape[1], own_ffn.shape[1]
    gate_t, up_t, down_t = (jnp.pad(w.T, ((0, 128 - part), (0, 0))) for w in shared)
    out_part, grad_part, rows, dy, he, dge, due, shared_grads = ffn_tuned(
        own_ffn,
        gates,
        everyone_grad,
        *(w.T for w in weights),
        jnp.concatenate([gate_t, up_t], axis=0),
        down_t,
        capacity,
    )
    rows, dy = rows.reshape(-1, features), dy.reshape(-1, features)
    he, dge, due = (a.reshape(-1, a.shape[2])[:, :hidden] for a in (he, dge, due))
    devices, rows_here = everyone_grad.shape[:2]
    return (
        out_part.reshape(devices, rows_here, -1),
        grad_part.reshape(devices, rows_here, -1),
        contract_first(rows, dge)[None],
        contract_first(rows, due)[None],
        contract_first(dy, he)[None],
        shared_grads.reshape(3, 128, features)[:, :part].reshape(3 * part, features),
    )


def ffn_plain(own_ffn, gates, everyone_grad, weights, shared, capacity, experts):
    own, devices = lax.axis_index("dp"), lax.axis_size("dp")
    rows_here, features = own_ffn.shape
    places = jnp.arange(rows_here, dtype=jnp.int32)
    expert_gate, expert_up, expert_down = weights
    part_gate, part_up, part_down = shared
    everyone_ffn = lax.all_gather(own_ffn, "dp", tiled=True)
    everyone_gates = lax.all_gather(gates, "dp")
    everyone_grad = everyone_grad.reshape(devices * rows_here, features)
    own_probs = lax.dynamic_slice_in_dim(everyone_gates, own, 1, 2).reshape(devices, rows_here)
    chooses = own_probs >= 0.0
    own_gates = jnp.where(chooses, own_probs, 0.0)
    upto = (places[:, None] <= places[None, :]).astype(jnp.bfloat16)
    slot = jnp.dot(chooses.astype(jnp.bfloat16), upto, preferred_element_type=jnp.float32) - 1.0
    slots = jnp.arange(capacity, dtype=jnp.float32)
    picked = chooses[:, None, :] & (slot[:, None, :] == slots[None, :, None])
    pick = picked.astype(jnp.bfloat16)
    slot_gates = jnp.sum(jnp.where(picked, own_gates[:, None, :], 0.0), axis=2).reshape(-1, 1)

    def pick_rows(values):
        blocks = values.reshape(devices, rows_here, features)
        return jnp.einsum(
            "jst,jtc->jsc", pick, blocks, preferred_element_type=jnp.float32
        ).astype(jnp.bfloat16).reshape(devices * capacity, features)

    def put_rows(values, hidden_parts, weights):
        blocks = values.astype(jnp.bfloat16).reshape(devices, capacity, features)
        left = jnp.concatenate(
            [pick.transpose(0, 2, 1)]
            + [h.reshape(devices, rows_here, h.shape[1]) for h in hidden_parts],
            axis=2,
        )
        right = jnp.concatenate(
            [blocks]
            + [
                jnp.broadcast_to(w.T[None], (devices, w.shape[1], features))
                for w in weights
            ],
            axis=1,
        )
        return (
            jnp.einsum("jtk,jkc->jtc", left, right, preferred_element_type=jnp.float32)
            .astype(jnp.bfloat16)
            .reshape(devices * rows_here, features)
        )

    expert_rows = pick_rows(everyone_ffn)
    grad_picked = pick_rows(everyone_grad)
    grad_rows = (slot_gates * grad_picked.astype(jnp.float32)).astype(jnp.bfloat16)

    gate_pre = jnp.dot(expert_rows, expert_gate, preferred_element_type=jnp.float32)
    up_pre = jnp.dot(expert_rows, expert_up, preferred_element_type=jnp.float32)
    gate_act, gate_slope = swish_parts(gate_pre)
    expert_hidden = (gate_act * up_pre).astype(jnp.bfloat16)
    expert_result = contract_last(expert_hidden, expert_down)
    slot_grads = jnp.sum(grad_picked.astype(jnp.float32) * expert_result, axis=1)
    grad_expert_down = contract_first(grad_rows, expert_hidden)[None]
    grad_expert_hidden = jnp.dot(grad_rows, expert_down, preferred_element_type=jnp.float32)
    grad_gate_pre = (grad_expert_hidden * up_pre * gate_slope).astype(jnp.bfloat16)
    grad_up_pre = (grad_expert_hidden * gate_act).astype(jnp.bfloat16)
    grad_expert_gate = contract_first(expert_rows, grad_gate_pre)[None]
    grad_expert_up = contract_first(expert_rows, grad_up_pre)[None]
    grad_rows_in = contract_last(grad_gate_pre, expert_gate) + contract_last(
        grad_up_pre, expert_up
    )

    shared_pre_gate = jnp.dot(everyone_ffn, part_gate, preferred_element_type=jnp.float32)
    shared_pre_up = jnp.dot(everyone_ffn, part_up, preferred_element_type=jnp.float32)
    shared_act, shared_slope = swish_parts(shared_pre_gate)
    shared_hidden = (shared_act * shared_pre_up).astype(jnp.bfloat16)
    grad_shared_hidden = jnp.dot(everyone_grad, part_down, preferred_element_type=jnp.float32)
    grad_shared_gate_pre = (grad_shared_hidden * shared_pre_up * shared_slope).astype(jnp.bfloat16)
    grad_shared_up_pre = (grad_shared_hidden * shared_act).astype(jnp.bfloat16)
    shared_grads = jnp.concatenate(
        [
            contract_first(grad_shared_gate_pre, everyone_ffn),
            contract_first(grad_shared_up_pre, everyone_ffn),
            contract_first(shared_hidden, everyone_grad),
        ],
        axis=0,
    ).astype(jnp.bfloat16)
    ffn_part = put_rows(slot_gates * expert_result, [shared_hidden], [part_down])
    pair_grads = jnp.sum(
        jnp.where(picked, slot_grads.reshape(devices, capacity, 1), 0.0), axis=1
    ).reshape(devices * rows_here, 1)
    pair_high = pair_grads.astype(jnp.bfloat16).astype(jnp.float32)
    column = jnp.arange(128, dtype=jnp.int32)[None, :]
    pair_columns = jnp.where(
        column == own,
        pair_high,
        jnp.where(column == own + experts, pair_grads - pair_high, 0.0),
    )
    grad_ffn_in = put_rows(
        grad_rows_in, [grad_shared_gate_pre, grad_shared_up_pre], [part_gate, part_up]
    )
    grad_part = jnp.concatenate([grad_ffn_in, pair_columns.astype(jnp.bfloat16)], axis=1)
    return (
        ffn_part.reshape(devices, rows_here, -1),
        grad_part.reshape(devices, rows_here, -1),
        grad_expert_gate,
        grad_expert_up,
        grad_expert_down,
        shared_grads,
    )


def shards(
    tokens,
    lengths,
    routes,
    grad_out,
    g_attn,
    w_query,
    key_value_down_weight,
    latent_norm_gain,
    key_value_up_weight,
    w_out,
    g_ffn,
    router,
    shared_gate,
    shared_up,
    shared_down,
    expert_gate,
    expert_up,
    expert_down,
):
    rows_here = tokens.shape[0]
    features = tokens.shape[1]
    heads_local = w_out.shape[1] // VALUE_HEAD_SIZE
    devices = lax.axis_size("dp")
    capacity = rows_here * TOPK * 4 // (3 * devices)
    experts = router.shape[1]
    highest = lax.Precision.HIGHEST
    softmax_scale = QK ** (-0.5)
    segment, token_position = doc_layout(lengths[0], rows_here)
    places = jnp.arange(rows_here, dtype=jnp.int32)
    allowed = (segment[:, None] == segment[None, :]) & (places[None, :] <= places[:, None])
    tokens_f = tokens.astype(jnp.float32)
    attn_normed, attn_unit, attn_factor = rms_normalize_pieces(tokens_f, g_attn)
    normed_bf = attn_normed.astype(jnp.bfloat16)
    query_full = jnp.dot(normed_bf, w_query, preferred_element_type=jnp.float32).reshape(
        rows_here, heads_local, QK
    )
    query_bf = jnp.concatenate(
        [
            query_full[..., :PLAIN_HEAD_SIZE],
            apply_rotation(query_full[..., PLAIN_HEAD_SIZE:], token_position),
        ],
        axis=-1,
    ).astype(jnp.bfloat16)
    latent_with_key = jnp.dot(normed_bf, key_value_down_weight, preferred_element_type=jnp.float32)
    key_turned_part = apply_rotation(latent_with_key[:, LATENT_RANK:], token_position).astype(
        jnp.bfloat16
    )
    latent_after_norm, latent_unit_scale, latent_norm_factor = rms_normalize_pieces(
        latent_with_key[:, :LATENT_RANK], latent_norm_gain
    )
    latent_bf = latent_after_norm.astype(jnp.bfloat16)
    key_value = (
        jnp.dot(latent_bf, key_value_up_weight, preferred_element_type=jnp.float32)
        .astype(jnp.bfloat16)
        .reshape(rows_here, heads_local, PLAIN_HEAD_SIZE + VALUE_HEAD_SIZE)
    )
    key_nope = key_value[..., :PLAIN_HEAD_SIZE]
    value = key_value[..., PLAIN_HEAD_SIZE:]

    def masked_scores():
        raw = jnp.einsum(
            "thd,shd->hts",
            query_bf[..., :PLAIN_HEAD_SIZE],
            key_nope,
            preferred_element_type=jnp.float32,
        )
        raw = raw + jnp.einsum(
            "thd,sd->hts",
            query_bf[..., PLAIN_HEAD_SIZE:],
            key_turned_part,
            preferred_element_type=jnp.float32,
        )
        return jnp.where(allowed[None], raw * softmax_scale, -jnp.inf)

    scores = masked_scores()
    top_score = jnp.max(scores, axis=-1, keepdims=True)
    expo = jnp.exp(scores - top_score)
    total = jnp.sum(expo, axis=-1, keepdims=True)
    log_total = top_score + jnp.log(total)
    attn_weights = (expo / total).astype(jnp.bfloat16)
    context = jnp.einsum("hts,shd->thd", attn_weights, value, preferred_element_type=jnp.float32)
    context = context.astype(jnp.bfloat16).reshape(rows_here, heads_local * VALUE_HEAD_SIZE)
    (attn,) = product_sum(context, w_out, [], 2)
    hidden = tokens_f + attn
    ffn_normed, ffn_unit, ffn_factor = rms_normalize_pieces(hidden, g_ffn)
    ffn_bf = ffn_normed.astype(jnp.bfloat16)
    router_probs = jax.nn.softmax(jnp.dot(ffn_normed, router, precision=highest), axis=-1)
    own = lax.axis_index("dp")

    named = jnp.any(routes[:, :, None] == jnp.arange(128, dtype=jnp.int32)[None, None, :], axis=1)
    dense_gates = jnp.where(named, jnp.pad(router_probs, ((0, 0), (0, 128 - experts))), -1.0)
    everyone_grad = lax.all_gather(grad_out, "dp")
    part = shared_gate.shape[1] // devices
    shared_parts = [
        lax.dynamic_slice_in_dim(w, own * part, part, 1)
        for w in (shared_gate, shared_up, shared_down)
    ]
    feed_forward = ffn_with_kernel if tuned() else ffn_plain
    (
        ffn_part,
        grad_ffn_part,
        grad_expert_gate,
        grad_expert_up,
        grad_expert_down,
        shared_grads,
    ) = feed_forward(
        ffn_bf,
        dense_gates,
        everyone_grad,
        [w[0] for w in (expert_gate, expert_up, expert_down)],
        shared_parts,
        capacity,
        experts,
    )
    share_rows = features // devices
    shared_grads = lax.all_to_all(
        shared_grads.reshape(3 * part, devices, share_rows).transpose(1, 2, 0),
        "dp",
        split_axis=0,
        concat_axis=0,
    ).astype(jnp.float32)
    grad_shared_gate, grad_shared_up, grad_shared_down = (
        shared_grads[:, :, i * part : (i + 1) * part]
        .transpose(1, 0, 2)
        .reshape(share_rows, devices * part)
        for i in range(3)
    )

    grad_top = grad_out.astype(jnp.float32)
    ffn_total = lax.psum_scatter(
        ffn_part.reshape(devices * rows_here, features), "dp", scatter_dimension=0, tiled=True
    )
    ffn_total = lax.psum(ffn_total, "tensor").astype(jnp.float32)
    output = (hidden + ffn_total).astype(jnp.bfloat16)
    (grad_ffn_sum,) = sum_home([grad_ffn_part], 3, True)
    dense_grad = (
        grad_ffn_sum[:, features : features + experts]
        + grad_ffn_sum[:, features + experts : features + 2 * experts]
    )
    grad_logits = router_probs * (
        dense_grad - jnp.sum(router_probs * dense_grad, axis=-1, keepdims=True)
    )
    grad_router_in = contract_last(grad_logits, router, highest)
    grad_router_part = contract_first(ffn_normed, grad_logits, highest)
    grad_ffn_total = grad_ffn_sum[:, :features] + grad_router_in
    grad_g_ffn = jnp.sum(grad_ffn_total * ffn_unit, axis=0)
    grad_hidden = grad_top + normalize_back(grad_ffn_total, ffn_unit, ffn_factor, g_ffn)
    grad_hidden_bf = grad_hidden.astype(jnp.bfloat16)
    grad_w_out = contract_first(grad_hidden_bf, context)
    grad_context = jnp.dot(grad_hidden_bf, w_out, preferred_element_type=jnp.float32).astype(
        jnp.bfloat16
    )
    grad_context = grad_context.reshape(rows_here, heads_local, VALUE_HEAD_SIZE)
    redone = jnp.exp(masked_scores() - log_total)
    redone_bf = redone.astype(jnp.bfloat16)
    grad_weights = jnp.einsum(
        "thd,shd->hts", grad_context, value, preferred_element_type=jnp.float32
    )
    grad_value = jnp.einsum(
        "hts,thd->shd", redone_bf, grad_context, preferred_element_type=jnp.float32
    )
    row_inner = jnp.sum(redone * grad_weights, axis=-1, keepdims=True)
    grad_raw = (redone * (grad_weights - row_inner) * softmax_scale).astype(jnp.bfloat16)
    grad_query_nope = jnp.einsum(
        "hts,shd->thd", grad_raw, key_nope, preferred_element_type=jnp.float32
    )
    grad_query_rot = jnp.einsum(
        "hts,sd->thd", grad_raw, key_turned_part, preferred_element_type=jnp.float32
    )
    grad_key_nope = jnp.einsum(
        "hts,thd->shd",
        grad_raw,
        query_bf[..., :PLAIN_HEAD_SIZE],
        preferred_element_type=jnp.float32,
    )
    grad_key_rot = jnp.einsum(
        "hts,thd->sd", grad_raw, query_bf[..., PLAIN_HEAD_SIZE:], preferred_element_type=jnp.float32
    )
    grad_query = jnp.concatenate(
        [grad_query_nope, apply_rotation(grad_query_rot, -token_position)], axis=-1
    )
    grad_query = grad_query.reshape(rows_here, heads_local * QK).astype(jnp.bfloat16)
    grad_w_query = contract_first(normed_bf, grad_query)
    grad_key_value = (
        jnp.concatenate([grad_key_nope, grad_value], axis=-1)
        .reshape(rows_here, heads_local * (PLAIN_HEAD_SIZE + VALUE_HEAD_SIZE))
        .astype(jnp.bfloat16)
    )
    grad_w_kv_up = contract_first(latent_bf, grad_key_value)
    grad_latent_normed = contract_last(grad_key_value, key_value_up_weight)
    grad_latent_part = jnp.concatenate(
        [grad_latent_normed, apply_rotation(grad_key_rot, -token_position)], axis=1
    ).astype(jnp.bfloat16)
    grad_in_summed, grad_latent_sum = product_sum(grad_query, w_query, [grad_latent_part], 4)
    grad_latent_normed = grad_latent_sum[:, :LATENT_RANK]
    grad_g_kv = jnp.sum(grad_latent_normed * latent_unit_scale, axis=0)
    grad_latent = normalize_back(
        grad_latent_normed, latent_unit_scale, latent_norm_factor, latent_norm_gain
    )
    grad_down = jnp.concatenate([grad_latent, grad_latent_sum[:, LATENT_RANK:]], axis=1)
    grad_down_bf = grad_down.astype(jnp.bfloat16)
    share = grad_down.shape[1] // lax.axis_size("tensor")
    grad_columns = lax.dynamic_slice_in_dim(
        grad_down_bf, lax.axis_index("tensor") * share, share, 1
    )
    grad_w_kv_down = contract_first(normed_bf, grad_columns)
    grad_attn_in = grad_in_summed + contract_last(grad_down_bf, key_value_down_weight)
    grad_g_attn = jnp.sum(grad_attn_in * attn_unit, axis=0)
    grad_tokens = grad_hidden + normalize_back(grad_attn_in, attn_unit, attn_factor, g_attn)
    vectors = jnp.concatenate(
        [
            grad_router_part,
            grad_g_attn[:, None],
            grad_g_ffn[:, None],
            jnp.pad(
                grad_g_kv.reshape(devices, -1), ((0, 0), (0, share_rows - LATENT_RANK // devices))
            ).reshape(-1, 1),
            jnp.zeros((features, 128 - experts - 3), jnp.float32),
        ],
        axis=1,
    )
    blocks = [
        a.astype(jnp.bfloat16).reshape(devices, a.shape[0] // devices, a.shape[1])
        for a in (grad_w_query, grad_w_out, grad_w_kv_up, grad_w_kv_down)
    ]
    grad_w_query, grad_w_out, grad_w_kv_up, grad_w_kv_down, vectors = sum_home(
        blocks + [vectors.reshape(devices, share_rows, 128)], 5
    )
    rank, ranks = lax.axis_index("tensor"), lax.axis_size("tensor")
    router_rows = share_rows // ranks
    grad_router = lax.dynamic_slice_in_dim(vectors[:, :experts], rank * router_rows, router_rows, 0)
    latent_rows = LATENT_RANK // devices // ranks
    grad_g_kv = lax.dynamic_slice_in_dim(
        vectors[:, experts + 2], rank * latent_rows, latent_rows, 0
    )
    return (
        output,
        grad_tokens,
        vectors[:, experts],
        grad_w_query,
        grad_w_kv_down,
        grad_g_kv,
        grad_w_kv_up,
        grad_w_out,
        vectors[:, experts + 1],
        grad_router,
        grad_shared_gate,
        grad_shared_up,
        grad_shared_down,
        grad_expert_gate,
        grad_expert_up,
        grad_expert_down,
    )


def solution(mesh):
    in_specs = (
        P("dp", None),
        P("dp", None),
        P("dp", None),
        P("dp", None),
        P(),
        P(None, "tensor"),
        P(),
        P(),
        P(None, "tensor"),
        P(None, "tensor"),
        P(),
        P(),
        P(None, "tensor"),
        P(None, "tensor"),
        P(None, "tensor"),
        P("dp", None, "tensor"),
        P("dp", None, "tensor"),
        P("dp", None, "tensor"),
    )
    out_specs = (
        P("dp", None),
        P("dp", None),
        P("dp"),
        P("dp", "tensor"),
        P("dp", "tensor"),
        P(("dp", "tensor")),
        P("dp", "tensor"),
        P("dp", "tensor"),
        P("dp"),
        P(("dp", "tensor"), None),
        P("dp", "tensor"),
        P("dp", "tensor"),
        P("dp", "tensor"),
        P("dp", None, "tensor"),
        P("dp", None, "tensor"),
        P("dp", None, "tensor"),
    )
    return jax.shard_map(shards, mesh=mesh, in_specs=in_specs, out_specs=out_specs, check_vma=False)
```

```python
import functools

import jax
import jax.numpy as jnp
from jax import lax
from jax.experimental import pallas as pl
from jax.experimental.pallas import tpu as pltpu
from jax.sharding import PartitionSpec as P

PLAIN_HEAD_SIZE = 128
VALUE_HEAD_SIZE = 128
QK = 192
LATENT_RANK = 512
TOPK = 6


epsilon = 1e-06


def rms_normalize_pieces(values, gain):
    factor = lax.rsqrt(jnp.mean(values * values, axis=-1, keepdims=True) + epsilon)
    unit = values * factor
    return (unit * gain, unit, factor)


def normalize_back(grad, unit, factor, gain):
    inner = grad * gain
    return factor * (inner - unit * jnp.mean(inner * unit, axis=-1, keepdims=True))


def apply_rotation(values, token_position):
    half = values.shape[-1] // 2
    freqs = 10000.0 ** (-jnp.arange(half, dtype=jnp.float32) / half)
    angles = token_position.astype(jnp.float32)[:, None] * freqs[None, :]
    shape = (angles.shape[0],) + (1,) * (values.ndim - 2) + (half,)
    cosine = jnp.cos(angles).reshape(shape)
    sine = jnp.sin(angles).reshape(shape)
    first = values[..., :half]
    second = values[..., half:]
    return jnp.concatenate(
        [first * cosine - second * sine, second * cosine + first * sine], axis=-1
    )


def doc_layout(lengths_row, rows_here):
    ends = jnp.cumsum(lengths_row)
    starts = ends - lengths_row
    places = jnp.arange(rows_here, dtype=jnp.int32)
    segment = jnp.sum((places[:, None] >= ends[None, :]).astype(jnp.int32), axis=1)
    member = segment[:, None] == jnp.arange(lengths_row.shape[0], dtype=jnp.int32)[None, :]
    begins = jnp.sum(jnp.where(member, starts[None, :], 0), axis=1)
    return (segment, places - begins)


def contract_last(left, right, precision=None):
    return lax.dot_general(
        left,
        right,
        (((1,), (1,)), ((), ())),
        precision=precision,
        preferred_element_type=jnp.float32,
    )


def contract_first(left, right, precision=None):
    return lax.dot_general(
        left,
        right,
        (((0,), (0,)), ((), ())),
        precision=precision,
        preferred_element_type=jnp.float32,
    )


def swish_parts(gate_pre):
    sigma = jax.nn.sigmoid(gate_pre)
    return (gate_pre * sigma, sigma * (1.0 + gate_pre * (1.0 - sigma)))


VMEM_LIMIT = 60 * 1024 * 1024


def place_of(x_size):
    me = lax.axis_index("dp")
    core = me % 2
    x = (me // 2) % x_size
    z = me // (2 * x_size)
    return z, x, core


def index_of(z, x, core, x_size):
    return (z * x_size + x) * 2 + core


def remote(src, dst, send_sem, recv_sem, target):
    return pltpu.make_async_remote_copy(
        src_ref=src,
        dst_ref=dst,
        send_sem=send_sem,
        recv_sem=recv_sem,
        device_id={"dp": target},
        device_id_type=pl.DeviceIdType.MESH,
    )


def greet(z, x, core, z_size, x_size, pair=False):
    barrier = pltpu.get_barrier_semaphore()

    def tell(target):
        pl.semaphore_signal(
            barrier, inc=1, device_id={"dp": target}, device_id_type=pl.DeviceIdType.MESH
        )

    tell(index_of(z, x, 1 - core, x_size))
    tell(index_of(z, 1 - x, core, x_size))

    @pl.when(z > 0)
    def _():
        tell(index_of(z - 1, x, core, x_size))

    @pl.when(z < z_size - 1)
    def _():
        tell(index_of(z + 1, x, core, x_size))

    inner = (z + z_size - 1) // z_size - z // (z_size - 1)
    if pair:
        pl.semaphore_signal(
            barrier,
            inc=1,
            device_id={"tensor": 1 - lax.axis_index("tensor")},
            device_id_type=pl.DeviceIdType.MESH,
        )
    pl.semaphore_wait(barrier, 3 + inner + (1 if pair else 0))


def add_into(dst, *srcs):
    rows = dst.shape[0]
    step = 32 if rows % 32 == 0 else 8

    def body(i, _):
        here = pl.ds(pl.multiple_of(i * step, step), step)
        total = dst[here, :].astype(jnp.float32)
        for src in srcs:
            total = total + src[here, :].astype(jnp.float32)
        dst[here, :] = total.astype(dst.dtype)
        return 0

    lax.fori_loop(0, rows // step, body, 0)


def scatter_kernel(x_size, parts, pair, *refs):
    z_size = 4
    ins, outs, refs = refs[:parts], refs[parts : 2 * parts], refs[2 * parts :]
    own, c_buf, x_buf, z_buf = (refs[i * parts : (i + 1) * parts] for i in range(4))
    refs = refs[4 * parts :]
    y_buf = None
    if pair:
        y_buf, y_s, y_r, refs = refs[:parts], refs[parts], refs[parts + 1], refs[parts + 2 :]
    l_sem, c_s, c_r, x_s, x_r, z_s, z_r = refs
    z, x, core = place_of(x_size)
    at = functools.partial(index_of, x_size=x_size)
    half = z // 2
    inner = ((z + 3) // 4) * ((6 - z) // 4)
    order = [3 - 3 * half, 2 - half, 1 - z + 4 * half, z]
    load = lambda p, w, v: pltpu.make_async_copy(
        ins[p].at[at(w, v, core)], own[p].at[w, v], l_sem.at[p, w, v]
    )
    beside = lambda p, w, v: remote(
        ins[p].at[at(w, v, 1 - core)],
        c_buf[p].at[w, v],
        c_s.at[p, w, v],
        c_r.at[p, w, v],
        at(z, x, 1 - core),
    )
    across = lambda p, w: remote(
        c_buf[p].at[w, 1 - x], x_buf[p].at[w], x_s.at[p, w], x_r.at[p, w], at(z, 1 - x, core)
    )

    def along(p, w, slot, target):
        return remote(
            c_buf[p].at[w, x], z_buf[p].at[slot], z_s.at[p, w], z_r.at[p, slot], at(target, x, core)
        )

    twin = lambda p: pltpu.make_async_remote_copy(
        src_ref=c_buf[p].at[z, x],
        dst_ref=y_buf[p],
        send_sem=y_s.at[p],
        recv_sem=y_r.at[p],
        device_id={"tensor": 1 - lax.axis_index("tensor")},
        device_id_type=pl.DeviceIdType.MESH,
    )

    for v in (1 - x, x):
        for w in order:
            for p in range(parts):
                load(p, w, v).start()
    greet(z, x, core, z_size, x_size, pair)
    for v in (1 - x, x):
        for w in order:
            for p in range(parts):
                beside(p, w, v).start()
    for w in order:
        for p in range(parts):
            load(p, w, 1 - x).wait()
            beside(p, w, 1 - x).wait_recv()
            add_into(c_buf[p].at[w, 1 - x], own[p].at[w, 1 - x])
            across(p, w).start()
    for k, w in enumerate(order):
        for p in range(parts):
            load(p, w, x).wait()
            beside(p, w, x).wait_recv()
            add_into(c_buf[p].at[w, x], own[p].at[w, x])
            across(p, w).wait_recv()
            if k < 3:

                @pl.when(inner == 1)
                def _():
                    along(p, w, w, z).wait_recv()
                    add_into(c_buf[p].at[w, x], x_buf[p].at[w], z_buf[p].at[w])

                @pl.when(inner == 0)
                def _():
                    add_into(c_buf[p].at[w, x], x_buf[p].at[w])

                @pl.when(w > z)
                def _():
                    along(p, w, w, z + 1).start()

                @pl.when(w < z - 1)
                def _():
                    along(p, w, w, z - 1).start()

                @pl.when(w == z - 1)
                def _():
                    along(p, w, z_size, z - 1).start()

            else:
                add_into(c_buf[p].at[w, x], x_buf[p].at[w])

                @pl.when(z > 0)
                def _():
                    along(p, w, z, z).wait_recv()
                    add_into(c_buf[p].at[w, x], z_buf[p].at[z])

                @pl.when(z < z_size - 1)
                def _():
                    along(p, w, z_size, z).wait_recv()
                    add_into(c_buf[p].at[w, x], z_buf[p].at[z_size])

                if pair:
                    twin(p).start()
                else:
                    outs[p][...] = c_buf[p][z, x].astype(outs[p].dtype)
    if pair:
        for p in range(parts):
            twin(p).wait()
            outs[p][...] = (
                c_buf[p][z, x].astype(jnp.float32) + y_buf[p][...].astype(jnp.float32)
            ).astype(outs[p].dtype)
    for w in range(z_size):
        for p in range(parts):
            for v in range(x_size):
                beside(p, w, v).wait_send()
            across(p, w).wait_send()

            @pl.when(z != w)
            def _():
                along(p, w, w, z).wait_send()


def scatter_sums(arrays, x_size, collective_id, out_dtype, pair=False):
    parts = len(arrays)
    dma = pltpu.SemaphoreType.DMA
    blocks = [a.shape[1:] for a in arrays]
    return pl.pallas_call(
        functools.partial(scatter_kernel, x_size, parts, pair),
        out_shape=[jax.ShapeDtypeStruct(b, out_dtype) for b in blocks],
        in_specs=[pl.BlockSpec(memory_space=pl.ANY)] * parts,
        out_specs=[pl.BlockSpec(memory_space=pltpu.VMEM)] * parts,
        scratch_shapes=[pltpu.VMEM((4, x_size) + b, a.dtype) for a, b in zip(arrays, blocks)]
        + [pltpu.VMEM((4, x_size) + b, a.dtype) for a, b in zip(arrays, blocks)]
        + [pltpu.VMEM((4,) + b, a.dtype) for a, b in zip(arrays, blocks)]
        + [pltpu.VMEM((5,) + b, a.dtype) for a, b in zip(arrays, blocks)]
        + ([pltpu.VMEM(b, a.dtype) for a, b in zip(arrays, blocks)] + [dma((parts,))] * 2 if pair else [])
        + [dma((parts, 4, x_size))] * 3
        + [dma((parts, 4))] * 3
        + [dma((parts, 5))],
        compiler_params=pltpu.CompilerParams(
            collective_id=collective_id, has_side_effects=True, vmem_limit_bytes=VMEM_LIMIT
        ),
        name="scatter_sums",
    )(*arrays)


def nn(left, right):
    return lax.dot_general(
        left, right, (((1,), (0,)), ((), ())), preferred_element_type=jnp.float32
    )


def is_at(j, where):
    low = (3 - j) // 3
    high = j // 3
    return (low, (4 - j) // 3 - low, (j + 1) // 3 - high, high)[where]


def ffn_kernel(
    x_size,
    own_ffn,
    own_gates,
    grad_all,
    gate_t,
    up_t,
    down_t,
    shared_in,
    shared_out,
    out_part,
    dx_part,
    rows_all,
    dy_all,
    he_all,
    dge_all,
    due_all,
    shared_grads,
    blk,
    gts,
    gate_v,
    up_v,
    down_v,
    s_in,
    s_out,
    g_buf,
    rows_b,
    grow_b,
    dy_b,
    he_b,
    dge_b,
    due_b,
    out_r,
    dx_r,
    out_l,
    dx_l,
    out_st,
    dx_st,
    acc,
    gate_col,
    dgate_acc,
    left_ffn,
    left_grad,
    own_sem,
    up_s,
    up_r,
    dn_s,
    dn_r,
    x_s,
    x_r,
    c_s,
    c_r,
    w_sem,
    g_sem,
    st_sem,
):
    z_size, bf16, f32 = 4, jnp.bfloat16, jnp.float32
    hidden = gate_t.shape[0]
    rows_here, features = own_ffn.shape
    slots = rows_b.shape[0] // 2
    wide = 512
    z, x, core = place_of(x_size)
    own = lax.axis_index("dp")
    at = functools.partial(index_of, x_size=x_size)
    ins, outs = (own_ffn, own_gates), (blk, gts)
    half = z // 2
    order = [z, (1 - z) * (1 - 2 * half), 2 * (1 - half) + half * (7 - 2 * z), 3 - 3 * half]

    def place(j):
        return sum(is_at(j, i) * order[i] for i in range(4))

    weights = [
        pltpu.make_async_copy(gate_t, gate_v.at[pl.ds(0, hidden)], w_sem.at[0]),
        pltpu.make_async_copy(up_t, up_v.at[pl.ds(0, hidden)], w_sem.at[1]),
        pltpu.make_async_copy(down_t, down_v.at[pl.ds(0, hidden)], w_sem.at[2]),
        pltpu.make_async_copy(shared_in, s_in, w_sem.at[3]),
        pltpu.make_async_copy(shared_out, s_out, w_sem.at[4]),
    ]
    keep = [
        pltpu.make_async_copy(ins[a], outs[a].at[at(z, x, core)], own_sem.at[a]) for a in range(2)
    ]

    def grad_copy(k):
        w, v = place(k // 2), x + (k % 2) * (1 - 2 * x)
        return pltpu.make_async_copy(
            grad_all.at[pl.ds(2 * (w * x_size + v), 2)], g_buf.at[k % 2], g_sem.at[k % 2]
        )

    for copy in keep + weights:
        copy.start()
    grad_copy(0).start()
    greet(z, x, core, z_size, x_size)

    def up(a, d):
        block = outs[a].at[at(z - d, x, core)]
        src = ins[a] if d == 0 else block
        return remote(src, block, up_s.at[a, d], up_r.at[a, d], at(z + 1, x, core))

    def down(a, d):
        block = outs[a].at[at(z + d, x, core)]
        src = ins[a] if d == 0 else block
        return remote(src, block, dn_s.at[a, d], dn_r.at[a, d], at(z - 1, x, core))

    def across(a, w, first=False):
        block = outs[a].at[at(w, x, core)]
        src = ins[a] if first else block
        return remote(src, block, x_s.at[a, w], x_r.at[a, w], at(z, 1 - x, core))

    def beside(a, w, v, first=False):
        block = outs[a].at[at(w, v, core)]
        src = ins[a] if first else block
        return remote(src, block, c_s.at[a, w, v], c_r.at[a, w, v], at(z, x, 1 - core))

    for a in (1, 0):
        beside(a, z, x, True).start()
        across(a, z, True).start()
        pl.when(z < z_size - 1)(lambda: up(a, 0).start())
        pl.when(z > 0)(lambda: down(a, 0).start())

    def pass_on(d):
        for a in (1, 0):

            @pl.when(z >= d)
            def _():
                up(a, d - 1).wait_recv()
                pl.when(z < z_size - 1)(lambda: up(a, d).start())
                across(a, z - d).start()
                beside(a, z - d, x).start()

            @pl.when(z + d < z_size)
            def _():
                down(a, d - 1).wait_recv()
                pl.when(z > 0)(lambda: down(a, d).start())
                across(a, z + d).start()
                beside(a, z + d, x).start()

    def from_across(w):
        for a in (1, 0):
            across(a, w).wait_recv()
            beside(a, w, 1 - x).start()

    gate_v[pl.ds(hidden, gate_v.shape[0] - hidden), :] = jnp.zeros(
        (gate_v.shape[0] - hidden, features), bf16
    )
    up_v[pl.ds(hidden, up_v.shape[0] - hidden), :] = jnp.zeros(
        (up_v.shape[0] - hidden, features), bf16
    )
    down_v[pl.ds(hidden, down_v.shape[0] - hidden), :] = jnp.zeros(
        (down_v.shape[0] - hidden, features), bf16
    )
    acc[...] = jnp.zeros(acc.shape, f32)
    for copy in weights:
        copy.wait()
    for a in range(2):
        out_r[a, pl.ds(slots, 128), :] = s_out[...]
        dx_r[a, pl.ds(slots, 256), :] = s_in[...]
    for copy in keep:
        copy.wait()
    lane = lax.broadcasted_iota(jnp.int32, (rows_here, 128), 1)
    earlier = lax.broadcasted_iota(jnp.int32, (rows_here, rows_here), 1)
    later = lax.broadcasted_iota(jnp.int32, (rows_here, rows_here), 0)
    upto = (earlier <= later).astype(bf16)
    slot_lane = lax.broadcasted_iota(jnp.int32, (rows_here, slots), 1).astype(f32)

    def staged(pair, which):
        pairs = [
            (rows_b, rows_all),
            (dy_b, dy_all),
            (he_b, he_all),
            (dge_b, dge_all),
            (due_b, due_all),
            (out_st, out_part),
            (dx_st, dx_part),
        ]
        return [
            pltpu.make_async_copy(pairs[i][0], pairs[i][1].at[pair], st_sem.at[i]) for i in which
        ]

    def start_staged(pair, which):
        for copy in staged(pair, which):
            copy.start()

    def wait_staged(k, which):
        @pl.when(k > 0)
        def _():
            for copy in staged(0, which):
                copy.wait()

    def body(k, _):
        w, v = place(k // 2), x + (k % 2) * (1 - 2 * x)
        pair = w * x_size + v
        block = 2 * pair
        here = k % 2
        for r in range(1, 5):

            @pl.when(k == 2 * r - 1)
            def _():
                if r < 4:
                    pass_on(r)
                from_across(order[r - 1])

        grad_copy(k).wait()
        pl.when(k < 7)(lambda: grad_copy(k + 1).start())
        for a in (1, 0):
            beside(a, w, v).wait_recv()

        for a in range(2):
            gates = gts[block + a]
            count = nn(upto, (gates >= 0.0).astype(bf16))
            gate = jnp.sum(jnp.where(lane == own, gates, 0.0), axis=1, keepdims=True)
            slot = jnp.sum(jnp.where(lane == own, count, 0.0), axis=1, keepdims=True) - 1.0
            pick = ((slot_lane == slot) & (gate >= 0.0)).astype(f32).astype(bf16)
            out_l[a, :, pl.ds(0, slots)] = pick
            dx_l[a, :, pl.ds(0, slots)] = pick
            high = gate.astype(bf16).astype(f32)
            middle = (gate - high).astype(bf16).astype(f32)
            low = gate - high - middle
            parts = jnp.where(
                lane == 0, high, jnp.where(lane == 1, middle, jnp.where(lane == 2, low, 0.0))
            ).astype(bf16)
            pick_t = pick.T
            left_ffn[a, pl.ds(0, slots), :] = pick_t
            left_grad[a, pl.ds(0, slots), :] = pick_t
            picked = jnp.sum(nn(pick_t, parts), axis=1, keepdims=True)
            gate_col[pl.ds(a * slots, slots), :] = jnp.broadcast_to(picked, (slots, 128))

        both = pl.ds(block, 2)
        pre = contract_last(blk[both].reshape(2 * rows_here, features), s_in[...])
        grad_hidden = contract_last(g_buf[here].reshape(2 * rows_here, features), s_out[...])
        act, slope = swish_parts(pre[:, :128])
        up_pre = pre[:, 128:]
        shared_units = (
            (act * up_pre).astype(bf16),
            (grad_hidden * up_pre * slope).astype(bf16),
            (grad_hidden * act).astype(bf16),
        )
        for a in range(2):
            mine = slice(a * rows_here, (a + 1) * rows_here)
            out_l[a, :, pl.ds(slots, 128)] = shared_units[0][mine]
            dx_l[a, :, pl.ds(slots, 128)] = shared_units[1][mine]
            dx_l[a, :, pl.ds(slots + 128, 128)] = shared_units[2][mine]
            left_ffn[a, pl.ds(slots, 128), :] = shared_units[1][mine].T
            left_ffn[a, pl.ds(slots + 128, 128), :] = shared_units[2][mine].T
            left_grad[a, pl.ds(slots, 128), :] = shared_units[0][mine].T

        def pick_rows(n, _):
            cols = pl.ds(pl.multiple_of(n * wide, wide), wide)
            for a in range(2):
                mine = pl.ds(a * slots, slots)
                product = nn(left_ffn[a], blk[block + a, :, cols])
                rows_b[mine, cols] = product[:slots].astype(bf16)
                acc[pl.ds(0, 256), cols] += product[slots:]
                product = nn(left_grad[a], g_buf[here, a, :, cols])
                grows = product[:slots]
                acc[pl.ds(256, 128), cols] += product[slots:]
                grow_b[mine, cols] = grows.astype(bf16)
                dy_b[mine, cols] = (gate_col[mine, pl.ds(0, 1)] * grows).astype(bf16)
            return 0

        wait_staged(k, (0, 1))
        lax.fori_loop(0, features // wide, pick_rows, 0)
        start_staged(pair, (0, 1))

        def hidden_units(n, _):
            units = pl.ds(pl.multiple_of(n * 256, 256), 256)
            gate_pre = contract_last(rows_b[...], gate_v[units, :])
            up_pre = contract_last(rows_b[...], up_v[units, :])
            grad_hidden = contract_last(dy_b[...], down_v[units, :])
            act, slope = swish_parts(gate_pre)
            he_b[:, units] = (act * up_pre).astype(bf16)
            dge_b[:, units] = (grad_hidden * up_pre * slope).astype(bf16)
            due_b[:, units] = (grad_hidden * act).astype(bf16)
            return 0

        wait_staged(k, (2, 3, 4))
        lax.fori_loop(0, gate_v.shape[0] // 256, hidden_units, 0)
        start_staged(pair, (2, 3, 4))
        dgate_acc[...] = jnp.zeros(dgate_acc.shape, f32)

        def back(n, _):
            cols = pl.ds(pl.multiple_of(n * wide, wide), wide)
            result = nn(he_b[...], down_v[:, cols])
            product = grow_b[:, cols].astype(f32) * result
            for i in range(wide // 128):
                dgate_acc[...] += product[:, i * 128 : (i + 1) * 128]
            result = (gate_col[:, pl.ds(0, 1)] * result).astype(bf16)
            grad_in = (nn(dge_b[...], gate_v[:, cols]) + nn(due_b[...], up_v[:, cols])).astype(bf16)
            for a in range(2):
                mine = slice(a * slots, (a + 1) * slots)
                out_r[a, pl.ds(0, slots), cols] = result[mine]
                dx_r[a, pl.ds(0, slots), cols] = grad_in[mine]
                out_st[a, :, cols] = nn(out_l[a], out_r[a, :, cols]).astype(bf16)
                dx_st[a, :, cols] = nn(dx_l[a], dx_r[a, :, cols]).astype(bf16)
            return 0

        wait_staged(k, (5, 6))
        lax.fori_loop(0, features // wide, back, 0)
        dgate = jnp.sum(dgate_acc[...], axis=1, keepdims=True)
        high = dgate.astype(bf16).astype(f32)
        spread = lax.broadcasted_iota(jnp.int32, (2 * slots, 128), 1)
        spread = jnp.where(
            spread == own, high, jnp.where(spread == own + 16, dgate - high, 0.0)
        ).astype(bf16)
        for a in range(2):
            dx_st[a, :, pl.ds(features, 128)] = nn(
                out_l[a, :, pl.ds(0, slots)], spread[a * slots : (a + 1) * slots]
            ).astype(bf16)
        start_staged(pair, (5, 6))
        return 0

    lax.fori_loop(0, 8, body, 0)
    wait_staged(1, range(7))
    shared_grads[...] = acc[...].astype(bf16)
    for a in range(2):
        for w in range(z_size):
            for v in range(x_size):
                beside(a, w, v).wait_send()
            across(a, w).wait_send()
    for d in range(z_size):
        for a in range(2):
            pl.when((z >= d) & (z < z_size - 1))(lambda: up(a, d).wait_send())
            pl.when((z + d < z_size) & (z > 0))(lambda: down(a, d).wait_send())


def ffn_tuned(own_ffn, own_gates, grad_all, gate_t, up_t, down_t, shared_in, shared_out, slots):
    rows, features = own_ffn.shape
    hidden = gate_t.shape[0]
    padded = -(-hidden // 256) * 256
    bf16, f32, dma = jnp.bfloat16, jnp.float32, pltpu.SemaphoreType.DMA
    anywhere = pl.BlockSpec(memory_space=pl.ANY)
    shape = jax.ShapeDtypeStruct
    return pl.pallas_call(
        functools.partial(ffn_kernel, 2),
        out_shape=[
            shape((8, 2, rows, features), bf16),
            shape((8, 2, rows, features + 128), bf16),
            shape((8, 2 * slots, features), bf16),
            shape((8, 2 * slots, features), bf16),
            shape((8, 2 * slots, padded), bf16),
            shape((8, 2 * slots, padded), bf16),
            shape((8, 2 * slots, padded), bf16),
            shape((384, features), bf16),
        ],
        in_specs=[anywhere] * 8,
        out_specs=[anywhere] * 7 + [pl.BlockSpec(memory_space=pltpu.VMEM)],
        scratch_shapes=[
            pltpu.VMEM((16, rows, features), bf16),
            pltpu.VMEM((16, rows, 128), f32),
            pltpu.VMEM((padded, features), bf16),
            pltpu.VMEM((padded, features), bf16),
            pltpu.VMEM((padded, features), bf16),
            pltpu.VMEM((256, features), bf16),
            pltpu.VMEM((128, features), bf16),
            pltpu.VMEM((2, 2, rows, features), bf16),
            pltpu.VMEM((2 * slots, features), bf16),
            pltpu.VMEM((2 * slots, features), bf16),
            pltpu.VMEM((2 * slots, features), bf16),
            pltpu.VMEM((2 * slots, padded), bf16),
            pltpu.VMEM((2 * slots, padded), bf16),
            pltpu.VMEM((2 * slots, padded), bf16),
            pltpu.VMEM((2, slots + 128, features), bf16),
            pltpu.VMEM((2, slots + 256, features), bf16),
            pltpu.VMEM((2, rows, slots + 128), bf16),
            pltpu.VMEM((2, rows, slots + 256), bf16),
            pltpu.VMEM((2, rows, features), bf16),
            pltpu.VMEM((2, rows, features + 128), bf16),
            pltpu.VMEM((384, features), f32),
            pltpu.VMEM((2 * slots, 128), f32),
            pltpu.VMEM((2 * slots, 128), f32),
            pltpu.VMEM((2, slots + 256, rows), bf16),
            pltpu.VMEM((2, slots + 128, rows), bf16),
            dma((2,)),
        ]
        + [dma((2, 4))] * 6
        + [dma((2, 4, 2))] * 2
        + [dma((5,)), dma((2,)), dma((7,))],
        compiler_params=pltpu.CompilerParams(
            collective_id=1, has_side_effects=True, vmem_limit_bytes=VMEM_LIMIT
        ),
        name="ffn",
    )(
        own_ffn,
        own_gates,
        grad_all.reshape(16, rows, features),
        gate_t,
        up_t,
        down_t,
        shared_in,
        shared_out,
    )


def first_half(shape):
    return lax.broadcasted_iota(jnp.int32, shape, 1) % 64 < 32


def turn(values, cosine, sine):
    partner = jnp.where(
        first_half(values.shape), pltpu.roll(values, 96, 1), pltpu.roll(values, 32, 1)
    )
    return values * cosine + partner * sine


def layout_of(lengths, rows, width):
    row = lax.broadcasted_iota(jnp.int32, (rows, width), 0)
    across = lax.broadcasted_iota(jnp.int32, (rows, rows), 1)
    down = lax.broadcasted_iota(jnp.int32, (rows, rows), 0)
    place, met, end = row, across <= down, 0
    for i in range(lengths.shape[1]):
        end = end + lengths[0, i]
        place = place - jnp.where(row >= end, lengths[0, i], 0)
        met = met & ((across >= end) == (down >= end))
    return place, met


def turn_tables(lengths, freqs, rows):
    place, met = layout_of(lengths, rows, 128)
    angles = place.astype(jnp.float32) * freqs[...]
    sine = jnp.sin(angles)
    return jnp.cos(angles), jnp.where(first_half(angles.shape), -sine, sine), met


def pair_copy(src, dst, send_sem, recv_sem):
    return pltpu.make_async_remote_copy(
        src_ref=src,
        dst_ref=dst,
        send_sem=send_sem,
        recv_sem=recv_sem,
        device_id={"tensor": 1 - lax.axis_index("tensor")},
        device_id_type=pl.DeviceIdType.MESH,
    )


def greet_pair():
    barrier = pltpu.get_barrier_semaphore()
    pl.semaphore_signal(
        barrier,
        inc=1,
        device_id={"tensor": 1 - lax.axis_index("tensor")},
        device_id_type=pl.DeviceIdType.MESH,
    )
    pl.semaphore_wait(barrier, 1)


def forward_kernel(
    lengths,
    freqs,
    tokens,
    routes,
    g_attn,
    g_latent,
    g_ffn,
    router_t,
    w_query,
    down_t,
    kv_up,
    w_out,
    hidden,
    ffn_bf,
    gates,
    probs,
    normed,
    queries,
    kv,
    key_turned,
    latent_bf,
    latent,
    context,
    log_totals,
    wq_v,
    down_v,
    up_v,
    out_v,
    sent,
    got,
    w_sem,
    s_sem,
    r_sem,
):
    bf16, f32 = jnp.bfloat16, jnp.float32
    rows, features = tokens.shape
    rank = kv_up.shape[0]
    heads = kv_up.shape[1] // 256
    turned = down_t.shape[0] - rank
    tail = pl.ds(rank, turned)
    loads = [
        pltpu.make_async_copy(down_t, down_v.at[pl.ds(0, rank + turned)], w_sem.at[0]),
        pltpu.make_async_copy(down_t.at[tail], down_v.at[pl.ds(rank + turned, turned)], w_sem.at[1]),
        pltpu.make_async_copy(kv_up, up_v, w_sem.at[2]),
        pltpu.make_async_copy(w_query, wq_v, w_sem.at[3]),
        pltpu.make_async_copy(w_out, out_v, w_sem.at[4]),
    ]
    for copy in loads:
        copy.start()
    greet_pair()
    cosine, sine, met = turn_tables(lengths, freqs, rows)
    values, _, _ = rms_normalize_pieces(tokens[...].astype(f32), g_attn[...])
    normed[...] = values.astype(bf16)
    loads[0].wait()
    loads[1].wait()
    low = contract_last(normed[...], down_v[...])
    latent[...] = low[:, :rank]
    key_turned[...] = turn(low[:, rank:], cosine, sine).astype(bf16)
    values, _, _ = rms_normalize_pieces(latent[...], g_latent[...])
    latent_bf[...] = values.astype(bf16)
    loads[2].wait()

    def keys(n, _):
        cols = pl.ds(pl.multiple_of(n * 512, 512), 512)
        kv[:, cols] = nn(latent_bf[...], up_v[:, cols]).astype(bf16)
        return 0

    lax.fori_loop(0, kv.shape[1] // 512, keys, 0)
    loads[3].wait()
    lane = lax.broadcasted_iota(jnp.int32, (rows, 128), 1)
    log_totals[...] = jnp.zeros(log_totals.shape, f32)

    def two_heads(i, _):
        three = nn(normed[...], wq_v[:, pl.ds(pl.multiple_of(i * 384, 384), 384)])
        middle, last = three[:, 128:256], three[:, 256:]
        plain = (
            three[:, :128],
            jnp.where(lane < 64, pltpu.roll(middle, 64, 1), pltpu.roll(last, 64, 1)),
        )
        spun = turn(jnp.where(lane < 64, middle, last), cosine, sine)
        for b in range(2):
            head = 2 * i + b
            queries[head, :, pl.ds(0, 128)] = plain[b].astype(bf16)
            queries[head, :, pl.ds(128, 128)] = jnp.where(
                (lane < 64) == (b == 0), spun, 0.0
            ).astype(bf16)
            at = pl.multiple_of(head * 256, 256)
            key = jnp.concatenate([kv[:, pl.ds(at, 128)], key_turned[...]], axis=1)
            raw = contract_last(queries[head], key)
            scores = jnp.where(met, raw * QK ** (-0.5), -jnp.inf)
            top = jnp.max(scores, axis=1, keepdims=True)
            expo = jnp.exp(scores - top)
            total = jnp.sum(expo, axis=1, keepdims=True)
            log_totals[...] = jnp.where(lane == head, top + jnp.log(total), log_totals[...])
            context[:, pl.ds(pl.multiple_of(head * 128, 128), 128)] = nn(
                (expo / total).astype(bf16), kv[:, pl.ds(at + 128, 128)]
            ).astype(bf16)
        return 0

    lax.fori_loop(0, heads // 2, two_heads, 0)
    loads[4].wait()
    chunks, width = sent.shape[0], sent.shape[2]
    chunk = lambda i: pair_copy(sent.at[i], got.at[i], s_sem.at[i], r_sem.at[i])

    def project(i, _):
        sent[i] = contract_last(
            context[...], out_v[pl.ds(pl.multiple_of(i * width, width), width), :]
        ).astype(bf16)
        chunk(i).start()
        return 0

    lax.fori_loop(0, chunks, project, 0)

    def join(i, _):
        chunk(i).wait()
        cols = pl.ds(pl.multiple_of(i * width, width), width)
        hidden[:, cols] = tokens[:, cols].astype(f32) + (sent[i].astype(f32) + got[i].astype(f32))
        return 0

    lax.fori_loop(0, chunks, join, 0)
    values, _, _ = rms_normalize_pieces(hidden[...], g_ffn[...])
    ffn_bf[...] = values.astype(bf16)
    experts = lax.axis_size("dp")
    logits = lax.dot_general(
        values,
        router_t[...],
        (((1,), (1,)), ((), ())),
        precision=lax.Precision.HIGHEST,
        preferred_element_type=f32,
    )
    logits = jnp.where(lane < experts, logits, -jnp.inf)
    expo = jnp.exp(logits - jnp.max(logits, axis=1, keepdims=True))
    share = expo / jnp.sum(expo, axis=1, keepdims=True)
    probs[...] = share
    named = lane < 0
    for i in range(routes.shape[1]):
        named = named | (lane == routes[:, pl.ds(i, 1)])
    gates[...] = jnp.where(named, share, -1.0)


def forward_tuned(
    lengths, freqs, tokens, routes, g_attn, g_latent, g_ffn, router_t, w_query, down_t, kv_up, w_out
):
    rows, features = tokens.shape
    rank, columns = kv_up.shape
    heads = columns // 256
    bf16, f32, dma = jnp.bfloat16, jnp.float32, pltpu.SemaphoreType.DMA
    vmem, anywhere = pl.BlockSpec(memory_space=pltpu.VMEM), pl.BlockSpec(memory_space=pl.ANY)
    smem = pl.BlockSpec(memory_space=pltpu.SMEM)
    shape = jax.ShapeDtypeStruct
    chunks = 8
    return pl.pallas_call(
        forward_kernel,
        out_shape=[
            shape((rows, features), f32),
            shape((rows, features), bf16),
            shape((rows, 128), f32),
            shape((rows, 128), f32),
            shape((rows, features), bf16),
            shape((heads, rows, 256), bf16),
            shape((rows, columns), bf16),
            shape((rows, 128), bf16),
            shape((rows, rank), bf16),
            shape((rows, rank), f32),
            shape((rows, heads * 128), bf16),
            shape((rows, 128), f32),
        ],
        in_specs=[smem] + [vmem] * 7 + [anywhere] * 4,
        out_specs=[vmem] * 12,
        scratch_shapes=[
            pltpu.VMEM(w_query.shape, bf16),
            pltpu.VMEM((rank + 128, features), bf16),
            pltpu.VMEM(kv_up.shape, bf16),
            pltpu.VMEM(w_out.shape, bf16),
            pltpu.VMEM((chunks, rows, features // chunks), bf16),
            pltpu.VMEM((chunks, rows, features // chunks), bf16),
            dma((5,)),
            dma((chunks,)),
            dma((chunks,)),
        ],
        compiler_params=pltpu.CompilerParams(
            collective_id=2, has_side_effects=True, vmem_limit_bytes=VMEM_LIMIT
        ),
        name="attention_forward",
    )(lengths, freqs, tokens, routes, g_attn, g_latent, g_ffn, router_t, w_query, down_t, kv_up, w_out)


def backward_kernel(
    lengths,
    freqs,
    sums,
    hidden,
    grad_out,
    tokens,
    probs,
    g_attn,
    g_latent,
    g_ffn,
    router_t,
    queries,
    kv,
    key_turned,
    latent,
    log_totals,
    w_query,
    down_t,
    kv_up,
    w_out,
    grad_tokens,
    grad_hidden_bf,
    grad_query,
    grad_kv,
    grad_low,
    vectors,
    wq_v,
    down_v,
    up_v,
    out_v,
    unit,
    grad_hidden,
    grad_context,
    grad_turned,
    sent,
    got,
    low_sent,
    low_got,
    w_sem,
    s_sem,
    r_sem,
    e_sem,
):
    bf16, f32 = jnp.bfloat16, jnp.float32
    highest = lax.Precision.HIGHEST
    rows, features = tokens.shape
    rank = kv_up.shape[0]
    heads = kv_up.shape[1] // 256
    turned = down_t.shape[0] - rank
    tail = pl.ds(rank, turned)
    loads = [
        pltpu.make_async_copy(w_out, out_v, w_sem.at[0]),
        pltpu.make_async_copy(kv_up, up_v, w_sem.at[1]),
        pltpu.make_async_copy(w_query, wq_v, w_sem.at[2]),
        pltpu.make_async_copy(down_t, down_v.at[pl.ds(0, rank + turned)], w_sem.at[3]),
        pltpu.make_async_copy(down_t.at[tail], down_v.at[pl.ds(rank + turned, turned)], w_sem.at[4]),
    ]
    for copy in loads:
        copy.start()
    greet_pair()
    cosine, sine, met = turn_tables(lengths, freqs, rows)
    lane = lax.broadcasted_iota(jnp.int32, (rows, 128), 1)
    experts = lax.axis_size("dp")

    extra = sums[:, pl.ds(features, 128)]
    dense = extra + pltpu.roll(extra, 128 - experts, 1)
    share = probs[...]
    dense = jnp.where(lane < experts, dense, 0.0)
    logits = share * (dense - jnp.sum(share * dense, axis=1, keepdims=True))
    grad_in = sums[:, pl.ds(0, features)] + lax.dot_general(
        logits,
        router_t[...],
        (((1,), (0,)), ((), ())),
        precision=highest,
        preferred_element_type=f32,
    )
    values, unit_rows, factor = rms_normalize_pieces(hidden[...], g_ffn[...])
    unit[...] = unit_rows
    vectors[pl.ds(0, experts), :] = lax.dot_general(
        logits, values, (((0,), (0,)), ((), ())), precision=highest, preferred_element_type=f32
    )[:experts]
    vectors[pl.ds(experts, 8), :] = jnp.zeros((8, features), f32)
    vectors[pl.ds(experts + 1, 1), :] = jnp.sum(grad_in * unit[...], axis=0, keepdims=True)
    grad_hidden[...] = grad_out[...].astype(f32) + normalize_back(
        grad_in, unit[...], factor, g_ffn[...]
    )
    grad_hidden_bf[...] = grad_hidden[...].astype(bf16)
    loads[0].wait()

    def back_out(n, _):
        cols = pl.ds(pl.multiple_of(n * 256, 256), 256)
        grad_context[:, cols] = nn(grad_hidden_bf[...], out_v[:, cols]).astype(bf16)
        return 0

    lax.fori_loop(0, grad_context.shape[1] // 256, back_out, 0)
    grad_turned[...] = jnp.zeros(grad_turned.shape, f32)

    def two_heads(i, _):
        pieces = []
        for b in range(2):
            head = 2 * i + b
            at = pl.multiple_of(head * 256, 256)
            key = jnp.concatenate([kv[:, pl.ds(at, 128)], key_turned[...]], axis=1)
            value = kv[:, pl.ds(at + 128, 128)]
            raw = contract_last(queries[head], key)
            log_total = jnp.sum(
                jnp.where(lane == head, log_totals[...], 0.0), axis=1, keepdims=True
            )
            weights = jnp.exp(jnp.where(met, raw * QK ** (-0.5), -jnp.inf) - log_total)
            grad_ctx = grad_context[:, pl.ds(pl.multiple_of(head * 128, 128), 128)]
            grad_weights = contract_last(grad_ctx, value)
            inner = jnp.sum(weights * grad_weights, axis=1, keepdims=True)
            grad_raw = (weights * (grad_weights - inner) * QK ** (-0.5)).astype(bf16)
            pieces.append(nn(grad_raw, key))
            back_key = contract_first(grad_raw, queries[head])
            grad_kv[:, pl.ds(at, 128)] = back_key[:, :128].astype(bf16)
            grad_turned[...] += back_key[:, 128:]
            grad_kv[:, pl.ds(at + 128, 128)] = contract_first(
                weights.astype(bf16), grad_ctx
            ).astype(bf16)
        even, odd = pieces
        spun = turn(jnp.where(lane < 64, even[:, 128:], odd[:, 128:]), cosine, -sine)
        moved = pltpu.roll(odd[:, :128], 64, 1)
        start = pl.multiple_of(i * 384, 384)
        grad_query[:, pl.ds(start, 128)] = even[:, :128].astype(bf16)
        grad_query[:, pl.ds(start + 128, 128)] = jnp.where(lane < 64, spun, moved).astype(bf16)
        grad_query[:, pl.ds(start + 256, 128)] = jnp.where(lane < 64, moved, spun).astype(bf16)
        return 0

    lax.fori_loop(0, heads // 2, two_heads, 0)
    loads[1].wait()
    low_sent[:, pl.ds(0, rank)] = contract_last(grad_kv[...], up_v[...]).astype(bf16)
    folded = turn(grad_turned[...] + pltpu.roll(grad_turned[...], 64, 1), cosine, -sine)
    low_sent[:, pl.ds(rank, 128)] = jnp.where(lane < turned, folded, 0.0).astype(bf16)
    low_copy = pair_copy(low_sent, low_got, e_sem.at[0], e_sem.at[1])
    low_copy.start()
    loads[2].wait()
    chunks, width = sent.shape[0], sent.shape[2]
    chunk = lambda i: pair_copy(sent.at[i], got.at[i], s_sem.at[i], r_sem.at[i])

    def project(i, _):
        sent[i] = contract_last(
            grad_query[...], wq_v[pl.ds(pl.multiple_of(i * width, width), width), :]
        ).astype(bf16)
        chunk(i).start()
        return 0

    lax.fori_loop(0, chunks, project, 0)
    loads[3].wait()
    loads[4].wait()
    low_copy.wait()
    low = low_sent[...].astype(f32) + low_got[...].astype(f32)
    grad_normed = low[:, :rank]
    _, latent_unit, latent_factor = rms_normalize_pieces(latent[...], g_latent[...])
    grad_gain = jnp.sum(grad_normed * latent_unit, axis=0, keepdims=True)
    for i in range(rank // 128):
        vectors[pl.ds(experts + 2 + i, 1), pl.ds(0, 128)] = grad_gain[:, i * 128 : (i + 1) * 128]
    grad_low[:, pl.ds(0, rank)] = normalize_back(
        grad_normed, latent_unit, latent_factor, g_latent[...]
    ).astype(bf16)
    grad_low[:, pl.ds(rank, 128)] = low[:, rank:].astype(bf16)

    def join(i, _):
        cols = pl.ds(pl.multiple_of(i * width, width), width)
        product = nn(grad_low[...], down_v[:, cols])
        chunk(i).wait()
        unit[:, cols] = product + (sent[i].astype(f32) + got[i].astype(f32))
        return 0

    lax.fori_loop(0, chunks, join, 0)
    _, attn_unit, attn_factor = rms_normalize_pieces(tokens[...].astype(f32), g_attn[...])
    vectors[pl.ds(experts, 1), :] = jnp.sum(unit[...] * attn_unit, axis=0, keepdims=True)
    grad_tokens[...] = grad_hidden[...] + normalize_back(
        unit[...], attn_unit, attn_factor, g_attn[...]
    )


def backward_tuned(lengths, freqs, sums, values, gains, router_t, saved, weights):
    hidden, grad_out, tokens, probs = values
    w_query, down_t, kv_up, w_out = weights
    rows, features = tokens.shape
    rank, columns = kv_up.shape
    heads = columns // 256
    bf16, f32, dma = jnp.bfloat16, jnp.float32, pltpu.SemaphoreType.DMA
    vmem, anywhere = pl.BlockSpec(memory_space=pltpu.VMEM), pl.BlockSpec(memory_space=pl.ANY)
    smem = pl.BlockSpec(memory_space=pltpu.SMEM)
    shape = jax.ShapeDtypeStruct
    chunks = 8
    experts = lax.axis_size("dp")
    return pl.pallas_call(
        backward_kernel,
        out_shape=[
            shape((rows, features), f32),
            shape((rows, features), bf16),
            shape((rows, w_query.shape[1]), bf16),
            shape((rows, columns), bf16),
            shape((rows, rank + 128), bf16),
            shape((experts + 8, features), f32),
        ],
        in_specs=[smem] + [vmem] * 15 + [anywhere] * 4,
        out_specs=[vmem] * 6,
        scratch_shapes=[
            pltpu.VMEM(w_query.shape, bf16),
            pltpu.VMEM((rank + 128, features), bf16),
            pltpu.VMEM(kv_up.shape, bf16),
            pltpu.VMEM(w_out.shape, bf16),
            pltpu.VMEM((rows, features), f32),
            pltpu.VMEM((rows, features), f32),
            pltpu.VMEM((rows, heads * 128), bf16),
            pltpu.VMEM((rows, 128), f32),
            pltpu.VMEM((chunks, rows, features // chunks), bf16),
            pltpu.VMEM((chunks, rows, features // chunks), bf16),
            pltpu.VMEM((rows, rank + 128), bf16),
            pltpu.VMEM((rows, rank + 128), bf16),
            dma((5,)),
            dma((chunks,)),
            dma((chunks,)),
            dma((2,)),
        ],
        compiler_params=pltpu.CompilerParams(
            collective_id=4, has_side_effects=True, vmem_limit_bytes=VMEM_LIMIT
        ),
        name="attention_backward",
    )(lengths, freqs, sums, hidden, grad_out, tokens, probs, *gains, router_t, *saved, *weights)


def sum_home(arrays, pair=False):
    sums = [lax.psum_scatter(a, "dp", scatter_dimension=0) for a in arrays]
    if pair:
        sums = [lax.psum(a.astype(jnp.float32), "tensor") for a in sums]
    return [a.astype(jnp.float32) for a in sums]


def product_sum(left, right, extras):
    product = contract_last(left, right).astype(jnp.bfloat16)
    return [lax.psum(a, "tensor").astype(jnp.float32) for a in [product] + extras]


def ffn_with_kernel(own_ffn, gates, everyone_grad, weights, shared, capacity, experts):
    part = shared[0].shape[1]
    hidden, features = weights[0].shape[1], own_ffn.shape[1]
    gate_t, up_t, down_t = (jnp.pad(w.T, ((0, 128 - part), (0, 0))) for w in shared)
    out_part, grad_part, rows, dy, he, dge, due, shared_grads = ffn_tuned(
        own_ffn,
        gates,
        everyone_grad,
        *(w.T for w in weights),
        jnp.concatenate([gate_t, up_t], axis=0),
        down_t,
        capacity,
    )
    rows, dy = rows.reshape(-1, features), dy.reshape(-1, features)
    he, dge, due = (a.reshape(-1, a.shape[2])[:, :hidden] for a in (he, dge, due))
    devices, rows_here = everyone_grad.shape[:2]
    return (
        out_part.reshape(devices, rows_here, -1),
        grad_part.reshape(devices, rows_here, -1),
        contract_first(rows, dge)[None],
        contract_first(rows, due)[None],
        contract_first(dy, he)[None],
        shared_grads.reshape(3, 128, features)[:, :part].reshape(3 * part, features),
    )


def ffn_plain(own_ffn, gates, everyone_grad, weights, shared, capacity, experts):
    own, devices = lax.axis_index("dp"), lax.axis_size("dp")
    rows_here, features = own_ffn.shape
    places = jnp.arange(rows_here, dtype=jnp.int32)
    expert_gate, expert_up, expert_down = weights
    part_gate, part_up, part_down = shared
    everyone_ffn = lax.all_gather(own_ffn, "dp", tiled=True)
    everyone_gates = lax.all_gather(gates, "dp")
    everyone_grad = everyone_grad.reshape(devices * rows_here, features)
    own_probs = lax.dynamic_slice_in_dim(everyone_gates, own, 1, 2).reshape(devices, rows_here)
    chooses = own_probs >= 0.0
    own_gates = jnp.where(chooses, own_probs, 0.0)
    upto = (places[:, None] <= places[None, :]).astype(jnp.bfloat16)
    slot = jnp.dot(chooses.astype(jnp.bfloat16), upto, preferred_element_type=jnp.float32) - 1.0
    slots = jnp.arange(capacity, dtype=jnp.float32)
    picked = chooses[:, None, :] & (slot[:, None, :] == slots[None, :, None])
    pick = picked.astype(jnp.bfloat16)
    slot_gates = jnp.sum(jnp.where(picked, own_gates[:, None, :], 0.0), axis=2).reshape(-1, 1)

    def pick_rows(values):
        blocks = values.reshape(devices, rows_here, features)
        return jnp.einsum(
            "jst,jtc->jsc", pick, blocks, preferred_element_type=jnp.float32
        ).astype(jnp.bfloat16).reshape(devices * capacity, features)

    def put_rows(values, hidden_parts, weights):
        blocks = values.astype(jnp.bfloat16).reshape(devices, capacity, features)
        left = jnp.concatenate(
            [pick.transpose(0, 2, 1)]
            + [h.reshape(devices, rows_here, h.shape[1]) for h in hidden_parts],
            axis=2,
        )
        right = jnp.concatenate(
            [blocks]
            + [
                jnp.broadcast_to(w.T[None], (devices, w.shape[1], features))
                for w in weights
            ],
            axis=1,
        )
        return (
            jnp.einsum("jtk,jkc->jtc", left, right, preferred_element_type=jnp.float32)
            .astype(jnp.bfloat16)
            .reshape(devices * rows_here, features)
        )

    expert_rows = pick_rows(everyone_ffn)
    grad_picked = pick_rows(everyone_grad)
    grad_rows = (slot_gates * grad_picked.astype(jnp.float32)).astype(jnp.bfloat16)

    gate_pre = jnp.dot(expert_rows, expert_gate, preferred_element_type=jnp.float32)
    up_pre = jnp.dot(expert_rows, expert_up, preferred_element_type=jnp.float32)
    gate_act, gate_slope = swish_parts(gate_pre)
    expert_hidden = (gate_act * up_pre).astype(jnp.bfloat16)
    expert_result = contract_last(expert_hidden, expert_down)
    slot_grads = jnp.sum(grad_picked.astype(jnp.float32) * expert_result, axis=1)
    grad_expert_down = contract_first(grad_rows, expert_hidden)[None]
    grad_expert_hidden = jnp.dot(grad_rows, expert_down, preferred_element_type=jnp.float32)
    grad_gate_pre = (grad_expert_hidden * up_pre * gate_slope).astype(jnp.bfloat16)
    grad_up_pre = (grad_expert_hidden * gate_act).astype(jnp.bfloat16)
    grad_expert_gate = contract_first(expert_rows, grad_gate_pre)[None]
    grad_expert_up = contract_first(expert_rows, grad_up_pre)[None]
    grad_rows_in = contract_last(grad_gate_pre, expert_gate) + contract_last(
        grad_up_pre, expert_up
    )

    shared_pre_gate = jnp.dot(everyone_ffn, part_gate, preferred_element_type=jnp.float32)
    shared_pre_up = jnp.dot(everyone_ffn, part_up, preferred_element_type=jnp.float32)
    shared_act, shared_slope = swish_parts(shared_pre_gate)
    shared_hidden = (shared_act * shared_pre_up).astype(jnp.bfloat16)
    grad_shared_hidden = jnp.dot(everyone_grad, part_down, preferred_element_type=jnp.float32)
    grad_shared_gate_pre = (grad_shared_hidden * shared_pre_up * shared_slope).astype(jnp.bfloat16)
    grad_shared_up_pre = (grad_shared_hidden * shared_act).astype(jnp.bfloat16)
    shared_grads = jnp.concatenate(
        [
            contract_first(grad_shared_gate_pre, everyone_ffn),
            contract_first(grad_shared_up_pre, everyone_ffn),
            contract_first(shared_hidden, everyone_grad),
        ],
        axis=0,
    ).astype(jnp.bfloat16)
    ffn_part = put_rows(slot_gates * expert_result, [shared_hidden], [part_down])
    pair_grads = jnp.sum(
        jnp.where(picked, slot_grads.reshape(devices, capacity, 1), 0.0), axis=1
    ).reshape(devices * rows_here, 1)
    pair_high = pair_grads.astype(jnp.bfloat16).astype(jnp.float32)
    column = jnp.arange(128, dtype=jnp.int32)[None, :]
    pair_columns = jnp.where(
        column == own,
        pair_high,
        jnp.where(column == own + experts, pair_grads - pair_high, 0.0),
    )
    grad_ffn_in = put_rows(
        grad_rows_in, [grad_shared_gate_pre, grad_shared_up_pre], [part_gate, part_up]
    )
    grad_part = jnp.concatenate([grad_ffn_in, pair_columns.astype(jnp.bfloat16)], axis=1)
    return (
        ffn_part.reshape(devices, rows_here, -1),
        grad_part.reshape(devices, rows_here, -1),
        grad_expert_gate,
        grad_expert_up,
        grad_expert_down,
        shared_grads,
    )


def shared_home(grads, part):
    devices = lax.axis_size("dp")
    share_rows = grads.shape[1] // devices
    grads = lax.all_to_all(
        grads.reshape(3 * part, devices, share_rows).transpose(1, 2, 0).astype(jnp.bfloat16),
        "dp",
        split_axis=0,
        concat_axis=0,
    ).astype(jnp.float32)
    return [
        grads[:, :, i * part : (i + 1) * part].transpose(1, 0, 2).reshape(share_rows, -1)
        for i in range(3)
    ]


def shards_tuned(
    tokens,
    lengths,
    routes,
    grad_out,
    g_attn,
    w_query,
    key_value_down_weight,
    latent_norm_gain,
    key_value_up_weight,
    w_out,
    g_ffn,
    router,
    shared_gate,
    shared_up,
    shared_down,
    expert_gate,
    expert_up,
    expert_down,
):
    rows_here, features = tokens.shape
    devices, ranks = lax.axis_size("dp"), lax.axis_size("tensor")
    own, rank = lax.axis_index("dp"), lax.axis_index("tensor")
    experts = router.shape[1]
    capacity = rows_here * TOPK * 4 // (3 * devices)
    half = (key_value_down_weight.shape[1] - LATENT_RANK) // 2
    freqs = 10000.0 ** (-jnp.arange(half, dtype=jnp.float32) / half)
    freqs = jnp.tile(freqs, 128 // half)[None, :]
    router_t = jnp.pad(router.T, ((0, 128 - experts), (0, 0)))
    gains = [g_attn[None, :], latent_norm_gain[None, :], g_ffn[None, :]]
    weights = [w_query, key_value_down_weight.T, key_value_up_weight, w_out]
    everyone_grad = lax.all_gather(grad_out, "dp")
    hidden, ffn_bf, dense_gates, probs, normed, *saved = forward_tuned(
        lengths, freqs, tokens, routes, *gains, router_t, *weights
    )
    queries, kv, key_turned, latent_bf, latent, context, log_totals = saved
    part = shared_gate.shape[1] // devices
    shared_parts = [
        lax.dynamic_slice_in_dim(w, own * part, part, 1)
        for w in (shared_gate, shared_up, shared_down)
    ]
    ffn_part, grad_ffn_part, *expert_grads, shared_grads = ffn_with_kernel(
        ffn_bf,
        dense_gates,
        everyone_grad,
        [w[0] for w in (expert_gate, expert_up, expert_down)],
        shared_parts,
        capacity,
        experts,
    )
    shared_grads = shared_home(shared_grads, part)
    ffn_total = lax.psum_scatter(
        ffn_part.reshape(devices * rows_here, features), "dp", scatter_dimension=0, tiled=True
    )
    ffn_total = lax.psum(ffn_total, "tensor").astype(jnp.float32)
    output = (hidden + ffn_total).astype(jnp.bfloat16)
    (sums,) = scatter_sums([grad_ffn_part], 2, 3, jnp.float32, True)
    grad_tokens, grad_hidden_bf, grad_query, grad_kv, grad_low, vectors = backward_tuned(
        lengths,
        freqs,
        sums,
        [hidden, grad_out, tokens, probs],
        gains,
        router_t,
        [queries, kv, key_turned, latent, log_totals],
        weights,
    )
    share_rows = features // devices
    columns = key_value_down_weight.shape[1]
    grad_columns = lax.dynamic_slice_in_dim(
        grad_low, rank * (columns // ranks), columns // ranks, 1
    )
    products = [
        contract_first(normed, grad_query),
        contract_first(grad_hidden_bf, context),
        contract_first(latent_bf, grad_kv),
        contract_first(normed, grad_columns),
    ]
    blocks = [
        a.astype(jnp.bfloat16).reshape(devices, a.shape[0] // devices, a.shape[1])
        for a in products
    ]
    vectors = vectors.reshape(experts + 8, devices, share_rows).transpose(1, 0, 2)
    vectors = vectors.at[:, experts + 2 : experts + 2 + LATENT_RANK // 128].set(
        vectors[:1, experts + 2 : experts + 2 + LATENT_RANK // 128]
    )
    grad_w_query, grad_w_out, grad_w_kv_up, grad_w_kv_down, vectors = scatter_sums(
        blocks + [vectors], 2, 5, jnp.float32
    )
    router_rows = share_rows // ranks
    grad_router = lax.dynamic_slice_in_dim(vectors[:experts], rank * router_rows, router_rows, 1).T
    latent_rows = LATENT_RANK // devices // ranks
    grad_g_kv = lax.dynamic_slice_in_dim(
        vectors[experts + 2 : experts + 2 + LATENT_RANK // 128].reshape(-1),
        (own * ranks + rank) * latent_rows,
        latent_rows,
        0,
    )
    return (
        output,
        grad_tokens,
        vectors[experts],
        grad_w_query,
        grad_w_kv_down,
        grad_g_kv,
        grad_w_kv_up,
        grad_w_out,
        vectors[experts + 1],
        grad_router,
        *shared_grads,
        *expert_grads,
    )


def shards(
    tokens,
    lengths,
    routes,
    grad_out,
    g_attn,
    w_query,
    key_value_down_weight,
    latent_norm_gain,
    key_value_up_weight,
    w_out,
    g_ffn,
    router,
    shared_gate,
    shared_up,
    shared_down,
    expert_gate,
    expert_up,
    expert_down,
):
    rows_here = tokens.shape[0]
    features = tokens.shape[1]
    heads_local = w_out.shape[1] // VALUE_HEAD_SIZE
    devices = lax.axis_size("dp")
    capacity = rows_here * TOPK * 4 // (3 * devices)
    experts = router.shape[1]
    highest = lax.Precision.HIGHEST
    softmax_scale = QK ** (-0.5)
    segment, token_position = doc_layout(lengths[0], rows_here)
    places = jnp.arange(rows_here, dtype=jnp.int32)
    allowed = (segment[:, None] == segment[None, :]) & (places[None, :] <= places[:, None])
    tokens_f = tokens.astype(jnp.float32)
    attn_normed, attn_unit, attn_factor = rms_normalize_pieces(tokens_f, g_attn)
    normed_bf = attn_normed.astype(jnp.bfloat16)
    query_full = jnp.dot(normed_bf, w_query, preferred_element_type=jnp.float32).reshape(
        rows_here, heads_local, QK
    )
    query_bf = jnp.concatenate(
        [
            query_full[..., :PLAIN_HEAD_SIZE],
            apply_rotation(query_full[..., PLAIN_HEAD_SIZE:], token_position),
        ],
        axis=-1,
    ).astype(jnp.bfloat16)
    latent_with_key = jnp.dot(normed_bf, key_value_down_weight, preferred_element_type=jnp.float32)
    key_turned_part = apply_rotation(latent_with_key[:, LATENT_RANK:], token_position).astype(
        jnp.bfloat16
    )
    latent_after_norm, latent_unit_scale, latent_norm_factor = rms_normalize_pieces(
        latent_with_key[:, :LATENT_RANK], latent_norm_gain
    )
    latent_bf = latent_after_norm.astype(jnp.bfloat16)
    key_value = (
        jnp.dot(latent_bf, key_value_up_weight, preferred_element_type=jnp.float32)
        .astype(jnp.bfloat16)
        .reshape(rows_here, heads_local, PLAIN_HEAD_SIZE + VALUE_HEAD_SIZE)
    )
    key_nope = key_value[..., :PLAIN_HEAD_SIZE]
    value = key_value[..., PLAIN_HEAD_SIZE:]

    def masked_scores():
        raw = jnp.einsum(
            "thd,shd->hts",
            query_bf[..., :PLAIN_HEAD_SIZE],
            key_nope,
            preferred_element_type=jnp.float32,
        )
        raw = raw + jnp.einsum(
            "thd,sd->hts",
            query_bf[..., PLAIN_HEAD_SIZE:],
            key_turned_part,
            preferred_element_type=jnp.float32,
        )
        return jnp.where(allowed[None], raw * softmax_scale, -jnp.inf)

    scores = masked_scores()
    top_score = jnp.max(scores, axis=-1, keepdims=True)
    expo = jnp.exp(scores - top_score)
    total = jnp.sum(expo, axis=-1, keepdims=True)
    log_total = top_score + jnp.log(total)
    attn_weights = (expo / total).astype(jnp.bfloat16)
    context = jnp.einsum("hts,shd->thd", attn_weights, value, preferred_element_type=jnp.float32)
    context = context.astype(jnp.bfloat16).reshape(rows_here, heads_local * VALUE_HEAD_SIZE)
    (attn,) = product_sum(context, w_out, [])
    hidden = tokens_f + attn
    ffn_normed, ffn_unit, ffn_factor = rms_normalize_pieces(hidden, g_ffn)
    ffn_bf = ffn_normed.astype(jnp.bfloat16)
    router_probs = jax.nn.softmax(jnp.dot(ffn_normed, router, precision=highest), axis=-1)
    own = lax.axis_index("dp")

    named = jnp.any(routes[:, :, None] == jnp.arange(128, dtype=jnp.int32)[None, None, :], axis=1)
    dense_gates = jnp.where(named, jnp.pad(router_probs, ((0, 0), (0, 128 - experts))), -1.0)
    everyone_grad = lax.all_gather(grad_out, "dp")
    part = shared_gate.shape[1] // devices
    shared_parts = [
        lax.dynamic_slice_in_dim(w, own * part, part, 1)
        for w in (shared_gate, shared_up, shared_down)
    ]
    (
        ffn_part,
        grad_ffn_part,
        grad_expert_gate,
        grad_expert_up,
        grad_expert_down,
        shared_grads,
    ) = ffn_plain(
        ffn_bf,
        dense_gates,
        everyone_grad,
        [w[0] for w in (expert_gate, expert_up, expert_down)],
        shared_parts,
        capacity,
        experts,
    )
    share_rows = features // devices
    grad_shared_gate, grad_shared_up, grad_shared_down = shared_home(shared_grads, part)

    grad_top = grad_out.astype(jnp.float32)
    ffn_total = lax.psum_scatter(
        ffn_part.reshape(devices * rows_here, features), "dp", scatter_dimension=0, tiled=True
    )
    ffn_total = lax.psum(ffn_total, "tensor").astype(jnp.float32)
    output = (hidden + ffn_total).astype(jnp.bfloat16)
    (grad_ffn_sum,) = sum_home([grad_ffn_part], True)
    dense_grad = (
        grad_ffn_sum[:, features : features + experts]
        + grad_ffn_sum[:, features + experts : features + 2 * experts]
    )
    grad_logits = router_probs * (
        dense_grad - jnp.sum(router_probs * dense_grad, axis=-1, keepdims=True)
    )
    grad_router_in = contract_last(grad_logits, router, highest)
    grad_router_part = contract_first(ffn_normed, grad_logits, highest)
    grad_ffn_total = grad_ffn_sum[:, :features] + grad_router_in
    grad_g_ffn = jnp.sum(grad_ffn_total * ffn_unit, axis=0)
    grad_hidden = grad_top + normalize_back(grad_ffn_total, ffn_unit, ffn_factor, g_ffn)
    grad_hidden_bf = grad_hidden.astype(jnp.bfloat16)
    grad_w_out = contract_first(grad_hidden_bf, context)
    grad_context = jnp.dot(grad_hidden_bf, w_out, preferred_element_type=jnp.float32).astype(
        jnp.bfloat16
    )
    grad_context = grad_context.reshape(rows_here, heads_local, VALUE_HEAD_SIZE)
    redone = jnp.exp(masked_scores() - log_total)
    redone_bf = redone.astype(jnp.bfloat16)
    grad_weights = jnp.einsum(
        "thd,shd->hts", grad_context, value, preferred_element_type=jnp.float32
    )
    grad_value = jnp.einsum(
        "hts,thd->shd", redone_bf, grad_context, preferred_element_type=jnp.float32
    )
    row_inner = jnp.sum(redone * grad_weights, axis=-1, keepdims=True)
    grad_raw = (redone * (grad_weights - row_inner) * softmax_scale).astype(jnp.bfloat16)
    grad_query_nope = jnp.einsum(
        "hts,shd->thd", grad_raw, key_nope, preferred_element_type=jnp.float32
    )
    grad_query_rot = jnp.einsum(
        "hts,sd->thd", grad_raw, key_turned_part, preferred_element_type=jnp.float32
    )
    grad_key_nope = jnp.einsum(
        "hts,thd->shd",
        grad_raw,
        query_bf[..., :PLAIN_HEAD_SIZE],
        preferred_element_type=jnp.float32,
    )
    grad_key_rot = jnp.einsum(
        "hts,thd->sd", grad_raw, query_bf[..., PLAIN_HEAD_SIZE:], preferred_element_type=jnp.float32
    )
    grad_query = jnp.concatenate(
        [grad_query_nope, apply_rotation(grad_query_rot, -token_position)], axis=-1
    )
    grad_query = grad_query.reshape(rows_here, heads_local * QK).astype(jnp.bfloat16)
    grad_w_query = contract_first(normed_bf, grad_query)
    grad_key_value = (
        jnp.concatenate([grad_key_nope, grad_value], axis=-1)
        .reshape(rows_here, heads_local * (PLAIN_HEAD_SIZE + VALUE_HEAD_SIZE))
        .astype(jnp.bfloat16)
    )
    grad_w_kv_up = contract_first(latent_bf, grad_key_value)
    grad_latent_normed = contract_last(grad_key_value, key_value_up_weight)
    grad_latent_part = jnp.concatenate(
        [grad_latent_normed, apply_rotation(grad_key_rot, -token_position)], axis=1
    ).astype(jnp.bfloat16)
    grad_in_summed, grad_latent_sum = product_sum(grad_query, w_query, [grad_latent_part])
    grad_latent_normed = grad_latent_sum[:, :LATENT_RANK]
    grad_g_kv = jnp.sum(grad_latent_normed * latent_unit_scale, axis=0)
    grad_latent = normalize_back(
        grad_latent_normed, latent_unit_scale, latent_norm_factor, latent_norm_gain
    )
    grad_down = jnp.concatenate([grad_latent, grad_latent_sum[:, LATENT_RANK:]], axis=1)
    grad_down_bf = grad_down.astype(jnp.bfloat16)
    share = grad_down.shape[1] // lax.axis_size("tensor")
    grad_columns = lax.dynamic_slice_in_dim(
        grad_down_bf, lax.axis_index("tensor") * share, share, 1
    )
    grad_w_kv_down = contract_first(normed_bf, grad_columns)
    grad_attn_in = grad_in_summed + contract_last(grad_down_bf, key_value_down_weight)
    grad_g_attn = jnp.sum(grad_attn_in * attn_unit, axis=0)
    grad_tokens = grad_hidden + normalize_back(grad_attn_in, attn_unit, attn_factor, g_attn)
    vectors = jnp.concatenate(
        [
            grad_router_part,
            grad_g_attn[:, None],
            grad_g_ffn[:, None],
            jnp.pad(
                grad_g_kv.reshape(devices, -1), ((0, 0), (0, share_rows - LATENT_RANK // devices))
            ).reshape(-1, 1),
            jnp.zeros((features, 128 - experts - 3), jnp.float32),
        ],
        axis=1,
    )
    blocks = [
        a.astype(jnp.bfloat16).reshape(devices, a.shape[0] // devices, a.shape[1])
        for a in (grad_w_query, grad_w_out, grad_w_kv_up, grad_w_kv_down)
    ]
    grad_w_query, grad_w_out, grad_w_kv_up, grad_w_kv_down, vectors = sum_home(
        blocks + [vectors.reshape(devices, share_rows, 128)]
    )
    rank, ranks = lax.axis_index("tensor"), lax.axis_size("tensor")
    router_rows = share_rows // ranks
    grad_router = lax.dynamic_slice_in_dim(vectors[:, :experts], rank * router_rows, router_rows, 0)
    latent_rows = LATENT_RANK // devices // ranks
    grad_g_kv = lax.dynamic_slice_in_dim(
        vectors[:, experts + 2], rank * latent_rows, latent_rows, 0
    )
    return (
        output,
        grad_tokens,
        vectors[:, experts],
        grad_w_query,
        grad_w_kv_down,
        grad_g_kv,
        grad_w_kv_up,
        grad_w_out,
        vectors[:, experts + 1],
        grad_router,
        grad_shared_gate,
        grad_shared_up,
        grad_shared_down,
        grad_expert_gate,
        grad_expert_up,
        grad_expert_down,
    )


def solution(mesh):
    in_specs = (
        P("dp", None),
        P("dp", None),
        P("dp", None),
        P("dp", None),
        P(),
        P(None, "tensor"),
        P(),
        P(),
        P(None, "tensor"),
        P(None, "tensor"),
        P(),
        P(),
        P(None, "tensor"),
        P(None, "tensor"),
        P(None, "tensor"),
        P("dp", None, "tensor"),
        P("dp", None, "tensor"),
        P("dp", None, "tensor"),
    )
    out_specs = (
        P("dp", None),
        P("dp", None),
        P("dp"),
        P("dp", "tensor"),
        P("dp", "tensor"),
        P(("dp", "tensor")),
        P("dp", "tensor"),
        P("dp", "tensor"),
        P("dp"),
        P(("dp", "tensor"), None),
        P("dp", "tensor"),
        P("dp", "tensor"),
        P("dp", "tensor"),
        P("dp", None, "tensor"),
        P("dp", None, "tensor"),
        P("dp", None, "tensor"),
    )
    tuned = mesh.shape["dp"] == 16 and mesh.shape["tensor"] == 2
    return jax.shard_map(
        shards_tuned if tuned else shards, mesh=mesh, in_specs=in_specs, out_specs=out_specs, check_vma=False)
```

```python
import functools

import jax
import jax.numpy as jnp
from jax import lax
from jax.experimental import pallas as pl
from jax.experimental.pallas import tpu as pltpu
from jax.sharding import PartitionSpec as P

PLAIN_HEAD_SIZE = 128
VALUE_HEAD_SIZE = 128
QK = 192
LATENT_RANK = 512
TOPK = 6


epsilon = 1e-06


def rms_normalize_pieces(values, gain):
    factor = lax.rsqrt(jnp.mean(values * values, axis=-1, keepdims=True) + epsilon)
    unit = values * factor
    return (unit * gain, unit, factor)


def normalize_back(grad, unit, factor, gain):
    inner = grad * gain
    return factor * (inner - unit * jnp.mean(inner * unit, axis=-1, keepdims=True))


def apply_rotation(values, token_position):
    half = values.shape[-1] // 2
    freqs = 10000.0 ** (-jnp.arange(half, dtype=jnp.float32) / half)
    angles = token_position.astype(jnp.float32)[:, None] * freqs[None, :]
    shape = (angles.shape[0],) + (1,) * (values.ndim - 2) + (half,)
    cosine = jnp.cos(angles).reshape(shape)
    sine = jnp.sin(angles).reshape(shape)
    first = values[..., :half]
    second = values[..., half:]
    return jnp.concatenate(
        [first * cosine - second * sine, second * cosine + first * sine], axis=-1
    )


def doc_layout(lengths_row, rows_here):
    ends = jnp.cumsum(lengths_row)
    starts = ends - lengths_row
    places = jnp.arange(rows_here, dtype=jnp.int32)
    segment = jnp.sum((places[:, None] >= ends[None, :]).astype(jnp.int32), axis=1)
    member = segment[:, None] == jnp.arange(lengths_row.shape[0], dtype=jnp.int32)[None, :]
    begins = jnp.sum(jnp.where(member, starts[None, :], 0), axis=1)
    return (segment, places - begins)


def contract_last(left, right, precision=None):
    return lax.dot_general(
        left,
        right,
        (((1,), (1,)), ((), ())),
        precision=precision,
        preferred_element_type=jnp.float32,
    )


def contract_first(left, right, precision=None):
    return lax.dot_general(
        left,
        right,
        (((0,), (0,)), ((), ())),
        precision=precision,
        preferred_element_type=jnp.float32,
    )


def swish_parts(gate_pre):
    sigma = jax.nn.sigmoid(gate_pre)
    return (gate_pre * sigma, sigma * (1.0 + gate_pre * (1.0 - sigma)))


VMEM_LIMIT = 60 * 1024 * 1024


def place_of(x_size):
    me = lax.axis_index("dp")
    core = me % 2
    x = (me // 2) % x_size
    z = me // (2 * x_size)
    return z, x, core


def index_of(z, x, core, x_size):
    return (z * x_size + x) * 2 + core


def remote(src, dst, send_sem, recv_sem, target):
    return pltpu.make_async_remote_copy(
        src_ref=src,
        dst_ref=dst,
        send_sem=send_sem,
        recv_sem=recv_sem,
        device_id={"dp": target},
        device_id_type=pl.DeviceIdType.MESH,
    )


def greet(z, x, core, z_size, x_size, pair=False):
    barrier = pltpu.get_barrier_semaphore()

    def tell(target):
        pl.semaphore_signal(
            barrier, inc=1, device_id={"dp": target}, device_id_type=pl.DeviceIdType.MESH
        )

    tell(index_of(z, x, 1 - core, x_size))
    tell(index_of(z, 1 - x, core, x_size))

    @pl.when(z > 0)
    def _():
        tell(index_of(z - 1, x, core, x_size))

    @pl.when(z < z_size - 1)
    def _():
        tell(index_of(z + 1, x, core, x_size))

    inner = (z + z_size - 1) // z_size - z // (z_size - 1)
    if pair:
        pl.semaphore_signal(
            barrier,
            inc=1,
            device_id={"tensor": 1 - lax.axis_index("tensor")},
            device_id_type=pl.DeviceIdType.MESH,
        )
    pl.semaphore_wait(barrier, 3 + inner + (1 if pair else 0))


def near_first(z):
    half = z // 2
    return [z, (1 - z) * (1 - 2 * half), 2 * (1 - half) + half * (7 - 2 * z), 3 - 3 * half]


def add_into(dst, *srcs):
    rows = dst.shape[0]
    step = 32 if rows % 32 == 0 else 8

    def body(i, _):
        here = pl.ds(pl.multiple_of(i * step, step), step)
        total = dst[here, :].astype(jnp.float32)
        for src in srcs:
            total = total + src[here, :].astype(jnp.float32)
        dst[here, :] = total.astype(dst.dtype)
        return 0

    lax.fori_loop(0, rows // step, body, 0)


def scatter_kernel(x_size, parts, pair, *refs):
    z_size = 4
    ins, outs, refs = refs[:parts], refs[parts : 2 * parts], refs[2 * parts :]
    own, c_buf, x_buf, z_buf = (refs[i * parts : (i + 1) * parts] for i in range(4))
    refs = refs[4 * parts :]
    y_buf = None
    if pair:
        y_buf, y_s, y_r, refs = refs[:parts], refs[parts], refs[parts + 1], refs[parts + 2 :]
    l_sem, c_s, c_r, x_s, x_r, z_s, z_r = refs
    z, x, core = place_of(x_size)
    at = functools.partial(index_of, x_size=x_size)
    half = z // 2
    inner = ((z + 3) // 4) * ((6 - z) // 4)
    order = [3 - 3 * half, 2 - half, 1 - z + 4 * half, z]
    load = lambda p, w, v: pltpu.make_async_copy(
        ins[p].at[at(w, v, core)], own[p].at[w, v], l_sem.at[p, w, v]
    )
    beside = lambda p, w, v: remote(
        ins[p].at[at(w, v, 1 - core)],
        c_buf[p].at[w, v],
        c_s.at[p, w, v],
        c_r.at[p, w, v],
        at(z, x, 1 - core),
    )
    across = lambda p, w: remote(
        c_buf[p].at[w, 1 - x], x_buf[p].at[w], x_s.at[p, w], x_r.at[p, w], at(z, 1 - x, core)
    )

    def along(p, w, slot, target):
        return remote(
            c_buf[p].at[w, x], z_buf[p].at[slot], z_s.at[p, w], z_r.at[p, slot], at(target, x, core)
        )

    twin = lambda p: pltpu.make_async_remote_copy(
        src_ref=c_buf[p].at[z, x],
        dst_ref=y_buf[p],
        send_sem=y_s.at[p],
        recv_sem=y_r.at[p],
        device_id={"tensor": 1 - lax.axis_index("tensor")},
        device_id_type=pl.DeviceIdType.MESH,
    )

    for v in (1 - x, x):
        for w in order:
            for p in range(parts):
                load(p, w, v).start()
    greet(z, x, core, z_size, x_size, pair)
    for v in (1 - x, x):
        for w in order:
            for p in range(parts):
                beside(p, w, v).start()
    for w in order:
        for p in range(parts):
            load(p, w, 1 - x).wait()
            beside(p, w, 1 - x).wait_recv()
            add_into(c_buf[p].at[w, 1 - x], own[p].at[w, 1 - x])
            across(p, w).start()
    for k, w in enumerate(order):
        for p in range(parts):
            load(p, w, x).wait()
            beside(p, w, x).wait_recv()
            add_into(c_buf[p].at[w, x], own[p].at[w, x])
            across(p, w).wait_recv()
            if k < 3:

                @pl.when(inner == 1)
                def _():
                    along(p, w, w, z).wait_recv()
                    add_into(c_buf[p].at[w, x], x_buf[p].at[w], z_buf[p].at[w])

                @pl.when(inner == 0)
                def _():
                    add_into(c_buf[p].at[w, x], x_buf[p].at[w])

                @pl.when(w > z)
                def _():
                    along(p, w, w, z + 1).start()

                @pl.when(w < z - 1)
                def _():
                    along(p, w, w, z - 1).start()

                @pl.when(w == z - 1)
                def _():
                    along(p, w, z_size, z - 1).start()

            else:
                add_into(c_buf[p].at[w, x], x_buf[p].at[w])

                @pl.when(z > 0)
                def _():
                    along(p, w, z, z).wait_recv()
                    add_into(c_buf[p].at[w, x], z_buf[p].at[z])

                @pl.when(z < z_size - 1)
                def _():
                    along(p, w, z_size, z).wait_recv()
                    add_into(c_buf[p].at[w, x], z_buf[p].at[z_size])

                if pair:
                    twin(p).start()
                else:
                    outs[p][...] = c_buf[p][z, x].astype(outs[p].dtype)
    if pair:
        for p in range(parts):
            twin(p).wait()
            outs[p][...] = (
                c_buf[p][z, x].astype(jnp.float32) + y_buf[p][...].astype(jnp.float32)
            ).astype(outs[p].dtype)
    for w in range(z_size):
        for p in range(parts):
            for v in range(x_size):
                beside(p, w, v).wait_send()
            across(p, w).wait_send()

            @pl.when(z != w)
            def _():
                along(p, w, w, z).wait_send()


def scatter_sums(arrays, x_size, collective_id, out_dtype, pair=False):
    parts = len(arrays)
    dma = pltpu.SemaphoreType.DMA
    blocks = [a.shape[1:] for a in arrays]
    return pl.pallas_call(
        functools.partial(scatter_kernel, x_size, parts, pair),
        out_shape=[jax.ShapeDtypeStruct(b, out_dtype) for b in blocks],
        in_specs=[pl.BlockSpec(memory_space=pl.ANY)] * parts,
        out_specs=[pl.BlockSpec(memory_space=pltpu.VMEM)] * parts,
        scratch_shapes=[pltpu.VMEM((4, x_size) + b, a.dtype) for a, b in zip(arrays, blocks)]
        + [pltpu.VMEM((4, x_size) + b, a.dtype) for a, b in zip(arrays, blocks)]
        + [pltpu.VMEM((4,) + b, a.dtype) for a, b in zip(arrays, blocks)]
        + [pltpu.VMEM((5,) + b, a.dtype) for a, b in zip(arrays, blocks)]
        + ([pltpu.VMEM(b, a.dtype) for a, b in zip(arrays, blocks)] + [dma((parts,))] * 2 if pair else [])
        + [dma((parts, 4, x_size))] * 3
        + [dma((parts, 4))] * 3
        + [dma((parts, 5))],
        compiler_params=pltpu.CompilerParams(
            collective_id=collective_id, has_side_effects=True, vmem_limit_bytes=VMEM_LIMIT
        ),
        name="scatter_sums",
    )(*arrays)


def nn(left, right):
    return lax.dot_general(
        left, right, (((1,), (0,)), ((), ())), preferred_element_type=jnp.float32
    )


def is_at(j, where):
    low = (3 - j) // 3
    high = j // 3
    return (low, (4 - j) // 3 - low, (j + 1) // 3 - high, high)[where]


def ffn_kernel(
    x_size,
    own_ffn,
    own_gates,
    grad_half,
    gate_t,
    up_t,
    down_t,
    shared_in,
    shared_out,
    out_part,
    dx_part,
    rows_all,
    dy_all,
    he_all,
    dge_all,
    due_all,
    shared_grads,
    grad_all,
    blk,
    gts,
    gate_v,
    up_v,
    down_v,
    s_in,
    s_out,
    g_buf,
    rows_b,
    grow_b,
    dy_b,
    he_b,
    dge_b,
    due_b,
    out_r,
    dx_r,
    out_l,
    dx_l,
    out_st,
    dx_st,
    acc,
    gate_col,
    dgate_acc,
    left_ffn,
    left_grad,
    own_sem,
    up_s,
    up_r,
    dn_s,
    dn_r,
    x_s,
    x_r,
    c_s,
    c_r,
    w_sem,
    g_sem,
    st_sem,
    h_s,
    h_r,
    y_s,
    y_r,
    hc_s,
    hc_r,
):
    z_size, bf16, f32 = 4, jnp.bfloat16, jnp.float32
    hidden = gate_t.shape[0]
    rows_here, features = own_ffn.shape
    slots = rows_b.shape[0] // 2
    wide = 512
    z, x, core = place_of(x_size)
    own = lax.axis_index("dp")
    at = functools.partial(index_of, x_size=x_size)
    ins, outs = (own_ffn, own_gates), (blk, gts)
    order = near_first(z)

    def place(j):
        return sum(is_at(j, i) * order[i] for i in range(4))

    weights = [
        pltpu.make_async_copy(gate_t, gate_v.at[pl.ds(0, hidden)], w_sem.at[0]),
        pltpu.make_async_copy(up_t, up_v.at[pl.ds(0, hidden)], w_sem.at[1]),
        pltpu.make_async_copy(down_t, down_v.at[pl.ds(0, hidden)], w_sem.at[2]),
        pltpu.make_async_copy(shared_in, s_in, w_sem.at[3]),
        pltpu.make_async_copy(shared_out, s_out, w_sem.at[4]),
    ]
    keep = [
        pltpu.make_async_copy(ins[a], outs[a].at[at(z, x, core)], own_sem.at[a]) for a in range(2)
    ]

    def grad_copy(k):
        w, v = place(k // 2), x + (k % 2) * (1 - 2 * x)
        return pltpu.make_async_copy(
            grad_all.at[pl.ds(2 * (w * x_size + v), 2)], g_buf.at[k % 2], g_sem.at[k % 2]
        )

    for copy in keep + weights:
        copy.start()
    grad_copy(0).start()
    greet(z, x, core, z_size, x_size, True)

    def up(a, d):
        block = outs[a].at[at(z - d, x, core)]
        src = ins[a] if d == 0 else block
        return remote(src, block, up_s.at[a, d], up_r.at[a, d], at(z + 1, x, core))

    def down(a, d):
        block = outs[a].at[at(z + d, x, core)]
        src = ins[a] if d == 0 else block
        return remote(src, block, dn_s.at[a, d], dn_r.at[a, d], at(z - 1, x, core))

    def across(a, w, first=False):
        block = outs[a].at[at(w, x, core)]
        src = ins[a] if first else block
        return remote(src, block, x_s.at[a, w], x_r.at[a, w], at(z, 1 - x, core))

    def beside(a, w, v, first=False):
        block = outs[a].at[at(w, v, core)]
        src = ins[a] if first else block
        return remote(src, block, c_s.at[a, w, v], c_r.at[a, w, v], at(z, x, 1 - core))

    rank = lax.axis_index("tensor")
    edge = 1 - ((z + 3) // 4) * ((6 - z) // 4)
    part_rows = rows_here // 2

    def part(j, v, which):
        store = blk if j in (1, 4) else grad_all
        rows = pl.ds(pl.multiple_of(which * part_rows, part_rows), part_rows)
        return store.at[at(order[2 if j < 2 else 3], v, core), rows]

    def link(j, target=0):
        block = part(j, x, rank)
        target = at(target, x, core) if j == 2 else at(z, 1 - x, core)
        return remote(block, block, h_s.at[j], h_r.at[j], target)

    landed = lambda j: x if j == 2 else 1 - x

    def swap(j):
        block = part(j, landed(j), rank)
        return pair_copy(block, block, y_s.at[j], y_r.at[j])

    def half_beside(j, i):
        block = part(j, landed(j), rank + i * (1 - 2 * rank))
        return remote(block, block, hc_s.at[j, i], hc_r.at[j, i], at(z, x, 1 - core))

    def link_done(j):
        link(j).wait_recv()
        swap(j).start()
        half_beside(j, 0).start()

    def swap_done(j):
        swap(j).wait_recv()
        half_beside(j, 1).start()

    def ready(j):
        half_beside(j, 0).wait_recv()
        half_beside(j, 1).wait_recv()

    for a in (1, 0):
        beside(a, z, x, True).start()
        across(a, z, True).start()
        pl.when(z < z_size - 1)(lambda: up(a, 0).start())
        pl.when(z > 0)(lambda: down(a, 0).start())

    def pass_on(d):
        for a in (1, 0):

            @pl.when(z >= d)
            def _():
                up(a, d - 1).wait_recv()
                pl.when(z < z_size - 1)(lambda: up(a, d).start())
                beside(a, z - d, x).start()

            @pl.when(z + d < z_size)
            def _():
                down(a, d - 1).wait_recv()
                pl.when(z > 0)(lambda: down(a, d).start())
                beside(a, z + d, x).start()

    def from_across(w, arrays=(1, 0)):
        for a in arrays:
            across(a, w).wait_recv()
            beside(a, w, 1 - x).start()

    def at_ends(do):
        pl.when(edge == 1)(do)

    def inside(do):
        pl.when(edge == 0)(do)

    def far_over_x():
        link(4).start()
        across(1, order[3]).start()

    def early(k):
        @pl.when(k == 1)
        def _():
            pass_on(1)
            for a in (1, 0):
                across(a, order[1]).start()
            link(0).start()
            from_across(order[0])

        @pl.when((k == 2) & (edge == 0))
        def _():
            link(2, 3 * (z - 1)).start()

        @pl.when(k == 3)
        def _():
            pass_on(2)
            link(1).start()
            across(1, order[2]).start()

            @inside
            def _():
                link(3).start()
                far_over_x()

            from_across(order[1])

        @pl.when((k == 4) & (edge == 1))
        def _():
            link_done(2)
            link(3).start()

        @pl.when(k == 5)
        def _():
            ready(0)
            grad_copy(5).start()
            pass_on(3)
            at_ends(far_over_x)
            swap_done(1)
            at_ends(lambda: swap_done(2))
            from_across(order[2], (1,))
            ready(1)

        @pl.when(k == 6)
        def _():
            link_done(4)
            from_across(order[3], (1,))

        @pl.when(k == 7)
        def _():
            ready(3)
            grad_copy(7).start()
            swap_done(4)
            ready(4)

    def midway(k):
        pl.when(k == 3)(lambda: link_done(0))

        @pl.when(k == 4)
        def _():
            link_done(1)
            swap_done(0)

        @pl.when(k == 5)
        def _():
            at_ends(lambda: ready(2))
            grad_copy(6).start()
            link_done(3)

        pl.when(k == 6)(lambda: swap_done(3))

    gate_v[pl.ds(hidden, gate_v.shape[0] - hidden), :] = jnp.zeros(
        (gate_v.shape[0] - hidden, features), bf16
    )
    up_v[pl.ds(hidden, up_v.shape[0] - hidden), :] = jnp.zeros(
        (up_v.shape[0] - hidden, features), bf16
    )
    down_v[pl.ds(hidden, down_v.shape[0] - hidden), :] = jnp.zeros(
        (down_v.shape[0] - hidden, features), bf16
    )
    acc[...] = jnp.zeros(acc.shape, f32)
    for copy in weights:
        copy.wait()
    for a in range(2):
        out_r[a, pl.ds(slots, 128), :] = s_out[...]
        dx_r[a, pl.ds(slots, 256), :] = s_in[...]
    for copy in keep:
        copy.wait()
    lane = lax.broadcasted_iota(jnp.int32, (rows_here, 128), 1)
    earlier = lax.broadcasted_iota(jnp.int32, (rows_here, rows_here), 1)
    later = lax.broadcasted_iota(jnp.int32, (rows_here, rows_here), 0)
    upto = (earlier <= later).astype(bf16)
    slot_lane = lax.broadcasted_iota(jnp.int32, (rows_here, slots), 1).astype(f32)

    def staged(pair, which):
        pairs = [
            (rows_b, rows_all),
            (dy_b, dy_all),
            (he_b, he_all),
            (dge_b, dge_all),
            (due_b, due_all),
            (out_st, out_part),
            (dx_st, dx_part),
        ]
        return [
            pltpu.make_async_copy(pairs[i][0], pairs[i][1].at[pair], st_sem.at[i]) for i in which
        ]

    def start_staged(pair, which):
        for copy in staged(pair, which):
            copy.start()

    def wait_staged(k, which):
        @pl.when(k > 0)
        def _():
            for copy in staged(0, which):
                copy.wait()

    def body(k, _):
        w, v = place(k // 2), x + (k % 2) * (1 - 2 * x)
        pair = w * x_size + v
        block = 2 * pair
        here = k % 2
        early(k)
        grad_copy(k).wait()
        pl.when(k < 4)(lambda: grad_copy(k + 1).start())
        pl.when((k != 5) & (k != 7))(lambda: beside(0, w, v).wait_recv())
        beside(1, w, v).wait_recv()

        for a in range(2):
            gates = gts[block + a]
            count = nn(upto, (gates >= 0.0).astype(bf16))
            gate = jnp.sum(jnp.where(lane == own, gates, 0.0), axis=1, keepdims=True)
            slot = jnp.sum(jnp.where(lane == own, count, 0.0), axis=1, keepdims=True) - 1.0
            pick = ((slot_lane == slot) & (gate >= 0.0)).astype(f32).astype(bf16)
            out_l[a, :, pl.ds(0, slots)] = pick
            dx_l[a, :, pl.ds(0, slots)] = pick
            high = gate.astype(bf16).astype(f32)
            middle = (gate - high).astype(bf16).astype(f32)
            low = gate - high - middle
            parts = jnp.where(
                lane == 0, high, jnp.where(lane == 1, middle, jnp.where(lane == 2, low, 0.0))
            ).astype(bf16)
            pick_t = pick.T
            left_ffn[a, pl.ds(0, slots), :] = pick_t
            left_grad[a, pl.ds(0, slots), :] = pick_t
            picked = jnp.sum(nn(pick_t, parts), axis=1, keepdims=True)
            gate_col[pl.ds(a * slots, slots), :] = jnp.broadcast_to(picked, (slots, 128))

        both = pl.ds(block, 2)
        pre = contract_last(blk[both].reshape(2 * rows_here, features), s_in[...])
        grad_hidden = contract_last(g_buf[here].reshape(2 * rows_here, features), s_out[...])
        act, slope = swish_parts(pre[:, :128])
        up_pre = pre[:, 128:]
        shared_units = (
            (act * up_pre).astype(bf16),
            (grad_hidden * up_pre * slope).astype(bf16),
            (grad_hidden * act).astype(bf16),
        )
        for a in range(2):
            mine = slice(a * rows_here, (a + 1) * rows_here)
            out_l[a, :, pl.ds(slots, 128)] = shared_units[0][mine]
            dx_l[a, :, pl.ds(slots, 128)] = shared_units[1][mine]
            dx_l[a, :, pl.ds(slots + 128, 128)] = shared_units[2][mine]
            left_ffn[a, pl.ds(slots, 128), :] = shared_units[1][mine].T
            left_ffn[a, pl.ds(slots + 128, 128), :] = shared_units[2][mine].T
            left_grad[a, pl.ds(slots, 128), :] = shared_units[0][mine].T

        def pick_rows(n, _):
            cols = pl.ds(pl.multiple_of(n * wide, wide), wide)
            for a in range(2):
                mine = pl.ds(a * slots, slots)
                product = nn(left_ffn[a], blk[block + a, :, cols])
                rows_b[mine, cols] = product[:slots].astype(bf16)
                acc[pl.ds(0, 256), cols] += product[slots:]
                product = nn(left_grad[a], g_buf[here, a, :, cols])
                grows = product[:slots]
                acc[pl.ds(256, 128), cols] += product[slots:]
                grow_b[mine, cols] = grows.astype(bf16)
                dy_b[mine, cols] = (gate_col[mine, pl.ds(0, 1)] * grows).astype(bf16)
            return 0

        wait_staged(k, (0, 1))
        lax.fori_loop(0, features // wide, pick_rows, 0)
        start_staged(pair, (0, 1))

        def hidden_units(n, _):
            units = pl.ds(pl.multiple_of(n * 256, 256), 256)
            gate_pre = contract_last(rows_b[...], gate_v[units, :])
            up_pre = contract_last(rows_b[...], up_v[units, :])
            grad_hidden = contract_last(dy_b[...], down_v[units, :])
            act, slope = swish_parts(gate_pre)
            he_b[:, units] = (act * up_pre).astype(bf16)
            dge_b[:, units] = (grad_hidden * up_pre * slope).astype(bf16)
            due_b[:, units] = (grad_hidden * act).astype(bf16)
            return 0

        wait_staged(k, (2, 3, 4))
        lax.fori_loop(0, gate_v.shape[0] // 256, hidden_units, 0)
        start_staged(pair, (2, 3, 4))
        midway(k)
        dgate_acc[...] = jnp.zeros(dgate_acc.shape, f32)

        def back(n, _):
            cols = pl.ds(pl.multiple_of(n * wide, wide), wide)
            result = nn(he_b[...], down_v[:, cols])
            product = grow_b[:, cols].astype(f32) * result
            for i in range(wide // 128):
                dgate_acc[...] += product[:, i * 128 : (i + 1) * 128]
            result = (gate_col[:, pl.ds(0, 1)] * result).astype(bf16)
            grad_in = (nn(dge_b[...], gate_v[:, cols]) + nn(due_b[...], up_v[:, cols])).astype(bf16)
            for a in range(2):
                mine = slice(a * slots, (a + 1) * slots)
                out_r[a, pl.ds(0, slots), cols] = result[mine]
                dx_r[a, pl.ds(0, slots), cols] = grad_in[mine]
                out_st[a, :, cols] = nn(out_l[a], out_r[a, :, cols]).astype(bf16)
                dx_st[a, :, cols] = nn(dx_l[a], dx_r[a, :, cols]).astype(bf16)
            return 0

        wait_staged(k, (5, 6))
        lax.fori_loop(0, features // wide, back, 0)
        dgate = jnp.sum(dgate_acc[...], axis=1, keepdims=True)
        high = dgate.astype(bf16).astype(f32)
        spread = lax.broadcasted_iota(jnp.int32, (2 * slots, 128), 1)
        spread = jnp.where(
            spread == own, high, jnp.where(spread == own + 16, dgate - high, 0.0)
        ).astype(bf16)
        for a in range(2):
            dx_st[a, :, pl.ds(features, 128)] = nn(
                out_l[a, :, pl.ds(0, slots)], spread[a * slots : (a + 1) * slots]
            ).astype(bf16)
        start_staged(pair, (5, 6))
        return 0

    lax.fori_loop(0, 8, body, 0)
    wait_staged(1, range(7))
    shared_grads[...] = acc[...].astype(bf16)
    for a in range(2):
        for i in range(z_size):
            beside(a, order[i], x).wait_send()
            if a == 1 or i < 2:
                beside(a, order[i], 1 - x).wait_send()
                across(a, order[i]).wait_send()
    for d in range(z_size):
        for a in range(2):
            pl.when((z >= d) & (z < z_size - 1))(lambda: up(a, d).wait_send())
            pl.when((z + d < z_size) & (z > 0))(lambda: down(a, d).wait_send())
    inside(lambda: link(2, 3 * (z - 1)).wait_send())
    for j in range(5):

        def sent_on(j=j):
            swap(j).wait_send()
            half_beside(j, 0).wait_send()
            half_beside(j, 1).wait_send()

        if j == 2:
            at_ends(sent_on)
        else:
            link(j).wait_send()
            sent_on()


def ffn_tuned(own_ffn, own_gates, grad_all, gate_t, up_t, down_t, shared_in, shared_out, slots):
    rows, features = own_ffn.shape
    hidden = gate_t.shape[0]
    padded = -(-hidden // 256) * 256
    bf16, f32, dma = jnp.bfloat16, jnp.float32, pltpu.SemaphoreType.DMA
    anywhere = pl.BlockSpec(memory_space=pl.ANY)
    shape = jax.ShapeDtypeStruct
    return pl.pallas_call(
        functools.partial(ffn_kernel, 2),
        out_shape=[
            shape((8, 2, rows, features), bf16),
            shape((8, 2, rows, features + 128), bf16),
            shape((8, 2 * slots, features), bf16),
            shape((8, 2 * slots, features), bf16),
            shape((8, 2 * slots, padded), bf16),
            shape((8, 2 * slots, padded), bf16),
            shape((8, 2 * slots, padded), bf16),
            shape((384, features), bf16),
            shape((16, rows, features), bf16),
        ],
        in_specs=[anywhere] * 8,
        out_specs=[anywhere] * 7 + [pl.BlockSpec(memory_space=pltpu.VMEM), anywhere],
        input_output_aliases={2: 8},
        scratch_shapes=[
            pltpu.VMEM((16, rows, features), bf16),
            pltpu.VMEM((16, rows, 128), f32),
            pltpu.VMEM((padded, features), bf16),
            pltpu.VMEM((padded, features), bf16),
            pltpu.VMEM((padded, features), bf16),
            pltpu.VMEM((256, features), bf16),
            pltpu.VMEM((128, features), bf16),
            pltpu.VMEM((2, 2, rows, features), bf16),
            pltpu.VMEM((2 * slots, features), bf16),
            pltpu.VMEM((2 * slots, features), bf16),
            pltpu.VMEM((2 * slots, features), bf16),
            pltpu.VMEM((2 * slots, padded), bf16),
            pltpu.VMEM((2 * slots, padded), bf16),
            pltpu.VMEM((2 * slots, padded), bf16),
            pltpu.VMEM((2, slots + 128, features), bf16),
            pltpu.VMEM((2, slots + 256, features), bf16),
            pltpu.VMEM((2, rows, slots + 128), bf16),
            pltpu.VMEM((2, rows, slots + 256), bf16),
            pltpu.VMEM((2, rows, features), bf16),
            pltpu.VMEM((2, rows, features + 128), bf16),
            pltpu.VMEM((384, features), f32),
            pltpu.VMEM((2 * slots, 128), f32),
            pltpu.VMEM((2 * slots, 128), f32),
            pltpu.VMEM((2, slots + 256, rows), bf16),
            pltpu.VMEM((2, slots + 128, rows), bf16),
            dma((2,)),
        ]
        + [dma((2, 4))] * 6
        + [dma((2, 4, 2))] * 2
        + [dma((5,)), dma((2,)), dma((7,))]
        + [dma((5,))] * 4
        + [dma((5, 2))] * 2,
        compiler_params=pltpu.CompilerParams(
            collective_id=1, has_side_effects=True, vmem_limit_bytes=VMEM_LIMIT
        ),
        name="ffn",
    )(
        own_ffn,
        own_gates,
        grad_all.reshape(16, rows, features),
        gate_t,
        up_t,
        down_t,
        shared_in,
        shared_out,
    )


def first_half(shape):
    return lax.broadcasted_iota(jnp.int32, shape, 1) % 64 < 32


def turn(values, cosine, sine):
    partner = jnp.where(
        first_half(values.shape), pltpu.roll(values, 96, 1), pltpu.roll(values, 32, 1)
    )
    return values * cosine + partner * sine


def layout_of(lengths, rows, width):
    row = lax.broadcasted_iota(jnp.int32, (rows, width), 0)
    across = lax.broadcasted_iota(jnp.int32, (rows, rows), 1)
    down = lax.broadcasted_iota(jnp.int32, (rows, rows), 0)
    place, met, end = row, across <= down, 0
    for i in range(lengths.shape[1]):
        end = end + lengths[0, i]
        place = place - jnp.where(row >= end, lengths[0, i], 0)
        met = met & ((across >= end) == (down >= end))
    return place, met


def turn_tables(lengths, freqs, rows):
    place, met = layout_of(lengths, rows, 128)
    angles = place.astype(jnp.float32) * freqs[...]
    sine = jnp.sin(angles)
    return jnp.cos(angles), jnp.where(first_half(angles.shape), -sine, sine), met


def pair_copy(src, dst, send_sem, recv_sem):
    return pltpu.make_async_remote_copy(
        src_ref=src,
        dst_ref=dst,
        send_sem=send_sem,
        recv_sem=recv_sem,
        device_id={"tensor": 1 - lax.axis_index("tensor")},
        device_id_type=pl.DeviceIdType.MESH,
    )


def greet_pair():
    barrier = pltpu.get_barrier_semaphore()
    pl.semaphore_signal(
        barrier,
        inc=1,
        device_id={"tensor": 1 - lax.axis_index("tensor")},
        device_id_type=pl.DeviceIdType.MESH,
    )
    pl.semaphore_wait(barrier, 1)


def forward_kernel(
    lengths,
    freqs,
    tokens,
    routes,
    g_attn,
    g_latent,
    g_ffn,
    router_t,
    w_query,
    down_t,
    kv_up,
    w_out,
    grad_out,
    hidden,
    ffn_bf,
    gates,
    probs,
    normed,
    queries,
    kv,
    key_turned,
    latent_bf,
    latent,
    context,
    log_totals,
    everyone,
    wq_v,
    down_v,
    up_v,
    out_v,
    sent,
    got,
    w_sem,
    s_sem,
    r_sem,
    own_sem,
    up_s,
    up_r,
    dn_s,
    dn_r,
    x_s,
    x_r,
    c_s,
    c_r,
):
    bf16, f32 = jnp.bfloat16, jnp.float32
    z_size, x_size = 4, 2
    z, x, core = place_of(x_size)
    at = functools.partial(index_of, x_size=x_size)
    rows, features = tokens.shape
    rank = kv_up.shape[0]
    heads = kv_up.shape[1] // 256
    turned = down_t.shape[0] - rank
    tail = pl.ds(rank, turned)
    loads = [
        pltpu.make_async_copy(down_t, down_v.at[pl.ds(0, rank + turned)], w_sem.at[0]),
        pltpu.make_async_copy(down_t.at[tail], down_v.at[pl.ds(rank + turned, turned)], w_sem.at[1]),
        pltpu.make_async_copy(kv_up, up_v, w_sem.at[2]),
        pltpu.make_async_copy(w_query, wq_v, w_sem.at[3]),
        pltpu.make_async_copy(w_out, out_v, w_sem.at[4]),
    ]
    keep = pltpu.make_async_copy(grad_out, everyone.at[at(z, x, core)], own_sem.at[0])

    def move(w, v, first, sems, target):
        block = everyone.at[at(w, v, core)]
        return remote(grad_out if first else block, block, *sems, target)

    up = lambda d: move(z - d, x, d == 0, (up_s.at[d], up_r.at[d]), at(z + 1, x, core))
    down = lambda d: move(z + d, x, d == 0, (dn_s.at[d], dn_r.at[d]), at(z - 1, x, core))
    across = lambda i, w: move(w, x, i == 0, (x_s.at[i], x_r.at[i]), at(z, 1 - x, core))
    beside = lambda w, v, first=False: move(
        w, v, first, (c_s.at[w, v], c_r.at[w, v]), at(z, x, 1 - core)
    )
    near = near_first(z)[1]

    def from_across(i, w):
        block = everyone.at[at(w, 1 - x, core)]
        remote(block, block, x_s.at[i], x_r.at[i], at(z, 1 - x, core)).wait_recv()
        beside(w, 1 - x).start()

    keep.start()
    for copy in loads:
        copy.start()
    greet(z, x, core, z_size, x_size, True)
    beside(z, x, True).start()
    across(0, z).start()
    pl.when(z < z_size - 1)(lambda: up(0).start())
    pl.when(z > 0)(lambda: down(0).start())
    cosine, sine, met = turn_tables(lengths, freqs, rows)
    values, _, _ = rms_normalize_pieces(tokens[...].astype(f32), g_attn[...])
    normed[...] = values.astype(bf16)
    loads[0].wait()
    loads[1].wait()
    low = contract_last(normed[...], down_v[...])
    latent[...] = low[:, :rank]
    key_turned[...] = turn(low[:, rank:], cosine, sine).astype(bf16)
    values, _, _ = rms_normalize_pieces(latent[...], g_latent[...])
    latent_bf[...] = values.astype(bf16)
    loads[2].wait()

    def keys(n, _):
        cols = pl.ds(pl.multiple_of(n * 512, 512), 512)
        kv[:, cols] = nn(latent_bf[...], up_v[:, cols]).astype(bf16)
        return 0

    lax.fori_loop(0, kv.shape[1] // 512, keys, 0)
    loads[3].wait()
    lane = lax.broadcasted_iota(jnp.int32, (rows, 128), 1)
    log_totals[...] = jnp.zeros(log_totals.shape, f32)

    def two_heads(i, _):
        three = nn(normed[...], wq_v[:, pl.ds(pl.multiple_of(i * 384, 384), 384)])
        middle, last = three[:, 128:256], three[:, 256:]
        plain = (
            three[:, :128],
            jnp.where(lane < 64, pltpu.roll(middle, 64, 1), pltpu.roll(last, 64, 1)),
        )
        spun = turn(jnp.where(lane < 64, middle, last), cosine, sine)
        for b in range(2):
            head = 2 * i + b
            queries[head, :, pl.ds(0, 128)] = plain[b].astype(bf16)
            queries[head, :, pl.ds(128, 128)] = jnp.where(
                (lane < 64) == (b == 0), spun, 0.0
            ).astype(bf16)
            at = pl.multiple_of(head * 256, 256)
            key = jnp.concatenate([kv[:, pl.ds(at, 128)], key_turned[...]], axis=1)
            raw = contract_last(queries[head], key)
            scores = jnp.where(met, raw * QK ** (-0.5), -jnp.inf)
            top = jnp.max(scores, axis=1, keepdims=True)
            expo = jnp.exp(scores - top)
            total = jnp.sum(expo, axis=1, keepdims=True)
            log_totals[...] = jnp.where(lane == head, top + jnp.log(total), log_totals[...])
            context[:, pl.ds(pl.multiple_of(head * 128, 128), 128)] = nn(
                (expo / total).astype(bf16), kv[:, pl.ds(at + 128, 128)]
            ).astype(bf16)
        return 0

    lax.fori_loop(0, heads // 2, two_heads, 0)

    loads[4].wait()
    chunks, width = sent.shape[0], sent.shape[2]
    chunk = lambda i: pair_copy(sent.at[i], got.at[i], s_sem.at[i], r_sem.at[i])

    def project(i, _):
        sent[i] = contract_last(
            context[...], out_v[pl.ds(pl.multiple_of(i * width, width), width), :]
        ).astype(bf16)
        chunk(i).start()
        return 0

    lax.fori_loop(0, chunks, project, 0)

    @pl.when(z > 0)
    def _():
        up(0).wait_recv()
        across(1, z - 1).start()
        pl.when(z < z_size - 1)(lambda: up(1).start())
        beside(z - 1, x).start()

    @pl.when(z < z_size - 1)
    def _():
        down(0).wait_recv()
        pl.when(z == 0)(lambda: across(1, z + 1).start())
        pl.when(z > 0)(lambda: down(1).start())
        beside(z + 1, x).start()

    from_across(0, z)

    def join(i, _):
        chunk(i).wait()
        cols = pl.ds(pl.multiple_of(i * width, width), width)
        hidden[:, cols] = tokens[:, cols].astype(f32) + (sent[i].astype(f32) + got[i].astype(f32))
        return 0

    lax.fori_loop(0, chunks, join, 0)
    values, _, _ = rms_normalize_pieces(hidden[...], g_ffn[...])
    ffn_bf[...] = values.astype(bf16)
    experts = lax.axis_size("dp")
    logits = lax.dot_general(
        values,
        router_t[...],
        (((1,), (1,)), ((), ())),
        precision=lax.Precision.HIGHEST,
        preferred_element_type=f32,
    )
    logits = jnp.where(lane < experts, logits, -jnp.inf)
    expo = jnp.exp(logits - jnp.max(logits, axis=1, keepdims=True))
    share = expo / jnp.sum(expo, axis=1, keepdims=True)
    probs[...] = share
    named = lane < 0
    for i in range(routes.shape[1]):
        named = named | (lane == routes[:, pl.ds(i, 1)])
    gates[...] = jnp.where(named, share, -1.0)

    @pl.when(z >= 2)
    def _():
        up(1).wait_recv()
        beside(z - 2, x).start()

    @pl.when(z < z_size - 2)
    def _():
        down(1).wait_recv()
        beside(z + 2, x).start()

    from_across(1, near)
    beside(z, x).wait()
    beside(z, 1 - x).wait()
    beside(near, 1 - x).wait()
    pl.when(z > 0)(lambda: beside(z - 1, x).wait())
    pl.when(z < z_size - 1)(lambda: beside(z + 1, x).wait())
    pl.when(z >= 2)(lambda: beside(z - 2, x).wait())
    pl.when(z < z_size - 2)(lambda: beside(z + 2, x).wait())
    across(0, z).wait_send()
    across(1, near).wait_send()
    pl.when(z < z_size - 1)(lambda: up(0).wait_send())
    pl.when(z > 0)(lambda: down(0).wait_send())
    pl.when((z > 0) & (z < z_size - 1))(lambda: up(1).wait_send())
    pl.when((z > 0) & (z < z_size - 1))(lambda: down(1).wait_send())
    keep.wait()


def forward_tuned(
    lengths,
    freqs,
    tokens,
    routes,
    g_attn,
    g_latent,
    g_ffn,
    router_t,
    w_query,
    down_t,
    kv_up,
    w_out,
    grad_out,
):
    rows, features = tokens.shape
    rank, columns = kv_up.shape
    heads = columns // 256
    bf16, f32, dma = jnp.bfloat16, jnp.float32, pltpu.SemaphoreType.DMA
    vmem, anywhere = pl.BlockSpec(memory_space=pltpu.VMEM), pl.BlockSpec(memory_space=pl.ANY)
    smem = pl.BlockSpec(memory_space=pltpu.SMEM)
    shape = jax.ShapeDtypeStruct
    chunks = 8
    return pl.pallas_call(
        forward_kernel,
        out_shape=[
            shape((rows, features), f32),
            shape((rows, features), bf16),
            shape((rows, 128), f32),
            shape((rows, 128), f32),
            shape((rows, features), bf16),
            shape((heads, rows, 256), bf16),
            shape((rows, columns), bf16),
            shape((rows, 128), bf16),
            shape((rows, rank), bf16),
            shape((rows, rank), f32),
            shape((rows, heads * 128), bf16),
            shape((rows, 128), f32),
            shape((16,) + grad_out.shape, bf16),
        ],
        in_specs=[smem] + [vmem] * 7 + [anywhere] * 5,
        out_specs=[vmem] * 12 + [anywhere],
        scratch_shapes=[
            pltpu.VMEM(w_query.shape, bf16),
            pltpu.VMEM((rank + 128, features), bf16),
            pltpu.VMEM(kv_up.shape, bf16),
            pltpu.VMEM(w_out.shape, bf16),
            pltpu.VMEM((chunks, rows, features // chunks), bf16),
            pltpu.VMEM((chunks, rows, features // chunks), bf16),
            dma((5,)),
            dma((chunks,)),
            dma((chunks,)),
            dma((1,)),
        ]
        + [dma((2,))] * 6
        + [dma((4, 2))] * 2,
        compiler_params=pltpu.CompilerParams(
            collective_id=2, has_side_effects=True, vmem_limit_bytes=VMEM_LIMIT
        ),
        name="attention_forward",
    )(
        lengths,
        freqs,
        tokens,
        routes,
        g_attn,
        g_latent,
        g_ffn,
        router_t,
        w_query,
        down_t,
        kv_up,
        w_out,
        grad_out,
    )


def backward_kernel(
    lengths,
    freqs,
    sums,
    hidden,
    grad_out,
    tokens,
    probs,
    g_attn,
    g_latent,
    g_ffn,
    router_t,
    queries,
    kv,
    key_turned,
    latent,
    log_totals,
    w_query,
    down_t,
    kv_up,
    w_out,
    grad_tokens,
    grad_hidden_bf,
    grad_query,
    grad_kv,
    grad_low,
    vectors,
    wq_v,
    down_v,
    up_v,
    out_v,
    unit,
    grad_hidden,
    grad_context,
    grad_turned,
    sent,
    got,
    low_sent,
    low_got,
    w_sem,
    s_sem,
    r_sem,
    e_sem,
):
    bf16, f32 = jnp.bfloat16, jnp.float32
    highest = lax.Precision.HIGHEST
    rows, features = tokens.shape
    rank = kv_up.shape[0]
    heads = kv_up.shape[1] // 256
    turned = down_t.shape[0] - rank
    tail = pl.ds(rank, turned)
    loads = [
        pltpu.make_async_copy(w_out, out_v, w_sem.at[0]),
        pltpu.make_async_copy(kv_up, up_v, w_sem.at[1]),
        pltpu.make_async_copy(w_query, wq_v, w_sem.at[2]),
        pltpu.make_async_copy(down_t, down_v.at[pl.ds(0, rank + turned)], w_sem.at[3]),
        pltpu.make_async_copy(down_t.at[tail], down_v.at[pl.ds(rank + turned, turned)], w_sem.at[4]),
    ]
    for copy in loads:
        copy.start()
    greet_pair()
    cosine, sine, met = turn_tables(lengths, freqs, rows)
    lane = lax.broadcasted_iota(jnp.int32, (rows, 128), 1)
    experts = lax.axis_size("dp")

    extra = sums[:, pl.ds(features, 128)]
    dense = extra + pltpu.roll(extra, 128 - experts, 1)
    share = probs[...]
    dense = jnp.where(lane < experts, dense, 0.0)
    logits = share * (dense - jnp.sum(share * dense, axis=1, keepdims=True))
    grad_in = sums[:, pl.ds(0, features)] + lax.dot_general(
        logits,
        router_t[...],
        (((1,), (0,)), ((), ())),
        precision=highest,
        preferred_element_type=f32,
    )
    values, unit_rows, factor = rms_normalize_pieces(hidden[...], g_ffn[...])
    unit[...] = unit_rows
    vectors[pl.ds(0, experts), :] = lax.dot_general(
        logits, values, (((0,), (0,)), ((), ())), precision=highest, preferred_element_type=f32
    )[:experts]
    vectors[pl.ds(experts, 8), :] = jnp.zeros((8, features), f32)
    vectors[pl.ds(experts + 1, 1), :] = jnp.sum(grad_in * unit[...], axis=0, keepdims=True)
    grad_hidden[...] = grad_out[...].astype(f32) + normalize_back(
        grad_in, unit[...], factor, g_ffn[...]
    )
    grad_hidden_bf[...] = grad_hidden[...].astype(bf16)
    loads[0].wait()

    def back_out(n, _):
        cols = pl.ds(pl.multiple_of(n * 256, 256), 256)
        grad_context[:, cols] = nn(grad_hidden_bf[...], out_v[:, cols]).astype(bf16)
        return 0

    lax.fori_loop(0, grad_context.shape[1] // 256, back_out, 0)
    grad_turned[...] = jnp.zeros(grad_turned.shape, f32)

    def two_heads(i, _):
        pieces = []
        for b in range(2):
            head = 2 * i + b
            at = pl.multiple_of(head * 256, 256)
            key = jnp.concatenate([kv[:, pl.ds(at, 128)], key_turned[...]], axis=1)
            value = kv[:, pl.ds(at + 128, 128)]
            raw = contract_last(queries[head], key)
            log_total = jnp.sum(
                jnp.where(lane == head, log_totals[...], 0.0), axis=1, keepdims=True
            )
            weights = jnp.exp(jnp.where(met, raw * QK ** (-0.5), -jnp.inf) - log_total)
            grad_ctx = grad_context[:, pl.ds(pl.multiple_of(head * 128, 128), 128)]
            grad_weights = contract_last(grad_ctx, value)
            inner = jnp.sum(weights * grad_weights, axis=1, keepdims=True)
            grad_raw = (weights * (grad_weights - inner) * QK ** (-0.5)).astype(bf16)
            pieces.append(nn(grad_raw, key))
            back_key = contract_first(grad_raw, queries[head])
            grad_kv[:, pl.ds(at, 128)] = back_key[:, :128].astype(bf16)
            grad_turned[...] += back_key[:, 128:]
            grad_kv[:, pl.ds(at + 128, 128)] = contract_first(
                weights.astype(bf16), grad_ctx
            ).astype(bf16)
        even, odd = pieces
        spun = turn(jnp.where(lane < 64, even[:, 128:], odd[:, 128:]), cosine, -sine)
        moved = pltpu.roll(odd[:, :128], 64, 1)
        start = pl.multiple_of(i * 384, 384)
        grad_query[:, pl.ds(start, 128)] = even[:, :128].astype(bf16)
        grad_query[:, pl.ds(start + 128, 128)] = jnp.where(lane < 64, spun, moved).astype(bf16)
        grad_query[:, pl.ds(start + 256, 128)] = jnp.where(lane < 64, moved, spun).astype(bf16)
        return 0

    lax.fori_loop(0, heads // 2, two_heads, 0)
    loads[1].wait()
    low_sent[:, pl.ds(0, rank)] = contract_last(grad_kv[...], up_v[...]).astype(bf16)
    folded = turn(grad_turned[...] + pltpu.roll(grad_turned[...], 64, 1), cosine, -sine)
    low_sent[:, pl.ds(rank, 128)] = jnp.where(lane < turned, folded, 0.0).astype(bf16)
    low_copy = pair_copy(low_sent, low_got, e_sem.at[0], e_sem.at[1])
    low_copy.start()
    loads[2].wait()
    chunks, width = sent.shape[0], sent.shape[2]
    chunk = lambda i: pair_copy(sent.at[i], got.at[i], s_sem.at[i], r_sem.at[i])

    def project(i, _):
        sent[i] = contract_last(
            grad_query[...], wq_v[pl.ds(pl.multiple_of(i * width, width), width), :]
        ).astype(bf16)
        chunk(i).start()
        return 0

    lax.fori_loop(0, chunks, project, 0)
    loads[3].wait()
    loads[4].wait()
    low_copy.wait()
    low = low_sent[...].astype(f32) + low_got[...].astype(f32)
    grad_normed = low[:, :rank]
    _, latent_unit, latent_factor = rms_normalize_pieces(latent[...], g_latent[...])
    grad_gain = jnp.sum(grad_normed * latent_unit, axis=0, keepdims=True)
    for i in range(rank // 128):
        vectors[pl.ds(experts + 2 + i, 1), pl.ds(0, 128)] = grad_gain[:, i * 128 : (i + 1) * 128]
    grad_low[:, pl.ds(0, rank)] = normalize_back(
        grad_normed, latent_unit, latent_factor, g_latent[...]
    ).astype(bf16)
    grad_low[:, pl.ds(rank, 128)] = low[:, rank:].astype(bf16)

    def join(i, _):
        cols = pl.ds(pl.multiple_of(i * width, width), width)
        product = nn(grad_low[...], down_v[:, cols])
        chunk(i).wait()
        unit[:, cols] = product + (sent[i].astype(f32) + got[i].astype(f32))
        return 0

    lax.fori_loop(0, chunks, join, 0)
    _, attn_unit, attn_factor = rms_normalize_pieces(tokens[...].astype(f32), g_attn[...])
    vectors[pl.ds(experts, 1), :] = jnp.sum(unit[...] * attn_unit, axis=0, keepdims=True)
    grad_tokens[...] = grad_hidden[...] + normalize_back(
        unit[...], attn_unit, attn_factor, g_attn[...]
    )


def backward_tuned(lengths, freqs, sums, values, gains, router_t, saved, weights):
    hidden, grad_out, tokens, probs = values
    w_query, down_t, kv_up, w_out = weights
    rows, features = tokens.shape
    rank, columns = kv_up.shape
    heads = columns // 256
    bf16, f32, dma = jnp.bfloat16, jnp.float32, pltpu.SemaphoreType.DMA
    vmem, anywhere = pl.BlockSpec(memory_space=pltpu.VMEM), pl.BlockSpec(memory_space=pl.ANY)
    smem = pl.BlockSpec(memory_space=pltpu.SMEM)
    shape = jax.ShapeDtypeStruct
    chunks = 8
    experts = lax.axis_size("dp")
    return pl.pallas_call(
        backward_kernel,
        out_shape=[
            shape((rows, features), f32),
            shape((rows, features), bf16),
            shape((rows, w_query.shape[1]), bf16),
            shape((rows, columns), bf16),
            shape((rows, rank + 128), bf16),
            shape((experts + 8, features), f32),
        ],
        in_specs=[smem] + [vmem] * 15 + [anywhere] * 4,
        out_specs=[vmem] * 6,
        scratch_shapes=[
            pltpu.VMEM(w_query.shape, bf16),
            pltpu.VMEM((rank + 128, features), bf16),
            pltpu.VMEM(kv_up.shape, bf16),
            pltpu.VMEM(w_out.shape, bf16),
            pltpu.VMEM((rows, features), f32),
            pltpu.VMEM((rows, features), f32),
            pltpu.VMEM((rows, heads * 128), bf16),
            pltpu.VMEM((rows, 128), f32),
            pltpu.VMEM((chunks, rows, features // chunks), bf16),
            pltpu.VMEM((chunks, rows, features // chunks), bf16),
            pltpu.VMEM((rows, rank + 128), bf16),
            pltpu.VMEM((rows, rank + 128), bf16),
            dma((5,)),
            dma((chunks,)),
            dma((chunks,)),
            dma((2,)),
        ],
        compiler_params=pltpu.CompilerParams(
            collective_id=4, has_side_effects=True, vmem_limit_bytes=VMEM_LIMIT
        ),
        name="attention_backward",
    )(lengths, freqs, sums, hidden, grad_out, tokens, probs, *gains, router_t, *saved, *weights)


def add_window(dst, start, width, *srcs):
    rows = dst.shape[0]
    step = 32 if rows % 32 == 0 else 8
    cols = pl.ds(pl.multiple_of(start, 128), width)

    def body(i, _):
        here = pl.ds(pl.multiple_of(i * step, step), step)
        total = dst[here, cols].astype(jnp.float32)
        for src in srcs:
            total = total + src[here, :].astype(jnp.float32)
        dst[here, cols] = total.astype(dst.dtype)
        return 0

    lax.fori_loop(0, rows // step, body, 0)


def home_kernel(x_size, parts, share, whole, total, *refs):
    z_size, f32 = 4, jnp.float32
    rows = whole.shape[1] // parts
    piece = lambda p: pl.ds(p * rows, rows)
    own, c_buf, x_buf, z_buf, y_buf, f_buf = (refs[i * parts : (i + 1) * parts] for i in range(6))
    refs = refs[6 * parts :]
    l_sem, c_s, c_r, x_s, x_r, z_s, z_r, y_s, y_r, f_s, f_r = refs
    z, x, core = place_of(x_size)
    rank = lax.axis_index("tensor")
    at = functools.partial(index_of, x_size=x_size)
    half = z // 2
    inner = ((z + 3) // 4) * ((6 - z) // 4)
    order = [3 - 3 * half, 2 - half, 1 - z + 4 * half, z]
    width = [c.shape[3] for c in c_buf]
    window = [w - share for w in width]
    begin = pl.multiple_of(rank * share, 128)
    mine = lambda p: pl.multiple_of(rank * window[p], 128)
    theirs = lambda p: pl.multiple_of((1 - rank) * window[p], 128)

    slots = own[0].shape[0]
    blocks = [(w, v) for v in (1 - x, x) for w in order]
    load = lambda p, i: pltpu.make_async_copy(
        whole.at[at(blocks[i][0], blocks[i][1], core), piece(p)],
        own[p].at[i % slots],
        l_sem.at[p, i % slots],
    )
    beside = lambda p, w, v: remote(
        whole.at[at(w, v, 1 - core), piece(p)],
        c_buf[p].at[w, v],
        c_s.at[p, w, v],
        c_r.at[p, w, v],
        at(z, x, 1 - core),
    )
    twin = lambda p, w, v: pair_copy(
        c_buf[p].at[w, v, :, pl.ds(theirs(p), share)],
        y_buf[p].at[w, v],
        y_s.at[p, w, v],
        y_r.at[p, w, v],
    )
    across = lambda p, w: remote(
        c_buf[p].at[w, 1 - x, :, pl.ds(begin, window[p])],
        x_buf[p].at[w],
        x_s.at[p, w],
        x_r.at[p, w],
        at(z, 1 - x, core),
    )

    def along(p, w, slot, target):
        return remote(
            c_buf[p].at[w, x, :, pl.ds(begin, window[p])],
            z_buf[p].at[slot],
            z_s.at[p, w],
            z_r.at[p, slot],
            at(target, x, core),
        )

    final = lambda p: pair_copy(
        c_buf[p].at[z, x, :, pl.ds(begin, window[p])], f_buf[p], f_s.at[p], f_r.at[p]
    )

    for p in range(parts):
        for i in range(slots):
            load(p, i).start()
    greet(z, x, core, z_size, x_size, True)
    for p in range(parts):
        for w, v in blocks:
            beside(p, w, v).start()
    def on_chip(p, i):
        w, v = blocks[i]
        load(p, i).wait()
        beside(p, w, v).wait_recv()
        add_into(c_buf[p].at[w, v], own[p].at[i % slots])
        if i + slots < len(blocks):
            load(p, i + slots).start()
        twin(p, w, v).start()

    def go_across(p, i):
        w, v = blocks[i]
        twin(p, w, v).wait()
        add_window(c_buf[p].at[w, v], mine(p), share, y_buf[p].at[w, v])
        across(p, w).start()

    def go_along(p, k):
        w = order[k]
        twin(p, w, x).wait()
        add_window(c_buf[p].at[w, x], mine(p), share, y_buf[p].at[w, x])
        across(p, w).wait_recv()
        if k < 3:

            @pl.when(inner == 1)
            def _():
                along(p, w, w, z).wait_recv()
                add_window(c_buf[p].at[w, x], begin, window[p], x_buf[p].at[w], z_buf[p].at[w])

            @pl.when(inner == 0)
            def _():
                add_window(c_buf[p].at[w, x], begin, window[p], x_buf[p].at[w])

            @pl.when(w > z)
            def _():
                along(p, w, w, z + 1).start()

            @pl.when(w < z - 1)
            def _():
                along(p, w, w, z - 1).start()

            @pl.when(w == z - 1)
            def _():
                along(p, w, z_size, z - 1).start()

        else:
            add_window(c_buf[p].at[w, x], begin, window[p], x_buf[p].at[w])

            @pl.when(z > 0)
            def _():
                along(p, w, z, z).wait_recv()
                add_window(c_buf[p].at[w, x], begin, window[p], z_buf[p].at[z])

            @pl.when(z < z_size - 1)
            def _():
                along(p, w, z_size, z).wait_recv()
                add_window(c_buf[p].at[w, x], begin, window[p], z_buf[p].at[z_size])

            final(p).start()

    def begin_part(p, between):
        for i in range(5):
            on_chip(p, i)
            if i >= 1:
                go_across(p, i - 1)
            between(i)
        for i in range(5, 8):
            on_chip(p, i)

    begin_part(0, lambda i: None)
    for p in range(parts):
        if p + 1 < parts:

            def between(i):
                if i < 4:
                    go_along(p, i)

            begin_part(p + 1, between)
        else:
            for k in range(4):
                go_along(p, k)
    for p in range(parts):
        final(p).wait()
        common = window[p] - share
        near, far = c_buf[p].at[z, x], f_buf[p]
        total[piece(p), pl.ds(mine(p), share)] = near[:, pl.ds(mine(p), share)].astype(f32)
        total[piece(p), pl.ds(theirs(p), share)] = far[
            :, pl.ds(pl.multiple_of((1 - rank) * common, 128), share)
        ].astype(f32)
        total[piece(p), pl.ds(share, common)] = near[:, pl.ds(share, common)].astype(f32) + far[
            :, pl.ds(pl.multiple_of(rank * share, 128), common)
        ].astype(f32)
    for p in range(parts):
        for w in range(z_size):
            for v in range(x_size):
                beside(p, w, v).wait_send()
            across(p, w).wait_send()

            @pl.when(z != w)
            def _():
                along(p, w, w, z).wait_send()


def home_sums(array, collective_id, parts, share=512):
    bf16, f32, dma = jnp.bfloat16, jnp.float32, pltpu.SemaphoreType.DMA
    rows, width = array.shape[1:]
    block = lambda *lead, cut=0: [pltpu.VMEM(lead + (rows // parts, width - cut), bf16)] * parts
    return pl.pallas_call(
        functools.partial(home_kernel, 2, parts, share),
        out_shape=jax.ShapeDtypeStruct((rows, width), f32),
        in_specs=[pl.BlockSpec(memory_space=pl.ANY)],
        out_specs=pl.BlockSpec(memory_space=pltpu.VMEM),
        scratch_shapes=block(3)
        + block(4, 2)
        + block(4, cut=share)
        + block(5, cut=share)
        + block(4, 2, cut=width - share)
        + block(cut=share)
        + [dma((parts, 3))]
        + [dma((parts, 4, 2))] * 2
        + [dma((parts, 4))] * 3
        + [dma((parts, 5))]
        + [dma((parts, 4, 2))] * 2
        + [dma((parts,))] * 2,
        compiler_params=pltpu.CompilerParams(
            collective_id=collective_id, has_side_effects=True, vmem_limit_bytes=VMEM_LIMIT
        ),
        name="home_sums",
    )(array)


def sum_home(arrays, pair=False):
    sums = [lax.psum_scatter(a, "dp", scatter_dimension=0) for a in arrays]
    if pair:
        sums = [lax.psum(a.astype(jnp.float32), "tensor") for a in sums]
    return [a.astype(jnp.float32) for a in sums]


def product_sum(left, right, extras):
    product = contract_last(left, right).astype(jnp.bfloat16)
    return [lax.psum(a, "tensor").astype(jnp.float32) for a in [product] + extras]


def ffn_with_kernel(own_ffn, gates, everyone_grad, weights, shared, capacity, experts):
    part = shared[0].shape[1]
    hidden, features = weights[0].shape[1], own_ffn.shape[1]
    gate_t, up_t, down_t = (jnp.pad(w.T, ((0, 128 - part), (0, 0))) for w in shared)
    out_part, grad_part, rows, dy, he, dge, due, shared_grads, _ = ffn_tuned(
        own_ffn,
        gates,
        everyone_grad,
        *(w.T for w in weights),
        jnp.concatenate([gate_t, up_t], axis=0),
        down_t,
        capacity,
    )
    rows, dy = rows.reshape(-1, features), dy.reshape(-1, features)
    he, dge, due = (a.reshape(-1, a.shape[2])[:, :hidden] for a in (he, dge, due))
    devices, rows_here = everyone_grad.shape[:2]
    return (
        out_part.reshape(devices, rows_here, -1),
        grad_part.reshape(devices, rows_here, -1),
        contract_first(rows, dge)[None],
        contract_first(rows, due)[None],
        contract_first(dy, he)[None],
        shared_grads.reshape(3, 128, features)[:, :part].reshape(3 * part, features),
    )


def ffn_plain(own_ffn, gates, everyone_grad, weights, shared, capacity, experts):
    own, devices = lax.axis_index("dp"), lax.axis_size("dp")
    rows_here, features = own_ffn.shape
    places = jnp.arange(rows_here, dtype=jnp.int32)
    expert_gate, expert_up, expert_down = weights
    part_gate, part_up, part_down = shared
    everyone_ffn = lax.all_gather(own_ffn, "dp", tiled=True)
    everyone_gates = lax.all_gather(gates, "dp")
    everyone_grad = everyone_grad.reshape(devices * rows_here, features)
    own_probs = lax.dynamic_slice_in_dim(everyone_gates, own, 1, 2).reshape(devices, rows_here)
    chooses = own_probs >= 0.0
    own_gates = jnp.where(chooses, own_probs, 0.0)
    upto = (places[:, None] <= places[None, :]).astype(jnp.bfloat16)
    slot = jnp.dot(chooses.astype(jnp.bfloat16), upto, preferred_element_type=jnp.float32) - 1.0
    slots = jnp.arange(capacity, dtype=jnp.float32)
    picked = chooses[:, None, :] & (slot[:, None, :] == slots[None, :, None])
    pick = picked.astype(jnp.bfloat16)
    slot_gates = jnp.sum(jnp.where(picked, own_gates[:, None, :], 0.0), axis=2).reshape(-1, 1)

    def pick_rows(values):
        blocks = values.reshape(devices, rows_here, features)
        return jnp.einsum(
            "jst,jtc->jsc", pick, blocks, preferred_element_type=jnp.float32
        ).astype(jnp.bfloat16).reshape(devices * capacity, features)

    def put_rows(values, hidden_parts, weights):
        blocks = values.astype(jnp.bfloat16).reshape(devices, capacity, features)
        left = jnp.concatenate(
            [pick.transpose(0, 2, 1)]
            + [h.reshape(devices, rows_here, h.shape[1]) for h in hidden_parts],
            axis=2,
        )
        right = jnp.concatenate(
            [blocks]
            + [
                jnp.broadcast_to(w.T[None], (devices, w.shape[1], features))
                for w in weights
            ],
            axis=1,
        )
        return (
            jnp.einsum("jtk,jkc->jtc", left, right, preferred_element_type=jnp.float32)
            .astype(jnp.bfloat16)
            .reshape(devices * rows_here, features)
        )

    expert_rows = pick_rows(everyone_ffn)
    grad_picked = pick_rows(everyone_grad)
    grad_rows = (slot_gates * grad_picked.astype(jnp.float32)).astype(jnp.bfloat16)

    gate_pre = jnp.dot(expert_rows, expert_gate, preferred_element_type=jnp.float32)
    up_pre = jnp.dot(expert_rows, expert_up, preferred_element_type=jnp.float32)
    gate_act, gate_slope = swish_parts(gate_pre)
    expert_hidden = (gate_act * up_pre).astype(jnp.bfloat16)
    expert_result = contract_last(expert_hidden, expert_down)
    slot_grads = jnp.sum(grad_picked.astype(jnp.float32) * expert_result, axis=1)
    grad_expert_down = contract_first(grad_rows, expert_hidden)[None]
    grad_expert_hidden = jnp.dot(grad_rows, expert_down, preferred_element_type=jnp.float32)
    grad_gate_pre = (grad_expert_hidden * up_pre * gate_slope).astype(jnp.bfloat16)
    grad_up_pre = (grad_expert_hidden * gate_act).astype(jnp.bfloat16)
    grad_expert_gate = contract_first(expert_rows, grad_gate_pre)[None]
    grad_expert_up = contract_first(expert_rows, grad_up_pre)[None]
    grad_rows_in = contract_last(grad_gate_pre, expert_gate) + contract_last(
        grad_up_pre, expert_up
    )

    shared_pre_gate = jnp.dot(everyone_ffn, part_gate, preferred_element_type=jnp.float32)
    shared_pre_up = jnp.dot(everyone_ffn, part_up, preferred_element_type=jnp.float32)
    shared_act, shared_slope = swish_parts(shared_pre_gate)
    shared_hidden = (shared_act * shared_pre_up).astype(jnp.bfloat16)
    grad_shared_hidden = jnp.dot(everyone_grad, part_down, preferred_element_type=jnp.float32)
    grad_shared_gate_pre = (grad_shared_hidden * shared_pre_up * shared_slope).astype(jnp.bfloat16)
    grad_shared_up_pre = (grad_shared_hidden * shared_act).astype(jnp.bfloat16)
    shared_grads = jnp.concatenate(
        [
            contract_first(grad_shared_gate_pre, everyone_ffn),
            contract_first(grad_shared_up_pre, everyone_ffn),
            contract_first(shared_hidden, everyone_grad),
        ],
        axis=0,
    ).astype(jnp.bfloat16)
    ffn_part = put_rows(slot_gates * expert_result, [shared_hidden], [part_down])
    pair_grads = jnp.sum(
        jnp.where(picked, slot_grads.reshape(devices, capacity, 1), 0.0), axis=1
    ).reshape(devices * rows_here, 1)
    pair_high = pair_grads.astype(jnp.bfloat16).astype(jnp.float32)
    column = jnp.arange(128, dtype=jnp.int32)[None, :]
    pair_columns = jnp.where(
        column == own,
        pair_high,
        jnp.where(column == own + experts, pair_grads - pair_high, 0.0),
    )
    grad_ffn_in = put_rows(
        grad_rows_in, [grad_shared_gate_pre, grad_shared_up_pre], [part_gate, part_up]
    )
    grad_part = jnp.concatenate([grad_ffn_in, pair_columns.astype(jnp.bfloat16)], axis=1)
    return (
        ffn_part.reshape(devices, rows_here, -1),
        grad_part.reshape(devices, rows_here, -1),
        grad_expert_gate,
        grad_expert_up,
        grad_expert_down,
        shared_grads,
    )


def shared_home(grads, part):
    devices = lax.axis_size("dp")
    share_rows = grads.shape[1] // devices
    grads = lax.all_to_all(
        grads.reshape(3 * part, devices, share_rows).transpose(1, 2, 0).astype(jnp.bfloat16),
        "dp",
        split_axis=0,
        concat_axis=0,
    ).astype(jnp.float32)
    return [
        grads[:, :, i * part : (i + 1) * part].transpose(1, 0, 2).reshape(share_rows, -1)
        for i in range(3)
    ]


def shards_tuned(
    tokens,
    lengths,
    routes,
    grad_out,
    g_attn,
    w_query,
    key_value_down_weight,
    latent_norm_gain,
    key_value_up_weight,
    w_out,
    g_ffn,
    router,
    shared_gate,
    shared_up,
    shared_down,
    expert_gate,
    expert_up,
    expert_down,
):
    rows_here, features = tokens.shape
    devices, ranks = lax.axis_size("dp"), lax.axis_size("tensor")
    own, rank = lax.axis_index("dp"), lax.axis_index("tensor")
    experts = router.shape[1]
    capacity = rows_here * TOPK * 4 // (3 * devices)
    half = (key_value_down_weight.shape[1] - LATENT_RANK) // 2
    freqs = 10000.0 ** (-jnp.arange(half, dtype=jnp.float32) / half)
    freqs = jnp.tile(freqs, 128 // half)[None, :]
    router_t = jnp.pad(router.T, ((0, 128 - experts), (0, 0)))
    gains = [g_attn[None, :], latent_norm_gain[None, :], g_ffn[None, :]]
    weights = [w_query, key_value_down_weight.T, key_value_up_weight, w_out]
    hidden, ffn_bf, dense_gates, probs, normed, *saved = forward_tuned(
        lengths, freqs, tokens, routes, *gains, router_t, *weights, grad_out
    )
    queries, kv, key_turned, latent_bf, latent, context, log_totals, everyone_grad = saved
    part = shared_gate.shape[1] // devices
    shared_parts = [
        lax.dynamic_slice_in_dim(w, own * part, part, 1)
        for w in (shared_gate, shared_up, shared_down)
    ]
    ffn_part, grad_ffn_part, *expert_grads, shared_grads = ffn_with_kernel(
        ffn_bf,
        dense_gates,
        everyone_grad,
        [w[0] for w in (expert_gate, expert_up, expert_down)],
        shared_parts,
        capacity,
        experts,
    )
    shared_grads = shared_home(shared_grads, part)
    ffn_total = lax.psum_scatter(
        ffn_part.reshape(devices * rows_here, features), "dp", scatter_dimension=0, tiled=True
    )
    ffn_total = lax.psum(ffn_total, "tensor").astype(jnp.float32)
    output = (hidden + ffn_total).astype(jnp.bfloat16)
    sums = home_sums(grad_ffn_part, 3, 2)
    grad_tokens, grad_hidden_bf, grad_query, grad_kv, grad_low, vectors = backward_tuned(
        lengths,
        freqs,
        sums,
        [hidden, grad_out, tokens, probs],
        gains,
        router_t,
        [queries, kv, key_turned, latent, log_totals],
        weights,
    )
    share_rows = features // devices
    columns = key_value_down_weight.shape[1]
    grad_columns = lax.dynamic_slice_in_dim(
        grad_low, rank * (columns // ranks), columns // ranks, 1
    )
    products = [
        contract_first(normed, grad_query),
        contract_first(grad_hidden_bf, context),
        contract_first(latent_bf, grad_kv),
        contract_first(normed, grad_columns),
    ]
    blocks = [
        a.astype(jnp.bfloat16).reshape(devices, a.shape[0] // devices, a.shape[1])
        for a in products
    ]
    vectors = vectors.reshape(experts + 8, devices, share_rows).transpose(1, 0, 2)
    vectors = vectors.at[:, experts + 2 : experts + 2 + LATENT_RANK // 128].set(
        vectors[:1, experts + 2 : experts + 2 + LATENT_RANK // 128]
    )
    grad_w_query, grad_w_out, grad_w_kv_up, grad_w_kv_down, vectors = scatter_sums(
        blocks + [vectors], 2, 5, jnp.float32
    )
    router_rows = share_rows // ranks
    grad_router = lax.dynamic_slice_in_dim(vectors[:experts], rank * router_rows, router_rows, 1).T
    latent_rows = LATENT_RANK // devices // ranks
    grad_g_kv = lax.dynamic_slice_in_dim(
        vectors[experts + 2 : experts + 2 + LATENT_RANK // 128].reshape(-1),
        (own * ranks + rank) * latent_rows,
        latent_rows,
        0,
    )
    return (
        output,
        grad_tokens,
        vectors[experts],
        grad_w_query,
        grad_w_kv_down,
        grad_g_kv,
        grad_w_kv_up,
        grad_w_out,
        vectors[experts + 1],
        grad_router,
        *shared_grads,
        *expert_grads,
    )


def shards(
    tokens,
    lengths,
    routes,
    grad_out,
    g_attn,
    w_query,
    key_value_down_weight,
    latent_norm_gain,
    key_value_up_weight,
    w_out,
    g_ffn,
    router,
    shared_gate,
    shared_up,
    shared_down,
    expert_gate,
    expert_up,
    expert_down,
):
    rows_here = tokens.shape[0]
    features = tokens.shape[1]
    heads_local = w_out.shape[1] // VALUE_HEAD_SIZE
    devices = lax.axis_size("dp")
    capacity = rows_here * TOPK * 4 // (3 * devices)
    experts = router.shape[1]
    highest = lax.Precision.HIGHEST
    softmax_scale = QK ** (-0.5)
    segment, token_position = doc_layout(lengths[0], rows_here)
    places = jnp.arange(rows_here, dtype=jnp.int32)
    allowed = (segment[:, None] == segment[None, :]) & (places[None, :] <= places[:, None])
    tokens_f = tokens.astype(jnp.float32)
    attn_normed, attn_unit, attn_factor = rms_normalize_pieces(tokens_f, g_attn)
    normed_bf = attn_normed.astype(jnp.bfloat16)
    query_full = jnp.dot(normed_bf, w_query, preferred_element_type=jnp.float32).reshape(
        rows_here, heads_local, QK
    )
    query_bf = jnp.concatenate(
        [
            query_full[..., :PLAIN_HEAD_SIZE],
            apply_rotation(query_full[..., PLAIN_HEAD_SIZE:], token_position),
        ],
        axis=-1,
    ).astype(jnp.bfloat16)
    latent_with_key = jnp.dot(normed_bf, key_value_down_weight, preferred_element_type=jnp.float32)
    key_turned_part = apply_rotation(latent_with_key[:, LATENT_RANK:], token_position).astype(
        jnp.bfloat16
    )
    latent_after_norm, latent_unit_scale, latent_norm_factor = rms_normalize_pieces(
        latent_with_key[:, :LATENT_RANK], latent_norm_gain
    )
    latent_bf = latent_after_norm.astype(jnp.bfloat16)
    key_value = (
        jnp.dot(latent_bf, key_value_up_weight, preferred_element_type=jnp.float32)
        .astype(jnp.bfloat16)
        .reshape(rows_here, heads_local, PLAIN_HEAD_SIZE + VALUE_HEAD_SIZE)
    )
    key_nope = key_value[..., :PLAIN_HEAD_SIZE]
    value = key_value[..., PLAIN_HEAD_SIZE:]

    def masked_scores():
        raw = jnp.einsum(
            "thd,shd->hts",
            query_bf[..., :PLAIN_HEAD_SIZE],
            key_nope,
            preferred_element_type=jnp.float32,
        )
        raw = raw + jnp.einsum(
            "thd,sd->hts",
            query_bf[..., PLAIN_HEAD_SIZE:],
            key_turned_part,
            preferred_element_type=jnp.float32,
        )
        return jnp.where(allowed[None], raw * softmax_scale, -jnp.inf)

    scores = masked_scores()
    top_score = jnp.max(scores, axis=-1, keepdims=True)
    expo = jnp.exp(scores - top_score)
    total = jnp.sum(expo, axis=-1, keepdims=True)
    log_total = top_score + jnp.log(total)
    attn_weights = (expo / total).astype(jnp.bfloat16)
    context = jnp.einsum("hts,shd->thd", attn_weights, value, preferred_element_type=jnp.float32)
    context = context.astype(jnp.bfloat16).reshape(rows_here, heads_local * VALUE_HEAD_SIZE)
    (attn,) = product_sum(context, w_out, [])
    hidden = tokens_f + attn
    ffn_normed, ffn_unit, ffn_factor = rms_normalize_pieces(hidden, g_ffn)
    ffn_bf = ffn_normed.astype(jnp.bfloat16)
    router_probs = jax.nn.softmax(jnp.dot(ffn_normed, router, precision=highest), axis=-1)
    own = lax.axis_index("dp")

    named = jnp.any(routes[:, :, None] == jnp.arange(128, dtype=jnp.int32)[None, None, :], axis=1)
    dense_gates = jnp.where(named, jnp.pad(router_probs, ((0, 0), (0, 128 - experts))), -1.0)
    everyone_grad = lax.all_gather(grad_out, "dp")
    part = shared_gate.shape[1] // devices
    shared_parts = [
        lax.dynamic_slice_in_dim(w, own * part, part, 1)
        for w in (shared_gate, shared_up, shared_down)
    ]
    (
        ffn_part,
        grad_ffn_part,
        grad_expert_gate,
        grad_expert_up,
        grad_expert_down,
        shared_grads,
    ) = ffn_plain(
        ffn_bf,
        dense_gates,
        everyone_grad,
        [w[0] for w in (expert_gate, expert_up, expert_down)],
        shared_parts,
        capacity,
        experts,
    )
    share_rows = features // devices
    grad_shared_gate, grad_shared_up, grad_shared_down = shared_home(shared_grads, part)

    grad_top = grad_out.astype(jnp.float32)
    ffn_total = lax.psum_scatter(
        ffn_part.reshape(devices * rows_here, features), "dp", scatter_dimension=0, tiled=True
    )
    ffn_total = lax.psum(ffn_total, "tensor").astype(jnp.float32)
    output = (hidden + ffn_total).astype(jnp.bfloat16)
    (grad_ffn_sum,) = sum_home([grad_ffn_part], True)
    dense_grad = (
        grad_ffn_sum[:, features : features + experts]
        + grad_ffn_sum[:, features + experts : features + 2 * experts]
    )
    grad_logits = router_probs * (
        dense_grad - jnp.sum(router_probs * dense_grad, axis=-1, keepdims=True)
    )
    grad_router_in = contract_last(grad_logits, router, highest)
    grad_router_part = contract_first(ffn_normed, grad_logits, highest)
    grad_ffn_total = grad_ffn_sum[:, :features] + grad_router_in
    grad_g_ffn = jnp.sum(grad_ffn_total * ffn_unit, axis=0)
    grad_hidden = grad_top + normalize_back(grad_ffn_total, ffn_unit, ffn_factor, g_ffn)
    grad_hidden_bf = grad_hidden.astype(jnp.bfloat16)
    grad_w_out = contract_first(grad_hidden_bf, context)
    grad_context = jnp.dot(grad_hidden_bf, w_out, preferred_element_type=jnp.float32).astype(
        jnp.bfloat16
    )
    grad_context = grad_context.reshape(rows_here, heads_local, VALUE_HEAD_SIZE)
    redone = jnp.exp(masked_scores() - log_total)
    redone_bf = redone.astype(jnp.bfloat16)
    grad_weights = jnp.einsum(
        "thd,shd->hts", grad_context, value, preferred_element_type=jnp.float32
    )
    grad_value = jnp.einsum(
        "hts,thd->shd", redone_bf, grad_context, preferred_element_type=jnp.float32
    )
    row_inner = jnp.sum(redone * grad_weights, axis=-1, keepdims=True)
    grad_raw = (redone * (grad_weights - row_inner) * softmax_scale).astype(jnp.bfloat16)
    grad_query_nope = jnp.einsum(
        "hts,shd->thd", grad_raw, key_nope, preferred_element_type=jnp.float32
    )
    grad_query_rot = jnp.einsum(
        "hts,sd->thd", grad_raw, key_turned_part, preferred_element_type=jnp.float32
    )
    grad_key_nope = jnp.einsum(
        "hts,thd->shd",
        grad_raw,
        query_bf[..., :PLAIN_HEAD_SIZE],
        preferred_element_type=jnp.float32,
    )
    grad_key_rot = jnp.einsum(
        "hts,thd->sd", grad_raw, query_bf[..., PLAIN_HEAD_SIZE:], preferred_element_type=jnp.float32
    )
    grad_query = jnp.concatenate(
        [grad_query_nope, apply_rotation(grad_query_rot, -token_position)], axis=-1
    )
    grad_query = grad_query.reshape(rows_here, heads_local * QK).astype(jnp.bfloat16)
    grad_w_query = contract_first(normed_bf, grad_query)
    grad_key_value = (
        jnp.concatenate([grad_key_nope, grad_value], axis=-1)
        .reshape(rows_here, heads_local * (PLAIN_HEAD_SIZE + VALUE_HEAD_SIZE))
        .astype(jnp.bfloat16)
    )
    grad_w_kv_up = contract_first(latent_bf, grad_key_value)
    grad_latent_normed = contract_last(grad_key_value, key_value_up_weight)
    grad_latent_part = jnp.concatenate(
        [grad_latent_normed, apply_rotation(grad_key_rot, -token_position)], axis=1
    ).astype(jnp.bfloat16)
    grad_in_summed, grad_latent_sum = product_sum(grad_query, w_query, [grad_latent_part])
    grad_latent_normed = grad_latent_sum[:, :LATENT_RANK]
    grad_g_kv = jnp.sum(grad_latent_normed * latent_unit_scale, axis=0)
    grad_latent = normalize_back(
        grad_latent_normed, latent_unit_scale, latent_norm_factor, latent_norm_gain
    )
    grad_down = jnp.concatenate([grad_latent, grad_latent_sum[:, LATENT_RANK:]], axis=1)
    grad_down_bf = grad_down.astype(jnp.bfloat16)
    share = grad_down.shape[1] // lax.axis_size("tensor")
    grad_columns = lax.dynamic_slice_in_dim(
        grad_down_bf, lax.axis_index("tensor") * share, share, 1
    )
    grad_w_kv_down = contract_first(normed_bf, grad_columns)
    grad_attn_in = grad_in_summed + contract_last(grad_down_bf, key_value_down_weight)
    grad_g_attn = jnp.sum(grad_attn_in * attn_unit, axis=0)
    grad_tokens = grad_hidden + normalize_back(grad_attn_in, attn_unit, attn_factor, g_attn)
    vectors = jnp.concatenate(
        [
            grad_router_part,
            grad_g_attn[:, None],
            grad_g_ffn[:, None],
            jnp.pad(
                grad_g_kv.reshape(devices, -1), ((0, 0), (0, share_rows - LATENT_RANK // devices))
            ).reshape(-1, 1),
            jnp.zeros((features, 128 - experts - 3), jnp.float32),
        ],
        axis=1,
    )
    blocks = [
        a.astype(jnp.bfloat16).reshape(devices, a.shape[0] // devices, a.shape[1])
        for a in (grad_w_query, grad_w_out, grad_w_kv_up, grad_w_kv_down)
    ]
    grad_w_query, grad_w_out, grad_w_kv_up, grad_w_kv_down, vectors = sum_home(
        blocks + [vectors.reshape(devices, share_rows, 128)]
    )
    rank, ranks = lax.axis_index("tensor"), lax.axis_size("tensor")
    router_rows = share_rows // ranks
    grad_router = lax.dynamic_slice_in_dim(vectors[:, :experts], rank * router_rows, router_rows, 0)
    latent_rows = LATENT_RANK // devices // ranks
    grad_g_kv = lax.dynamic_slice_in_dim(
        vectors[:, experts + 2], rank * latent_rows, latent_rows, 0
    )
    return (
        output,
        grad_tokens,
        vectors[:, experts],
        grad_w_query,
        grad_w_kv_down,
        grad_g_kv,
        grad_w_kv_up,
        grad_w_out,
        vectors[:, experts + 1],
        grad_router,
        grad_shared_gate,
        grad_shared_up,
        grad_shared_down,
        grad_expert_gate,
        grad_expert_up,
        grad_expert_down,
    )


def solution(mesh):
    in_specs = (
        P("dp", None),
        P("dp", None),
        P("dp", None),
        P("dp", None),
        P(),
        P(None, "tensor"),
        P(),
        P(),
        P(None, "tensor"),
        P(None, "tensor"),
        P(),
        P(),
        P(None, "tensor"),
        P(None, "tensor"),
        P(None, "tensor"),
        P("dp", None, "tensor"),
        P("dp", None, "tensor"),
        P("dp", None, "tensor"),
    )
    out_specs = (
        P("dp", None),
        P("dp", None),
        P("dp"),
        P("dp", "tensor"),
        P("dp", "tensor"),
        P(("dp", "tensor")),
        P("dp", "tensor"),
        P("dp", "tensor"),
        P("dp"),
        P(("dp", "tensor"), None),
        P("dp", "tensor"),
        P("dp", "tensor"),
        P("dp", "tensor"),
        P("dp", None, "tensor"),
        P("dp", None, "tensor"),
        P("dp", None, "tensor"),
    )
    tuned = mesh.shape["dp"] == 16 and mesh.shape["tensor"] == 2
    return jax.shard_map(
        shards_tuned if tuned else shards, mesh=mesh, in_specs=in_specs, out_specs=out_specs, check_vma=False)
```

```python
import functools

import jax
import jax.numpy as jnp
from jax import lax
from jax.experimental import pallas as pl
from jax.experimental.pallas import tpu as pltpu
from jax.sharding import PartitionSpec as P

PLAIN_HEAD_SIZE = 128
VALUE_HEAD_SIZE = 128
QK = 192
LATENT_RANK = 512
TOPK = 6


epsilon = 1e-06


def rms_normalize_pieces(values, gain):
    factor = lax.rsqrt(jnp.mean(values * values, axis=-1, keepdims=True) + epsilon)
    unit = values * factor
    return (unit * gain, unit, factor)


def normalize_back(grad, unit, factor, gain):
    inner = grad * gain
    return factor * (inner - unit * jnp.mean(inner * unit, axis=-1, keepdims=True))


def apply_rotation(values, token_position):
    half = values.shape[-1] // 2
    freqs = 10000.0 ** (-jnp.arange(half, dtype=jnp.float32) / half)
    angles = token_position.astype(jnp.float32)[:, None] * freqs[None, :]
    shape = (angles.shape[0],) + (1,) * (values.ndim - 2) + (half,)
    cosine = jnp.cos(angles).reshape(shape)
    sine = jnp.sin(angles).reshape(shape)
    first = values[..., :half]
    second = values[..., half:]
    return jnp.concatenate(
        [first * cosine - second * sine, second * cosine + first * sine], axis=-1
    )


def doc_layout(lengths_row, rows_here):
    ends = jnp.cumsum(lengths_row)
    starts = ends - lengths_row
    places = jnp.arange(rows_here, dtype=jnp.int32)
    segment = jnp.sum((places[:, None] >= ends[None, :]).astype(jnp.int32), axis=1)
    member = segment[:, None] == jnp.arange(lengths_row.shape[0], dtype=jnp.int32)[None, :]
    begins = jnp.sum(jnp.where(member, starts[None, :], 0), axis=1)
    return (segment, places - begins)


def contract_last(left, right, precision=None):
    return lax.dot_general(
        left,
        right,
        (((1,), (1,)), ((), ())),
        precision=precision,
        preferred_element_type=jnp.float32,
    )


def contract_first(left, right, precision=None):
    return lax.dot_general(
        left,
        right,
        (((0,), (0,)), ((), ())),
        precision=precision,
        preferred_element_type=jnp.float32,
    )


def swish_parts(gate_pre):
    sigma = jax.nn.sigmoid(gate_pre)
    return (gate_pre * sigma, sigma * (1.0 + gate_pre * (1.0 - sigma)))


VMEM_LIMIT = 60 * 1024 * 1024


def place_of(x_size):
    me = lax.axis_index("dp")
    core = me % 2
    x = (me // 2) % x_size
    z = me // (2 * x_size)
    return z, x, core


def index_of(z, x, core, x_size):
    return (z * x_size + x) * 2 + core


def remote(src, dst, send_sem, recv_sem, target):
    return pltpu.make_async_remote_copy(
        src_ref=src,
        dst_ref=dst,
        send_sem=send_sem,
        recv_sem=recv_sem,
        device_id={"dp": target},
        device_id_type=pl.DeviceIdType.MESH,
    )


def greet(z, x, core, z_size, x_size, pair=False):
    barrier = pltpu.get_barrier_semaphore()

    def tell(target):
        pl.semaphore_signal(
            barrier, inc=1, device_id={"dp": target}, device_id_type=pl.DeviceIdType.MESH
        )

    tell(index_of(z, x, 1 - core, x_size))
    tell(index_of(z, 1 - x, core, x_size))

    @pl.when(z > 0)
    def _():
        tell(index_of(z - 1, x, core, x_size))

    @pl.when(z < z_size - 1)
    def _():
        tell(index_of(z + 1, x, core, x_size))

    inner = (z + z_size - 1) // z_size - z // (z_size - 1)
    if pair:
        pl.semaphore_signal(
            barrier,
            inc=1,
            device_id={"tensor": 1 - lax.axis_index("tensor")},
            device_id_type=pl.DeviceIdType.MESH,
        )
    pl.semaphore_wait(barrier, 3 + inner + (1 if pair else 0))


def near_first(z):
    half = z // 2
    return [z, (1 - z) * (1 - 2 * half), 2 * (1 - half) + half * (7 - 2 * z), 3 - 3 * half]


def add_into(dst, *srcs):
    rows = dst.shape[0]
    step = 32 if rows % 32 == 0 else 8

    def body(i, _):
        here = pl.ds(pl.multiple_of(i * step, step), step)
        total = dst[here, :].astype(jnp.float32)
        for src in srcs:
            total = total + src[here, :].astype(jnp.float32)
        dst[here, :] = total.astype(dst.dtype)
        return 0

    lax.fori_loop(0, rows // step, body, 0)


def nn(left, right):
    return lax.dot_general(
        left, right, (((1,), (0,)), ((), ())), preferred_element_type=jnp.float32
    )


def is_at(j, where):
    low = (3 - j) // 3
    high = j // 3
    return (low, (4 - j) // 3 - low, (j + 1) // 3 - high, high)[where]


def ffn_kernel(
    x_size,
    own_ffn,
    own_gates,
    grad_half,
    gate_t,
    up_t,
    down_t,
    shared_in,
    shared_out,
    out_part,
    dx_part,
    rows_all,
    dy_all,
    he_all,
    dge_all,
    due_all,
    shared_grads,
    grad_all,
    blk,
    gts,
    gate_v,
    up_v,
    down_v,
    s_in,
    s_out,
    g_buf,
    rows_b,
    grow_b,
    dy_b,
    he_b,
    dge_b,
    due_b,
    out_r,
    dx_r,
    out_l,
    dx_l,
    out_st,
    dx_st,
    acc,
    gate_col,
    dgate_acc,
    left_ffn,
    left_grad,
    own_sem,
    up_s,
    up_r,
    dn_s,
    dn_r,
    x_s,
    x_r,
    c_s,
    c_r,
    w_sem,
    g_sem,
    st_sem,
    h_s,
    h_r,
    y_s,
    y_r,
    hc_s,
    hc_r,
):
    z_size, bf16, f32 = 4, jnp.bfloat16, jnp.float32
    hidden = gate_t.shape[0]
    rows_here, features = own_ffn.shape
    slots = rows_b.shape[0] // 2
    wide = 512
    z, x, core = place_of(x_size)
    own = lax.axis_index("dp")
    at = functools.partial(index_of, x_size=x_size)
    ins, outs = (own_ffn, own_gates), (blk, gts)
    order = near_first(z)

    def place(j):
        return sum(is_at(j, i) * order[i] for i in range(4))

    weights = [
        pltpu.make_async_copy(gate_t, gate_v.at[pl.ds(0, hidden)], w_sem.at[0]),
        pltpu.make_async_copy(up_t, up_v.at[pl.ds(0, hidden)], w_sem.at[1]),
        pltpu.make_async_copy(down_t, down_v.at[pl.ds(0, hidden)], w_sem.at[2]),
        pltpu.make_async_copy(shared_in, s_in, w_sem.at[3]),
        pltpu.make_async_copy(shared_out, s_out, w_sem.at[4]),
    ]
    keep = [
        pltpu.make_async_copy(ins[a], outs[a].at[at(z, x, core)], own_sem.at[a]) for a in range(2)
    ]

    def grad_copy(k):
        w, v = place(k // 2), x + (k % 2) * (1 - 2 * x)
        return pltpu.make_async_copy(
            grad_all.at[pl.ds(2 * (w * x_size + v), 2)], g_buf.at[k % 2], g_sem.at[k % 2]
        )

    for copy in keep + weights:
        copy.start()
    grad_copy(0).start()
    greet(z, x, core, z_size, x_size, True)

    def up(a, d):
        block = outs[a].at[at(z - d, x, core)]
        src = ins[a] if d == 0 else block
        return remote(src, block, up_s.at[a, d], up_r.at[a, d], at(z + 1, x, core))

    def down(a, d):
        block = outs[a].at[at(z + d, x, core)]
        src = ins[a] if d == 0 else block
        return remote(src, block, dn_s.at[a, d], dn_r.at[a, d], at(z - 1, x, core))

    def across(a, w, first=False):
        block = outs[a].at[at(w, x, core)]
        src = ins[a] if first else block
        return remote(src, block, x_s.at[a, w], x_r.at[a, w], at(z, 1 - x, core))

    def beside(a, w, v, first=False):
        block = outs[a].at[at(w, v, core)]
        src = ins[a] if first else block
        return remote(src, block, c_s.at[a, w, v], c_r.at[a, w, v], at(z, x, 1 - core))

    rank = lax.axis_index("tensor")
    edge = 1 - ((z + 3) // 4) * ((6 - z) // 4)
    part_rows = rows_here // 2
    whose = (order[2], order[2], order[3], order[3], order[3], z, (z + 2) % 4, order[3])

    def part(store, w, v, which):
        rows = pl.ds(pl.multiple_of(which * part_rows, part_rows), part_rows)
        return store.at[at(w, v, core), rows]

    store_of = lambda j: grad_all if j in (0, 2, 3) else blk

    def link(j, w=None, target=None):
        block = part(store_of(j), whose[j] if w is None else w, x, rank)
        src = block
        if j == 5:
            src = own_ffn.at[pl.ds(pl.multiple_of(rank * part_rows, part_rows), part_rows)]
        way = 0
        if j in (2, 6, 7):
            target = z if target is None else target
            way = (target - z + 1) // 2
            target = at(target, x, core)
        else:
            target = at(z, 1 - x, core)
        return remote(src, block, h_s.at[j, way], h_r.at[j], target)

    landed = lambda j: x if j in (2, 6, 7) else 1 - x

    def swap(j):
        block = part(store_of(j), whose[j], landed(j), rank)
        return pair_copy(block, block, y_s.at[j], y_r.at[j])

    def half_beside(j, i):
        block = part(store_of(j), whose[j], landed(j), rank + i * (1 - 2 * rank))
        return remote(block, block, hc_s.at[j, i], hc_r.at[j, i], at(z, x, 1 - core))

    def link_done(j):
        link(j).wait_recv()
        swap(j).start()
        half_beside(j, 0).start()

    def swap_done(j):
        swap(j).wait_recv()
        half_beside(j, 1).start()

    def ready(j):
        half_beside(j, 0).wait_recv()
        half_beside(j, 1).wait_recv()

    def at_ends(do):
        pl.when(edge == 1)(do)

    def inside(do):
        pl.when(edge == 0)(do)

    for a in (1, 0):
        beside(a, z, x, True).start()
        if a == 1:
            across(a, z, True).start()
        else:
            link(5).start()
        pl.when(z < z_size - 1)(lambda: up(a, 0).start())
        pl.when(z > 0)(lambda: down(a, 0).start())
    link(0).start()

    def pass_on(d):
        for a in (1, 0) if d == 1 else (1,):

            @pl.when(z >= d)
            def _():
                up(a, d - 1).wait_recv()
                if a == 1:
                    pl.when(z < z_size - 1)(lambda: up(a, d).start())
                else:
                    inside(lambda: link(6, z - 1, z + 1).start())
                beside(a, z - d, x).start()

            @pl.when(z + d < z_size)
            def _():
                down(a, d - 1).wait_recv()
                if a == 1:
                    pl.when(z > 0)(lambda: down(a, d).start())
                else:
                    inside(lambda: link(6, z + 1, z - 1).start())
                beside(a, z + d, x).start()

    def from_across(w, arrays=(1, 0)):
        for a in arrays:
            across(a, w).wait_recv()
            beside(a, w, 1 - x).start()

    def early(k):
        @pl.when(k == 1)
        def _():
            pass_on(1)
            for a in (1, 0):
                across(a, order[1]).start()
            swap_done(5)
            link_done(0)
            from_across(z, (1,))
            ready(5)

        @pl.when(k == 2)
        def _():
            link_done(6)
            link(1).start()

            @inside
            def _():
                link(7, None, 3 * (z - 1)).start()
                link(2, None, 3 * (z - 1)).start()
                link(4).start()
                link(3).start()

            pass_on(2)
            across(1, order[2]).start()
            swap_done(0)

        @pl.when(k == 3)
        def _():
            from_across(order[1])
            swap_done(6)

            @at_ends
            def _():
                link_done(7)
                link(4).start()

        @pl.when(k == 4)
        def _():
            ready(0)
            link_done(1)

            @at_ends
            def _():
                ready(6)
                link_done(2)
                link(3).start()

            pass_on(3)
            across(1, order[3]).start()
            from_across(order[2], (1,))

        @pl.when(k == 5)
        def _():
            grad_copy(5).start()
            at_ends(lambda: swap_done(7))
            swap_done(1)
            ready(1)

        @pl.when(k == 6)
        def _():
            from_across(order[3], (1,))
            at_ends(lambda: ready(7))
            inside(lambda: ready(6))

        @pl.when(k == 7)
        def _():
            swap_done(3)
            ready(3)
            grad_copy(7).start()
            ready(4)

    def midway(k):
        pl.when(k == 0)(lambda: link_done(5))
        pl.when(k == 4)(lambda: link_done(4))

        @pl.when(k == 5)
        def _():
            @at_ends
            def _():
                swap_done(2)
                ready(2)

            grad_copy(6).start()
            link_done(3)

        pl.when(k == 6)(lambda: swap_done(4))

    gate_v[pl.ds(hidden, gate_v.shape[0] - hidden), :] = jnp.zeros(
        (gate_v.shape[0] - hidden, features), bf16
    )
    up_v[pl.ds(hidden, up_v.shape[0] - hidden), :] = jnp.zeros(
        (up_v.shape[0] - hidden, features), bf16
    )
    down_v[pl.ds(hidden, down_v.shape[0] - hidden), :] = jnp.zeros(
        (down_v.shape[0] - hidden, features), bf16
    )
    acc[...] = jnp.zeros(acc.shape, f32)
    for copy in weights:
        copy.wait()
    for a in range(2):
        out_r[a, pl.ds(slots, 128), :] = s_out[...]
        dx_r[a, pl.ds(slots, 256), :] = s_in[...]
    for copy in keep:
        copy.wait()
    lane = lax.broadcasted_iota(jnp.int32, (rows_here, 128), 1)
    earlier = lax.broadcasted_iota(jnp.int32, (rows_here, rows_here), 1)
    later = lax.broadcasted_iota(jnp.int32, (rows_here, rows_here), 0)
    upto = (earlier <= later).astype(bf16)
    slot_lane = lax.broadcasted_iota(jnp.int32, (rows_here, slots), 1).astype(f32)

    def staged(pair, which):
        pairs = [
            (rows_b, rows_all),
            (dy_b, dy_all),
            (he_b, he_all),
            (dge_b, dge_all),
            (due_b, due_all),
            (out_st, out_part),
            (dx_st, dx_part),
        ]
        return [
            pltpu.make_async_copy(pairs[i][0], pairs[i][1].at[pair], st_sem.at[i]) for i in which
        ]

    def start_staged(pair, which):
        for copy in staged(pair, which):
            copy.start()

    def wait_staged(k, which):
        @pl.when(k > 0)
        def _():
            for copy in staged(0, which):
                copy.wait()

    def body(k, _):
        w, v = place(k // 2), x + (k % 2) * (1 - 2 * x)
        pair = w * x_size + v
        block = 2 * pair
        here = k % 2
        early(k)
        grad_copy(k).wait()
        pl.when(k < 4)(lambda: grad_copy(k + 1).start())
        beside(1, w, v).wait_recv()
        whole = (k == 0) | (k == 2) | (k == 3) | ((k == 4) & (edge == 0))
        pl.when(whole)(lambda: beside(0, w, v).wait_recv())

        for a in range(2):
            gates = gts[block + a]
            count = nn(upto, (gates >= 0.0).astype(bf16))
            gate = jnp.sum(jnp.where(lane == own, gates, 0.0), axis=1, keepdims=True)
            slot = jnp.sum(jnp.where(lane == own, count, 0.0), axis=1, keepdims=True) - 1.0
            pick = ((slot_lane == slot) & (gate >= 0.0)).astype(f32).astype(bf16)
            out_l[a, :, pl.ds(0, slots)] = pick
            dx_l[a, :, pl.ds(0, slots)] = pick
            high = gate.astype(bf16).astype(f32)
            middle = (gate - high).astype(bf16).astype(f32)
            low = gate - high - middle
            parts = jnp.where(
                lane == 0, high, jnp.where(lane == 1, middle, jnp.where(lane == 2, low, 0.0))
            ).astype(bf16)
            pick_t = pick.T
            left_ffn[a, pl.ds(0, slots), :] = pick_t
            left_grad[a, pl.ds(0, slots), :] = pick_t
            picked = jnp.sum(nn(pick_t, parts), axis=1, keepdims=True)
            gate_col[pl.ds(a * slots, slots), :] = jnp.broadcast_to(picked, (slots, 128))

        both = pl.ds(block, 2)
        pre = contract_last(blk[both].reshape(2 * rows_here, features), s_in[...])
        grad_hidden = contract_last(g_buf[here].reshape(2 * rows_here, features), s_out[...])
        act, slope = swish_parts(pre[:, :128])
        up_pre = pre[:, 128:]
        shared_units = (
            (act * up_pre).astype(bf16),
            (grad_hidden * up_pre * slope).astype(bf16),
            (grad_hidden * act).astype(bf16),
        )
        for a in range(2):
            mine = slice(a * rows_here, (a + 1) * rows_here)
            out_l[a, :, pl.ds(slots, 128)] = shared_units[0][mine]
            dx_l[a, :, pl.ds(slots, 128)] = shared_units[1][mine]
            dx_l[a, :, pl.ds(slots + 128, 128)] = shared_units[2][mine]
            left_ffn[a, pl.ds(slots, 128), :] = shared_units[1][mine].T
            left_ffn[a, pl.ds(slots + 128, 128), :] = shared_units[2][mine].T
            left_grad[a, pl.ds(slots, 128), :] = shared_units[0][mine].T

        def pick_rows(n, _):
            cols = pl.ds(pl.multiple_of(n * wide, wide), wide)
            for a in range(2):
                mine = pl.ds(a * slots, slots)
                product = nn(left_ffn[a], blk[block + a, :, cols])
                rows_b[mine, cols] = product[:slots].astype(bf16)
                acc[pl.ds(0, 256), cols] += product[slots:]
                product = nn(left_grad[a], g_buf[here, a, :, cols])
                grows = product[:slots]
                acc[pl.ds(256, 128), cols] += product[slots:]
                grow_b[mine, cols] = grows.astype(bf16)
                dy_b[mine, cols] = (gate_col[mine, pl.ds(0, 1)] * grows).astype(bf16)
            return 0

        wait_staged(k, (0, 1))
        lax.fori_loop(0, features // wide, pick_rows, 0)
        start_staged(pair, (0, 1))

        def hidden_units(n, _):
            units = pl.ds(pl.multiple_of(n * 256, 256), 256)
            gate_pre = contract_last(rows_b[...], gate_v[units, :])
            up_pre = contract_last(rows_b[...], up_v[units, :])
            grad_hidden = contract_last(dy_b[...], down_v[units, :])
            act, slope = swish_parts(gate_pre)
            he_b[:, units] = (act * up_pre).astype(bf16)
            dge_b[:, units] = (grad_hidden * up_pre * slope).astype(bf16)
            due_b[:, units] = (grad_hidden * act).astype(bf16)
            return 0

        wait_staged(k, (2, 3, 4))
        lax.fori_loop(0, gate_v.shape[0] // 256, hidden_units, 0)
        start_staged(pair, (2, 3, 4))
        midway(k)
        dgate_acc[...] = jnp.zeros(dgate_acc.shape, f32)

        def back(n, _):
            cols = pl.ds(pl.multiple_of(n * wide, wide), wide)
            result = nn(he_b[...], down_v[:, cols])
            product = grow_b[:, cols].astype(f32) * result
            for i in range(wide // 128):
                dgate_acc[...] += product[:, i * 128 : (i + 1) * 128]
            result = (gate_col[:, pl.ds(0, 1)] * result).astype(bf16)
            grad_in = (nn(dge_b[...], gate_v[:, cols]) + nn(due_b[...], up_v[:, cols])).astype(bf16)
            for a in range(2):
                mine = slice(a * slots, (a + 1) * slots)
                out_r[a, pl.ds(0, slots), cols] = result[mine]
                dx_r[a, pl.ds(0, slots), cols] = grad_in[mine]
                out_st[a, :, cols] = nn(out_l[a], out_r[a, :, cols]).astype(bf16)
                dx_st[a, :, cols] = nn(dx_l[a], dx_r[a, :, cols]).astype(bf16)
            return 0

        wait_staged(k, (5, 6))
        lax.fori_loop(0, features // wide, back, 0)
        dgate = jnp.sum(dgate_acc[...], axis=1, keepdims=True)
        high = dgate.astype(bf16).astype(f32)
        spread = lax.broadcasted_iota(jnp.int32, (2 * slots, 128), 1)
        spread = jnp.where(
            spread == own, high, jnp.where(spread == own + 16, dgate - high, 0.0)
        ).astype(bf16)
        for a in range(2):
            dx_st[a, :, pl.ds(features, 128)] = nn(
                out_l[a, :, pl.ds(0, slots)], spread[a * slots : (a + 1) * slots]
            ).astype(bf16)
        start_staged(pair, (5, 6))
        return 0

    lax.fori_loop(0, 8, body, 0)
    wait_staged(1, range(7))
    shared_grads[...] = acc[...].astype(bf16)
    for i in range(z_size):
        beside(1, order[i], x).wait_send()
        beside(1, order[i], 1 - x).wait_send()
        across(1, order[i]).wait_send()
    for i in range(2):
        beside(0, order[i], x).wait_send()
    inside(lambda: beside(0, order[2], x).wait_send())
    beside(0, order[1], 1 - x).wait_send()
    across(0, order[1]).wait_send()
    for d in range(z_size):
        for a in range(2) if d == 0 else (1,):
            pl.when((z >= d) & (z < z_size - 1))(lambda: up(a, d).wait_send())
            pl.when((z + d < z_size) & (z > 0))(lambda: down(a, d).wait_send())

    @inside
    def _():
        link(2, None, 3 * (z - 1)).wait_send()
        link(7, None, 3 * (z - 1)).wait_send()
        link(6, z - 1, z + 1).wait_send()
        link(6, z + 1, z - 1).wait_send()

    for j in range(8):

        def sent_on(j=j):
            swap(j).wait_send()
            half_beside(j, 0).wait_send()
            half_beside(j, 1).wait_send()

        if j in (2, 7):
            at_ends(sent_on)
        else:
            sent_on()
        if j not in (2, 6, 7):
            link(j).wait_send()


def ffn_tuned(own_ffn, own_gates, grad_all, gate_t, up_t, down_t, shared_in, shared_out, slots):
    rows, features = own_ffn.shape
    hidden = gate_t.shape[0]
    padded = -(-hidden // 256) * 256
    bf16, f32, dma = jnp.bfloat16, jnp.float32, pltpu.SemaphoreType.DMA
    anywhere = pl.BlockSpec(memory_space=pl.ANY)
    shape = jax.ShapeDtypeStruct
    return pl.pallas_call(
        functools.partial(ffn_kernel, 2),
        out_shape=[
            shape((8, 2, rows, features), bf16),
            shape((8, 2, rows, features + 128), bf16),
            shape((8, 2 * slots, features), bf16),
            shape((8, 2 * slots, features), bf16),
            shape((8, 2 * slots, padded), bf16),
            shape((8, 2 * slots, padded), bf16),
            shape((8, 2 * slots, padded), bf16),
            shape((384, features), bf16),
            shape((16, rows, features), bf16),
        ],
        in_specs=[anywhere] * 8,
        out_specs=[anywhere] * 7 + [pl.BlockSpec(memory_space=pltpu.VMEM), anywhere],
        input_output_aliases={2: 8},
        scratch_shapes=[
            pltpu.VMEM((16, rows, features), bf16),
            pltpu.VMEM((16, rows, 128), f32),
            pltpu.VMEM((padded, features), bf16),
            pltpu.VMEM((padded, features), bf16),
            pltpu.VMEM((padded, features), bf16),
            pltpu.VMEM((256, features), bf16),
            pltpu.VMEM((128, features), bf16),
            pltpu.VMEM((2, 2, rows, features), bf16),
            pltpu.VMEM((2 * slots, features), bf16),
            pltpu.VMEM((2 * slots, features), bf16),
            pltpu.VMEM((2 * slots, features), bf16),
            pltpu.VMEM((2 * slots, padded), bf16),
            pltpu.VMEM((2 * slots, padded), bf16),
            pltpu.VMEM((2 * slots, padded), bf16),
            pltpu.VMEM((2, slots + 128, features), bf16),
            pltpu.VMEM((2, slots + 256, features), bf16),
            pltpu.VMEM((2, rows, slots + 128), bf16),
            pltpu.VMEM((2, rows, slots + 256), bf16),
            pltpu.VMEM((2, rows, features), bf16),
            pltpu.VMEM((2, rows, features + 128), bf16),
            pltpu.VMEM((384, features), f32),
            pltpu.VMEM((2 * slots, 128), f32),
            pltpu.VMEM((2 * slots, 128), f32),
            pltpu.VMEM((2, slots + 256, rows), bf16),
            pltpu.VMEM((2, slots + 128, rows), bf16),
            dma((2,)),
        ]
        + [dma((2, 4))] * 6
        + [dma((2, 4, 2))] * 2
        + [dma((5,)), dma((2,)), dma((7,))]
        + [dma((8, 2))]
        + [dma((8,))] * 3
        + [dma((8, 2))] * 2,
        compiler_params=pltpu.CompilerParams(
            collective_id=1, has_side_effects=True, vmem_limit_bytes=VMEM_LIMIT
        ),
        name="ffn",
    )(
        own_ffn,
        own_gates,
        grad_all.reshape(16, rows, features),
        gate_t,
        up_t,
        down_t,
        shared_in,
        shared_out,
    )


def first_half(shape):
    return lax.broadcasted_iota(jnp.int32, shape, 1) % 64 < 32


def turn(values, cosine, sine):
    partner = jnp.where(
        first_half(values.shape), pltpu.roll(values, 96, 1), pltpu.roll(values, 32, 1)
    )
    return values * cosine + partner * sine


def layout_of(lengths, rows, width):
    row = lax.broadcasted_iota(jnp.int32, (rows, width), 0)
    across = lax.broadcasted_iota(jnp.int32, (rows, rows), 1)
    down = lax.broadcasted_iota(jnp.int32, (rows, rows), 0)
    place, met, end = row, across <= down, 0
    for i in range(lengths.shape[1]):
        end = end + lengths[0, i]
        place = place - jnp.where(row >= end, lengths[0, i], 0)
        met = met & ((across >= end) == (down >= end))
    return place, met


def turn_tables(lengths, freqs, rows):
    place, met = layout_of(lengths, rows, 128)
    angles = place.astype(jnp.float32) * freqs[...]
    sine = jnp.sin(angles)
    return jnp.cos(angles), jnp.where(first_half(angles.shape), -sine, sine), met


def pair_copy(src, dst, send_sem, recv_sem):
    return pltpu.make_async_remote_copy(
        src_ref=src,
        dst_ref=dst,
        send_sem=send_sem,
        recv_sem=recv_sem,
        device_id={"tensor": 1 - lax.axis_index("tensor")},
        device_id_type=pl.DeviceIdType.MESH,
    )


def greet_pair():
    barrier = pltpu.get_barrier_semaphore()
    pl.semaphore_signal(
        barrier,
        inc=1,
        device_id={"tensor": 1 - lax.axis_index("tensor")},
        device_id_type=pl.DeviceIdType.MESH,
    )
    pl.semaphore_wait(barrier, 1)


def forward_kernel(
    lengths,
    freqs,
    tokens,
    routes,
    g_attn,
    g_latent,
    g_ffn,
    router_t,
    w_query,
    down_t,
    kv_up,
    w_out,
    grad_out,
    hidden,
    ffn_bf,
    gates,
    probs,
    normed,
    queries,
    kv,
    key_turned,
    latent_bf,
    latent,
    context,
    log_totals,
    everyone,
    wq_v,
    down_v,
    up_v,
    out_v,
    sent,
    got,
    w_sem,
    s_sem,
    r_sem,
    own_sem,
    up_s,
    up_r,
    dn_s,
    dn_r,
    x_s,
    x_r,
    c_s,
    c_r,
):
    bf16, f32 = jnp.bfloat16, jnp.float32
    z_size, x_size = 4, 2
    z, x, core = place_of(x_size)
    at = functools.partial(index_of, x_size=x_size)
    rows, features = tokens.shape
    rank = kv_up.shape[0]
    heads = kv_up.shape[1] // 256
    turned = down_t.shape[0] - rank
    tail = pl.ds(rank, turned)
    loads = [
        pltpu.make_async_copy(down_t, down_v.at[pl.ds(0, rank + turned)], w_sem.at[0]),
        pltpu.make_async_copy(down_t.at[tail], down_v.at[pl.ds(rank + turned, turned)], w_sem.at[1]),
        pltpu.make_async_copy(kv_up, up_v, w_sem.at[2]),
        pltpu.make_async_copy(w_query, wq_v, w_sem.at[3]),
        pltpu.make_async_copy(w_out, out_v, w_sem.at[4]),
    ]
    keep = pltpu.make_async_copy(grad_out, everyone.at[at(z, x, core)], own_sem.at[0])

    def move(w, v, first, sems, target):
        block = everyone.at[at(w, v, core)]
        return remote(grad_out if first else block, block, *sems, target)

    up = lambda d: move(z - d, x, d == 0, (up_s.at[d], up_r.at[d]), at(z + 1, x, core))
    down = lambda d: move(z + d, x, d == 0, (dn_s.at[d], dn_r.at[d]), at(z - 1, x, core))
    across = lambda i, w: move(w, x, i == 0, (x_s.at[i], x_r.at[i]), at(z, 1 - x, core))
    beside = lambda w, v, first=False: move(
        w, v, first, (c_s.at[w, v], c_r.at[w, v]), at(z, x, 1 - core)
    )
    near = near_first(z)[1]

    def from_across(i, w):
        block = everyone.at[at(w, 1 - x, core)]
        remote(block, block, x_s.at[i], x_r.at[i], at(z, 1 - x, core)).wait_recv()
        beside(w, 1 - x).start()

    keep.start()
    for copy in loads:
        copy.start()
    greet(z, x, core, z_size, x_size, True)
    beside(z, x, True).start()
    across(0, z).start()
    pl.when(z < z_size - 1)(lambda: up(0).start())
    pl.when(z > 0)(lambda: down(0).start())
    cosine, sine, met = turn_tables(lengths, freqs, rows)
    values, _, _ = rms_normalize_pieces(tokens[...].astype(f32), g_attn[...])
    normed[...] = values.astype(bf16)
    loads[0].wait()
    loads[1].wait()
    low = contract_last(normed[...], down_v[...])
    latent[...] = low[:, :rank]
    key_turned[...] = turn(low[:, rank:], cosine, sine).astype(bf16)
    values, _, _ = rms_normalize_pieces(latent[...], g_latent[...])
    latent_bf[...] = values.astype(bf16)
    loads[2].wait()

    def keys(n, _):
        cols = pl.ds(pl.multiple_of(n * 512, 512), 512)
        kv[:, cols] = nn(latent_bf[...], up_v[:, cols]).astype(bf16)
        return 0

    lax.fori_loop(0, kv.shape[1] // 512, keys, 0)
    loads[3].wait()
    lane = lax.broadcasted_iota(jnp.int32, (rows, 128), 1)
    log_totals[...] = jnp.zeros(log_totals.shape, f32)

    def two_heads(i, _):
        three = nn(normed[...], wq_v[:, pl.ds(pl.multiple_of(i * 384, 384), 384)])
        middle, last = three[:, 128:256], three[:, 256:]
        plain = (
            three[:, :128],
            jnp.where(lane < 64, pltpu.roll(middle, 64, 1), pltpu.roll(last, 64, 1)),
        )
        spun = turn(jnp.where(lane < 64, middle, last), cosine, sine)
        for b in range(2):
            head = 2 * i + b
            queries[head, :, pl.ds(0, 128)] = plain[b].astype(bf16)
            queries[head, :, pl.ds(128, 128)] = jnp.where(
                (lane < 64) == (b == 0), spun, 0.0
            ).astype(bf16)
            at = pl.multiple_of(head * 256, 256)
            key = jnp.concatenate([kv[:, pl.ds(at, 128)], key_turned[...]], axis=1)
            raw = contract_last(queries[head], key)
            scores = jnp.where(met, raw * QK ** (-0.5), -jnp.inf)
            top = jnp.max(scores, axis=1, keepdims=True)
            expo = jnp.exp(scores - top)
            total = jnp.sum(expo, axis=1, keepdims=True)
            log_totals[...] = jnp.where(lane == head, top + jnp.log(total), log_totals[...])
            context[:, pl.ds(pl.multiple_of(head * 128, 128), 128)] = nn(
                (expo / total).astype(bf16), kv[:, pl.ds(at + 128, 128)]
            ).astype(bf16)
        return 0

    lax.fori_loop(0, heads // 2, two_heads, 0)

    loads[4].wait()
    chunks, width = sent.shape[0], sent.shape[2]
    chunk = lambda i: pair_copy(sent.at[i], got.at[i], s_sem.at[i], r_sem.at[i])

    def project(i, _):
        sent[i] = contract_last(
            context[...], out_v[pl.ds(pl.multiple_of(i * width, width), width), :]
        ).astype(bf16)
        chunk(i).start()
        return 0

    lax.fori_loop(0, chunks, project, 0)

    @pl.when(z > 0)
    def _():
        up(0).wait_recv()
        across(1, z - 1).start()
        pl.when(z < z_size - 1)(lambda: up(1).start())
        beside(z - 1, x).start()

    @pl.when(z < z_size - 1)
    def _():
        down(0).wait_recv()
        pl.when(z == 0)(lambda: across(1, z + 1).start())
        pl.when(z > 0)(lambda: down(1).start())
        beside(z + 1, x).start()

    from_across(0, z)

    def join(i, _):
        chunk(i).wait()
        cols = pl.ds(pl.multiple_of(i * width, width), width)
        hidden[:, cols] = tokens[:, cols].astype(f32) + (sent[i].astype(f32) + got[i].astype(f32))
        return 0

    lax.fori_loop(0, chunks, join, 0)
    values, _, _ = rms_normalize_pieces(hidden[...], g_ffn[...])
    ffn_bf[...] = values.astype(bf16)
    experts = lax.axis_size("dp")
    logits = lax.dot_general(
        values,
        router_t[...],
        (((1,), (1,)), ((), ())),
        precision=lax.Precision.HIGHEST,
        preferred_element_type=f32,
    )
    logits = jnp.where(lane < experts, logits, -jnp.inf)
    expo = jnp.exp(logits - jnp.max(logits, axis=1, keepdims=True))
    share = expo / jnp.sum(expo, axis=1, keepdims=True)
    probs[...] = share
    named = lane < 0
    for i in range(routes.shape[1]):
        named = named | (lane == routes[:, pl.ds(i, 1)])
    gates[...] = jnp.where(named, share, -1.0)

    @pl.when(z >= 2)
    def _():
        up(1).wait_recv()
        beside(z - 2, x).start()

    @pl.when(z < z_size - 2)
    def _():
        down(1).wait_recv()
        beside(z + 2, x).start()

    from_across(1, near)
    beside(z, x).wait()
    beside(z, 1 - x).wait()
    beside(near, 1 - x).wait()
    pl.when(z > 0)(lambda: beside(z - 1, x).wait())
    pl.when(z < z_size - 1)(lambda: beside(z + 1, x).wait())
    pl.when(z >= 2)(lambda: beside(z - 2, x).wait())
    pl.when(z < z_size - 2)(lambda: beside(z + 2, x).wait())
    across(0, z).wait_send()
    across(1, near).wait_send()
    pl.when(z < z_size - 1)(lambda: up(0).wait_send())
    pl.when(z > 0)(lambda: down(0).wait_send())
    pl.when((z > 0) & (z < z_size - 1))(lambda: up(1).wait_send())
    pl.when((z > 0) & (z < z_size - 1))(lambda: down(1).wait_send())
    keep.wait()


def forward_tuned(
    lengths,
    freqs,
    tokens,
    routes,
    g_attn,
    g_latent,
    g_ffn,
    router_t,
    w_query,
    down_t,
    kv_up,
    w_out,
    grad_out,
):
    rows, features = tokens.shape
    rank, columns = kv_up.shape
    heads = columns // 256
    bf16, f32, dma = jnp.bfloat16, jnp.float32, pltpu.SemaphoreType.DMA
    vmem, anywhere = pl.BlockSpec(memory_space=pltpu.VMEM), pl.BlockSpec(memory_space=pl.ANY)
    smem = pl.BlockSpec(memory_space=pltpu.SMEM)
    shape = jax.ShapeDtypeStruct
    chunks = 8
    return pl.pallas_call(
        forward_kernel,
        out_shape=[
            shape((rows, features), f32),
            shape((rows, features), bf16),
            shape((rows, 128), f32),
            shape((rows, 128), f32),
            shape((rows, features), bf16),
            shape((heads, rows, 256), bf16),
            shape((rows, columns), bf16),
            shape((rows, 128), bf16),
            shape((rows, rank), bf16),
            shape((rows, rank), f32),
            shape((rows, heads * 128), bf16),
            shape((rows, 128), f32),
            shape((16,) + grad_out.shape, bf16),
        ],
        in_specs=[smem] + [vmem] * 7 + [anywhere] * 5,
        out_specs=[vmem] * 12 + [anywhere],
        scratch_shapes=[
            pltpu.VMEM(w_query.shape, bf16),
            pltpu.VMEM((rank + 128, features), bf16),
            pltpu.VMEM(kv_up.shape, bf16),
            pltpu.VMEM(w_out.shape, bf16),
            pltpu.VMEM((chunks, rows, features // chunks), bf16),
            pltpu.VMEM((chunks, rows, features // chunks), bf16),
            dma((5,)),
            dma((chunks,)),
            dma((chunks,)),
            dma((1,)),
        ]
        + [dma((2,))] * 6
        + [dma((4, 2))] * 2,
        compiler_params=pltpu.CompilerParams(
            collective_id=2, has_side_effects=True, vmem_limit_bytes=VMEM_LIMIT
        ),
        name="attention_forward",
    )(
        lengths,
        freqs,
        tokens,
        routes,
        g_attn,
        g_latent,
        g_ffn,
        router_t,
        w_query,
        down_t,
        kv_up,
        w_out,
        grad_out,
    )


def backward_kernel(
    lengths,
    freqs,
    sums,
    hidden,
    grad_out,
    tokens,
    probs,
    g_attn,
    g_latent,
    g_ffn,
    router_t,
    queries,
    kv,
    key_turned,
    latent,
    log_totals,
    normed,
    context,
    latent_bf,
    w_query,
    down_t,
    kv_up,
    w_out,
    grad_tokens,
    out_grad,
    query_grad,
    up_grad,
    down_grad,
    vector_grad,
    wq_v,
    down_v,
    up_v,
    unit,
    grad_hidden_bf,
    grad_query,
    grad_kv,
    grad_low,
    vectors,
    hidden_t,
    normed_t,
    latent_t,
    low_t,
    send_wide,
    send_up,
    send_down,
    send_vector,
    out_c,
    query_c,
    up_c,
    down_c,
    vector_c,
    out_x,
    query_x,
    up_x,
    down_x,
    vector_x,
    out_z,
    query_z,
    up_z,
    down_z,
    vector_z,
    grad_context,
    grad_turned,
    sent,
    got,
    low_sent,
    low_got,
    w_sem,
    s_sem,
    r_sem,
    e_sem,
    c_s,
    c_r,
    x_s,
    x_r,
    z_s,
    z_r,
):
    grad_hidden = grad_tokens
    z_size, x_size = 4, 2
    z, x, core = place_of(x_size)
    place_rank = lax.axis_index("tensor")
    at = functools.partial(index_of, x_size=x_size)
    half = z // 2
    inner = ((z + 3) // 4) * ((6 - z) // 4)
    order = [3 - 3 * half, 2 - half, 1 - z + 4 * half, z]
    blocks = [(w, v) for v in (1 - x, x) for w in order]
    outs = (out_grad, query_grad, up_grad, down_grad, vector_grad)
    c_buf = (out_c, query_c, up_c, down_c, vector_c)
    x_buf = (out_x, query_x, up_x, down_x, vector_x)
    z_buf = (out_z, query_z, up_z, down_z, vector_z)

    def product(p, owner):
        rows = lambda size: pl.ds(pl.multiple_of(owner * size, size), size)
        if p == 0:
            return nn(hidden_t[rows(128), :], context[...])
        if p == 1:
            return nn(normed_t[rows(128), :], grad_query[...])
        if p == 2:
            size = up_grad.shape[0]
            return nn(latent_t[rows(size), :], grad_kv[...])
        if p == 3:
            size = down_grad.shape[0]
            mine = pl.ds(pl.multiple_of(place_rank * size, 32), size)
            return nn(low_t[mine, :], normed[:, rows(128)])
        return vectors[:, rows(128)]

    def staging(p, i):
        if p == 0:
            return send_wide.at[i, :, pl.ds(0, out_grad.shape[1])]
        return (None, send_wide, send_up, send_down, send_vector)[p].at[i]

    def beside(p, i):
        w, v = blocks[i]
        return remote(
            staging(p, i), c_buf[p].at[w, v], c_s.at[p, i], c_r.at[p, w, v], at(z, x, 1 - core)
        )

    across = lambda p, w: remote(
        c_buf[p].at[w, 1 - x], x_buf[p].at[w], x_s.at[p, w], x_r.at[p, w], at(z, 1 - x, core)
    )

    def along(p, w, slot, target):
        return remote(
            c_buf[p].at[w, x], z_buf[p].at[slot], z_s.at[p, w], z_r.at[p, slot], at(target, x, core)
        )

    def to_sibling(p):
        for i, (w, v) in enumerate(blocks):
            staging(p, i)[...] = product(p, at(w, v, 1 - core)).astype(c_buf[p].dtype)
            beside(p, i).start()

    def over_x(p):
        for i, (w, v) in enumerate(blocks):
            beside(p, i).wait_recv()
            total = c_buf[p][w, v].astype(jnp.float32) + product(p, at(w, v, core))
            c_buf[p][w, v] = total.astype(c_buf[p].dtype)
            if i < 4:
                across(p, w).start()

    def over_z(p, k):
        w = order[k]
        across(p, w).wait_recv()
        if k < 3:

            @pl.when(inner == 1)
            def _():
                along(p, w, w, z).wait_recv()
                add_into(c_buf[p].at[w, x], x_buf[p].at[w], z_buf[p].at[w])

            @pl.when(inner == 0)
            def _():
                add_into(c_buf[p].at[w, x], x_buf[p].at[w])

            @pl.when(w > z)
            def _():
                along(p, w, w, z + 1).start()

            @pl.when(w < z - 1)
            def _():
                along(p, w, w, z - 1).start()

            @pl.when(w == z - 1)
            def _():
                along(p, w, z_size, z - 1).start()

        else:
            add_into(c_buf[p].at[w, x], x_buf[p].at[w])

            @pl.when(z > 0)
            def _():
                along(p, w, z, z).wait_recv()
                add_into(c_buf[p].at[w, x], z_buf[p].at[z])

            @pl.when(z < z_size - 1)
            def _():
                along(p, w, z_size, z).wait_recv()
                add_into(c_buf[p].at[w, x], z_buf[p].at[z_size])

            outs[p][...] = c_buf[p][z, x].astype(outs[p].dtype)

    bf16, f32 = jnp.bfloat16, jnp.float32
    highest = lax.Precision.HIGHEST
    rows, features = tokens.shape
    rank = kv_up.shape[0]
    heads = kv_up.shape[1] // 256
    turned = down_t.shape[0] - rank
    tail = pl.ds(rank, turned)
    out_v = wq_v.at[:, pl.ds(0, w_out.shape[1])]
    loads = [
        pltpu.make_async_copy(w_out, out_v, w_sem.at[0]),
        pltpu.make_async_copy(kv_up, up_v, w_sem.at[1]),
        pltpu.make_async_copy(w_query, wq_v, w_sem.at[2]),
        pltpu.make_async_copy(down_t, down_v.at[pl.ds(0, rank + turned)], w_sem.at[3]),
        pltpu.make_async_copy(down_t.at[tail], down_v.at[pl.ds(rank + turned, turned)], w_sem.at[4]),
    ]
    rows_copy = pltpu.make_async_copy(hidden, unit, w_sem.at[5])
    rows_copy.start()
    for copy in loads[:2] + loads[3:]:
        copy.start()
    greet(z, x, core, z_size, x_size, True)
    cosine, sine, met = turn_tables(lengths, freqs, rows)
    lane = lax.broadcasted_iota(jnp.int32, (rows, 128), 1)
    experts = lax.axis_size("dp")

    extra = sums[:, pl.ds(features, 128)]
    dense = extra + pltpu.roll(extra, 128 - experts, 1)
    share = probs[...]
    dense = jnp.where(lane < experts, dense, 0.0)
    logits = share * (dense - jnp.sum(share * dense, axis=1, keepdims=True))
    grad_in = sums[:, pl.ds(0, features)] + lax.dot_general(
        logits,
        router_t[...],
        (((1,), (0,)), ((), ())),
        precision=highest,
        preferred_element_type=f32,
    )
    rows_copy.wait()
    values, unit_rows, factor = rms_normalize_pieces(unit[...], g_ffn[...])
    unit[...] = unit_rows
    vectors[pl.ds(0, experts), :] = lax.dot_general(
        logits, values, (((0,), (0,)), ((), ())), precision=highest, preferred_element_type=f32
    )[:experts]
    vectors[pl.ds(experts, 8), :] = jnp.zeros((8, features), f32)
    vectors[pl.ds(experts + 1, 1), :] = jnp.sum(grad_in * unit[...], axis=0, keepdims=True)
    grad_hidden[...] = grad_out[...].astype(f32) + normalize_back(
        grad_in, unit[...], factor, g_ffn[...]
    )
    grad_hidden_bf[...] = grad_hidden[...].astype(bf16)
    hidden_t[...] = grad_hidden_bf[...].T
    to_sibling(0)
    loads[0].wait()

    def back_out(n, _):
        cols = pl.ds(pl.multiple_of(n * 256, 256), 256)
        grad_context[:, cols] = nn(grad_hidden_bf[...], out_v[:, cols]).astype(bf16)
        return 0

    lax.fori_loop(0, grad_context.shape[1] // 256, back_out, 0)
    loads[2].start()
    grad_turned[...] = jnp.zeros(grad_turned.shape, f32)
    over_x(0)
    normed_t[...] = normed[...].T
    latent_t[...] = latent_bf[...].T

    def two_heads(i, _):
        pieces = []
        for b in range(2):
            head = 2 * i + b
            at = pl.multiple_of(head * 256, 256)
            key = jnp.concatenate([kv[:, pl.ds(at, 128)], key_turned[...]], axis=1)
            value = kv[:, pl.ds(at + 128, 128)]
            raw = contract_last(queries[head], key)
            log_total = jnp.sum(
                jnp.where(lane == head, log_totals[...], 0.0), axis=1, keepdims=True
            )
            weights = jnp.exp(jnp.where(met, raw * QK ** (-0.5), -jnp.inf) - log_total)
            grad_ctx = grad_context[:, pl.ds(pl.multiple_of(head * 128, 128), 128)]
            grad_weights = contract_last(grad_ctx, value)
            inner = jnp.sum(weights * grad_weights, axis=1, keepdims=True)
            grad_raw = (weights * (grad_weights - inner) * QK ** (-0.5)).astype(bf16)
            pieces.append(nn(grad_raw, key))
            back_key = contract_first(grad_raw, queries[head])
            grad_kv[:, pl.ds(at, 128)] = back_key[:, :128].astype(bf16)
            grad_turned[...] += back_key[:, 128:]
            grad_kv[:, pl.ds(at + 128, 128)] = contract_first(
                weights.astype(bf16), grad_ctx
            ).astype(bf16)
        even, odd = pieces
        spun = turn(jnp.where(lane < 64, even[:, 128:], odd[:, 128:]), cosine, -sine)
        moved = pltpu.roll(odd[:, :128], 64, 1)
        start = pl.multiple_of(i * 384, 384)
        grad_query[:, pl.ds(start, 128)] = even[:, :128].astype(bf16)
        grad_query[:, pl.ds(start + 128, 128)] = jnp.where(lane < 64, spun, moved).astype(bf16)
        grad_query[:, pl.ds(start + 256, 128)] = jnp.where(lane < 64, moved, spun).astype(bf16)
        return 0

    lax.fori_loop(0, heads // 2, two_heads, 0)
    for i in range(8):
        beside(0, i).wait_send()
    to_sibling(1)
    loads[1].wait()
    low_sent[:, pl.ds(0, rank)] = contract_last(grad_kv[...], up_v[...]).astype(bf16)
    folded = turn(grad_turned[...] + pltpu.roll(grad_turned[...], 64, 1), cosine, -sine)
    low_sent[:, pl.ds(rank, 128)] = jnp.where(lane < turned, folded, 0.0).astype(bf16)
    low_copy = pair_copy(low_sent, low_got, e_sem.at[0], e_sem.at[1])
    low_copy.start()
    loads[2].wait()
    chunks, width = sent.shape[0], sent.shape[2]
    chunk = lambda i: pair_copy(sent.at[i], got.at[i], s_sem.at[i], r_sem.at[i])

    def project(i, _):
        sent[i] = contract_last(
            grad_query[...], wq_v[pl.ds(pl.multiple_of(i * width, width), width), :]
        ).astype(bf16)
        chunk(i).start()
        return 0

    lax.fori_loop(0, chunks, project, 0)
    over_x(1)
    to_sibling(2)
    for k in range(3):
        over_z(0, k)
    over_x(2)
    loads[3].wait()
    loads[4].wait()
    low_copy.wait()
    low = low_sent[...].astype(f32) + low_got[...].astype(f32)
    grad_normed = low[:, :rank]
    _, latent_unit, latent_factor = rms_normalize_pieces(latent[...], g_latent[...])
    grad_gain = jnp.sum(grad_normed * latent_unit, axis=0, keepdims=True)
    for i in range(rank // 128):
        vectors[pl.ds(experts + 2 + i, 1), :] = jnp.concatenate(
            [grad_gain[:, i * 128 : (i + 1) * 128]] * (features // 128), axis=1
        )
    grad_low[:, pl.ds(0, rank)] = normalize_back(
        grad_normed, latent_unit, latent_factor, g_latent[...]
    ).astype(bf16)
    grad_low[:, pl.ds(rank, 128)] = low[:, rank:].astype(bf16)
    low_t[...] = grad_low[...].T
    to_sibling(3)
    over_x(3)
    over_z(0, 3)

    def join(i, _):
        cols = pl.ds(pl.multiple_of(i * width, width), width)
        product = nn(grad_low[...], down_v[:, cols])
        chunk(i).wait()
        unit[:, cols] = product + (sent[i].astype(f32) + got[i].astype(f32))
        return 0

    lax.fori_loop(0, chunks, join, 0)
    _, attn_unit, attn_factor = rms_normalize_pieces(tokens[...].astype(f32), g_attn[...])
    vectors[pl.ds(experts, 1), :] = jnp.sum(unit[...] * attn_unit, axis=0, keepdims=True)
    to_sibling(4)
    grad_tokens[...] = grad_hidden[...] + normalize_back(
        unit[...], attn_unit, attn_factor, g_attn[...]
    )
    over_x(4)
    for p in range(1, 5):
        for k in range(4):
            over_z(p, k)
    for p in range(5):
        for i in range(8):
            if p > 0:
                beside(p, i).wait_send()
        for w in range(z_size):
            across(p, w).wait_send()

            @pl.when(z != w)
            def _():
                along(p, w, w, z).wait_send()


def backward_tuned(lengths, freqs, sums, values, gains, router_t, saved, weights):
    hidden, grad_out, tokens, probs = values
    w_query, down_t, kv_up, w_out = weights
    rows, features = tokens.shape
    rank, columns = kv_up.shape
    heads = columns // 256
    bf16, f32, dma = jnp.bfloat16, jnp.float32, pltpu.SemaphoreType.DMA
    vmem, anywhere = pl.BlockSpec(memory_space=pltpu.VMEM), pl.BlockSpec(memory_space=pl.ANY)
    smem = pl.BlockSpec(memory_space=pltpu.SMEM)
    shape = jax.ShapeDtypeStruct
    chunks = 8
    experts, ranks = lax.axis_size("dp"), lax.axis_size("tensor")
    devices = experts
    share_rows = features // devices
    blocks = [
        ((share_rows, w_out.shape[1]), bf16),
        ((share_rows, w_query.shape[1]), bf16),
        ((rank // devices, columns), bf16),
        ((down_t.shape[0] // ranks, share_rows), bf16),
        ((experts + 8, share_rows), f32),
    ]
    several = lambda *lead: [pltpu.VMEM(lead + b, kind) for b, kind in blocks]
    return pl.pallas_call(
        backward_kernel,
        out_shape=[shape((rows, features), f32)] + [shape(b, f32) for b, _ in blocks],
        in_specs=[smem, vmem, vmem, anywhere] + [vmem] * 15 + [anywhere] * 4,
        out_specs=[vmem] * 6,
        scratch_shapes=[
            pltpu.VMEM(w_query.shape, bf16),
            pltpu.VMEM((rank + 128, features), bf16),
            pltpu.VMEM(kv_up.shape, bf16),
            pltpu.VMEM((rows, features), f32),
            pltpu.VMEM((rows, features), bf16),
            pltpu.VMEM((rows, w_query.shape[1]), bf16),
            pltpu.VMEM((rows, columns), bf16),
            pltpu.VMEM((rows, rank + 128), bf16),
            pltpu.VMEM((experts + 8, features), f32),
            pltpu.VMEM((features, rows), bf16),
            pltpu.VMEM((features, rows), bf16),
            pltpu.VMEM((rank, rows), bf16),
            pltpu.VMEM((rank + 128, rows), bf16),
        ]
        + several(8)[1:]
        + several(4, 2)
        + several(4)
        + several(5)
        + [
            pltpu.VMEM((rows, heads * 128), bf16),
            pltpu.VMEM((rows, 128), f32),
            pltpu.VMEM((chunks, rows, features // chunks), bf16),
            pltpu.VMEM((chunks, rows, features // chunks), bf16),
            pltpu.VMEM((rows, rank + 128), bf16),
            pltpu.VMEM((rows, rank + 128), bf16),
            dma((6,)),
            dma((chunks,)),
            dma((chunks,)),
            dma((2,)),
            dma((5, 8)),
            dma((5, 4, 2)),
            dma((5, 4)),
            dma((5, 4)),
            dma((5, 4)),
            dma((5, 5)),
        ],
        compiler_params=pltpu.CompilerParams(
            collective_id=4, has_side_effects=True, vmem_limit_bytes=VMEM_LIMIT
        ),
        name="attention_backward",
    )(lengths, freqs, sums, hidden, grad_out, tokens, probs, *gains, router_t, *saved, *weights)


def add_window(dst, start, width, *srcs):
    rows = dst.shape[0]
    step = 32 if rows % 32 == 0 else 8
    cols = pl.ds(pl.multiple_of(start, 128), width)

    def body(i, _):
        here = pl.ds(pl.multiple_of(i * step, step), step)
        total = dst[here, cols].astype(jnp.float32)
        for src in srcs:
            total = total + src[here, :].astype(jnp.float32)
        dst[here, cols] = total.astype(dst.dtype)
        return 0

    lax.fori_loop(0, rows // step, body, 0)


def home_kernel(x_size, parts, share, whole, total, *refs):
    z_size, f32 = 4, jnp.float32
    rows = whole.shape[1] // parts
    piece = lambda p: pl.ds(p * rows, rows)
    own, c_buf, x_buf, z_buf, y_buf, f_buf = (refs[i * parts : (i + 1) * parts] for i in range(6))
    refs = refs[6 * parts :]
    l_sem, c_s, c_r, x_s, x_r, z_s, z_r, y_s, y_r, f_s, f_r = refs
    z, x, core = place_of(x_size)
    rank = lax.axis_index("tensor")
    at = functools.partial(index_of, x_size=x_size)
    half = z // 2
    inner = ((z + 3) // 4) * ((6 - z) // 4)
    order = [3 - 3 * half, 2 - half, 1 - z + 4 * half, z]
    width = [c.shape[3] for c in c_buf]
    window = [w - share for w in width]
    begin = pl.multiple_of(rank * share, 128)
    mine = lambda p: pl.multiple_of(rank * window[p], 128)
    theirs = lambda p: pl.multiple_of((1 - rank) * window[p], 128)

    slots = own[0].shape[0]
    blocks = [(w, v) for v in (1 - x, x) for w in order]
    load = lambda p, i: pltpu.make_async_copy(
        whole.at[at(blocks[i][0], blocks[i][1], core), piece(p)],
        own[p].at[i % slots],
        l_sem.at[p, i % slots],
    )
    beside = lambda p, w, v: remote(
        whole.at[at(w, v, 1 - core), piece(p)],
        c_buf[p].at[w, v],
        c_s.at[p, w, v],
        c_r.at[p, w, v],
        at(z, x, 1 - core),
    )
    twin = lambda p, w, v: pair_copy(
        c_buf[p].at[w, v, :, pl.ds(theirs(p), share)],
        y_buf[p].at[w, v],
        y_s.at[p, w, v],
        y_r.at[p, w, v],
    )
    across = lambda p, w: remote(
        c_buf[p].at[w, 1 - x, :, pl.ds(begin, window[p])],
        x_buf[p].at[w],
        x_s.at[p, w],
        x_r.at[p, w],
        at(z, 1 - x, core),
    )

    def along(p, w, slot, target):
        return remote(
            c_buf[p].at[w, x, :, pl.ds(begin, window[p])],
            z_buf[p].at[slot],
            z_s.at[p, w],
            z_r.at[p, slot],
            at(target, x, core),
        )

    final = lambda p: pair_copy(
        c_buf[p].at[z, x, :, pl.ds(begin, window[p])], f_buf[p], f_s.at[p], f_r.at[p]
    )

    for p in range(parts):
        for i in range(slots):
            load(p, i).start()
    greet(z, x, core, z_size, x_size, True)
    for p in range(parts):
        for w, v in blocks:
            beside(p, w, v).start()
    def on_chip(p, i):
        w, v = blocks[i]
        load(p, i).wait()
        beside(p, w, v).wait_recv()
        add_into(c_buf[p].at[w, v], own[p].at[i % slots])
        if i + slots < len(blocks):
            load(p, i + slots).start()
        twin(p, w, v).start()

    def go_across(p, i):
        w, v = blocks[i]
        twin(p, w, v).wait()
        add_window(c_buf[p].at[w, v], mine(p), share, y_buf[p].at[w, v])
        across(p, w).start()

    def go_along(p, k):
        w = order[k]
        twin(p, w, x).wait()
        add_window(c_buf[p].at[w, x], mine(p), share, y_buf[p].at[w, x])
        across(p, w).wait_recv()
        if k < 3:

            @pl.when(inner == 1)
            def _():
                along(p, w, w, z).wait_recv()
                add_window(c_buf[p].at[w, x], begin, window[p], x_buf[p].at[w], z_buf[p].at[w])

            @pl.when(inner == 0)
            def _():
                add_window(c_buf[p].at[w, x], begin, window[p], x_buf[p].at[w])

            @pl.when(w > z)
            def _():
                along(p, w, w, z + 1).start()

            @pl.when(w < z - 1)
            def _():
                along(p, w, w, z - 1).start()

            @pl.when(w == z - 1)
            def _():
                along(p, w, z_size, z - 1).start()

        else:
            add_window(c_buf[p].at[w, x], begin, window[p], x_buf[p].at[w])

            @pl.when(z > 0)
            def _():
                along(p, w, z, z).wait_recv()
                add_window(c_buf[p].at[w, x], begin, window[p], z_buf[p].at[z])

            @pl.when(z < z_size - 1)
            def _():
                along(p, w, z_size, z).wait_recv()
                add_window(c_buf[p].at[w, x], begin, window[p], z_buf[p].at[z_size])

            final(p).start()

    def begin_part(p, between):
        for i in range(5):
            on_chip(p, i)
            if i >= 1:
                go_across(p, i - 1)
            between(i)
        for i in range(5, 8):
            on_chip(p, i)

    begin_part(0, lambda i: None)
    for p in range(parts):
        if p + 1 < parts:

            def between(i):
                if i < 4:
                    go_along(p, i)

            begin_part(p + 1, between)
        else:
            for k in range(4):
                go_along(p, k)
    for p in range(parts):
        final(p).wait()
        common = window[p] - share
        near, far = c_buf[p].at[z, x], f_buf[p]
        total[piece(p), pl.ds(mine(p), share)] = near[:, pl.ds(mine(p), share)].astype(f32)
        total[piece(p), pl.ds(theirs(p), share)] = far[
            :, pl.ds(pl.multiple_of((1 - rank) * common, 128), share)
        ].astype(f32)
        total[piece(p), pl.ds(share, common)] = near[:, pl.ds(share, common)].astype(f32) + far[
            :, pl.ds(pl.multiple_of(rank * share, 128), common)
        ].astype(f32)
    for p in range(parts):
        for w in range(z_size):
            for v in range(x_size):
                beside(p, w, v).wait_send()
            across(p, w).wait_send()

            @pl.when(z != w)
            def _():
                along(p, w, w, z).wait_send()


def home_sums(array, collective_id, parts, share=512):
    bf16, f32, dma = jnp.bfloat16, jnp.float32, pltpu.SemaphoreType.DMA
    rows, width = array.shape[1:]
    block = lambda *lead, cut=0: [pltpu.VMEM(lead + (rows // parts, width - cut), bf16)] * parts
    return pl.pallas_call(
        functools.partial(home_kernel, 2, parts, share),
        out_shape=jax.ShapeDtypeStruct((rows, width), f32),
        in_specs=[pl.BlockSpec(memory_space=pl.ANY)],
        out_specs=pl.BlockSpec(memory_space=pltpu.VMEM),
        scratch_shapes=block(3)
        + block(4, 2)
        + block(4, cut=share)
        + block(5, cut=share)
        + block(4, 2, cut=width - share)
        + block(cut=share)
        + [dma((parts, 3))]
        + [dma((parts, 4, 2))] * 2
        + [dma((parts, 4))] * 3
        + [dma((parts, 5))]
        + [dma((parts, 4, 2))] * 2
        + [dma((parts,))] * 2,
        compiler_params=pltpu.CompilerParams(
            collective_id=collective_id, has_side_effects=True, vmem_limit_bytes=VMEM_LIMIT
        ),
        name="home_sums",
    )(array)


def sum_home(arrays, pair=False):
    sums = [lax.psum_scatter(a, "dp", scatter_dimension=0) for a in arrays]
    if pair:
        sums = [lax.psum(a.astype(jnp.float32), "tensor") for a in sums]
    return [a.astype(jnp.float32) for a in sums]


def product_sum(left, right, extras):
    product = contract_last(left, right).astype(jnp.bfloat16)
    return [lax.psum(a, "tensor").astype(jnp.float32) for a in [product] + extras]


def ffn_with_kernel(own_ffn, gates, everyone_grad, weights, shared, capacity, experts):
    part = shared[0].shape[1]
    hidden, features = weights[0].shape[1], own_ffn.shape[1]
    gate_t, up_t, down_t = (jnp.pad(w.T, ((0, 128 - part), (0, 0))) for w in shared)
    out_part, grad_part, rows, dy, he, dge, due, shared_grads, _ = ffn_tuned(
        own_ffn,
        gates,
        everyone_grad,
        *(w.T for w in weights),
        jnp.concatenate([gate_t, up_t], axis=0),
        down_t,
        capacity,
    )
    rows, dy = rows.reshape(-1, features), dy.reshape(-1, features)
    he, dge, due = (a.reshape(-1, a.shape[2]) for a in (he, dge, due))
    devices, rows_here = everyone_grad.shape[:2]
    return (
        out_part.reshape(devices * rows_here, -1),
        grad_part.reshape(devices, rows_here, -1),
        [rows, dy, he, dge, due],
        shared_grads.reshape(3, 128, features)[:, :part].reshape(3 * part, features),
    )


def ffn_plain(own_ffn, gates, everyone_grad, weights, shared, capacity, experts):
    own, devices = lax.axis_index("dp"), lax.axis_size("dp")
    rows_here, features = own_ffn.shape
    places = jnp.arange(rows_here, dtype=jnp.int32)
    expert_gate, expert_up, expert_down = weights
    part_gate, part_up, part_down = shared
    everyone_ffn = lax.all_gather(own_ffn, "dp", tiled=True)
    everyone_gates = lax.all_gather(gates, "dp")
    everyone_grad = everyone_grad.reshape(devices * rows_here, features)
    own_probs = lax.dynamic_slice_in_dim(everyone_gates, own, 1, 2).reshape(devices, rows_here)
    chooses = own_probs >= 0.0
    own_gates = jnp.where(chooses, own_probs, 0.0)
    upto = (places[:, None] <= places[None, :]).astype(jnp.bfloat16)
    slot = jnp.dot(chooses.astype(jnp.bfloat16), upto, preferred_element_type=jnp.float32) - 1.0
    slots = jnp.arange(capacity, dtype=jnp.float32)
    picked = chooses[:, None, :] & (slot[:, None, :] == slots[None, :, None])
    pick = picked.astype(jnp.bfloat16)
    slot_gates = jnp.sum(jnp.where(picked, own_gates[:, None, :], 0.0), axis=2).reshape(-1, 1)

    def pick_rows(values):
        blocks = values.reshape(devices, rows_here, features)
        return jnp.einsum(
            "jst,jtc->jsc", pick, blocks, preferred_element_type=jnp.float32
        ).astype(jnp.bfloat16).reshape(devices * capacity, features)

    def put_rows(values, hidden_parts, weights):
        blocks = values.astype(jnp.bfloat16).reshape(devices, capacity, features)
        left = jnp.concatenate(
            [pick.transpose(0, 2, 1)]
            + [h.reshape(devices, rows_here, h.shape[1]) for h in hidden_parts],
            axis=2,
        )
        right = jnp.concatenate(
            [blocks]
            + [
                jnp.broadcast_to(w.T[None], (devices, w.shape[1], features))
                for w in weights
            ],
            axis=1,
        )
        return (
            jnp.einsum("jtk,jkc->jtc", left, right, preferred_element_type=jnp.float32)
            .astype(jnp.bfloat16)
            .reshape(devices * rows_here, features)
        )

    expert_rows = pick_rows(everyone_ffn)
    grad_picked = pick_rows(everyone_grad)
    grad_rows = (slot_gates * grad_picked.astype(jnp.float32)).astype(jnp.bfloat16)

    gate_pre = jnp.dot(expert_rows, expert_gate, preferred_element_type=jnp.float32)
    up_pre = jnp.dot(expert_rows, expert_up, preferred_element_type=jnp.float32)
    gate_act, gate_slope = swish_parts(gate_pre)
    expert_hidden = (gate_act * up_pre).astype(jnp.bfloat16)
    expert_result = contract_last(expert_hidden, expert_down)
    slot_grads = jnp.sum(grad_picked.astype(jnp.float32) * expert_result, axis=1)
    grad_expert_down = contract_first(grad_rows, expert_hidden)[None]
    grad_expert_hidden = jnp.dot(grad_rows, expert_down, preferred_element_type=jnp.float32)
    grad_gate_pre = (grad_expert_hidden * up_pre * gate_slope).astype(jnp.bfloat16)
    grad_up_pre = (grad_expert_hidden * gate_act).astype(jnp.bfloat16)
    grad_expert_gate = contract_first(expert_rows, grad_gate_pre)[None]
    grad_expert_up = contract_first(expert_rows, grad_up_pre)[None]
    grad_rows_in = contract_last(grad_gate_pre, expert_gate) + contract_last(
        grad_up_pre, expert_up
    )

    shared_pre_gate = jnp.dot(everyone_ffn, part_gate, preferred_element_type=jnp.float32)
    shared_pre_up = jnp.dot(everyone_ffn, part_up, preferred_element_type=jnp.float32)
    shared_act, shared_slope = swish_parts(shared_pre_gate)
    shared_hidden = (shared_act * shared_pre_up).astype(jnp.bfloat16)
    grad_shared_hidden = jnp.dot(everyone_grad, part_down, preferred_element_type=jnp.float32)
    grad_shared_gate_pre = (grad_shared_hidden * shared_pre_up * shared_slope).astype(jnp.bfloat16)
    grad_shared_up_pre = (grad_shared_hidden * shared_act).astype(jnp.bfloat16)
    shared_grads = jnp.concatenate(
        [
            contract_first(grad_shared_gate_pre, everyone_ffn),
            contract_first(grad_shared_up_pre, everyone_ffn),
            contract_first(shared_hidden, everyone_grad),
        ],
        axis=0,
    ).astype(jnp.bfloat16)
    ffn_part = put_rows(slot_gates * expert_result, [shared_hidden], [part_down])
    pair_grads = jnp.sum(
        jnp.where(picked, slot_grads.reshape(devices, capacity, 1), 0.0), axis=1
    ).reshape(devices * rows_here, 1)
    pair_high = pair_grads.astype(jnp.bfloat16).astype(jnp.float32)
    column = jnp.arange(128, dtype=jnp.int32)[None, :]
    pair_columns = jnp.where(
        column == own,
        pair_high,
        jnp.where(column == own + experts, pair_grads - pair_high, 0.0),
    )
    grad_ffn_in = put_rows(
        grad_rows_in, [grad_shared_gate_pre, grad_shared_up_pre], [part_gate, part_up]
    )
    grad_part = jnp.concatenate([grad_ffn_in, pair_columns.astype(jnp.bfloat16)], axis=1)
    return (
        ffn_part.reshape(devices, rows_here, -1),
        grad_part.reshape(devices, rows_here, -1),
        grad_expert_gate,
        grad_expert_up,
        grad_expert_down,
        shared_grads,
    )


def shared_home(grads, part):
    devices = lax.axis_size("dp")
    share_rows = grads.shape[1] // devices
    grads = lax.all_to_all(
        grads.reshape(3 * part, devices, share_rows).transpose(1, 2, 0).astype(jnp.bfloat16),
        "dp",
        split_axis=0,
        concat_axis=0,
    ).astype(jnp.float32)
    return [
        grads[:, :, i * part : (i + 1) * part].transpose(1, 0, 2).reshape(share_rows, -1)
        for i in range(3)
    ]


def shards_tuned(
    tokens,
    lengths,
    routes,
    grad_out,
    g_attn,
    w_query,
    key_value_down_weight,
    latent_norm_gain,
    key_value_up_weight,
    w_out,
    g_ffn,
    router,
    shared_gate,
    shared_up,
    shared_down,
    expert_gate,
    expert_up,
    expert_down,
):
    rows_here, features = tokens.shape
    devices, ranks = lax.axis_size("dp"), lax.axis_size("tensor")
    own, rank = lax.axis_index("dp"), lax.axis_index("tensor")
    experts = router.shape[1]
    capacity = rows_here * TOPK * 4 // (3 * devices)
    half = (key_value_down_weight.shape[1] - LATENT_RANK) // 2
    freqs = 10000.0 ** (-jnp.arange(half, dtype=jnp.float32) / half)
    freqs = jnp.tile(freqs, 128 // half)[None, :]
    router_t = jnp.pad(router.T, ((0, 128 - experts), (0, 0)))
    gains = [g_attn[None, :], latent_norm_gain[None, :], g_ffn[None, :]]
    weights = [w_query, key_value_down_weight.T, key_value_up_weight, w_out]
    hidden, ffn_bf, dense_gates, probs, normed, *saved = forward_tuned(
        lengths, freqs, tokens, routes, *gains, router_t, *weights, grad_out
    )
    queries, kv, key_turned, latent_bf, latent, context, log_totals, everyone_grad = saved
    part = shared_gate.shape[1] // devices
    shared_parts = [
        lax.dynamic_slice_in_dim(w, own * part, part, 1)
        for w in (shared_gate, shared_up, shared_down)
    ]
    ffn_part, grad_ffn_part, expert_saved, shared_grads = ffn_with_kernel(
        ffn_bf,
        dense_gates,
        everyone_grad,
        [w[0] for w in (expert_gate, expert_up, expert_down)],
        shared_parts,
        capacity,
        experts,
    )
    shared_grads = shared_home(shared_grads, part)
    ffn_sum = lax.psum_scatter(ffn_part, "dp", scatter_dimension=0, tiled=True)
    sums = home_sums(grad_ffn_part, 3, 2)
    (
        grad_tokens,
        grad_w_out,
        grad_w_query,
        grad_w_kv_up,
        grad_w_kv_down,
        vectors,
    ) = backward_tuned(
        lengths,
        freqs,
        sums,
        [hidden, grad_out, tokens, probs],
        gains,
        router_t,
        [queries, kv, key_turned, latent, log_totals, normed, context, latent_bf],
        weights,
    )
    grad_tokens, ffn_sum, *expert_saved = lax.optimization_barrier(
        (grad_tokens, ffn_sum, *expert_saved)
    )
    ffn_twin = lax.ppermute(ffn_sum, "tensor", [(0, 1), (1, 0)])
    rows, dy, he, dge, due = expert_saved
    units = expert_gate.shape[2]
    expert_grads = [
        contract_first(rows, dge[:, :units])[None],
        contract_first(rows, due[:, :units])[None],
        contract_first(dy, he[:, :units])[None],
    ]
    output = (
        hidden + (ffn_sum.astype(jnp.float32) + ffn_twin.astype(jnp.float32))
    ).astype(jnp.bfloat16)
    share_rows = features // devices
    router_rows = share_rows // ranks
    grad_router = lax.dynamic_slice_in_dim(vectors[:experts], rank * router_rows, router_rows, 1).T
    latent_rows = LATENT_RANK // devices // ranks
    grad_g_kv = lax.dynamic_slice_in_dim(
        vectors[experts + 2 : experts + 2 + LATENT_RANK // 128].reshape(-1),
        (own * ranks + rank) * latent_rows,
        latent_rows,
        0,
    )
    return (
        output,
        grad_tokens,
        vectors[experts],
        grad_w_query,
        grad_w_kv_down.T,
        grad_g_kv,
        grad_w_kv_up,
        grad_w_out,
        vectors[experts + 1],
        grad_router,
        *shared_grads,
        *expert_grads,
    )


def shards(
    tokens,
    lengths,
    routes,
    grad_out,
    g_attn,
    w_query,
    key_value_down_weight,
    latent_norm_gain,
    key_value_up_weight,
    w_out,
    g_ffn,
    router,
    shared_gate,
    shared_up,
    shared_down,
    expert_gate,
    expert_up,
    expert_down,
):
    rows_here = tokens.shape[0]
    features = tokens.shape[1]
    heads_local = w_out.shape[1] // VALUE_HEAD_SIZE
    devices = lax.axis_size("dp")
    capacity = rows_here * TOPK * 4 // (3 * devices)
    experts = router.shape[1]
    highest = lax.Precision.HIGHEST
    softmax_scale = QK ** (-0.5)
    segment, token_position = doc_layout(lengths[0], rows_here)
    places = jnp.arange(rows_here, dtype=jnp.int32)
    allowed = (segment[:, None] == segment[None, :]) & (places[None, :] <= places[:, None])
    tokens_f = tokens.astype(jnp.float32)
    attn_normed, attn_unit, attn_factor = rms_normalize_pieces(tokens_f, g_attn)
    normed_bf = attn_normed.astype(jnp.bfloat16)
    query_full = jnp.dot(normed_bf, w_query, preferred_element_type=jnp.float32).reshape(
        rows_here, heads_local, QK
    )
    query_bf = jnp.concatenate(
        [
            query_full[..., :PLAIN_HEAD_SIZE],
            apply_rotation(query_full[..., PLAIN_HEAD_SIZE:], token_position),
        ],
        axis=-1,
    ).astype(jnp.bfloat16)
    latent_with_key = jnp.dot(normed_bf, key_value_down_weight, preferred_element_type=jnp.float32)
    key_turned_part = apply_rotation(latent_with_key[:, LATENT_RANK:], token_position).astype(
        jnp.bfloat16
    )
    latent_after_norm, latent_unit_scale, latent_norm_factor = rms_normalize_pieces(
        latent_with_key[:, :LATENT_RANK], latent_norm_gain
    )
    latent_bf = latent_after_norm.astype(jnp.bfloat16)
    key_value = (
        jnp.dot(latent_bf, key_value_up_weight, preferred_element_type=jnp.float32)
        .astype(jnp.bfloat16)
        .reshape(rows_here, heads_local, PLAIN_HEAD_SIZE + VALUE_HEAD_SIZE)
    )
    key_nope = key_value[..., :PLAIN_HEAD_SIZE]
    value = key_value[..., PLAIN_HEAD_SIZE:]

    def masked_scores():
        raw = jnp.einsum(
            "thd,shd->hts",
            query_bf[..., :PLAIN_HEAD_SIZE],
            key_nope,
            preferred_element_type=jnp.float32,
        )
        raw = raw + jnp.einsum(
            "thd,sd->hts",
            query_bf[..., PLAIN_HEAD_SIZE:],
            key_turned_part,
            preferred_element_type=jnp.float32,
        )
        return jnp.where(allowed[None], raw * softmax_scale, -jnp.inf)

    scores = masked_scores()
    top_score = jnp.max(scores, axis=-1, keepdims=True)
    expo = jnp.exp(scores - top_score)
    total = jnp.sum(expo, axis=-1, keepdims=True)
    log_total = top_score + jnp.log(total)
    attn_weights = (expo / total).astype(jnp.bfloat16)
    context = jnp.einsum("hts,shd->thd", attn_weights, value, preferred_element_type=jnp.float32)
    context = context.astype(jnp.bfloat16).reshape(rows_here, heads_local * VALUE_HEAD_SIZE)
    (attn,) = product_sum(context, w_out, [])
    hidden = tokens_f + attn
    ffn_normed, ffn_unit, ffn_factor = rms_normalize_pieces(hidden, g_ffn)
    ffn_bf = ffn_normed.astype(jnp.bfloat16)
    router_probs = jax.nn.softmax(jnp.dot(ffn_normed, router, precision=highest), axis=-1)
    own = lax.axis_index("dp")

    named = jnp.any(routes[:, :, None] == jnp.arange(128, dtype=jnp.int32)[None, None, :], axis=1)
    dense_gates = jnp.where(named, jnp.pad(router_probs, ((0, 0), (0, 128 - experts))), -1.0)
    everyone_grad = lax.all_gather(grad_out, "dp")
    part = shared_gate.shape[1] // devices
    shared_parts = [
        lax.dynamic_slice_in_dim(w, own * part, part, 1)
        for w in (shared_gate, shared_up, shared_down)
    ]
    (
        ffn_part,
        grad_ffn_part,
        grad_expert_gate,
        grad_expert_up,
        grad_expert_down,
        shared_grads,
    ) = ffn_plain(
        ffn_bf,
        dense_gates,
        everyone_grad,
        [w[0] for w in (expert_gate, expert_up, expert_down)],
        shared_parts,
        capacity,
        experts,
    )
    share_rows = features // devices
    grad_shared_gate, grad_shared_up, grad_shared_down = shared_home(shared_grads, part)

    grad_top = grad_out.astype(jnp.float32)
    ffn_total = lax.psum_scatter(
        ffn_part.reshape(devices * rows_here, features), "dp", scatter_dimension=0, tiled=True
    )
    ffn_total = lax.psum(ffn_total, "tensor").astype(jnp.float32)
    output = (hidden + ffn_total).astype(jnp.bfloat16)
    (grad_ffn_sum,) = sum_home([grad_ffn_part], True)
    dense_grad = (
        grad_ffn_sum[:, features : features + experts]
        + grad_ffn_sum[:, features + experts : features + 2 * experts]
    )
    grad_logits = router_probs * (
        dense_grad - jnp.sum(router_probs * dense_grad, axis=-1, keepdims=True)
    )
    grad_router_in = contract_last(grad_logits, router, highest)
    grad_router_part = contract_first(ffn_normed, grad_logits, highest)
    grad_ffn_total = grad_ffn_sum[:, :features] + grad_router_in
    grad_g_ffn = jnp.sum(grad_ffn_total * ffn_unit, axis=0)
    grad_hidden = grad_top + normalize_back(grad_ffn_total, ffn_unit, ffn_factor, g_ffn)
    grad_hidden_bf = grad_hidden.astype(jnp.bfloat16)
    grad_w_out = contract_first(grad_hidden_bf, context)
    grad_context = jnp.dot(grad_hidden_bf, w_out, preferred_element_type=jnp.float32).astype(
        jnp.bfloat16
    )
    grad_context = grad_context.reshape(rows_here, heads_local, VALUE_HEAD_SIZE)
    redone = jnp.exp(masked_scores() - log_total)
    redone_bf = redone.astype(jnp.bfloat16)
    grad_weights = jnp.einsum(
        "thd,shd->hts", grad_context, value, preferred_element_type=jnp.float32
    )
    grad_value = jnp.einsum(
        "hts,thd->shd", redone_bf, grad_context, preferred_element_type=jnp.float32
    )
    row_inner = jnp.sum(redone * grad_weights, axis=-1, keepdims=True)
    grad_raw = (redone * (grad_weights - row_inner) * softmax_scale).astype(jnp.bfloat16)
    grad_query_nope = jnp.einsum(
        "hts,shd->thd", grad_raw, key_nope, preferred_element_type=jnp.float32
    )
    grad_query_rot = jnp.einsum(
        "hts,sd->thd", grad_raw, key_turned_part, preferred_element_type=jnp.float32
    )
    grad_key_nope = jnp.einsum(
        "hts,thd->shd",
        grad_raw,
        query_bf[..., :PLAIN_HEAD_SIZE],
        preferred_element_type=jnp.float32,
    )
    grad_key_rot = jnp.einsum(
        "hts,thd->sd", grad_raw, query_bf[..., PLAIN_HEAD_SIZE:], preferred_element_type=jnp.float32
    )
    grad_query = jnp.concatenate(
        [grad_query_nope, apply_rotation(grad_query_rot, -token_position)], axis=-1
    )
    grad_query = grad_query.reshape(rows_here, heads_local * QK).astype(jnp.bfloat16)
    grad_w_query = contract_first(normed_bf, grad_query)
    grad_key_value = (
        jnp.concatenate([grad_key_nope, grad_value], axis=-1)
        .reshape(rows_here, heads_local * (PLAIN_HEAD_SIZE + VALUE_HEAD_SIZE))
        .astype(jnp.bfloat16)
    )
    grad_w_kv_up = contract_first(latent_bf, grad_key_value)
    grad_latent_normed = contract_last(grad_key_value, key_value_up_weight)
    grad_latent_part = jnp.concatenate(
        [grad_latent_normed, apply_rotation(grad_key_rot, -token_position)], axis=1
    ).astype(jnp.bfloat16)
    grad_in_summed, grad_latent_sum = product_sum(grad_query, w_query, [grad_latent_part])
    grad_latent_normed = grad_latent_sum[:, :LATENT_RANK]
    grad_g_kv = jnp.sum(grad_latent_normed * latent_unit_scale, axis=0)
    grad_latent = normalize_back(
        grad_latent_normed, latent_unit_scale, latent_norm_factor, latent_norm_gain
    )
    grad_down = jnp.concatenate([grad_latent, grad_latent_sum[:, LATENT_RANK:]], axis=1)
    grad_down_bf = grad_down.astype(jnp.bfloat16)
    share = grad_down.shape[1] // lax.axis_size("tensor")
    grad_columns = lax.dynamic_slice_in_dim(
        grad_down_bf, lax.axis_index("tensor") * share, share, 1
    )
    grad_w_kv_down = contract_first(normed_bf, grad_columns)
    grad_attn_in = grad_in_summed + contract_last(grad_down_bf, key_value_down_weight)
    grad_g_attn = jnp.sum(grad_attn_in * attn_unit, axis=0)
    grad_tokens = grad_hidden + normalize_back(grad_attn_in, attn_unit, attn_factor, g_attn)
    vectors = jnp.concatenate(
        [
            grad_router_part,
            grad_g_attn[:, None],
            grad_g_ffn[:, None],
            jnp.pad(
                grad_g_kv.reshape(devices, -1), ((0, 0), (0, share_rows - LATENT_RANK // devices))
            ).reshape(-1, 1),
            jnp.zeros((features, 128 - experts - 3), jnp.float32),
        ],
        axis=1,
    )
    blocks = [
        a.astype(jnp.bfloat16).reshape(devices, a.shape[0] // devices, a.shape[1])
        for a in (grad_w_query, grad_w_out, grad_w_kv_up, grad_w_kv_down)
    ]
    grad_w_query, grad_w_out, grad_w_kv_up, grad_w_kv_down, vectors = sum_home(
        blocks + [vectors.reshape(devices, share_rows, 128)]
    )
    rank, ranks = lax.axis_index("tensor"), lax.axis_size("tensor")
    router_rows = share_rows // ranks
    grad_router = lax.dynamic_slice_in_dim(vectors[:, :experts], rank * router_rows, router_rows, 0)
    latent_rows = LATENT_RANK // devices // ranks
    grad_g_kv = lax.dynamic_slice_in_dim(
        vectors[:, experts + 2], rank * latent_rows, latent_rows, 0
    )
    return (
        output,
        grad_tokens,
        vectors[:, experts],
        grad_w_query,
        grad_w_kv_down,
        grad_g_kv,
        grad_w_kv_up,
        grad_w_out,
        vectors[:, experts + 1],
        grad_router,
        grad_shared_gate,
        grad_shared_up,
        grad_shared_down,
        grad_expert_gate,
        grad_expert_up,
        grad_expert_down,
    )


def solution(mesh):
    in_specs = (
        P("dp", None),
        P("dp", None),
        P("dp", None),
        P("dp", None),
        P(),
        P(None, "tensor"),
        P(),
        P(),
        P(None, "tensor"),
        P(None, "tensor"),
        P(),
        P(),
        P(None, "tensor"),
        P(None, "tensor"),
        P(None, "tensor"),
        P("dp", None, "tensor"),
        P("dp", None, "tensor"),
        P("dp", None, "tensor"),
    )
    out_specs = (
        P("dp", None),
        P("dp", None),
        P("dp"),
        P("dp", "tensor"),
        P("dp", "tensor"),
        P(("dp", "tensor")),
        P("dp", "tensor"),
        P("dp", "tensor"),
        P("dp"),
        P(("dp", "tensor"), None),
        P("dp", "tensor"),
        P("dp", "tensor"),
        P("dp", "tensor"),
        P("dp", None, "tensor"),
        P("dp", None, "tensor"),
        P("dp", None, "tensor"),
    )
    tuned = mesh.shape["dp"] == 16 and mesh.shape["tensor"] == 2
    return jax.shard_map(
        shards_tuned if tuned else shards, mesh=mesh, in_specs=in_specs, out_specs=out_specs, check_vma=False)
```

```python
import functools

import jax
import jax.numpy as jnp
import numpy as np
from jax import lax
from jax.experimental import pallas as pl
from jax.experimental.pallas import tpu as pltpu
from jax.sharding import PartitionSpec as P

PLAIN_HEAD_SIZE = 128
VALUE_HEAD_SIZE = 128
QK = 192
LATENT_RANK = 512
TOPK = 6


epsilon = 1e-06


def rms_normalize_pieces(values, gain):
    factor = lax.rsqrt(jnp.mean(values * values, axis=-1, keepdims=True) + epsilon)
    unit = values * factor
    return (unit * gain, unit, factor)


def normalize_back(grad, unit, factor, gain):
    inner = grad * gain
    return factor * (inner - unit * jnp.mean(inner * unit, axis=-1, keepdims=True))


def apply_rotation(values, token_position):
    half = values.shape[-1] // 2
    freqs = 10000.0 ** (-jnp.arange(half, dtype=jnp.float32) / half)
    angles = token_position.astype(jnp.float32)[:, None] * freqs[None, :]
    shape = (angles.shape[0],) + (1,) * (values.ndim - 2) + (half,)
    cosine = jnp.cos(angles).reshape(shape)
    sine = jnp.sin(angles).reshape(shape)
    first = values[..., :half]
    second = values[..., half:]
    return jnp.concatenate(
        [first * cosine - second * sine, second * cosine + first * sine], axis=-1
    )


def doc_layout(lengths_row, rows_here):
    ends = jnp.cumsum(lengths_row)
    starts = ends - lengths_row
    places = jnp.arange(rows_here, dtype=jnp.int32)
    segment = jnp.sum((places[:, None] >= ends[None, :]).astype(jnp.int32), axis=1)
    member = segment[:, None] == jnp.arange(lengths_row.shape[0], dtype=jnp.int32)[None, :]
    begins = jnp.sum(jnp.where(member, starts[None, :], 0), axis=1)
    return (segment, places - begins)


def contract_last(left, right, precision=None):
    return lax.dot_general(
        left,
        right,
        (((1,), (1,)), ((), ())),
        precision=precision,
        preferred_element_type=jnp.float32,
    )


def contract_first(left, right, precision=None):
    return lax.dot_general(
        left,
        right,
        (((0,), (0,)), ((), ())),
        precision=precision,
        preferred_element_type=jnp.float32,
    )


def swish_parts(gate_pre):
    sigma = jax.nn.sigmoid(gate_pre)
    return (gate_pre * sigma, sigma * (1.0 + gate_pre * (1.0 - sigma)))


VMEM_LIMIT = 60 * 1024 * 1024


def place_of(x_size):
    me = lax.axis_index("dp")
    core = me % 2
    x = (me // 2) % x_size
    z = me // (2 * x_size)
    return z, x, core


def index_of(z, x, core, x_size):
    return (z * x_size + x) * 2 + core


def remote(src, dst, send_sem, recv_sem, target):
    return pltpu.make_async_remote_copy(
        src_ref=src,
        dst_ref=dst,
        send_sem=send_sem,
        recv_sem=recv_sem,
        device_id={"dp": target},
        device_id_type=pl.DeviceIdType.MESH,
    )


def greet(z, x, core, z_size, x_size, pair=False):
    barrier = pltpu.get_barrier_semaphore()

    def tell(target):
        pl.semaphore_signal(
            barrier, inc=1, device_id={"dp": target}, device_id_type=pl.DeviceIdType.MESH
        )

    tell(index_of(z, x, 1 - core, x_size))
    tell(index_of(z, 1 - x, core, x_size))

    @pl.when(z > 0)
    def _():
        tell(index_of(z - 1, x, core, x_size))

    @pl.when(z < z_size - 1)
    def _():
        tell(index_of(z + 1, x, core, x_size))

    inner = (z + z_size - 1) // z_size - z // (z_size - 1)
    if pair:
        pl.semaphore_signal(
            barrier,
            inc=1,
            device_id={"tensor": 1 - lax.axis_index("tensor")},
            device_id_type=pl.DeviceIdType.MESH,
        )
    pl.semaphore_wait(barrier, 3 + inner + (1 if pair else 0))


def near_first(z):
    half = z // 2
    return [z, (1 - z) * (1 - 2 * half), 2 * (1 - half) + half * (7 - 2 * z), 3 - 3 * half]


def add_into(dst, *srcs):
    rows = dst.shape[0]
    step = 32 if rows % 32 == 0 else 8

    def body(i, _):
        here = pl.ds(pl.multiple_of(i * step, step), step)
        total = dst[here, :].astype(jnp.float32)
        for src in srcs:
            total = total + src[here, :].astype(jnp.float32)
        dst[here, :] = total.astype(dst.dtype)
        return 0

    lax.fori_loop(0, rows // step, body, 0)


def nn(left, right):
    return lax.dot_general(
        left, right, (((1,), (0,)), ((), ())), preferred_element_type=jnp.float32
    )


def is_at(j, where):
    low = (3 - j) // 3
    high = j // 3
    return (low, (4 - j) // 3 - low, (j + 1) // 3 - high, high)[where]


def ffn_kernel(
    x_size,
    own_ffn,
    own_gates,
    grad_half,
    gate_t,
    up_t,
    down_t,
    shared_in,
    shared_out,
    out_part,
    dx_part,
    rows_all,
    dy_all,
    he_all,
    dge_all,
    due_all,
    shared_grads,
    grad_all,
    blk,
    gts,
    gate_v,
    up_v,
    down_v,
    s_in,
    s_out,
    g_buf,
    rows_b,
    grow_b,
    dy_b,
    he_b,
    dge_b,
    due_b,
    out_r,
    dx_r,
    out_l,
    dx_l,
    out_st,
    dx_st,
    acc,
    gate_col,
    dgate_acc,
    left_ffn,
    left_grad,
    own_sem,
    up_s,
    up_r,
    dn_s,
    dn_r,
    x_s,
    x_r,
    c_s,
    c_r,
    w_sem,
    g_sem,
    st_sem,
    h_s,
    h_r,
    y_s,
    y_r,
    hc_s,
    hc_r,
):
    z_size, bf16, f32 = 4, jnp.bfloat16, jnp.float32
    hidden = gate_t.shape[0]
    rows_here, features = own_ffn.shape
    slots = rows_b.shape[0] // 2
    wide = 512
    z, x, core = place_of(x_size)
    own = lax.axis_index("dp")
    at = functools.partial(index_of, x_size=x_size)
    ins, outs = (own_ffn, own_gates), (blk, gts)
    order = near_first(z)

    def place(j):
        return sum(is_at(j, i) * order[i] for i in range(4))

    weights = [
        pltpu.make_async_copy(gate_t, gate_v.at[pl.ds(0, hidden)], w_sem.at[0]),
        pltpu.make_async_copy(up_t, up_v.at[pl.ds(0, hidden)], w_sem.at[1]),
        pltpu.make_async_copy(down_t, down_v.at[pl.ds(0, hidden)], w_sem.at[2]),
        pltpu.make_async_copy(shared_in, s_in, w_sem.at[3]),
        pltpu.make_async_copy(shared_out, s_out, w_sem.at[4]),
    ]
    keep = [
        pltpu.make_async_copy(ins[a], outs[a].at[at(z, x, core)], own_sem.at[a]) for a in range(2)
    ]

    def grad_copy(k):
        w, v = place(k // 2), x + (k % 2) * (1 - 2 * x)
        return pltpu.make_async_copy(
            grad_all.at[pl.ds(2 * (w * x_size + v), 2)], g_buf.at[k % 2], g_sem.at[k % 2]
        )

    for copy in keep + weights:
        copy.start()
    grad_copy(0).start()
    greet(z, x, core, z_size, x_size, True)

    def up(a, d):
        block = outs[a].at[at(z - d, x, core)]
        src = ins[a] if d == 0 else block
        return remote(src, block, up_s.at[a, d], up_r.at[a, d], at(z + 1, x, core))

    def down(a, d):
        block = outs[a].at[at(z + d, x, core)]
        src = ins[a] if d == 0 else block
        return remote(src, block, dn_s.at[a, d], dn_r.at[a, d], at(z - 1, x, core))

    def across(a, w, first=False):
        block = outs[a].at[at(w, x, core)]
        src = ins[a] if first else block
        return remote(src, block, x_s.at[a, w], x_r.at[a, w], at(z, 1 - x, core))

    def beside(a, w, v, first=False):
        block = outs[a].at[at(w, v, core)]
        src = ins[a] if first else block
        return remote(src, block, c_s.at[a, w, v], c_r.at[a, w, v], at(z, x, 1 - core))

    rank = lax.axis_index("tensor")
    edge = 1 - ((z + 3) // 4) * ((6 - z) // 4)
    part_rows = rows_here // 2
    whose = (order[2], order[2], order[3], order[3], order[3], z, (z + 2) % 4, order[3])

    def part(store, w, v, which):
        rows = pl.ds(pl.multiple_of(which * part_rows, part_rows), part_rows)
        return store.at[at(w, v, core), rows]

    store_of = lambda j: grad_all if j in (0, 2, 3) else blk

    def link(j, w=None, target=None):
        block = part(store_of(j), whose[j] if w is None else w, x, rank)
        src = block
        if j == 5:
            src = own_ffn.at[pl.ds(pl.multiple_of(rank * part_rows, part_rows), part_rows)]
        way = 0
        if j in (2, 6, 7):
            target = z if target is None else target
            way = (target - z + 1) // 2
            target = at(target, x, core)
        else:
            target = at(z, 1 - x, core)
        return remote(src, block, h_s.at[j, way], h_r.at[j], target)

    landed = lambda j: x if j in (2, 6, 7) else 1 - x

    def swap(j):
        block = part(store_of(j), whose[j], landed(j), rank)
        return pair_copy(block, block, y_s.at[j], y_r.at[j])

    def half_beside(j, i):
        block = part(store_of(j), whose[j], landed(j), rank + i * (1 - 2 * rank))
        return remote(block, block, hc_s.at[j, i], hc_r.at[j, i], at(z, x, 1 - core))

    def link_done(j):
        link(j).wait_recv()
        swap(j).start()
        half_beside(j, 0).start()

    def swap_done(j):
        swap(j).wait_recv()
        half_beside(j, 1).start()

    def ready(j):
        half_beside(j, 0).wait_recv()
        half_beside(j, 1).wait_recv()

    def at_ends(do):
        pl.when(edge == 1)(do)

    def inside(do):
        pl.when(edge == 0)(do)

    for a in (1, 0):
        beside(a, z, x, True).start()
        if a == 1:
            across(a, z, True).start()
        else:
            link(5).start()
        pl.when(z < z_size - 1)(lambda: up(a, 0).start())
        pl.when(z > 0)(lambda: down(a, 0).start())
    link(0).start()

    def pass_on(d):
        for a in (1, 0) if d == 1 else (1,):

            @pl.when(z >= d)
            def _():
                up(a, d - 1).wait_recv()
                if a == 1:
                    pl.when(z < z_size - 1)(lambda: up(a, d).start())
                else:
                    inside(lambda: link(6, z - 1, z + 1).start())
                beside(a, z - d, x).start()

            @pl.when(z + d < z_size)
            def _():
                down(a, d - 1).wait_recv()
                if a == 1:
                    pl.when(z > 0)(lambda: down(a, d).start())
                else:
                    inside(lambda: link(6, z + 1, z - 1).start())
                beside(a, z + d, x).start()

    def from_across(w, arrays=(1, 0)):
        for a in arrays:
            across(a, w).wait_recv()
            beside(a, w, 1 - x).start()

    def early(k):
        @pl.when(k == 1)
        def _():
            pass_on(1)
            for a in (1, 0):
                across(a, order[1]).start()
            swap_done(5)
            link_done(0)
            from_across(z, (1,))
            ready(5)

        @pl.when(k == 2)
        def _():
            link_done(6)
            link(1).start()

            @inside
            def _():
                link(7, None, 3 * (z - 1)).start()
                link(2, None, 3 * (z - 1)).start()
                link(4).start()
                link(3).start()

            pass_on(2)
            across(1, order[2]).start()
            swap_done(0)

        @pl.when(k == 3)
        def _():
            from_across(order[1])
            swap_done(6)

            @at_ends
            def _():
                link_done(7)
                link(4).start()

        @pl.when(k == 4)
        def _():
            ready(0)
            link_done(1)

            @at_ends
            def _():
                ready(6)
                link_done(2)
                link(3).start()

            pass_on(3)
            across(1, order[3]).start()
            from_across(order[2], (1,))

        @pl.when(k == 5)
        def _():
            grad_copy(5).start()
            at_ends(lambda: swap_done(7))
            swap_done(1)
            ready(1)

        @pl.when(k == 6)
        def _():
            from_across(order[3], (1,))
            at_ends(lambda: ready(7))
            inside(lambda: ready(6))

        @pl.when(k == 7)
        def _():
            swap_done(3)
            ready(3)
            grad_copy(7).start()
            ready(4)

    def midway(k):
        pl.when(k == 0)(lambda: link_done(5))
        pl.when(k == 4)(lambda: link_done(4))

        @pl.when(k == 5)
        def _():
            @at_ends
            def _():
                swap_done(2)
                ready(2)

            grad_copy(6).start()
            link_done(3)

        pl.when(k == 6)(lambda: swap_done(4))

    gate_v[pl.ds(hidden, gate_v.shape[0] - hidden), :] = jnp.zeros(
        (gate_v.shape[0] - hidden, features), bf16
    )
    up_v[pl.ds(hidden, up_v.shape[0] - hidden), :] = jnp.zeros(
        (up_v.shape[0] - hidden, features), bf16
    )
    down_v[pl.ds(hidden, down_v.shape[0] - hidden), :] = jnp.zeros(
        (down_v.shape[0] - hidden, features), bf16
    )
    acc[...] = jnp.zeros(acc.shape, f32)
    for copy in weights:
        copy.wait()
    for a in range(2):
        out_r[a, pl.ds(slots, 128), :] = s_out[...]
        dx_r[a, pl.ds(slots, 256), :] = s_in[...]
    for copy in keep:
        copy.wait()
    expert = lax.broadcasted_iota(jnp.int32, (rows_here, own_gates.shape[0]), 1)
    lane = lax.broadcasted_iota(jnp.int32, (rows_here, 128), 1)
    earlier = lax.broadcasted_iota(jnp.int32, (rows_here, rows_here), 1)
    later = lax.broadcasted_iota(jnp.int32, (rows_here, rows_here), 0)
    upto = (earlier <= later).astype(bf16)
    slot_lane = lax.broadcasted_iota(jnp.int32, (rows_here, slots), 1).astype(f32)

    def staged(pair, which):
        pairs = [
            (rows_b, rows_all),
            (dy_b, dy_all),
            (he_b, he_all),
            (dge_b, dge_all),
            (due_b, due_all),
            (out_st, out_part),
            (dx_st, dx_part),
        ]
        return [
            pltpu.make_async_copy(pairs[i][0], pairs[i][1].at[pair], st_sem.at[i]) for i in which
        ]

    def start_staged(pair, which):
        for copy in staged(pair, which):
            copy.start()

    def wait_staged(k, which):
        @pl.when(k > 0)
        def _():
            for copy in staged(0, which):
                copy.wait()

    def body(k, _):
        w, v = place(k // 2), x + (k % 2) * (1 - 2 * x)
        pair = w * x_size + v
        block = 2 * pair
        here = k % 2
        early(k)
        grad_copy(k).wait()
        pl.when(k < 4)(lambda: grad_copy(k + 1).start())
        beside(1, w, v).wait_recv()
        whole = (k == 0) | (k == 2) | (k == 3) | ((k == 4) & (edge == 0))
        pl.when(whole)(lambda: beside(0, w, v).wait_recv())

        for a in range(2):
            gates = gts[block + a].T
            count = nn(upto, (gates >= 0.0).astype(bf16))
            gate = jnp.sum(jnp.where(expert == own, gates, 0.0), axis=1, keepdims=True)
            slot = jnp.sum(jnp.where(expert == own, count, 0.0), axis=1, keepdims=True) - 1.0
            pick = ((slot_lane == slot) & (gate >= 0.0)).astype(f32).astype(bf16)
            out_l[a, :, pl.ds(0, slots)] = pick
            dx_l[a, :, pl.ds(0, slots)] = pick
            high = gate.astype(bf16).astype(f32)
            middle = (gate - high).astype(bf16).astype(f32)
            low = gate - high - middle
            parts = jnp.where(
                lane == 0, high, jnp.where(lane == 1, middle, jnp.where(lane == 2, low, 0.0))
            ).astype(bf16)
            pick_t = pick.T
            left_ffn[a, pl.ds(0, slots), :] = pick_t
            left_grad[a, pl.ds(0, slots), :] = pick_t
            picked = jnp.sum(nn(pick_t, parts), axis=1, keepdims=True)
            gate_col[pl.ds(a * slots, slots), :] = jnp.broadcast_to(picked, (slots, 128))

        both = pl.ds(block, 2)
        pre = contract_last(blk[both].reshape(2 * rows_here, features), s_in[...])
        grad_hidden = contract_last(g_buf[here].reshape(2 * rows_here, features), s_out[...])
        act, slope = swish_parts(pre[:, :128])
        up_pre = pre[:, 128:]
        shared_units = (
            (act * up_pre).astype(bf16),
            (grad_hidden * up_pre * slope).astype(bf16),
            (grad_hidden * act).astype(bf16),
        )
        for a in range(2):
            mine = slice(a * rows_here, (a + 1) * rows_here)
            out_l[a, :, pl.ds(slots, 128)] = shared_units[0][mine]
            dx_l[a, :, pl.ds(slots, 128)] = shared_units[1][mine]
            dx_l[a, :, pl.ds(slots + 128, 128)] = shared_units[2][mine]
            left_ffn[a, pl.ds(slots, 128), :] = shared_units[1][mine].T
            left_ffn[a, pl.ds(slots + 128, 128), :] = shared_units[2][mine].T
            left_grad[a, pl.ds(slots, 128), :] = shared_units[0][mine].T

        def pick_rows(n, _):
            cols = pl.ds(pl.multiple_of(n * wide, wide), wide)
            for a in range(2):
                mine = pl.ds(a * slots, slots)
                product = nn(left_ffn[a], blk[block + a, :, cols])
                rows_b[mine, cols] = product[:slots].astype(bf16)
                acc[pl.ds(0, 256), cols] += product[slots:]
                product = nn(left_grad[a], g_buf[here, a, :, cols])
                grows = product[:slots]
                acc[pl.ds(256, 128), cols] += product[slots:]
                grow_b[mine, cols] = grows.astype(bf16)
                dy_b[mine, cols] = (gate_col[mine, pl.ds(0, 1)] * grows).astype(bf16)
            return 0

        wait_staged(k, (0, 1))
        lax.fori_loop(0, features // wide, pick_rows, 0)
        start_staged(pair, (0, 1))

        def hidden_units(n, _):
            units = pl.ds(pl.multiple_of(n * 256, 256), 256)
            gate_pre = contract_last(rows_b[...], gate_v[units, :])
            up_pre = contract_last(rows_b[...], up_v[units, :])
            grad_hidden = contract_last(dy_b[...], down_v[units, :])
            act, slope = swish_parts(gate_pre)
            he_b[:, units] = (act * up_pre).astype(bf16)
            dge_b[:, units] = (grad_hidden * up_pre * slope).astype(bf16)
            due_b[:, units] = (grad_hidden * act).astype(bf16)
            return 0

        wait_staged(k, (2, 3, 4))
        lax.fori_loop(0, gate_v.shape[0] // 256, hidden_units, 0)
        start_staged(pair, (2, 3, 4))
        midway(k)
        dgate_acc[...] = jnp.zeros(dgate_acc.shape, f32)

        def back(n, _):
            cols = pl.ds(pl.multiple_of(n * wide, wide), wide)
            result = nn(he_b[...], down_v[:, cols])
            product = grow_b[:, cols].astype(f32) * result
            for i in range(wide // 128):
                dgate_acc[...] += product[:, i * 128 : (i + 1) * 128]
            result = (gate_col[:, pl.ds(0, 1)] * result).astype(bf16)
            grad_in = (nn(dge_b[...], gate_v[:, cols]) + nn(due_b[...], up_v[:, cols])).astype(bf16)
            for a in range(2):
                mine = slice(a * slots, (a + 1) * slots)
                out_r[a, pl.ds(0, slots), cols] = result[mine]
                dx_r[a, pl.ds(0, slots), cols] = grad_in[mine]
                out_st[a, :, cols] = nn(out_l[a], out_r[a, :, cols]).astype(bf16)
                dx_st[a, :, cols] = nn(dx_l[a], dx_r[a, :, cols]).astype(bf16)
            return 0

        wait_staged(k, (5, 6))
        lax.fori_loop(0, features // wide, back, 0)
        dgate = jnp.sum(dgate_acc[...], axis=1, keepdims=True)
        high = dgate.astype(bf16).astype(f32)
        spread = lax.broadcasted_iota(jnp.int32, (2 * slots, 128), 1)
        spread = jnp.where(
            spread == own, high, jnp.where(spread == own + 16, dgate - high, 0.0)
        ).astype(bf16)
        for a in range(2):
            dx_st[a, :, pl.ds(features, 128)] = nn(
                out_l[a, :, pl.ds(0, slots)], spread[a * slots : (a + 1) * slots]
            ).astype(bf16)
        start_staged(pair, (5, 6))
        return 0

    lax.fori_loop(0, 8, body, 0)
    wait_staged(1, range(7))
    shared_grads[...] = acc[...].astype(bf16)
    for i in range(z_size):
        beside(1, order[i], x).wait_send()
        beside(1, order[i], 1 - x).wait_send()
        across(1, order[i]).wait_send()
    for i in range(2):
        beside(0, order[i], x).wait_send()
    inside(lambda: beside(0, order[2], x).wait_send())
    beside(0, order[1], 1 - x).wait_send()
    across(0, order[1]).wait_send()
    for d in range(z_size):
        for a in range(2) if d == 0 else (1,):
            pl.when((z >= d) & (z < z_size - 1))(lambda: up(a, d).wait_send())
            pl.when((z + d < z_size) & (z > 0))(lambda: down(a, d).wait_send())

    @inside
    def _():
        link(2, None, 3 * (z - 1)).wait_send()
        link(7, None, 3 * (z - 1)).wait_send()
        link(6, z - 1, z + 1).wait_send()
        link(6, z + 1, z - 1).wait_send()

    for j in range(8):

        def sent_on(j=j):
            swap(j).wait_send()
            half_beside(j, 0).wait_send()
            half_beside(j, 1).wait_send()

        if j in (2, 7):
            at_ends(sent_on)
        else:
            sent_on()
        if j not in (2, 6, 7):
            link(j).wait_send()


def ffn_tuned(own_ffn, own_gates, grad_all, gate_t, up_t, down_t, shared_in, shared_out, slots):
    rows, features = own_ffn.shape
    hidden = gate_t.shape[0]
    padded = -(-hidden // 256) * 256
    bf16, f32, dma = jnp.bfloat16, jnp.float32, pltpu.SemaphoreType.DMA
    anywhere = pl.BlockSpec(memory_space=pl.ANY)
    shape = jax.ShapeDtypeStruct
    return pl.pallas_call(
        functools.partial(ffn_kernel, 2),
        out_shape=[
            shape((8, 2, rows, features), bf16),
            shape((8, 2, rows, features + 128), bf16),
            shape((8, 2 * slots, features), bf16),
            shape((8, 2 * slots, features), bf16),
            shape((8, 2 * slots, padded), bf16),
            shape((8, 2 * slots, padded), bf16),
            shape((8, 2 * slots, padded), bf16),
            shape((384, features), bf16),
            shape((16, rows, features), bf16),
        ],
        in_specs=[anywhere] * 8,
        out_specs=[anywhere] * 7 + [pl.BlockSpec(memory_space=pltpu.VMEM), anywhere],
        input_output_aliases={2: 8},
        scratch_shapes=[
            pltpu.VMEM((16, rows, features), bf16),
            pltpu.VMEM((16,) + own_gates.shape, f32),
            pltpu.VMEM((padded, features), bf16),
            pltpu.VMEM((padded, features), bf16),
            pltpu.VMEM((padded, features), bf16),
            pltpu.VMEM((256, features), bf16),
            pltpu.VMEM((128, features), bf16),
            pltpu.VMEM((2, 2, rows, features), bf16),
            pltpu.VMEM((2 * slots, features), bf16),
            pltpu.VMEM((2 * slots, features), bf16),
            pltpu.VMEM((2 * slots, features), bf16),
            pltpu.VMEM((2 * slots, padded), bf16),
            pltpu.VMEM((2 * slots, padded), bf16),
            pltpu.VMEM((2 * slots, padded), bf16),
            pltpu.VMEM((2, slots + 128, features), bf16),
            pltpu.VMEM((2, slots + 256, features), bf16),
            pltpu.VMEM((2, rows, slots + 128), bf16),
            pltpu.VMEM((2, rows, slots + 256), bf16),
            pltpu.VMEM((2, rows, features), bf16),
            pltpu.VMEM((2, rows, features + 128), bf16),
            pltpu.VMEM((384, features), f32),
            pltpu.VMEM((2 * slots, 128), f32),
            pltpu.VMEM((2 * slots, 128), f32),
            pltpu.VMEM((2, slots + 256, rows), bf16),
            pltpu.VMEM((2, slots + 128, rows), bf16),
            dma((2,)),
        ]
        + [dma((2, 4))] * 6
        + [dma((2, 4, 2))] * 2
        + [dma((5,)), dma((2,)), dma((7,))]
        + [dma((8, 2))]
        + [dma((8,))] * 3
        + [dma((8, 2))] * 2,
        compiler_params=pltpu.CompilerParams(
            collective_id=1, has_side_effects=True, vmem_limit_bytes=VMEM_LIMIT
        ),
        name="ffn",
    )(
        own_ffn,
        own_gates,
        grad_all.reshape(16, rows, features),
        gate_t,
        up_t,
        down_t,
        shared_in,
        shared_out,
    )


def first_half(shape):
    return lax.broadcasted_iota(jnp.int32, shape, 1) % 64 < 32


def turn(values, cosine, sine):
    partner = jnp.where(
        first_half(values.shape), pltpu.roll(values, 96, 1), pltpu.roll(values, 32, 1)
    )
    return values * cosine + partner * sine


def layout_of(lengths, rows, width):
    row = lax.broadcasted_iota(jnp.int32, (rows, width), 0)
    across = lax.broadcasted_iota(jnp.int32, (rows, rows), 1)
    down = lax.broadcasted_iota(jnp.int32, (rows, rows), 0)
    place, met, end = row, across <= down, 0
    for i in range(lengths.shape[1]):
        end = end + lengths[0, i]
        place = place - jnp.where(row >= end, lengths[0, i], 0)
        met = met & ((across >= end) == (down >= end))
    return place, met


def turn_tables(lengths, freqs, rows):
    place, met = layout_of(lengths, rows, 128)
    angles = place.astype(jnp.float32) * freqs[...]
    sine = jnp.sin(angles)
    return jnp.cos(angles), jnp.where(first_half(angles.shape), -sine, sine), met


def pair_copy(src, dst, send_sem, recv_sem):
    return pltpu.make_async_remote_copy(
        src_ref=src,
        dst_ref=dst,
        send_sem=send_sem,
        recv_sem=recv_sem,
        device_id={"tensor": 1 - lax.axis_index("tensor")},
        device_id_type=pl.DeviceIdType.MESH,
    )


def greet_pair():
    barrier = pltpu.get_barrier_semaphore()
    pl.semaphore_signal(
        barrier,
        inc=1,
        device_id={"tensor": 1 - lax.axis_index("tensor")},
        device_id_type=pl.DeviceIdType.MESH,
    )
    pl.semaphore_wait(barrier, 1)


def forward_kernel(
    lengths,
    freqs,
    tokens,
    routes,
    g_attn,
    g_latent,
    g_ffn,
    router_t,
    w_query,
    down_t,
    kv_up,
    w_out,
    grad_out,
    hidden,
    ffn_bf,
    gates,
    probs,
    normed,
    queries,
    kv,
    key_turned,
    latent_bf,
    latent,
    context,
    log_totals,
    everyone,
    wq_v,
    down_v,
    up_v,
    out_v,
    sent,
    got,
    w_sem,
    s_sem,
    r_sem,
    own_sem,
    up_s,
    up_r,
    dn_s,
    dn_r,
    x_s,
    x_r,
    c_s,
    c_r,
):
    bf16, f32 = jnp.bfloat16, jnp.float32
    z_size, x_size = 4, 2
    z, x, core = place_of(x_size)
    at = functools.partial(index_of, x_size=x_size)
    rows, features = tokens.shape
    rank = kv_up.shape[0]
    heads = kv_up.shape[1] // 256
    turned = down_t.shape[0] - rank
    tail = pl.ds(rank, turned)
    loads = [
        pltpu.make_async_copy(down_t, down_v.at[pl.ds(0, rank + turned)], w_sem.at[0]),
        pltpu.make_async_copy(down_t.at[tail], down_v.at[pl.ds(rank + turned, turned)], w_sem.at[1]),
        pltpu.make_async_copy(kv_up, up_v, w_sem.at[2]),
        pltpu.make_async_copy(w_query, wq_v, w_sem.at[3]),
        pltpu.make_async_copy(w_out, out_v, w_sem.at[4]),
    ]
    keep = pltpu.make_async_copy(grad_out, everyone.at[at(z, x, core)], own_sem.at[0])

    def move(w, v, first, sems, target):
        block = everyone.at[at(w, v, core)]
        return remote(grad_out if first else block, block, *sems, target)

    up = lambda d: move(z - d, x, d == 0, (up_s.at[d], up_r.at[d]), at(z + 1, x, core))
    down = lambda d: move(z + d, x, d == 0, (dn_s.at[d], dn_r.at[d]), at(z - 1, x, core))
    across = lambda i, w: move(w, x, i == 0, (x_s.at[i], x_r.at[i]), at(z, 1 - x, core))
    beside = lambda w, v, first=False: move(
        w, v, first, (c_s.at[w, v], c_r.at[w, v]), at(z, x, 1 - core)
    )
    near = near_first(z)[1]

    def from_across(i, w):
        block = everyone.at[at(w, 1 - x, core)]
        remote(block, block, x_s.at[i], x_r.at[i], at(z, 1 - x, core)).wait_recv()
        beside(w, 1 - x).start()

    keep.start()
    for copy in loads:
        copy.start()
    greet(z, x, core, z_size, x_size, True)
    beside(z, x, True).start()
    across(0, z).start()
    pl.when(z < z_size - 1)(lambda: up(0).start())
    pl.when(z > 0)(lambda: down(0).start())
    cosine, sine, met = turn_tables(lengths, freqs, rows)
    values, _, _ = rms_normalize_pieces(tokens[...].astype(f32), g_attn[...])
    normed[...] = values.astype(bf16)
    loads[0].wait()
    loads[1].wait()
    low = contract_last(normed[...], down_v[...])
    latent[...] = low[:, :rank]
    key_turned[...] = turn(low[:, rank:], cosine, sine).astype(bf16)
    values, _, _ = rms_normalize_pieces(latent[...], g_latent[...])
    latent_bf[...] = values.astype(bf16)
    loads[2].wait()

    def keys(n, _):
        cols = pl.ds(pl.multiple_of(n * 512, 512), 512)
        kv[:, cols] = nn(latent_bf[...], up_v[:, cols]).astype(bf16)
        return 0

    lax.fori_loop(0, kv.shape[1] // 512, keys, 0)
    loads[3].wait()
    lane = lax.broadcasted_iota(jnp.int32, (rows, 128), 1)
    log_totals[...] = jnp.zeros(log_totals.shape, f32)

    def two_heads(i, _):
        three = nn(normed[...], wq_v[:, pl.ds(pl.multiple_of(i * 384, 384), 384)])
        middle, last = three[:, 128:256], three[:, 256:]
        plain = (
            three[:, :128],
            jnp.where(lane < 64, pltpu.roll(middle, 64, 1), pltpu.roll(last, 64, 1)),
        )
        spun = turn(jnp.where(lane < 64, middle, last), cosine, sine)
        for b in range(2):
            head = 2 * i + b
            queries[head, :, pl.ds(0, 128)] = plain[b].astype(bf16)
            queries[head, :, pl.ds(128, 128)] = jnp.where(
                (lane < 64) == (b == 0), spun, 0.0
            ).astype(bf16)
            at = pl.multiple_of(head * 256, 256)
            key = jnp.concatenate([kv[:, pl.ds(at, 128)], key_turned[...]], axis=1)
            raw = contract_last(queries[head], key)
            scores = jnp.where(met, raw * QK ** (-0.5), -jnp.inf)
            top = jnp.max(scores, axis=1, keepdims=True)
            expo = jnp.exp(scores - top)
            total = jnp.sum(expo, axis=1, keepdims=True)
            log_totals[...] = jnp.where(lane == head, top + jnp.log(total), log_totals[...])
            context[:, pl.ds(pl.multiple_of(head * 128, 128), 128)] = nn(
                (expo / total).astype(bf16), kv[:, pl.ds(at + 128, 128)]
            ).astype(bf16)
        return 0

    lax.fori_loop(0, heads // 2, two_heads, 0)

    loads[4].wait()
    chunks, width = sent.shape[0], sent.shape[2]
    chunk = lambda i: pair_copy(sent.at[i], got.at[i], s_sem.at[i], r_sem.at[i])

    def project(i, _):
        sent[i] = contract_last(
            context[...], out_v[pl.ds(pl.multiple_of(i * width, width), width), :]
        ).astype(bf16)
        chunk(i).start()
        return 0

    lax.fori_loop(0, chunks, project, 0)

    @pl.when(z > 0)
    def _():
        up(0).wait_recv()
        across(1, z - 1).start()
        pl.when(z < z_size - 1)(lambda: up(1).start())
        beside(z - 1, x).start()

    @pl.when(z < z_size - 1)
    def _():
        down(0).wait_recv()
        pl.when(z == 0)(lambda: across(1, z + 1).start())
        pl.when(z > 0)(lambda: down(1).start())
        beside(z + 1, x).start()

    from_across(0, z)

    def join(i, _):
        chunk(i).wait()
        cols = pl.ds(pl.multiple_of(i * width, width), width)
        hidden[:, cols] = tokens[:, cols].astype(f32) + (sent[i].astype(f32) + got[i].astype(f32))
        return 0

    lax.fori_loop(0, chunks, join, 0)
    values, _, _ = rms_normalize_pieces(hidden[...], g_ffn[...])
    ffn_bf[...] = values.astype(bf16)
    experts = lax.axis_size("dp")
    logits = lax.dot_general(
        values,
        router_t[...],
        (((1,), (1,)), ((), ())),
        precision=lax.Precision.HIGHEST,
        preferred_element_type=f32,
    )
    logits = jnp.where(lane < experts, logits, -jnp.inf)
    expo = jnp.exp(logits - jnp.max(logits, axis=1, keepdims=True))
    share = expo / jnp.sum(expo, axis=1, keepdims=True)
    probs[...] = share
    named = lane < 0
    for i in range(routes.shape[1]):
        named = named | (lane == routes[:, pl.ds(i, 1)])
    gates[...] = jnp.where(named, share, -1.0).T[: gates.shape[0]]

    @pl.when(z >= 2)
    def _():
        up(1).wait_recv()
        beside(z - 2, x).start()

    @pl.when(z < z_size - 2)
    def _():
        down(1).wait_recv()
        beside(z + 2, x).start()

    from_across(1, near)
    beside(z, x).wait()
    beside(z, 1 - x).wait()
    beside(near, 1 - x).wait()
    pl.when(z > 0)(lambda: beside(z - 1, x).wait())
    pl.when(z < z_size - 1)(lambda: beside(z + 1, x).wait())
    pl.when(z >= 2)(lambda: beside(z - 2, x).wait())
    pl.when(z < z_size - 2)(lambda: beside(z + 2, x).wait())
    across(0, z).wait_send()
    across(1, near).wait_send()
    pl.when(z < z_size - 1)(lambda: up(0).wait_send())
    pl.when(z > 0)(lambda: down(0).wait_send())
    pl.when((z > 0) & (z < z_size - 1))(lambda: up(1).wait_send())
    pl.when((z > 0) & (z < z_size - 1))(lambda: down(1).wait_send())
    keep.wait()


def forward_tuned(
    lengths,
    freqs,
    tokens,
    routes,
    g_attn,
    g_latent,
    g_ffn,
    router_t,
    w_query,
    down_t,
    kv_up,
    w_out,
    grad_out,
):
    rows, features = tokens.shape
    rank, columns = kv_up.shape
    heads = columns // 256
    bf16, f32, dma = jnp.bfloat16, jnp.float32, pltpu.SemaphoreType.DMA
    vmem, anywhere = pl.BlockSpec(memory_space=pltpu.VMEM), pl.BlockSpec(memory_space=pl.ANY)
    smem = pl.BlockSpec(memory_space=pltpu.SMEM)
    shape = jax.ShapeDtypeStruct
    chunks = 8
    return pl.pallas_call(
        forward_kernel,
        out_shape=[
            shape((rows, features), f32),
            shape((rows, features), bf16),
            shape((lax.axis_size("dp"), rows), f32),
            shape((rows, 128), f32),
            shape((rows, features), bf16),
            shape((heads, rows, 256), bf16),
            shape((rows, columns), bf16),
            shape((rows, 128), bf16),
            shape((rows, rank), bf16),
            shape((rows, rank), f32),
            shape((rows, heads * 128), bf16),
            shape((rows, 128), f32),
            shape((16,) + grad_out.shape, bf16),
        ],
        in_specs=[smem] + [vmem] * 7 + [anywhere] * 5,
        out_specs=[vmem] * 12 + [anywhere],
        scratch_shapes=[
            pltpu.VMEM(w_query.shape, bf16),
            pltpu.VMEM((rank + 128, features), bf16),
            pltpu.VMEM(kv_up.shape, bf16),
            pltpu.VMEM(w_out.shape, bf16),
            pltpu.VMEM((chunks, rows, features // chunks), bf16),
            pltpu.VMEM((chunks, rows, features // chunks), bf16),
            dma((5,)),
            dma((chunks,)),
            dma((chunks,)),
            dma((1,)),
        ]
        + [dma((2,))] * 6
        + [dma((4, 2))] * 2,
        compiler_params=pltpu.CompilerParams(
            collective_id=2, has_side_effects=True, vmem_limit_bytes=VMEM_LIMIT
        ),
        name="attention_forward",
    )(
        lengths,
        freqs,
        tokens,
        routes,
        g_attn,
        g_latent,
        g_ffn,
        router_t,
        w_query,
        down_t,
        kv_up,
        w_out,
        grad_out,
    )


def backward_kernel(
    lengths,
    freqs,
    sums,
    hidden,
    grad_out,
    tokens,
    probs,
    g_attn,
    g_latent,
    g_ffn,
    router_t,
    queries,
    kv,
    key_turned,
    latent,
    log_totals,
    normed,
    context,
    latent_bf,
    w_query,
    down_t,
    kv_up,
    w_out,
    grad_tokens,
    out_grad,
    query_grad,
    up_grad,
    down_grad,
    vector_grad,
    wq_v,
    down_v,
    up_v,
    unit,
    grad_hidden_bf,
    grad_query,
    grad_kv,
    grad_low,
    vectors,
    hidden_t,
    normed_t,
    latent_t,
    low_t,
    send_wide,
    send_up,
    send_down,
    send_vector,
    out_c,
    query_c,
    up_c,
    down_c,
    vector_c,
    out_x,
    query_x,
    up_x,
    down_x,
    vector_x,
    out_z,
    query_z,
    up_z,
    down_z,
    vector_z,
    grad_context,
    grad_turned,
    sent,
    got,
    low_sent,
    low_got,
    w_sem,
    s_sem,
    r_sem,
    e_sem,
    c_s,
    c_r,
    x_s,
    x_r,
    z_s,
    z_r,
):
    grad_hidden = grad_tokens
    z_size, x_size = 4, 2
    z, x, core = place_of(x_size)
    place_rank = lax.axis_index("tensor")
    at = functools.partial(index_of, x_size=x_size)
    half = z // 2
    inner = ((z + 3) // 4) * ((6 - z) // 4)
    order = [3 - 3 * half, 2 - half, 1 - z + 4 * half, z]
    blocks = [(w, v) for v in (1 - x, x) for w in order]
    outs = (out_grad, query_grad, up_grad, down_grad, vector_grad)
    c_buf = (out_c, query_c, up_c, down_c, vector_c)
    x_buf = (out_x, query_x, up_x, down_x, vector_x)
    z_buf = (out_z, query_z, up_z, down_z, vector_z)

    def product(p, owner):
        rows = lambda size: pl.ds(pl.multiple_of(owner * size, size), size)
        if p == 0:
            return nn(hidden_t[rows(128), :], context[...])
        if p == 1:
            return nn(normed_t[rows(128), :], grad_query[...])
        if p == 2:
            size = up_grad.shape[0]
            return nn(latent_t[rows(size), :], grad_kv[...])
        if p == 3:
            size = down_grad.shape[0]
            mine = pl.ds(pl.multiple_of(place_rank * size, 32), size)
            return nn(low_t[mine, :], normed[:, rows(128)])
        return vectors[:, rows(128)]

    def staging(p, i):
        if p == 0:
            return send_wide.at[i, :, pl.ds(0, out_grad.shape[1])]
        return (None, send_wide, send_up, send_down, send_vector)[p].at[i]

    def beside(p, i):
        w, v = blocks[i]
        return remote(
            staging(p, i), c_buf[p].at[w, v], c_s.at[p, i], c_r.at[p, w, v], at(z, x, 1 - core)
        )

    across = lambda p, w: remote(
        c_buf[p].at[w, 1 - x], x_buf[p].at[w], x_s.at[p, w], x_r.at[p, w], at(z, 1 - x, core)
    )

    def along(p, w, slot, target):
        return remote(
            c_buf[p].at[w, x], z_buf[p].at[slot], z_s.at[p, w], z_r.at[p, slot], at(target, x, core)
        )

    def to_sibling(p):
        for i, (w, v) in enumerate(blocks):
            staging(p, i)[...] = product(p, at(w, v, 1 - core)).astype(c_buf[p].dtype)
            beside(p, i).start()

    def over_x(p):
        for i, (w, v) in enumerate(blocks):
            beside(p, i).wait_recv()
            total = c_buf[p][w, v].astype(jnp.float32) + product(p, at(w, v, core))
            c_buf[p][w, v] = total.astype(c_buf[p].dtype)
            if i < 4:
                across(p, w).start()

    def over_z(p, k):
        w = order[k]
        across(p, w).wait_recv()
        if k < 3:

            @pl.when(inner == 1)
            def _():
                along(p, w, w, z).wait_recv()
                add_into(c_buf[p].at[w, x], x_buf[p].at[w], z_buf[p].at[w])

            @pl.when(inner == 0)
            def _():
                add_into(c_buf[p].at[w, x], x_buf[p].at[w])

            @pl.when(w > z)
            def _():
                along(p, w, w, z + 1).start()

            @pl.when(w < z - 1)
            def _():
                along(p, w, w, z - 1).start()

            @pl.when(w == z - 1)
            def _():
                along(p, w, z_size, z - 1).start()

        else:
            add_into(c_buf[p].at[w, x], x_buf[p].at[w])

            @pl.when(z > 0)
            def _():
                along(p, w, z, z).wait_recv()
                add_into(c_buf[p].at[w, x], z_buf[p].at[z])

            @pl.when(z < z_size - 1)
            def _():
                along(p, w, z_size, z).wait_recv()
                add_into(c_buf[p].at[w, x], z_buf[p].at[z_size])

            outs[p][...] = c_buf[p][z, x].astype(outs[p].dtype)

    bf16, f32 = jnp.bfloat16, jnp.float32
    highest = lax.Precision.HIGHEST
    rows, features = tokens.shape
    rank = kv_up.shape[0]
    heads = kv_up.shape[1] // 256
    turned = down_t.shape[0] - rank
    tail = pl.ds(rank, turned)
    out_v = wq_v.at[:, pl.ds(0, w_out.shape[1])]
    loads = [
        pltpu.make_async_copy(w_out, out_v, w_sem.at[0]),
        pltpu.make_async_copy(kv_up, up_v, w_sem.at[1]),
        pltpu.make_async_copy(w_query, wq_v, w_sem.at[2]),
        pltpu.make_async_copy(down_t, down_v.at[pl.ds(0, rank + turned)], w_sem.at[3]),
        pltpu.make_async_copy(down_t.at[tail], down_v.at[pl.ds(rank + turned, turned)], w_sem.at[4]),
    ]
    rows_copy = pltpu.make_async_copy(hidden, unit, w_sem.at[5])
    rows_copy.start()
    for copy in loads[:2] + loads[3:]:
        copy.start()
    greet(z, x, core, z_size, x_size, True)
    cosine, sine, met = turn_tables(lengths, freqs, rows)
    lane = lax.broadcasted_iota(jnp.int32, (rows, 128), 1)
    experts = lax.axis_size("dp")

    extra = sums[:, pl.ds(features, 128)]
    dense = extra + pltpu.roll(extra, 128 - experts, 1)
    share = probs[...]
    dense = jnp.where(lane < experts, dense, 0.0)
    logits = share * (dense - jnp.sum(share * dense, axis=1, keepdims=True))
    grad_in = sums[:, pl.ds(0, features)] + lax.dot_general(
        logits,
        router_t[...],
        (((1,), (0,)), ((), ())),
        precision=highest,
        preferred_element_type=f32,
    )
    rows_copy.wait()
    values, unit_rows, factor = rms_normalize_pieces(unit[...], g_ffn[...])
    unit[...] = unit_rows
    vectors[pl.ds(0, experts), :] = lax.dot_general(
        logits, values, (((0,), (0,)), ((), ())), precision=highest, preferred_element_type=f32
    )[:experts]
    vectors[pl.ds(experts, 8), :] = jnp.zeros((8, features), f32)
    vectors[pl.ds(experts + 1, 1), :] = jnp.sum(grad_in * unit[...], axis=0, keepdims=True)
    grad_hidden[...] = grad_out[...].astype(f32) + normalize_back(
        grad_in, unit[...], factor, g_ffn[...]
    )
    grad_hidden_bf[...] = grad_hidden[...].astype(bf16)
    hidden_t[...] = grad_hidden_bf[...].T
    to_sibling(0)
    loads[0].wait()

    def back_out(n, _):
        cols = pl.ds(pl.multiple_of(n * 256, 256), 256)
        grad_context[:, cols] = nn(grad_hidden_bf[...], out_v[:, cols]).astype(bf16)
        return 0

    lax.fori_loop(0, grad_context.shape[1] // 256, back_out, 0)
    loads[2].start()
    grad_turned[...] = jnp.zeros(grad_turned.shape, f32)
    over_x(0)
    normed_t[...] = normed[...].T
    latent_t[...] = latent_bf[...].T

    def two_heads(i, _):
        pieces = []
        for b in range(2):
            head = 2 * i + b
            at = pl.multiple_of(head * 256, 256)
            key = jnp.concatenate([kv[:, pl.ds(at, 128)], key_turned[...]], axis=1)
            value = kv[:, pl.ds(at + 128, 128)]
            raw = contract_last(queries[head], key)
            log_total = jnp.sum(
                jnp.where(lane == head, log_totals[...], 0.0), axis=1, keepdims=True
            )
            weights = jnp.exp(jnp.where(met, raw * QK ** (-0.5), -jnp.inf) - log_total)
            grad_ctx = grad_context[:, pl.ds(pl.multiple_of(head * 128, 128), 128)]
            grad_weights = contract_last(grad_ctx, value)
            inner = jnp.sum(weights * grad_weights, axis=1, keepdims=True)
            grad_raw = (weights * (grad_weights - inner) * QK ** (-0.5)).astype(bf16)
            pieces.append(nn(grad_raw, key))
            back_key = contract_first(grad_raw, queries[head])
            grad_kv[:, pl.ds(at, 128)] = back_key[:, :128].astype(bf16)
            grad_turned[...] += back_key[:, 128:]
            grad_kv[:, pl.ds(at + 128, 128)] = contract_first(
                weights.astype(bf16), grad_ctx
            ).astype(bf16)
        even, odd = pieces
        spun = turn(jnp.where(lane < 64, even[:, 128:], odd[:, 128:]), cosine, -sine)
        moved = pltpu.roll(odd[:, :128], 64, 1)
        start = pl.multiple_of(i * 384, 384)
        grad_query[:, pl.ds(start, 128)] = even[:, :128].astype(bf16)
        grad_query[:, pl.ds(start + 128, 128)] = jnp.where(lane < 64, spun, moved).astype(bf16)
        grad_query[:, pl.ds(start + 256, 128)] = jnp.where(lane < 64, moved, spun).astype(bf16)
        return 0

    lax.fori_loop(0, heads // 2, two_heads, 0)
    for i in range(8):
        beside(0, i).wait_send()
    to_sibling(1)
    loads[1].wait()
    low_sent[:, pl.ds(0, rank)] = contract_last(grad_kv[...], up_v[...]).astype(bf16)
    folded = turn(grad_turned[...] + pltpu.roll(grad_turned[...], 64, 1), cosine, -sine)
    low_sent[:, pl.ds(rank, 128)] = jnp.where(lane < turned, folded, 0.0).astype(bf16)
    low_copy = pair_copy(low_sent, low_got, e_sem.at[0], e_sem.at[1])
    low_copy.start()
    loads[2].wait()
    chunks, width = sent.shape[0], sent.shape[2]
    chunk = lambda i: pair_copy(sent.at[i], got.at[i], s_sem.at[i], r_sem.at[i])

    def project(i, _):
        sent[i] = contract_last(
            grad_query[...], wq_v[pl.ds(pl.multiple_of(i * width, width), width), :]
        ).astype(bf16)
        chunk(i).start()
        return 0

    lax.fori_loop(0, chunks, project, 0)
    over_x(1)
    to_sibling(2)
    for k in range(3):
        over_z(0, k)
    over_x(2)
    loads[3].wait()
    loads[4].wait()
    low_copy.wait()
    low = low_sent[...].astype(f32) + low_got[...].astype(f32)
    grad_normed = low[:, :rank]
    _, latent_unit, latent_factor = rms_normalize_pieces(latent[...], g_latent[...])
    grad_gain = jnp.sum(grad_normed * latent_unit, axis=0, keepdims=True)
    for i in range(rank // 128):
        vectors[pl.ds(experts + 2 + i, 1), :] = jnp.concatenate(
            [grad_gain[:, i * 128 : (i + 1) * 128]] * (features // 128), axis=1
        )
    grad_low[:, pl.ds(0, rank)] = normalize_back(
        grad_normed, latent_unit, latent_factor, g_latent[...]
    ).astype(bf16)
    grad_low[:, pl.ds(rank, 128)] = low[:, rank:].astype(bf16)
    low_t[...] = grad_low[...].T
    to_sibling(3)
    over_x(3)
    over_z(0, 3)

    def join(i, _):
        cols = pl.ds(pl.multiple_of(i * width, width), width)
        product = nn(grad_low[...], down_v[:, cols])
        chunk(i).wait()
        unit[:, cols] = product + (sent[i].astype(f32) + got[i].astype(f32))
        return 0

    lax.fori_loop(0, chunks, join, 0)
    _, attn_unit, attn_factor = rms_normalize_pieces(tokens[...].astype(f32), g_attn[...])
    vectors[pl.ds(experts, 1), :] = jnp.sum(unit[...] * attn_unit, axis=0, keepdims=True)
    to_sibling(4)
    grad_tokens[...] = grad_hidden[...] + normalize_back(
        unit[...], attn_unit, attn_factor, g_attn[...]
    )
    over_x(4)
    for p in range(1, 5):
        for k in range(4):
            over_z(p, k)
    for p in range(5):
        for i in range(8):
            if p > 0:
                beside(p, i).wait_send()
        for w in range(z_size):
            across(p, w).wait_send()

            @pl.when(z != w)
            def _():
                along(p, w, w, z).wait_send()


def backward_tuned(lengths, freqs, sums, values, gains, router_t, saved, weights):
    hidden, grad_out, tokens, probs = values
    w_query, down_t, kv_up, w_out = weights
    rows, features = tokens.shape
    rank, columns = kv_up.shape
    heads = columns // 256
    bf16, f32, dma = jnp.bfloat16, jnp.float32, pltpu.SemaphoreType.DMA
    vmem, anywhere = pl.BlockSpec(memory_space=pltpu.VMEM), pl.BlockSpec(memory_space=pl.ANY)
    smem = pl.BlockSpec(memory_space=pltpu.SMEM)
    shape = jax.ShapeDtypeStruct
    chunks = 8
    experts, ranks = lax.axis_size("dp"), lax.axis_size("tensor")
    devices = experts
    share_rows = features // devices
    blocks = [
        ((share_rows, w_out.shape[1]), bf16),
        ((share_rows, w_query.shape[1]), bf16),
        ((rank // devices, columns), bf16),
        ((down_t.shape[0] // ranks, share_rows), bf16),
        ((experts + 8, share_rows), f32),
    ]
    several = lambda *lead: [pltpu.VMEM(lead + b, kind) for b, kind in blocks]
    return pl.pallas_call(
        backward_kernel,
        out_shape=[shape((rows, features), f32)] + [shape(b, f32) for b, _ in blocks],
        in_specs=[smem, vmem, vmem, anywhere] + [vmem] * 15 + [anywhere] * 4,
        out_specs=[vmem] * 6,
        scratch_shapes=[
            pltpu.VMEM(w_query.shape, bf16),
            pltpu.VMEM((rank + 128, features), bf16),
            pltpu.VMEM(kv_up.shape, bf16),
            pltpu.VMEM((rows, features), f32),
            pltpu.VMEM((rows, features), bf16),
            pltpu.VMEM((rows, w_query.shape[1]), bf16),
            pltpu.VMEM((rows, columns), bf16),
            pltpu.VMEM((rows, rank + 128), bf16),
            pltpu.VMEM((experts + 8, features), f32),
            pltpu.VMEM((features, rows), bf16),
            pltpu.VMEM((features, rows), bf16),
            pltpu.VMEM((rank, rows), bf16),
            pltpu.VMEM((rank + 128, rows), bf16),
        ]
        + several(8)[1:]
        + several(4, 2)
        + several(4)
        + several(5)
        + [
            pltpu.VMEM((rows, heads * 128), bf16),
            pltpu.VMEM((rows, 128), f32),
            pltpu.VMEM((chunks, rows, features // chunks), bf16),
            pltpu.VMEM((chunks, rows, features // chunks), bf16),
            pltpu.VMEM((rows, rank + 128), bf16),
            pltpu.VMEM((rows, rank + 128), bf16),
            dma((6,)),
            dma((chunks,)),
            dma((chunks,)),
            dma((2,)),
            dma((5, 8)),
            dma((5, 4, 2)),
            dma((5, 4)),
            dma((5, 4)),
            dma((5, 4)),
            dma((5, 5)),
        ],
        compiler_params=pltpu.CompilerParams(
            collective_id=4, has_side_effects=True, vmem_limit_bytes=VMEM_LIMIT
        ),
        name="attention_backward",
    )(lengths, freqs, sums, hidden, grad_out, tokens, probs, *gains, router_t, *saved, *weights)


def add_window(dst, start, width, *srcs):
    rows = dst.shape[0]
    step = 32 if rows % 32 == 0 else 8
    cols = pl.ds(pl.multiple_of(start, 128), width)

    def body(i, _):
        here = pl.ds(pl.multiple_of(i * step, step), step)
        total = dst[here, cols].astype(jnp.float32)
        for src in srcs:
            total = total + src[here, :].astype(jnp.float32)
        dst[here, cols] = total.astype(dst.dtype)
        return 0

    lax.fori_loop(0, rows // step, body, 0)


def home_kernel(x_size, parts, share, whole, total, *refs):
    z_size, f32 = 4, jnp.float32
    rows = whole.shape[1] // parts
    piece = lambda p: pl.ds(p * rows, rows)
    own, c_buf, x_buf, z_buf, y_buf, f_buf = (refs[i * parts : (i + 1) * parts] for i in range(6))
    refs = refs[6 * parts :]
    l_sem, c_s, c_r, x_s, x_r, z_s, z_r, y_s, y_r, f_s, f_r = refs
    z, x, core = place_of(x_size)
    rank = lax.axis_index("tensor")
    at = functools.partial(index_of, x_size=x_size)
    half = z // 2
    inner = ((z + 3) // 4) * ((6 - z) // 4)
    order = [3 - 3 * half, 2 - half, 1 - z + 4 * half, z]
    width = [c.shape[3] for c in c_buf]
    window = [w - share for w in width]
    begin = pl.multiple_of(rank * share, 128)
    mine = lambda p: pl.multiple_of(rank * window[p], 128)
    theirs = lambda p: pl.multiple_of((1 - rank) * window[p], 128)

    slots = own[0].shape[0]
    blocks = [(w, v) for v in (1 - x, x) for w in order]
    load = lambda p, i: pltpu.make_async_copy(
        whole.at[at(blocks[i][0], blocks[i][1], core), piece(p)],
        own[p].at[i % slots],
        l_sem.at[p, i % slots],
    )
    beside = lambda p, w, v: remote(
        whole.at[at(w, v, 1 - core), piece(p)],
        c_buf[p].at[w, v],
        c_s.at[p, w, v],
        c_r.at[p, w, v],
        at(z, x, 1 - core),
    )
    twin = lambda p, w, v: pair_copy(
        c_buf[p].at[w, v, :, pl.ds(theirs(p), share)],
        y_buf[p].at[w, v],
        y_s.at[p, w, v],
        y_r.at[p, w, v],
    )
    across = lambda p, w: remote(
        c_buf[p].at[w, 1 - x, :, pl.ds(begin, window[p])],
        x_buf[p].at[w],
        x_s.at[p, w],
        x_r.at[p, w],
        at(z, 1 - x, core),
    )

    def along(p, w, slot, target):
        return remote(
            c_buf[p].at[w, x, :, pl.ds(begin, window[p])],
            z_buf[p].at[slot],
            z_s.at[p, w],
            z_r.at[p, slot],
            at(target, x, core),
        )

    final = lambda p: pair_copy(
        c_buf[p].at[z, x, :, pl.ds(begin, window[p])], f_buf[p], f_s.at[p], f_r.at[p]
    )

    for p in range(parts):
        for i in range(slots):
            load(p, i).start()
    greet(z, x, core, z_size, x_size, True)
    for p in range(parts):
        for w, v in blocks:
            beside(p, w, v).start()
    def on_chip(p, i):
        w, v = blocks[i]
        load(p, i).wait()
        beside(p, w, v).wait_recv()
        add_into(c_buf[p].at[w, v], own[p].at[i % slots])
        if i + slots < len(blocks):
            load(p, i + slots).start()
        twin(p, w, v).start()

    def go_across(p, i):
        w, v = blocks[i]
        twin(p, w, v).wait()
        add_window(c_buf[p].at[w, v], mine(p), share, y_buf[p].at[w, v])
        across(p, w).start()

    def go_along(p, k):
        w = order[k]
        twin(p, w, x).wait()
        add_window(c_buf[p].at[w, x], mine(p), share, y_buf[p].at[w, x])
        across(p, w).wait_recv()
        if k < 3:

            @pl.when(inner == 1)
            def _():
                along(p, w, w, z).wait_recv()
                add_window(c_buf[p].at[w, x], begin, window[p], x_buf[p].at[w], z_buf[p].at[w])

            @pl.when(inner == 0)
            def _():
                add_window(c_buf[p].at[w, x], begin, window[p], x_buf[p].at[w])

            @pl.when(w > z)
            def _():
                along(p, w, w, z + 1).start()

            @pl.when(w < z - 1)
            def _():
                along(p, w, w, z - 1).start()

            @pl.when(w == z - 1)
            def _():
                along(p, w, z_size, z - 1).start()

        else:
            add_window(c_buf[p].at[w, x], begin, window[p], x_buf[p].at[w])

            @pl.when(z > 0)
            def _():
                along(p, w, z, z).wait_recv()
                add_window(c_buf[p].at[w, x], begin, window[p], z_buf[p].at[z])

            @pl.when(z < z_size - 1)
            def _():
                along(p, w, z_size, z).wait_recv()
                add_window(c_buf[p].at[w, x], begin, window[p], z_buf[p].at[z_size])

            final(p).start()

    def begin_part(p, between):
        for i in range(5):
            on_chip(p, i)
            if i >= 1:
                go_across(p, i - 1)
            between(i)
        for i in range(5, 8):
            on_chip(p, i)

    begin_part(0, lambda i: None)
    for p in range(parts):
        if p + 1 < parts:

            def between(i):
                if i < 4:
                    go_along(p, i)

            begin_part(p + 1, between)
        else:
            for k in range(4):
                go_along(p, k)
    for p in range(parts):
        final(p).wait()
        common = window[p] - share
        near, far = c_buf[p].at[z, x], f_buf[p]
        total[piece(p), pl.ds(mine(p), share)] = near[:, pl.ds(mine(p), share)].astype(f32)
        total[piece(p), pl.ds(theirs(p), share)] = far[
            :, pl.ds(pl.multiple_of((1 - rank) * common, 128), share)
        ].astype(f32)
        total[piece(p), pl.ds(share, common)] = near[:, pl.ds(share, common)].astype(f32) + far[
            :, pl.ds(pl.multiple_of(rank * share, 128), common)
        ].astype(f32)
    for p in range(parts):
        for w in range(z_size):
            for v in range(x_size):
                beside(p, w, v).wait_send()
            across(p, w).wait_send()

            @pl.when(z != w)
            def _():
                along(p, w, w, z).wait_send()


def home_sums(array, collective_id, parts, share=512):
    bf16, f32, dma = jnp.bfloat16, jnp.float32, pltpu.SemaphoreType.DMA
    rows, width = array.shape[1:]
    block = lambda *lead, cut=0: [pltpu.VMEM(lead + (rows // parts, width - cut), bf16)] * parts
    return pl.pallas_call(
        functools.partial(home_kernel, 2, parts, share),
        out_shape=jax.ShapeDtypeStruct((rows, width), f32),
        in_specs=[pl.BlockSpec(memory_space=pl.ANY)],
        out_specs=pl.BlockSpec(memory_space=pltpu.VMEM),
        scratch_shapes=block(3)
        + block(4, 2)
        + block(4, cut=share)
        + block(5, cut=share)
        + block(4, 2, cut=width - share)
        + block(cut=share)
        + [dma((parts, 3))]
        + [dma((parts, 4, 2))] * 2
        + [dma((parts, 4))] * 3
        + [dma((parts, 5))]
        + [dma((parts, 4, 2))] * 2
        + [dma((parts,))] * 2,
        compiler_params=pltpu.CompilerParams(
            collective_id=collective_id, has_side_effects=True, vmem_limit_bytes=VMEM_LIMIT
        ),
        name="home_sums",
    )(array)


def sum_home(arrays, pair=False):
    sums = [lax.psum_scatter(a, "dp", scatter_dimension=0) for a in arrays]
    if pair:
        sums = [lax.psum(a.astype(jnp.float32), "tensor") for a in sums]
    return [a.astype(jnp.float32) for a in sums]


def product_sum(left, right, extras):
    product = contract_last(left, right).astype(jnp.bfloat16)
    return [lax.psum(a, "tensor").astype(jnp.float32) for a in [product] + extras]


def ffn_with_kernel(own_ffn, gates, everyone_grad, weights, shared, capacity, experts):
    part = shared[0].shape[1]
    hidden, features = weights[0].shape[1], own_ffn.shape[1]
    gate_t, up_t, down_t = (jnp.pad(w.T, ((0, 128 - part), (0, 0))) for w in shared)
    out_part, grad_part, rows, dy, he, dge, due, shared_grads, _ = ffn_tuned(
        own_ffn,
        gates,
        everyone_grad,
        *(w.T for w in weights),
        jnp.concatenate([gate_t, up_t], axis=0),
        down_t,
        capacity,
    )
    rows, dy = rows.reshape(-1, features), dy.reshape(-1, features)
    he, dge, due = (a.reshape(-1, a.shape[2]) for a in (he, dge, due))
    devices, rows_here = everyone_grad.shape[:2]
    return (
        out_part.reshape(devices * rows_here, -1),
        grad_part.reshape(devices, rows_here, -1),
        [rows, dy, he, dge, due],
        shared_grads.reshape(3, 128, features)[:, :part].reshape(3 * part, features),
    )


def ffn_plain(own_ffn, gates, everyone_grad, weights, shared, capacity, experts):
    own, devices = lax.axis_index("dp"), lax.axis_size("dp")
    rows_here, features = own_ffn.shape
    places = jnp.arange(rows_here, dtype=jnp.int32)
    expert_gate, expert_up, expert_down = weights
    part_gate, part_up, part_down = shared
    everyone_ffn = lax.all_gather(own_ffn, "dp", tiled=True)
    everyone_gates = lax.all_gather(gates, "dp")
    everyone_grad = everyone_grad.reshape(devices * rows_here, features)
    own_probs = lax.dynamic_slice_in_dim(everyone_gates, own, 1, 2).reshape(devices, rows_here)
    chooses = own_probs >= 0.0
    own_gates = jnp.where(chooses, own_probs, 0.0)
    upto = (places[:, None] <= places[None, :]).astype(jnp.bfloat16)
    slot = jnp.dot(chooses.astype(jnp.bfloat16), upto, preferred_element_type=jnp.float32) - 1.0
    slots = jnp.arange(capacity, dtype=jnp.float32)
    picked = chooses[:, None, :] & (slot[:, None, :] == slots[None, :, None])
    pick = picked.astype(jnp.bfloat16)
    slot_gates = jnp.sum(jnp.where(picked, own_gates[:, None, :], 0.0), axis=2).reshape(-1, 1)

    def pick_rows(values):
        blocks = values.reshape(devices, rows_here, features)
        return jnp.einsum(
            "jst,jtc->jsc", pick, blocks, preferred_element_type=jnp.float32
        ).astype(jnp.bfloat16).reshape(devices * capacity, features)

    def put_rows(values, hidden_parts, weights):
        blocks = values.astype(jnp.bfloat16).reshape(devices, capacity, features)
        left = jnp.concatenate(
            [pick.transpose(0, 2, 1)]
            + [h.reshape(devices, rows_here, h.shape[1]) for h in hidden_parts],
            axis=2,
        )
        right = jnp.concatenate(
            [blocks]
            + [
                jnp.broadcast_to(w.T[None], (devices, w.shape[1], features))
                for w in weights
            ],
            axis=1,
        )
        return (
            jnp.einsum("jtk,jkc->jtc", left, right, preferred_element_type=jnp.float32)
            .astype(jnp.bfloat16)
            .reshape(devices * rows_here, features)
        )

    expert_rows = pick_rows(everyone_ffn)
    grad_picked = pick_rows(everyone_grad)
    grad_rows = (slot_gates * grad_picked.astype(jnp.float32)).astype(jnp.bfloat16)

    gate_pre = jnp.dot(expert_rows, expert_gate, preferred_element_type=jnp.float32)
    up_pre = jnp.dot(expert_rows, expert_up, preferred_element_type=jnp.float32)
    gate_act, gate_slope = swish_parts(gate_pre)
    expert_hidden = (gate_act * up_pre).astype(jnp.bfloat16)
    expert_result = contract_last(expert_hidden, expert_down)
    slot_grads = jnp.sum(grad_picked.astype(jnp.float32) * expert_result, axis=1)
    grad_expert_down = contract_first(grad_rows, expert_hidden)[None]
    grad_expert_hidden = jnp.dot(grad_rows, expert_down, preferred_element_type=jnp.float32)
    grad_gate_pre = (grad_expert_hidden * up_pre * gate_slope).astype(jnp.bfloat16)
    grad_up_pre = (grad_expert_hidden * gate_act).astype(jnp.bfloat16)
    grad_expert_gate = contract_first(expert_rows, grad_gate_pre)[None]
    grad_expert_up = contract_first(expert_rows, grad_up_pre)[None]
    grad_rows_in = contract_last(grad_gate_pre, expert_gate) + contract_last(
        grad_up_pre, expert_up
    )

    shared_pre_gate = jnp.dot(everyone_ffn, part_gate, preferred_element_type=jnp.float32)
    shared_pre_up = jnp.dot(everyone_ffn, part_up, preferred_element_type=jnp.float32)
    shared_act, shared_slope = swish_parts(shared_pre_gate)
    shared_hidden = (shared_act * shared_pre_up).astype(jnp.bfloat16)
    grad_shared_hidden = jnp.dot(everyone_grad, part_down, preferred_element_type=jnp.float32)
    grad_shared_gate_pre = (grad_shared_hidden * shared_pre_up * shared_slope).astype(jnp.bfloat16)
    grad_shared_up_pre = (grad_shared_hidden * shared_act).astype(jnp.bfloat16)
    shared_grads = jnp.concatenate(
        [
            contract_first(grad_shared_gate_pre, everyone_ffn),
            contract_first(grad_shared_up_pre, everyone_ffn),
            contract_first(shared_hidden, everyone_grad),
        ],
        axis=0,
    ).astype(jnp.bfloat16)
    ffn_part = put_rows(slot_gates * expert_result, [shared_hidden], [part_down])
    pair_grads = jnp.sum(
        jnp.where(picked, slot_grads.reshape(devices, capacity, 1), 0.0), axis=1
    ).reshape(devices * rows_here, 1)
    pair_high = pair_grads.astype(jnp.bfloat16).astype(jnp.float32)
    column = jnp.arange(128, dtype=jnp.int32)[None, :]
    pair_columns = jnp.where(
        column == own,
        pair_high,
        jnp.where(column == own + experts, pair_grads - pair_high, 0.0),
    )
    grad_ffn_in = put_rows(
        grad_rows_in, [grad_shared_gate_pre, grad_shared_up_pre], [part_gate, part_up]
    )
    grad_part = jnp.concatenate([grad_ffn_in, pair_columns.astype(jnp.bfloat16)], axis=1)
    return (
        ffn_part.reshape(devices, rows_here, -1),
        grad_part.reshape(devices, rows_here, -1),
        grad_expert_gate,
        grad_expert_up,
        grad_expert_down,
        shared_grads,
    )


def shared_home(grads, part):
    devices = lax.axis_size("dp")
    share_rows = grads.shape[1] // devices
    grads = lax.all_to_all(
        grads.reshape(3 * part, devices, share_rows).transpose(1, 2, 0).astype(jnp.bfloat16),
        "dp",
        split_axis=0,
        concat_axis=0,
    ).astype(jnp.float32)
    return [
        grads[:, :, i * part : (i + 1) * part].transpose(1, 0, 2).reshape(share_rows, -1)
        for i in range(3)
    ]


def shards_tuned(
    tokens,
    lengths,
    routes,
    grad_out,
    g_attn,
    w_query,
    key_value_down_weight,
    latent_norm_gain,
    key_value_up_weight,
    w_out,
    g_ffn,
    router,
    shared_gate,
    shared_up,
    shared_down,
    expert_gate,
    expert_up,
    expert_down,
):
    rows_here, features = tokens.shape
    devices, ranks = lax.axis_size("dp"), lax.axis_size("tensor")
    own, rank = lax.axis_index("dp"), lax.axis_index("tensor")
    experts = router.shape[1]
    capacity = rows_here * TOPK * 4 // (3 * devices)
    half = (key_value_down_weight.shape[1] - LATENT_RANK) // 2
    freqs = (10000.0 ** (-np.arange(half) / half)).astype(np.float32)
    freqs = np.tile(freqs, 128 // half)[None, :]
    router_t = jnp.pad(router.T, ((0, 128 - experts), (0, 0)))
    gains = [g_attn[None, :], latent_norm_gain[None, :], g_ffn[None, :]]
    weights = [w_query, key_value_down_weight.T, key_value_up_weight, w_out]
    hidden, ffn_bf, dense_gates, probs, normed, *saved = forward_tuned(
        lengths, freqs, tokens, routes, *gains, router_t, *weights, grad_out
    )
    queries, kv, key_turned, latent_bf, latent, context, log_totals, everyone_grad = saved
    part = shared_gate.shape[1] // devices
    shared_parts = [
        lax.dynamic_slice_in_dim(w, own * part, part, 1)
        for w in (shared_gate, shared_up, shared_down)
    ]
    ffn_part, grad_ffn_part, expert_saved, shared_grads = ffn_with_kernel(
        ffn_bf,
        dense_gates,
        everyone_grad,
        [w[0] for w in (expert_gate, expert_up, expert_down)],
        shared_parts,
        capacity,
        experts,
    )
    shared_grads = shared_home(shared_grads, part)
    ffn_sum = lax.psum_scatter(ffn_part, "dp", scatter_dimension=0, tiled=True)
    sums = home_sums(grad_ffn_part, 3, 2)
    (
        grad_tokens,
        grad_w_out,
        grad_w_query,
        grad_w_kv_up,
        grad_w_kv_down,
        vectors,
    ) = backward_tuned(
        lengths,
        freqs,
        sums,
        [hidden, grad_out, tokens, probs],
        gains,
        router_t,
        [queries, kv, key_turned, latent, log_totals, normed, context, latent_bf],
        weights,
    )
    grad_tokens, ffn_sum, *expert_saved = lax.optimization_barrier(
        (grad_tokens, ffn_sum, *expert_saved)
    )
    ffn_twin = lax.ppermute(ffn_sum, "tensor", [(0, 1), (1, 0)])
    rows, dy, he, dge, due = expert_saved
    units = expert_gate.shape[2]
    expert_grads = [
        contract_first(rows, dge[:, :units])[None],
        contract_first(rows, due[:, :units])[None],
        contract_first(dy, he[:, :units])[None],
    ]
    output = (
        hidden + (ffn_sum.astype(jnp.float32) + ffn_twin.astype(jnp.float32))
    ).astype(jnp.bfloat16)
    share_rows = features // devices
    router_rows = share_rows // ranks
    grad_router = lax.dynamic_slice_in_dim(vectors[:experts], rank * router_rows, router_rows, 1).T
    latent_rows = LATENT_RANK // devices // ranks
    grad_g_kv = lax.dynamic_slice_in_dim(
        vectors[experts + 2 : experts + 2 + LATENT_RANK // 128].reshape(-1),
        (own * ranks + rank) * latent_rows,
        latent_rows,
        0,
    )
    return (
        output,
        grad_tokens,
        vectors[experts],
        grad_w_query,
        grad_w_kv_down.T,
        grad_g_kv,
        grad_w_kv_up,
        grad_w_out,
        vectors[experts + 1],
        grad_router,
        *shared_grads,
        *expert_grads,
    )


def shards(
    tokens,
    lengths,
    routes,
    grad_out,
    g_attn,
    w_query,
    key_value_down_weight,
    latent_norm_gain,
    key_value_up_weight,
    w_out,
    g_ffn,
    router,
    shared_gate,
    shared_up,
    shared_down,
    expert_gate,
    expert_up,
    expert_down,
):
    rows_here = tokens.shape[0]
    features = tokens.shape[1]
    heads_local = w_out.shape[1] // VALUE_HEAD_SIZE
    devices = lax.axis_size("dp")
    capacity = rows_here * TOPK * 4 // (3 * devices)
    experts = router.shape[1]
    highest = lax.Precision.HIGHEST
    softmax_scale = QK ** (-0.5)
    segment, token_position = doc_layout(lengths[0], rows_here)
    places = jnp.arange(rows_here, dtype=jnp.int32)
    allowed = (segment[:, None] == segment[None, :]) & (places[None, :] <= places[:, None])
    tokens_f = tokens.astype(jnp.float32)
    attn_normed, attn_unit, attn_factor = rms_normalize_pieces(tokens_f, g_attn)
    normed_bf = attn_normed.astype(jnp.bfloat16)
    query_full = jnp.dot(normed_bf, w_query, preferred_element_type=jnp.float32).reshape(
        rows_here, heads_local, QK
    )
    query_bf = jnp.concatenate(
        [
            query_full[..., :PLAIN_HEAD_SIZE],
            apply_rotation(query_full[..., PLAIN_HEAD_SIZE:], token_position),
        ],
        axis=-1,
    ).astype(jnp.bfloat16)
    latent_with_key = jnp.dot(normed_bf, key_value_down_weight, preferred_element_type=jnp.float32)
    key_turned_part = apply_rotation(latent_with_key[:, LATENT_RANK:], token_position).astype(
        jnp.bfloat16
    )
    latent_after_norm, latent_unit_scale, latent_norm_factor = rms_normalize_pieces(
        latent_with_key[:, :LATENT_RANK], latent_norm_gain
    )
    latent_bf = latent_after_norm.astype(jnp.bfloat16)
    key_value = (
        jnp.dot(latent_bf, key_value_up_weight, preferred_element_type=jnp.float32)
        .astype(jnp.bfloat16)
        .reshape(rows_here, heads_local, PLAIN_HEAD_SIZE + VALUE_HEAD_SIZE)
    )
    key_nope = key_value[..., :PLAIN_HEAD_SIZE]
    value = key_value[..., PLAIN_HEAD_SIZE:]

    def masked_scores():
        raw = jnp.einsum(
            "thd,shd->hts",
            query_bf[..., :PLAIN_HEAD_SIZE],
            key_nope,
            preferred_element_type=jnp.float32,
        )
        raw = raw + jnp.einsum(
            "thd,sd->hts",
            query_bf[..., PLAIN_HEAD_SIZE:],
            key_turned_part,
            preferred_element_type=jnp.float32,
        )
        return jnp.where(allowed[None], raw * softmax_scale, -jnp.inf)

    scores = masked_scores()
    top_score = jnp.max(scores, axis=-1, keepdims=True)
    expo = jnp.exp(scores - top_score)
    total = jnp.sum(expo, axis=-1, keepdims=True)
    log_total = top_score + jnp.log(total)
    attn_weights = (expo / total).astype(jnp.bfloat16)
    context = jnp.einsum("hts,shd->thd", attn_weights, value, preferred_element_type=jnp.float32)
    context = context.astype(jnp.bfloat16).reshape(rows_here, heads_local * VALUE_HEAD_SIZE)
    (attn,) = product_sum(context, w_out, [])
    hidden = tokens_f + attn
    ffn_normed, ffn_unit, ffn_factor = rms_normalize_pieces(hidden, g_ffn)
    ffn_bf = ffn_normed.astype(jnp.bfloat16)
    router_probs = jax.nn.softmax(jnp.dot(ffn_normed, router, precision=highest), axis=-1)
    own = lax.axis_index("dp")

    named = jnp.any(routes[:, :, None] == jnp.arange(128, dtype=jnp.int32)[None, None, :], axis=1)
    dense_gates = jnp.where(named, jnp.pad(router_probs, ((0, 0), (0, 128 - experts))), -1.0)
    everyone_grad = lax.all_gather(grad_out, "dp")
    part = shared_gate.shape[1] // devices
    shared_parts = [
        lax.dynamic_slice_in_dim(w, own * part, part, 1)
        for w in (shared_gate, shared_up, shared_down)
    ]
    (
        ffn_part,
        grad_ffn_part,
        grad_expert_gate,
        grad_expert_up,
        grad_expert_down,
        shared_grads,
    ) = ffn_plain(
        ffn_bf,
        dense_gates,
        everyone_grad,
        [w[0] for w in (expert_gate, expert_up, expert_down)],
        shared_parts,
        capacity,
        experts,
    )
    share_rows = features // devices
    grad_shared_gate, grad_shared_up, grad_shared_down = shared_home(shared_grads, part)

    grad_top = grad_out.astype(jnp.float32)
    ffn_total = lax.psum_scatter(
        ffn_part.reshape(devices * rows_here, features), "dp", scatter_dimension=0, tiled=True
    )
    ffn_total = lax.psum(ffn_total, "tensor").astype(jnp.float32)
    output = (hidden + ffn_total).astype(jnp.bfloat16)
    (grad_ffn_sum,) = sum_home([grad_ffn_part], True)
    dense_grad = (
        grad_ffn_sum[:, features : features + experts]
        + grad_ffn_sum[:, features + experts : features + 2 * experts]
    )
    grad_logits = router_probs * (
        dense_grad - jnp.sum(router_probs * dense_grad, axis=-1, keepdims=True)
    )
    grad_router_in = contract_last(grad_logits, router, highest)
    grad_router_part = contract_first(ffn_normed, grad_logits, highest)
    grad_ffn_total = grad_ffn_sum[:, :features] + grad_router_in
    grad_g_ffn = jnp.sum(grad_ffn_total * ffn_unit, axis=0)
    grad_hidden = grad_top + normalize_back(grad_ffn_total, ffn_unit, ffn_factor, g_ffn)
    grad_hidden_bf = grad_hidden.astype(jnp.bfloat16)
    grad_w_out = contract_first(grad_hidden_bf, context)
    grad_context = jnp.dot(grad_hidden_bf, w_out, preferred_element_type=jnp.float32).astype(
        jnp.bfloat16
    )
    grad_context = grad_context.reshape(rows_here, heads_local, VALUE_HEAD_SIZE)
    redone = jnp.exp(masked_scores() - log_total)
    redone_bf = redone.astype(jnp.bfloat16)
    grad_weights = jnp.einsum(
        "thd,shd->hts", grad_context, value, preferred_element_type=jnp.float32
    )
    grad_value = jnp.einsum(
        "hts,thd->shd", redone_bf, grad_context, preferred_element_type=jnp.float32
    )
    row_inner = jnp.sum(redone * grad_weights, axis=-1, keepdims=True)
    grad_raw = (redone * (grad_weights - row_inner) * softmax_scale).astype(jnp.bfloat16)
    grad_query_nope = jnp.einsum(
        "hts,shd->thd", grad_raw, key_nope, preferred_element_type=jnp.float32
    )
    grad_query_rot = jnp.einsum(
        "hts,sd->thd", grad_raw, key_turned_part, preferred_element_type=jnp.float32
    )
    grad_key_nope = jnp.einsum(
        "hts,thd->shd",
        grad_raw,
        query_bf[..., :PLAIN_HEAD_SIZE],
        preferred_element_type=jnp.float32,
    )
    grad_key_rot = jnp.einsum(
        "hts,thd->sd", grad_raw, query_bf[..., PLAIN_HEAD_SIZE:], preferred_element_type=jnp.float32
    )
    grad_query = jnp.concatenate(
        [grad_query_nope, apply_rotation(grad_query_rot, -token_position)], axis=-1
    )
    grad_query = grad_query.reshape(rows_here, heads_local * QK).astype(jnp.bfloat16)
    grad_w_query = contract_first(normed_bf, grad_query)
    grad_key_value = (
        jnp.concatenate([grad_key_nope, grad_value], axis=-1)
        .reshape(rows_here, heads_local * (PLAIN_HEAD_SIZE + VALUE_HEAD_SIZE))
        .astype(jnp.bfloat16)
    )
    grad_w_kv_up = contract_first(latent_bf, grad_key_value)
    grad_latent_normed = contract_last(grad_key_value, key_value_up_weight)
    grad_latent_part = jnp.concatenate(
        [grad_latent_normed, apply_rotation(grad_key_rot, -token_position)], axis=1
    ).astype(jnp.bfloat16)
    grad_in_summed, grad_latent_sum = product_sum(grad_query, w_query, [grad_latent_part])
    grad_latent_normed = grad_latent_sum[:, :LATENT_RANK]
    grad_g_kv = jnp.sum(grad_latent_normed * latent_unit_scale, axis=0)
    grad_latent = normalize_back(
        grad_latent_normed, latent_unit_scale, latent_norm_factor, latent_norm_gain
    )
    grad_down = jnp.concatenate([grad_latent, grad_latent_sum[:, LATENT_RANK:]], axis=1)
    grad_down_bf = grad_down.astype(jnp.bfloat16)
    share = grad_down.shape[1] // lax.axis_size("tensor")
    grad_columns = lax.dynamic_slice_in_dim(
        grad_down_bf, lax.axis_index("tensor") * share, share, 1
    )
    grad_w_kv_down = contract_first(normed_bf, grad_columns)
    grad_attn_in = grad_in_summed + contract_last(grad_down_bf, key_value_down_weight)
    grad_g_attn = jnp.sum(grad_attn_in * attn_unit, axis=0)
    grad_tokens = grad_hidden + normalize_back(grad_attn_in, attn_unit, attn_factor, g_attn)
    vectors = jnp.concatenate(
        [
            grad_router_part,
            grad_g_attn[:, None],
            grad_g_ffn[:, None],
            jnp.pad(
                grad_g_kv.reshape(devices, -1), ((0, 0), (0, share_rows - LATENT_RANK // devices))
            ).reshape(-1, 1),
            jnp.zeros((features, 128 - experts - 3), jnp.float32),
        ],
        axis=1,
    )
    blocks = [
        a.astype(jnp.bfloat16).reshape(devices, a.shape[0] // devices, a.shape[1])
        for a in (grad_w_query, grad_w_out, grad_w_kv_up, grad_w_kv_down)
    ]
    grad_w_query, grad_w_out, grad_w_kv_up, grad_w_kv_down, vectors = sum_home(
        blocks + [vectors.reshape(devices, share_rows, 128)]
    )
    rank, ranks = lax.axis_index("tensor"), lax.axis_size("tensor")
    router_rows = share_rows // ranks
    grad_router = lax.dynamic_slice_in_dim(vectors[:, :experts], rank * router_rows, router_rows, 0)
    latent_rows = LATENT_RANK // devices // ranks
    grad_g_kv = lax.dynamic_slice_in_dim(
        vectors[:, experts + 2], rank * latent_rows, latent_rows, 0
    )
    return (
        output,
        grad_tokens,
        vectors[:, experts],
        grad_w_query,
        grad_w_kv_down,
        grad_g_kv,
        grad_w_kv_up,
        grad_w_out,
        vectors[:, experts + 1],
        grad_router,
        grad_shared_gate,
        grad_shared_up,
        grad_shared_down,
        grad_expert_gate,
        grad_expert_up,
        grad_expert_down,
    )


def solution(mesh):
    in_specs = (
        P("dp", None),
        P("dp", None),
        P("dp", None),
        P("dp", None),
        P(),
        P(None, "tensor"),
        P(),
        P(),
        P(None, "tensor"),
        P(None, "tensor"),
        P(),
        P(),
        P(None, "tensor"),
        P(None, "tensor"),
        P(None, "tensor"),
        P("dp", None, "tensor"),
        P("dp", None, "tensor"),
        P("dp", None, "tensor"),
    )
    out_specs = (
        P("dp", None),
        P("dp", None),
        P("dp"),
        P("dp", "tensor"),
        P("dp", "tensor"),
        P(("dp", "tensor")),
        P("dp", "tensor"),
        P("dp", "tensor"),
        P("dp"),
        P(("dp", "tensor"), None),
        P("dp", "tensor"),
        P("dp", "tensor"),
        P("dp", "tensor"),
        P("dp", None, "tensor"),
        P("dp", None, "tensor"),
        P("dp", None, "tensor"),
    )
    tuned = mesh.shape["dp"] == 16 and mesh.shape["tensor"] == 2
    return jax.shard_map(
        shards_tuned if tuned else shards, mesh=mesh, in_specs=in_specs, out_specs=out_specs, check_vma=False)
```

```python
import functools

import jax
import jax.numpy as jnp
import numpy as np
from jax import lax
from jax.experimental import pallas as pl
from jax.experimental.pallas import tpu as pltpu
from jax.sharding import PartitionSpec as P

PLAIN_HEAD_SIZE = 128
VALUE_HEAD_SIZE = 128
QK = 192
LATENT_RANK = 512
TOPK = 6


epsilon = 1e-06


def rms_normalize_pieces(values, gain):
    factor = lax.rsqrt(jnp.mean(values * values, axis=-1, keepdims=True) + epsilon)
    unit = values * factor
    return (unit * gain, unit, factor)


def normalize_back(grad, unit, factor, gain):
    inner = grad * gain
    return factor * (inner - unit * jnp.mean(inner * unit, axis=-1, keepdims=True))


def apply_rotation(values, token_position):
    half = values.shape[-1] // 2
    freqs = 10000.0 ** (-jnp.arange(half, dtype=jnp.float32) / half)
    angles = token_position.astype(jnp.float32)[:, None] * freqs[None, :]
    shape = (angles.shape[0],) + (1,) * (values.ndim - 2) + (half,)
    cosine = jnp.cos(angles).reshape(shape)
    sine = jnp.sin(angles).reshape(shape)
    first = values[..., :half]
    second = values[..., half:]
    return jnp.concatenate(
        [first * cosine - second * sine, second * cosine + first * sine], axis=-1
    )


def doc_layout(lengths_row, rows_here):
    ends = jnp.cumsum(lengths_row)
    starts = ends - lengths_row
    places = jnp.arange(rows_here, dtype=jnp.int32)
    segment = jnp.sum((places[:, None] >= ends[None, :]).astype(jnp.int32), axis=1)
    member = segment[:, None] == jnp.arange(lengths_row.shape[0], dtype=jnp.int32)[None, :]
    begins = jnp.sum(jnp.where(member, starts[None, :], 0), axis=1)
    return (segment, places - begins)


def contract_last(left, right, precision=None):
    return lax.dot_general(
        left,
        right,
        (((1,), (1,)), ((), ())),
        precision=precision,
        preferred_element_type=jnp.float32,
    )


def contract_first(left, right, precision=None):
    return lax.dot_general(
        left,
        right,
        (((0,), (0,)), ((), ())),
        precision=precision,
        preferred_element_type=jnp.float32,
    )


def swish_parts(gate_pre):
    sigma = jax.nn.sigmoid(gate_pre)
    return (gate_pre * sigma, sigma * (1.0 + gate_pre * (1.0 - sigma)))


VMEM_LIMIT = 60 * 1024 * 1024


def place_of(x_size):
    me = lax.axis_index("dp")
    core = me % 2
    x = (me // 2) % x_size
    z = me // (2 * x_size)
    return z, x, core


def index_of(z, x, core, x_size):
    return (z * x_size + x) * 2 + core


def remote(src, dst, send_sem, recv_sem, target):
    return pltpu.make_async_remote_copy(
        src_ref=src,
        dst_ref=dst,
        send_sem=send_sem,
        recv_sem=recv_sem,
        device_id={"dp": target},
        device_id_type=pl.DeviceIdType.MESH,
    )


def greet(z, x, core, z_size, x_size, pair=False):
    barrier = pltpu.get_barrier_semaphore()

    def tell(target):
        pl.semaphore_signal(
            barrier, inc=1, device_id={"dp": target}, device_id_type=pl.DeviceIdType.MESH
        )

    tell(index_of(z, x, 1 - core, x_size))
    tell(index_of(z, 1 - x, core, x_size))

    @pl.when(z > 0)
    def _():
        tell(index_of(z - 1, x, core, x_size))

    @pl.when(z < z_size - 1)
    def _():
        tell(index_of(z + 1, x, core, x_size))

    inner = (z + z_size - 1) // z_size - z // (z_size - 1)
    if pair:
        pl.semaphore_signal(
            barrier,
            inc=1,
            device_id={"tensor": 1 - lax.axis_index("tensor")},
            device_id_type=pl.DeviceIdType.MESH,
        )
    pl.semaphore_wait(barrier, 3 + inner + (1 if pair else 0))


def near_first(z):
    half = z // 2
    return [z, (1 - z) * (1 - 2 * half), 2 * (1 - half) + half * (7 - 2 * z), 3 - 3 * half]


def add_into(dst, *srcs):
    rows = dst.shape[0]
    step = 32 if rows % 32 == 0 else 8

    def body(i, _):
        here = pl.ds(pl.multiple_of(i * step, step), step)
        total = dst[here, :].astype(jnp.float32)
        for src in srcs:
            total = total + src[here, :].astype(jnp.float32)
        dst[here, :] = total.astype(dst.dtype)
        return 0

    lax.fori_loop(0, rows // step, body, 0)


def nn(left, right):
    return lax.dot_general(
        left, right, (((1,), (0,)), ((), ())), preferred_element_type=jnp.float32
    )


def is_at(j, where):
    low = (3 - j) // 3
    high = j // 3
    return (low, (4 - j) // 3 - low, (j + 1) // 3 - high, high)[where]


def ffn_kernel(
    x_size,
    own_ffn,
    own_gates,
    grad_half,
    gate_t,
    up_t,
    down_t,
    shared_in,
    shared_out,
    out_part,
    dx_part,
    rows_all,
    dy_all,
    he_all,
    dge_all,
    due_all,
    shared_grads,
    grad_all,
    blk,
    gts,
    gate_v,
    up_v,
    down_v,
    s_in,
    s_out,
    g_buf,
    rows_b,
    grow_b,
    dy_b,
    he_b,
    dge_b,
    due_b,
    out_r,
    dx_r,
    out_l,
    dx_l,
    out_st,
    dx_st,
    acc,
    gate_col,
    dgate_acc,
    left_ffn,
    left_grad,
    own_sem,
    up_s,
    up_r,
    dn_s,
    dn_r,
    x_s,
    x_r,
    c_s,
    c_r,
    w_sem,
    g_sem,
    st_sem,
    h_s,
    h_r,
    y_s,
    y_r,
    hc_s,
    hc_r,
):
    z_size, bf16, f32 = 4, jnp.bfloat16, jnp.float32
    hidden = gate_t.shape[0]
    rows_here, features = own_ffn.shape
    slots = rows_b.shape[0] // 2
    wide = 512
    z, x, core = place_of(x_size)
    own = lax.axis_index("dp")
    at = functools.partial(index_of, x_size=x_size)
    ins, outs = (own_ffn, own_gates), (blk, gts)
    order = near_first(z)

    def place(j):
        return sum(is_at(j, i) * order[i] for i in range(4))

    weights = [
        pltpu.make_async_copy(gate_t, gate_v.at[pl.ds(0, hidden)], w_sem.at[0]),
        pltpu.make_async_copy(up_t, up_v.at[pl.ds(0, hidden)], w_sem.at[1]),
        pltpu.make_async_copy(down_t, down_v.at[pl.ds(0, hidden)], w_sem.at[2]),
        pltpu.make_async_copy(shared_in, s_in, w_sem.at[3]),
        pltpu.make_async_copy(shared_out, s_out, w_sem.at[4]),
    ]
    keep = [
        pltpu.make_async_copy(ins[a], outs[a].at[at(z, x, core)], own_sem.at[a]) for a in range(2)
    ]

    def grad_copy(k):
        w, v = place(k // 2), x + (k % 2) * (1 - 2 * x)
        return pltpu.make_async_copy(
            grad_all.at[pl.ds(2 * (w * x_size + v), 2)], g_buf.at[k % 2], g_sem.at[k % 2]
        )

    for copy in keep + weights:
        copy.start()
    grad_copy(0).start()
    greet(z, x, core, z_size, x_size, True)

    def up(a, d):
        block = outs[a].at[at(z - d, x, core)]
        src = ins[a] if d == 0 else block
        return remote(src, block, up_s.at[a, d], up_r.at[a, d], at(z + 1, x, core))

    def down(a, d):
        block = outs[a].at[at(z + d, x, core)]
        src = ins[a] if d == 0 else block
        return remote(src, block, dn_s.at[a, d], dn_r.at[a, d], at(z - 1, x, core))

    def across(a, w, first=False):
        block = outs[a].at[at(w, x, core)]
        src = ins[a] if first else block
        return remote(src, block, x_s.at[a, w], x_r.at[a, w], at(z, 1 - x, core))

    def beside(a, w, v, first=False):
        block = outs[a].at[at(w, v, core)]
        src = ins[a] if first else block
        return remote(src, block, c_s.at[a, w, v], c_r.at[a, w, v], at(z, x, 1 - core))

    rank = lax.axis_index("tensor")
    edge = 1 - ((z + 3) // 4) * ((6 - z) // 4)
    part_rows = rows_here // 2
    whose = (order[2], order[2], order[3], order[3], order[3], z, (z + 2) % 4, order[3])

    def part(store, w, v, which):
        rows = pl.ds(pl.multiple_of(which * part_rows, part_rows), part_rows)
        return store.at[at(w, v, core), rows]

    store_of = lambda j: grad_all if j in (0, 2, 3) else blk

    def link(j, w=None, target=None):
        block = part(store_of(j), whose[j] if w is None else w, x, rank)
        src = block
        if j == 5:
            src = own_ffn.at[pl.ds(pl.multiple_of(rank * part_rows, part_rows), part_rows)]
        way = 0
        if j in (2, 6, 7):
            target = z if target is None else target
            way = (target - z + 1) // 2
            target = at(target, x, core)
        else:
            target = at(z, 1 - x, core)
        return remote(src, block, h_s.at[j, way], h_r.at[j], target)

    landed = lambda j: x if j in (2, 6, 7) else 1 - x

    def swap(j):
        block = part(store_of(j), whose[j], landed(j), rank)
        return pair_copy(block, block, y_s.at[j], y_r.at[j])

    def half_beside(j, i):
        block = part(store_of(j), whose[j], landed(j), rank + i * (1 - 2 * rank))
        return remote(block, block, hc_s.at[j, i], hc_r.at[j, i], at(z, x, 1 - core))

    def link_done(j):
        link(j).wait_recv()
        swap(j).start()
        half_beside(j, 0).start()

    def swap_done(j):
        swap(j).wait_recv()
        half_beside(j, 1).start()

    def ready(j):
        half_beside(j, 0).wait_recv()
        half_beside(j, 1).wait_recv()

    def at_ends(do):
        pl.when(edge == 1)(do)

    def inside(do):
        pl.when(edge == 0)(do)

    for a in (1, 0):
        beside(a, z, x, True).start()
        if a == 1:
            across(a, z, True).start()
        else:
            link(5).start()
        pl.when(z < z_size - 1)(lambda: up(a, 0).start())
        pl.when(z > 0)(lambda: down(a, 0).start())
    link(0).start()

    def pass_on(d):
        for a in (1, 0) if d == 1 else (1,):

            @pl.when(z >= d)
            def _():
                up(a, d - 1).wait_recv()
                if a == 1:
                    pl.when(z < z_size - 1)(lambda: up(a, d).start())
                else:
                    inside(lambda: link(6, z - 1, z + 1).start())
                beside(a, z - d, x).start()

            @pl.when(z + d < z_size)
            def _():
                down(a, d - 1).wait_recv()
                if a == 1:
                    pl.when(z > 0)(lambda: down(a, d).start())
                else:
                    inside(lambda: link(6, z + 1, z - 1).start())
                beside(a, z + d, x).start()

    def from_across(w, arrays=(1, 0)):
        for a in arrays:
            across(a, w).wait_recv()
            beside(a, w, 1 - x).start()

    def early(k):
        @pl.when(k == 1)
        def _():
            pass_on(1)
            for a in (1, 0):
                across(a, order[1]).start()
            swap_done(5)
            link_done(0)
            from_across(z, (1,))
            ready(5)

        @pl.when(k == 2)
        def _():
            link_done(6)
            link(1).start()

            @inside
            def _():
                link(7, None, 3 * (z - 1)).start()
                link(2, None, 3 * (z - 1)).start()
                link(4).start()
                link(3).start()

            pass_on(2)
            across(1, order[2]).start()
            swap_done(0)

        @pl.when(k == 3)
        def _():
            from_across(order[1])
            swap_done(6)

            @at_ends
            def _():
                link_done(7)
                link(4).start()

        @pl.when(k == 4)
        def _():
            ready(0)
            link_done(1)

            @at_ends
            def _():
                ready(6)
                link_done(2)
                link(3).start()

            pass_on(3)
            across(1, order[3]).start()
            from_across(order[2], (1,))

        @pl.when(k == 5)
        def _():
            grad_copy(5).start()
            at_ends(lambda: swap_done(7))
            swap_done(1)
            ready(1)

        @pl.when(k == 6)
        def _():
            from_across(order[3], (1,))
            at_ends(lambda: ready(7))
            inside(lambda: ready(6))

        @pl.when(k == 7)
        def _():
            swap_done(3)
            ready(3)
            grad_copy(7).start()
            ready(4)

    def midway(k):
        pl.when(k == 0)(lambda: link_done(5))
        pl.when(k == 4)(lambda: link_done(4))

        @pl.when(k == 5)
        def _():
            @at_ends
            def _():
                swap_done(2)
                ready(2)

            grad_copy(6).start()
            link_done(3)

        pl.when(k == 6)(lambda: swap_done(4))

    gate_v[pl.ds(hidden, gate_v.shape[0] - hidden), :] = jnp.zeros(
        (gate_v.shape[0] - hidden, features), bf16
    )
    up_v[pl.ds(hidden, up_v.shape[0] - hidden), :] = jnp.zeros(
        (up_v.shape[0] - hidden, features), bf16
    )
    down_v[pl.ds(hidden, down_v.shape[0] - hidden), :] = jnp.zeros(
        (down_v.shape[0] - hidden, features), bf16
    )
    acc[...] = jnp.zeros(acc.shape, f32)
    for copy in weights:
        copy.wait()
    for a in range(2):
        out_r[a, pl.ds(slots, 128), :] = s_out[...]
        dx_r[a, pl.ds(slots, 256), :] = s_in[...]
    for copy in keep:
        copy.wait()
    expert = lax.broadcasted_iota(jnp.int32, (rows_here, own_gates.shape[0]), 1)
    lane = lax.broadcasted_iota(jnp.int32, (rows_here, 128), 1)
    earlier = lax.broadcasted_iota(jnp.int32, (rows_here, rows_here), 1)
    later = lax.broadcasted_iota(jnp.int32, (rows_here, rows_here), 0)
    upto = (earlier <= later).astype(bf16)
    slot_lane = lax.broadcasted_iota(jnp.int32, (rows_here, slots), 1).astype(f32)

    def staged(pair, which):
        pairs = [
            (rows_b, rows_all),
            (dy_b, dy_all),
            (he_b, he_all),
            (dge_b, dge_all),
            (due_b, due_all),
            (out_st, out_part),
            (dx_st, dx_part),
        ]
        return [
            pltpu.make_async_copy(pairs[i][0], pairs[i][1].at[pair], st_sem.at[i]) for i in which
        ]

    def start_staged(pair, which):
        for copy in staged(pair, which):
            copy.start()

    def wait_staged(k, which):
        @pl.when(k > 0)
        def _():
            for copy in staged(0, which):
                copy.wait()

    def body(k, _):
        w, v = place(k // 2), x + (k % 2) * (1 - 2 * x)
        pair = w * x_size + v
        block = 2 * pair
        here = k % 2
        early(k)
        grad_copy(k).wait()
        pl.when(k < 4)(lambda: grad_copy(k + 1).start())
        beside(1, w, v).wait_recv()
        whole = (k == 0) | (k == 2) | (k == 3) | ((k == 4) & (edge == 0))
        pl.when(whole)(lambda: beside(0, w, v).wait_recv())

        for a in range(2):
            gates = gts[block + a].T
            count = nn(upto, (gates >= 0.0).astype(bf16))
            gate = jnp.sum(jnp.where(expert == own, gates, 0.0), axis=1, keepdims=True)
            slot = jnp.sum(jnp.where(expert == own, count, 0.0), axis=1, keepdims=True) - 1.0
            pick = ((slot_lane == slot) & (gate >= 0.0)).astype(f32).astype(bf16)
            out_l[a, :, pl.ds(0, slots)] = pick
            dx_l[a, :, pl.ds(0, slots)] = pick
            high = gate.astype(bf16).astype(f32)
            middle = (gate - high).astype(bf16).astype(f32)
            low = gate - high - middle
            parts = jnp.where(
                lane == 0, high, jnp.where(lane == 1, middle, jnp.where(lane == 2, low, 0.0))
            ).astype(bf16)
            pick_t = pick.T
            left_ffn[a, pl.ds(0, slots), :] = pick_t
            left_grad[a, pl.ds(0, slots), :] = pick_t
            picked = jnp.sum(nn(pick_t, parts), axis=1, keepdims=True)
            gate_col[pl.ds(a * slots, slots), :] = jnp.broadcast_to(picked, (slots, 128))

        both = pl.ds(block, 2)
        pre = contract_last(blk[both].reshape(2 * rows_here, features), s_in[...])
        grad_hidden = contract_last(g_buf[here].reshape(2 * rows_here, features), s_out[...])
        act, slope = swish_parts(pre[:, :128])
        up_pre = pre[:, 128:]
        shared_units = (
            (act * up_pre).astype(bf16),
            (grad_hidden * up_pre * slope).astype(bf16),
            (grad_hidden * act).astype(bf16),
        )
        for a in range(2):
            mine = slice(a * rows_here, (a + 1) * rows_here)
            out_l[a, :, pl.ds(slots, 128)] = shared_units[0][mine]
            dx_l[a, :, pl.ds(slots, 128)] = shared_units[1][mine]
            dx_l[a, :, pl.ds(slots + 128, 128)] = shared_units[2][mine]
            left_ffn[a, pl.ds(slots, 128), :] = shared_units[1][mine].T
            left_ffn[a, pl.ds(slots + 128, 128), :] = shared_units[2][mine].T
            left_grad[a, pl.ds(slots, 128), :] = shared_units[0][mine].T

        def pick_rows(n, _):
            cols = pl.ds(pl.multiple_of(n * wide, wide), wide)
            for a in range(2):
                mine = pl.ds(a * slots, slots)
                product = nn(left_ffn[a], blk[block + a, :, cols])
                rows_b[mine, cols] = product[:slots].astype(bf16)
                acc[pl.ds(0, 256), cols] += product[slots:]
                product = nn(left_grad[a], g_buf[here, a, :, cols])
                grows = product[:slots]
                acc[pl.ds(256, 128), cols] += product[slots:]
                grow_b[mine, cols] = grows.astype(bf16)
                dy_b[mine, cols] = (gate_col[mine, pl.ds(0, 1)] * grows).astype(bf16)
            return 0

        wait_staged(k, (0, 1))
        lax.fori_loop(0, features // wide, pick_rows, 0)
        start_staged(pair, (0, 1))

        def hidden_units(n, _):
            units = pl.ds(pl.multiple_of(n * 256, 256), 256)
            gate_pre = contract_last(rows_b[...], gate_v[units, :])
            up_pre = contract_last(rows_b[...], up_v[units, :])
            grad_hidden = contract_last(dy_b[...], down_v[units, :])
            act, slope = swish_parts(gate_pre)
            he_b[:, units] = (act * up_pre).astype(bf16)
            dge_b[:, units] = (grad_hidden * up_pre * slope).astype(bf16)
            due_b[:, units] = (grad_hidden * act).astype(bf16)
            return 0

        wait_staged(k, (2, 3, 4))
        lax.fori_loop(0, gate_v.shape[0] // 256, hidden_units, 0)
        start_staged(pair, (2, 3, 4))
        midway(k)
        dgate_acc[...] = jnp.zeros(dgate_acc.shape, f32)

        def back(n, _):
            cols = pl.ds(pl.multiple_of(n * wide, wide), wide)
            result = nn(he_b[...], down_v[:, cols])
            product = grow_b[:, cols].astype(f32) * result
            for i in range(wide // 128):
                dgate_acc[...] += product[:, i * 128 : (i + 1) * 128]
            result = (gate_col[:, pl.ds(0, 1)] * result).astype(bf16)
            grad_in = (nn(dge_b[...], gate_v[:, cols]) + nn(due_b[...], up_v[:, cols])).astype(bf16)
            for a in range(2):
                mine = slice(a * slots, (a + 1) * slots)
                out_r[a, pl.ds(0, slots), cols] = result[mine]
                dx_r[a, pl.ds(0, slots), cols] = grad_in[mine]
                out_st[a, :, cols] = nn(out_l[a], out_r[a, :, cols]).astype(bf16)
                dx_st[a, :, cols] = nn(dx_l[a], dx_r[a, :, cols]).astype(bf16)
            return 0

        wait_staged(k, (5, 6))
        lax.fori_loop(0, features // wide, back, 0)
        dgate = jnp.sum(dgate_acc[...], axis=1, keepdims=True)
        high = dgate.astype(bf16).astype(f32)
        spread = lax.broadcasted_iota(jnp.int32, (2 * slots, 128), 1)
        spread = jnp.where(
            spread == own, high, jnp.where(spread == own + 16, dgate - high, 0.0)
        ).astype(bf16)
        for a in range(2):
            dx_st[a, :, pl.ds(features, 128)] = nn(
                out_l[a, :, pl.ds(0, slots)], spread[a * slots : (a + 1) * slots]
            ).astype(bf16)
        start_staged(pair, (5, 6))
        return 0

    lax.fori_loop(0, 8, body, 0)
    wait_staged(1, range(7))
    shared_grads[...] = acc[...].astype(bf16)
    for i in range(z_size):
        beside(1, order[i], x).wait_send()
        beside(1, order[i], 1 - x).wait_send()
        across(1, order[i]).wait_send()
    for i in range(2):
        beside(0, order[i], x).wait_send()
    inside(lambda: beside(0, order[2], x).wait_send())
    beside(0, order[1], 1 - x).wait_send()
    across(0, order[1]).wait_send()
    for d in range(z_size):
        for a in range(2) if d == 0 else (1,):
            pl.when((z >= d) & (z < z_size - 1))(lambda: up(a, d).wait_send())
            pl.when((z + d < z_size) & (z > 0))(lambda: down(a, d).wait_send())

    @inside
    def _():
        link(2, None, 3 * (z - 1)).wait_send()
        link(7, None, 3 * (z - 1)).wait_send()
        link(6, z - 1, z + 1).wait_send()
        link(6, z + 1, z - 1).wait_send()

    for j in range(8):

        def sent_on(j=j):
            swap(j).wait_send()
            half_beside(j, 0).wait_send()
            half_beside(j, 1).wait_send()

        if j in (2, 7):
            at_ends(sent_on)
        else:
            sent_on()
        if j not in (2, 6, 7):
            link(j).wait_send()


def ffn_tuned(own_ffn, own_gates, grad_all, gate_t, up_t, down_t, shared_in, shared_out, slots):
    rows, features = own_ffn.shape
    hidden = gate_t.shape[0]
    padded = -(-hidden // 256) * 256
    bf16, f32, dma = jnp.bfloat16, jnp.float32, pltpu.SemaphoreType.DMA
    anywhere = pl.BlockSpec(memory_space=pl.ANY)
    shape = jax.ShapeDtypeStruct
    return pl.pallas_call(
        functools.partial(ffn_kernel, 2),
        out_shape=[
            shape((8, 2, rows, features), bf16),
            shape((8, 2, rows, features + 128), bf16),
            shape((8, 2 * slots, features), bf16),
            shape((8, 2 * slots, features), bf16),
            shape((8, 2 * slots, padded), bf16),
            shape((8, 2 * slots, padded), bf16),
            shape((8, 2 * slots, padded), bf16),
            shape((384, features), bf16),
            shape((16, rows, features), bf16),
        ],
        in_specs=[anywhere] * 8,
        out_specs=[anywhere] * 7 + [pl.BlockSpec(memory_space=pltpu.VMEM), anywhere],
        input_output_aliases={2: 8},
        scratch_shapes=[
            pltpu.VMEM((16, rows, features), bf16),
            pltpu.VMEM((16,) + own_gates.shape, f32),
            pltpu.VMEM((padded, features), bf16),
            pltpu.VMEM((padded, features), bf16),
            pltpu.VMEM((padded, features), bf16),
            pltpu.VMEM((256, features), bf16),
            pltpu.VMEM((128, features), bf16),
            pltpu.VMEM((2, 2, rows, features), bf16),
            pltpu.VMEM((2 * slots, features), bf16),
            pltpu.VMEM((2 * slots, features), bf16),
            pltpu.VMEM((2 * slots, features), bf16),
            pltpu.VMEM((2 * slots, padded), bf16),
            pltpu.VMEM((2 * slots, padded), bf16),
            pltpu.VMEM((2 * slots, padded), bf16),
            pltpu.VMEM((2, slots + 128, features), bf16),
            pltpu.VMEM((2, slots + 256, features), bf16),
            pltpu.VMEM((2, rows, slots + 128), bf16),
            pltpu.VMEM((2, rows, slots + 256), bf16),
            pltpu.VMEM((2, rows, features), bf16),
            pltpu.VMEM((2, rows, features + 128), bf16),
            pltpu.VMEM((384, features), f32),
            pltpu.VMEM((2 * slots, 128), f32),
            pltpu.VMEM((2 * slots, 128), f32),
            pltpu.VMEM((2, slots + 256, rows), bf16),
            pltpu.VMEM((2, slots + 128, rows), bf16),
            dma((2,)),
        ]
        + [dma((2, 4))] * 6
        + [dma((2, 4, 2))] * 2
        + [dma((5,)), dma((2,)), dma((7,))]
        + [dma((8, 2))]
        + [dma((8,))] * 3
        + [dma((8, 2))] * 2,
        compiler_params=pltpu.CompilerParams(
            collective_id=1, has_side_effects=True, vmem_limit_bytes=VMEM_LIMIT
        ),
        name="ffn",
    )(
        own_ffn,
        own_gates,
        grad_all.reshape(16, rows, features),
        gate_t,
        up_t,
        down_t,
        shared_in,
        shared_out,
    )


def first_half(shape):
    return lax.broadcasted_iota(jnp.int32, shape, 1) % 64 < 32


def turn(values, cosine, sine):
    partner = jnp.where(
        first_half(values.shape), pltpu.roll(values, 96, 1), pltpu.roll(values, 32, 1)
    )
    return values * cosine + partner * sine


def layout_of(lengths, rows, width):
    row = lax.broadcasted_iota(jnp.int32, (rows, width), 0)
    across = lax.broadcasted_iota(jnp.int32, (rows, rows), 1)
    down = lax.broadcasted_iota(jnp.int32, (rows, rows), 0)
    place, met, end = row, across <= down, 0
    for i in range(lengths.shape[1]):
        end = end + lengths[0, i]
        place = place - jnp.where(row >= end, lengths[0, i], 0)
        met = met & ((across >= end) == (down >= end))
    return place, met


def turn_tables(lengths, freqs, rows):
    place, met = layout_of(lengths, rows, 128)
    angles = place.astype(jnp.float32) * freqs[...]
    sine = jnp.sin(angles)
    return jnp.cos(angles), jnp.where(first_half(angles.shape), -sine, sine), met


def pair_copy(src, dst, send_sem, recv_sem):
    return pltpu.make_async_remote_copy(
        src_ref=src,
        dst_ref=dst,
        send_sem=send_sem,
        recv_sem=recv_sem,
        device_id={"tensor": 1 - lax.axis_index("tensor")},
        device_id_type=pl.DeviceIdType.MESH,
    )


def greet_pair():
    barrier = pltpu.get_barrier_semaphore()
    pl.semaphore_signal(
        barrier,
        inc=1,
        device_id={"tensor": 1 - lax.axis_index("tensor")},
        device_id_type=pl.DeviceIdType.MESH,
    )
    pl.semaphore_wait(barrier, 1)


def forward_kernel(
    lengths,
    freqs,
    tokens,
    routes,
    g_attn,
    g_latent,
    g_ffn,
    router_t,
    w_query,
    down_t,
    kv_up,
    w_out,
    grad_out,
    hidden,
    ffn_bf,
    gates,
    probs,
    normed,
    queries,
    kv,
    key_turned,
    latent_bf,
    latent,
    context,
    log_totals,
    everyone,
    wq_v,
    down_v,
    up_v,
    out_v,
    sent,
    got,
    w_sem,
    s_sem,
    r_sem,
    own_sem,
    up_s,
    up_r,
    dn_s,
    dn_r,
    x_s,
    x_r,
    c_s,
    c_r,
):
    bf16, f32 = jnp.bfloat16, jnp.float32
    z_size, x_size = 4, 2
    z, x, core = place_of(x_size)
    at = functools.partial(index_of, x_size=x_size)
    rows, features = tokens.shape
    rank = kv_up.shape[0]
    heads = kv_up.shape[1] // 256
    turned = down_t.shape[0] - rank
    tail = pl.ds(rank, turned)
    loads = [
        pltpu.make_async_copy(down_t, down_v.at[pl.ds(0, rank + turned)], w_sem.at[0]),
        pltpu.make_async_copy(down_t.at[tail], down_v.at[pl.ds(rank + turned, turned)], w_sem.at[1]),
        pltpu.make_async_copy(kv_up, up_v, w_sem.at[2]),
        pltpu.make_async_copy(w_query, wq_v, w_sem.at[3]),
        pltpu.make_async_copy(w_out, out_v, w_sem.at[4]),
    ]
    keep = pltpu.make_async_copy(grad_out, everyone.at[at(z, x, core)], own_sem.at[0])

    def move(w, v, first, sems, target):
        block = everyone.at[at(w, v, core)]
        return remote(grad_out if first else block, block, *sems, target)

    up = lambda d: move(z - d, x, d == 0, (up_s.at[d], up_r.at[d]), at(z + 1, x, core))
    down = lambda d: move(z + d, x, d == 0, (dn_s.at[d], dn_r.at[d]), at(z - 1, x, core))
    across = lambda i, w: move(w, x, i == 0, (x_s.at[i], x_r.at[i]), at(z, 1 - x, core))
    beside = lambda w, v, first=False: move(
        w, v, first, (c_s.at[w, v], c_r.at[w, v]), at(z, x, 1 - core)
    )
    near = near_first(z)[1]

    def from_across(i, w):
        block = everyone.at[at(w, 1 - x, core)]
        remote(block, block, x_s.at[i], x_r.at[i], at(z, 1 - x, core)).wait_recv()
        beside(w, 1 - x).start()

    keep.start()
    for copy in loads:
        copy.start()
    greet(z, x, core, z_size, x_size, True)
    beside(z, x, True).start()
    across(0, z).start()
    pl.when(z < z_size - 1)(lambda: up(0).start())
    pl.when(z > 0)(lambda: down(0).start())
    cosine, sine, met = turn_tables(lengths, freqs, rows)
    values, _, _ = rms_normalize_pieces(tokens[...].astype(f32), g_attn[...])
    normed[...] = values.astype(bf16)
    loads[0].wait()
    loads[1].wait()
    low = contract_last(normed[...], down_v[...])
    latent[...] = low[:, :rank]
    key_turned[...] = turn(low[:, rank:], cosine, sine).astype(bf16)
    values, _, _ = rms_normalize_pieces(latent[...], g_latent[...])
    latent_bf[...] = values.astype(bf16)
    loads[2].wait()

    def keys(n, _):
        cols = pl.ds(pl.multiple_of(n * 512, 512), 512)
        kv[:, cols] = nn(latent_bf[...], up_v[:, cols]).astype(bf16)
        return 0

    lax.fori_loop(0, kv.shape[1] // 512, keys, 0)
    loads[3].wait()
    lane = lax.broadcasted_iota(jnp.int32, (rows, 128), 1)
    log_totals[...] = jnp.zeros(log_totals.shape, f32)

    def two_heads(i, _):
        three = nn(normed[...], wq_v[:, pl.ds(pl.multiple_of(i * 384, 384), 384)])
        middle, last = three[:, 128:256], three[:, 256:]
        plain = (
            three[:, :128],
            jnp.where(lane < 64, pltpu.roll(middle, 64, 1), pltpu.roll(last, 64, 1)),
        )
        spun = turn(jnp.where(lane < 64, middle, last), cosine, sine)
        for b in range(2):
            head = 2 * i + b
            queries[head, :, pl.ds(0, 128)] = plain[b].astype(bf16)
            queries[head, :, pl.ds(128, 128)] = jnp.where(
                (lane < 64) == (b == 0), spun, 0.0
            ).astype(bf16)
            at = pl.multiple_of(head * 256, 256)
            key = jnp.concatenate([kv[:, pl.ds(at, 128)], key_turned[...]], axis=1)
            raw = contract_last(queries[head], key)
            scores = jnp.where(met, raw * QK ** (-0.5), -jnp.inf)
            top = jnp.max(scores, axis=1, keepdims=True)
            expo = jnp.exp(scores - top)
            total = jnp.sum(expo, axis=1, keepdims=True)
            log_totals[...] = jnp.where(lane == head, top + jnp.log(total), log_totals[...])
            context[:, pl.ds(pl.multiple_of(head * 128, 128), 128)] = nn(
                (expo / total).astype(bf16), kv[:, pl.ds(at + 128, 128)]
            ).astype(bf16)
        return 0

    lax.fori_loop(0, heads // 2, two_heads, 0)

    loads[4].wait()
    chunks, width = sent.shape[0], sent.shape[2]
    chunk = lambda i: pair_copy(sent.at[i], got.at[i], s_sem.at[i], r_sem.at[i])

    def project(i, _):
        sent[i] = contract_last(
            context[...], out_v[pl.ds(pl.multiple_of(i * width, width), width), :]
        ).astype(bf16)
        chunk(i).start()
        return 0

    lax.fori_loop(0, chunks, project, 0)

    @pl.when(z > 0)
    def _():
        up(0).wait_recv()
        across(1, z - 1).start()
        pl.when(z < z_size - 1)(lambda: up(1).start())
        beside(z - 1, x).start()

    @pl.when(z < z_size - 1)
    def _():
        down(0).wait_recv()
        pl.when(z == 0)(lambda: across(1, z + 1).start())
        pl.when(z > 0)(lambda: down(1).start())
        beside(z + 1, x).start()

    from_across(0, z)

    def join(i, _):
        chunk(i).wait()
        cols = pl.ds(pl.multiple_of(i * width, width), width)
        hidden[:, cols] = tokens[:, cols].astype(f32) + (sent[i].astype(f32) + got[i].astype(f32))
        return 0

    lax.fori_loop(0, chunks, join, 0)
    values, _, _ = rms_normalize_pieces(hidden[...], g_ffn[...])
    ffn_bf[...] = values.astype(bf16)
    experts = lax.axis_size("dp")
    logits = lax.dot_general(
        values,
        router_t[...],
        (((1,), (1,)), ((), ())),
        precision=lax.Precision.HIGHEST,
        preferred_element_type=f32,
    )
    logits = jnp.where(lane < experts, logits, -jnp.inf)
    expo = jnp.exp(logits - jnp.max(logits, axis=1, keepdims=True))
    share = expo / jnp.sum(expo, axis=1, keepdims=True)
    probs[...] = share
    named = lane < 0
    for i in range(routes.shape[1]):
        named = named | (lane == routes[:, pl.ds(i, 1)])
    gates[...] = jnp.where(named, share, -1.0).T[: gates.shape[0]]

    @pl.when(z >= 2)
    def _():
        up(1).wait_recv()
        beside(z - 2, x).start()

    @pl.when(z < z_size - 2)
    def _():
        down(1).wait_recv()
        beside(z + 2, x).start()

    from_across(1, near)
    beside(z, x).wait()
    beside(z, 1 - x).wait()
    beside(near, 1 - x).wait()
    pl.when(z > 0)(lambda: beside(z - 1, x).wait())
    pl.when(z < z_size - 1)(lambda: beside(z + 1, x).wait())
    pl.when(z >= 2)(lambda: beside(z - 2, x).wait())
    pl.when(z < z_size - 2)(lambda: beside(z + 2, x).wait())
    across(0, z).wait_send()
    across(1, near).wait_send()
    pl.when(z < z_size - 1)(lambda: up(0).wait_send())
    pl.when(z > 0)(lambda: down(0).wait_send())
    pl.when((z > 0) & (z < z_size - 1))(lambda: up(1).wait_send())
    pl.when((z > 0) & (z < z_size - 1))(lambda: down(1).wait_send())
    keep.wait()


def forward_tuned(
    lengths,
    freqs,
    tokens,
    routes,
    g_attn,
    g_latent,
    g_ffn,
    router_t,
    w_query,
    down_t,
    kv_up,
    w_out,
    grad_out,
):
    rows, features = tokens.shape
    rank, columns = kv_up.shape
    heads = columns // 256
    bf16, f32, dma = jnp.bfloat16, jnp.float32, pltpu.SemaphoreType.DMA
    vmem, anywhere = pl.BlockSpec(memory_space=pltpu.VMEM), pl.BlockSpec(memory_space=pl.ANY)
    smem = pl.BlockSpec(memory_space=pltpu.SMEM)
    shape = jax.ShapeDtypeStruct
    chunks = 8
    return pl.pallas_call(
        forward_kernel,
        out_shape=[
            shape((rows, features), f32),
            shape((rows, features), bf16),
            shape((lax.axis_size("dp"), rows), f32),
            shape((rows, 128), f32),
            shape((rows, features), bf16),
            shape((heads, rows, 256), bf16),
            shape((rows, columns), bf16),
            shape((rows, 128), bf16),
            shape((rows, rank), bf16),
            shape((rows, rank), f32),
            shape((rows, heads * 128), bf16),
            shape((rows, 128), f32),
            shape((16,) + grad_out.shape, bf16),
        ],
        in_specs=[smem] + [vmem] * 7 + [anywhere] * 5,
        out_specs=[vmem] * 12 + [anywhere],
        scratch_shapes=[
            pltpu.VMEM(w_query.shape, bf16),
            pltpu.VMEM((rank + 128, features), bf16),
            pltpu.VMEM(kv_up.shape, bf16),
            pltpu.VMEM(w_out.shape, bf16),
            pltpu.VMEM((chunks, rows, features // chunks), bf16),
            pltpu.VMEM((chunks, rows, features // chunks), bf16),
            dma((5,)),
            dma((chunks,)),
            dma((chunks,)),
            dma((1,)),
        ]
        + [dma((2,))] * 6
        + [dma((4, 2))] * 2,
        compiler_params=pltpu.CompilerParams(
            collective_id=2, has_side_effects=True, vmem_limit_bytes=VMEM_LIMIT
        ),
        name="attention_forward",
    )(
        lengths,
        freqs,
        tokens,
        routes,
        g_attn,
        g_latent,
        g_ffn,
        router_t,
        w_query,
        down_t,
        kv_up,
        w_out,
        grad_out,
    )


def backward_kernel(
    lengths,
    freqs,
    sums,
    hidden,
    grad_out,
    tokens,
    probs,
    g_attn,
    g_latent,
    g_ffn,
    router_t,
    queries,
    kv,
    key_turned,
    latent,
    log_totals,
    normed,
    context,
    latent_bf,
    w_query,
    down_t,
    kv_up,
    w_out,
    grad_tokens,
    out_grad,
    query_grad,
    up_grad,
    down_grad,
    vector_grad,
    wq_v,
    down_v,
    up_v,
    unit,
    grad_hidden_bf,
    grad_query,
    grad_kv,
    grad_low,
    vectors,
    hidden_t,
    normed_t,
    latent_t,
    low_t,
    send_wide,
    send_up,
    send_down,
    send_vector,
    out_c,
    query_c,
    up_c,
    down_c,
    vector_c,
    out_x,
    query_x,
    up_x,
    down_x,
    vector_x,
    out_z,
    query_z,
    up_z,
    down_z,
    vector_z,
    grad_context,
    grad_turned,
    sent,
    got,
    low_sent,
    low_got,
    w_sem,
    s_sem,
    r_sem,
    e_sem,
    c_s,
    c_r,
    x_s,
    x_r,
    z_s,
    z_r,
):
    grad_hidden = grad_tokens
    z_size, x_size = 4, 2
    z, x, core = place_of(x_size)
    place_rank = lax.axis_index("tensor")
    at = functools.partial(index_of, x_size=x_size)
    half = z // 2
    inner = ((z + 3) // 4) * ((6 - z) // 4)
    order = [3 - 3 * half, 2 - half, 1 - z + 4 * half, z]
    blocks = [(w, v) for v in (1 - x, x) for w in order]
    outs = (out_grad, query_grad, up_grad, down_grad, vector_grad)
    c_buf = (out_c, query_c, up_c, down_c, vector_c)
    x_buf = (out_x, query_x, up_x, down_x, vector_x)
    z_buf = (out_z, query_z, up_z, down_z, vector_z)

    def product(p, owner):
        rows = lambda size: pl.ds(pl.multiple_of(owner * size, size), size)
        if p == 0:
            return nn(hidden_t[rows(128), :], context[...])
        if p == 1:
            return nn(normed_t[rows(128), :], grad_query[...])
        if p == 2:
            size = up_grad.shape[0]
            return nn(latent_t[rows(size), :], grad_kv[...])
        if p == 3:
            size = down_grad.shape[0]
            mine = pl.ds(pl.multiple_of(place_rank * size, 32), size)
            return nn(low_t[mine, :], normed[:, rows(128)])
        return vectors[:, rows(128)]

    def staging(p, i):
        if p == 0:
            return send_wide.at[i, :, pl.ds(0, out_grad.shape[1])]
        return (None, send_wide, send_up, send_down, send_vector)[p].at[i]

    def beside(p, i):
        w, v = blocks[i]
        return remote(
            staging(p, i), c_buf[p].at[w, v], c_s.at[p, i], c_r.at[p, w, v], at(z, x, 1 - core)
        )

    across = lambda p, w: remote(
        c_buf[p].at[w, 1 - x], x_buf[p].at[w], x_s.at[p, w], x_r.at[p, w], at(z, 1 - x, core)
    )

    def along(p, w, slot, target):
        return remote(
            c_buf[p].at[w, x], z_buf[p].at[slot], z_s.at[p, w], z_r.at[p, slot], at(target, x, core)
        )

    def to_sibling(p):
        for i, (w, v) in enumerate(blocks):
            staging(p, i)[...] = product(p, at(w, v, 1 - core)).astype(c_buf[p].dtype)
            beside(p, i).start()

    def over_x(p):
        for i, (w, v) in enumerate(blocks):
            beside(p, i).wait_recv()
            total = c_buf[p][w, v].astype(jnp.float32) + product(p, at(w, v, core))
            c_buf[p][w, v] = total.astype(c_buf[p].dtype)
            if i < 4:
                across(p, w).start()

    def over_z(p, k):
        w = order[k]
        across(p, w).wait_recv()
        if k < 3:

            @pl.when(inner == 1)
            def _():
                along(p, w, w, z).wait_recv()
                add_into(c_buf[p].at[w, x], x_buf[p].at[w], z_buf[p].at[w])

            @pl.when(inner == 0)
            def _():
                add_into(c_buf[p].at[w, x], x_buf[p].at[w])

            @pl.when(w > z)
            def _():
                along(p, w, w, z + 1).start()

            @pl.when(w < z - 1)
            def _():
                along(p, w, w, z - 1).start()

            @pl.when(w == z - 1)
            def _():
                along(p, w, z_size, z - 1).start()

        else:
            add_into(c_buf[p].at[w, x], x_buf[p].at[w])

            @pl.when(z > 0)
            def _():
                along(p, w, z, z).wait_recv()
                add_into(c_buf[p].at[w, x], z_buf[p].at[z])

            @pl.when(z < z_size - 1)
            def _():
                along(p, w, z_size, z).wait_recv()
                add_into(c_buf[p].at[w, x], z_buf[p].at[z_size])

            outs[p][...] = c_buf[p][z, x].astype(outs[p].dtype)

    bf16, f32 = jnp.bfloat16, jnp.float32
    highest = lax.Precision.HIGHEST
    rows, features = tokens.shape
    rank = kv_up.shape[0]
    heads = kv_up.shape[1] // 256
    turned = down_t.shape[0] - rank
    tail = pl.ds(rank, turned)
    out_v = wq_v.at[:, pl.ds(0, w_out.shape[1])]
    loads = [
        pltpu.make_async_copy(w_out, out_v, w_sem.at[0]),
        pltpu.make_async_copy(kv_up, up_v, w_sem.at[1]),
        pltpu.make_async_copy(w_query, wq_v, w_sem.at[2]),
        pltpu.make_async_copy(down_t, down_v.at[pl.ds(0, rank + turned)], w_sem.at[3]),
        pltpu.make_async_copy(down_t.at[tail], down_v.at[pl.ds(rank + turned, turned)], w_sem.at[4]),
    ]
    rows_copy = pltpu.make_async_copy(hidden, unit, w_sem.at[5])
    rows_copy.start()
    for copy in loads[:2] + loads[3:]:
        copy.start()
    greet(z, x, core, z_size, x_size, True)
    cosine, sine, met = turn_tables(lengths, freqs, rows)
    lane = lax.broadcasted_iota(jnp.int32, (rows, 128), 1)
    experts = lax.axis_size("dp")

    extra = sums[:, pl.ds(features, 128)]
    dense = extra + pltpu.roll(extra, 128 - experts, 1)
    share = probs[...]
    dense = jnp.where(lane < experts, dense, 0.0)
    logits = share * (dense - jnp.sum(share * dense, axis=1, keepdims=True))
    grad_in = sums[:, pl.ds(0, features)] + lax.dot_general(
        logits,
        router_t[...],
        (((1,), (0,)), ((), ())),
        precision=highest,
        preferred_element_type=f32,
    )
    rows_copy.wait()
    values, unit_rows, factor = rms_normalize_pieces(unit[...], g_ffn[...])
    unit[...] = unit_rows
    vectors[pl.ds(0, experts), :] = lax.dot_general(
        logits, values, (((0,), (0,)), ((), ())), precision=highest, preferred_element_type=f32
    )[:experts]
    vectors[pl.ds(experts, 8), :] = jnp.zeros((8, features), f32)
    vectors[pl.ds(experts + 1, 1), :] = jnp.sum(grad_in * unit[...], axis=0, keepdims=True)
    grad_hidden[...] = grad_out[...].astype(f32) + normalize_back(
        grad_in, unit[...], factor, g_ffn[...]
    )
    grad_hidden_bf[...] = grad_hidden[...].astype(bf16)
    hidden_t[...] = grad_hidden_bf[...].T
    to_sibling(0)
    loads[0].wait()

    def back_out(n, _):
        cols = pl.ds(pl.multiple_of(n * 256, 256), 256)
        grad_context[:, cols] = nn(grad_hidden_bf[...], out_v[:, cols]).astype(bf16)
        return 0

    lax.fori_loop(0, grad_context.shape[1] // 256, back_out, 0)
    loads[2].start()
    grad_turned[...] = jnp.zeros(grad_turned.shape, f32)
    over_x(0)
    normed_t[...] = normed[...].T
    latent_t[...] = latent_bf[...].T

    def two_heads(i, _):
        pieces = []
        for b in range(2):
            head = 2 * i + b
            at = pl.multiple_of(head * 256, 256)
            key = jnp.concatenate([kv[:, pl.ds(at, 128)], key_turned[...]], axis=1)
            value = kv[:, pl.ds(at + 128, 128)]
            raw = contract_last(queries[head], key)
            log_total = jnp.sum(
                jnp.where(lane == head, log_totals[...], 0.0), axis=1, keepdims=True
            )
            weights = jnp.exp(jnp.where(met, raw * QK ** (-0.5), -jnp.inf) - log_total)
            grad_ctx = grad_context[:, pl.ds(pl.multiple_of(head * 128, 128), 128)]
            grad_weights = contract_last(grad_ctx, value)
            inner = jnp.sum(weights * grad_weights, axis=1, keepdims=True)
            grad_raw = (weights * (grad_weights - inner) * QK ** (-0.5)).astype(bf16)
            pieces.append(nn(grad_raw, key))
            back_key = contract_first(grad_raw, queries[head])
            grad_kv[:, pl.ds(at, 128)] = back_key[:, :128].astype(bf16)
            grad_turned[...] += back_key[:, 128:]
            grad_kv[:, pl.ds(at + 128, 128)] = contract_first(
                weights.astype(bf16), grad_ctx
            ).astype(bf16)
        even, odd = pieces
        spun = turn(jnp.where(lane < 64, even[:, 128:], odd[:, 128:]), cosine, -sine)
        moved = pltpu.roll(odd[:, :128], 64, 1)
        start = pl.multiple_of(i * 384, 384)
        grad_query[:, pl.ds(start, 128)] = even[:, :128].astype(bf16)
        grad_query[:, pl.ds(start + 128, 128)] = jnp.where(lane < 64, spun, moved).astype(bf16)
        grad_query[:, pl.ds(start + 256, 128)] = jnp.where(lane < 64, moved, spun).astype(bf16)
        return 0

    lax.fori_loop(0, heads // 2, two_heads, 0)
    for i in range(8):
        beside(0, i).wait_send()
    to_sibling(1)
    loads[1].wait()
    low_sent[:, pl.ds(0, rank)] = contract_last(grad_kv[...], up_v[...]).astype(bf16)
    folded = turn(grad_turned[...] + pltpu.roll(grad_turned[...], 64, 1), cosine, -sine)
    low_sent[:, pl.ds(rank, 128)] = jnp.where(lane < turned, folded, 0.0).astype(bf16)
    low_copy = pair_copy(low_sent, low_got, e_sem.at[0], e_sem.at[1])
    low_copy.start()
    loads[2].wait()
    chunks, width = sent.shape[0], sent.shape[2]
    chunk = lambda i: pair_copy(sent.at[i], got.at[i], s_sem.at[i], r_sem.at[i])

    def project(i, _):
        sent[i] = contract_last(
            grad_query[...], wq_v[pl.ds(pl.multiple_of(i * width, width), width), :]
        ).astype(bf16)
        chunk(i).start()
        return 0

    lax.fori_loop(0, chunks, project, 0)
    over_x(1)
    to_sibling(2)
    for k in range(3):
        over_z(0, k)
    over_x(2)
    loads[3].wait()
    loads[4].wait()
    low_copy.wait()
    low = low_sent[...].astype(f32) + low_got[...].astype(f32)
    grad_normed = low[:, :rank]
    _, latent_unit, latent_factor = rms_normalize_pieces(latent[...], g_latent[...])
    grad_gain = jnp.sum(grad_normed * latent_unit, axis=0, keepdims=True)
    for i in range(rank // 128):
        vectors[pl.ds(experts + 2 + i, 1), :] = jnp.concatenate(
            [grad_gain[:, i * 128 : (i + 1) * 128]] * (features // 128), axis=1
        )
    grad_low[:, pl.ds(0, rank)] = normalize_back(
        grad_normed, latent_unit, latent_factor, g_latent[...]
    ).astype(bf16)
    grad_low[:, pl.ds(rank, 128)] = low[:, rank:].astype(bf16)
    low_t[...] = grad_low[...].T
    to_sibling(3)
    over_x(3)
    over_z(0, 3)

    def join(i, _):
        cols = pl.ds(pl.multiple_of(i * width, width), width)
        product = nn(grad_low[...], down_v[:, cols])
        chunk(i).wait()
        unit[:, cols] = product + (sent[i].astype(f32) + got[i].astype(f32))
        return 0

    lax.fori_loop(0, chunks, join, 0)
    _, attn_unit, attn_factor = rms_normalize_pieces(tokens[...].astype(f32), g_attn[...])
    vectors[pl.ds(experts, 1), :] = jnp.sum(unit[...] * attn_unit, axis=0, keepdims=True)
    to_sibling(4)
    grad_tokens[...] = grad_hidden[...] + normalize_back(
        unit[...], attn_unit, attn_factor, g_attn[...]
    )
    over_x(4)
    for p in range(1, 5):
        for k in range(4):
            over_z(p, k)
    for p in range(5):
        for i in range(8):
            if p > 0:
                beside(p, i).wait_send()
        for w in range(z_size):
            across(p, w).wait_send()

            @pl.when(z != w)
            def _():
                along(p, w, w, z).wait_send()


def backward_tuned(lengths, freqs, sums, values, gains, router_t, saved, weights):
    hidden, grad_out, tokens, probs = values
    w_query, down_t, kv_up, w_out = weights
    rows, features = tokens.shape
    rank, columns = kv_up.shape
    heads = columns // 256
    bf16, f32, dma = jnp.bfloat16, jnp.float32, pltpu.SemaphoreType.DMA
    vmem, anywhere = pl.BlockSpec(memory_space=pltpu.VMEM), pl.BlockSpec(memory_space=pl.ANY)
    smem = pl.BlockSpec(memory_space=pltpu.SMEM)
    shape = jax.ShapeDtypeStruct
    chunks = 8
    experts, ranks = lax.axis_size("dp"), lax.axis_size("tensor")
    devices = experts
    share_rows = features // devices
    blocks = [
        ((share_rows, w_out.shape[1]), bf16),
        ((share_rows, w_query.shape[1]), bf16),
        ((rank // devices, columns), bf16),
        ((down_t.shape[0] // ranks, share_rows), bf16),
        ((experts + 8, share_rows), f32),
    ]
    several = lambda *lead: [pltpu.VMEM(lead + b, kind) for b, kind in blocks]
    return pl.pallas_call(
        backward_kernel,
        out_shape=[shape((rows, features), f32)] + [shape(b, f32) for b, _ in blocks],
        in_specs=[smem, vmem, vmem, anywhere] + [vmem] * 15 + [anywhere] * 4,
        out_specs=[vmem] * 6,
        scratch_shapes=[
            pltpu.VMEM(w_query.shape, bf16),
            pltpu.VMEM((rank + 128, features), bf16),
            pltpu.VMEM(kv_up.shape, bf16),
            pltpu.VMEM((rows, features), f32),
            pltpu.VMEM((rows, features), bf16),
            pltpu.VMEM((rows, w_query.shape[1]), bf16),
            pltpu.VMEM((rows, columns), bf16),
            pltpu.VMEM((rows, rank + 128), bf16),
            pltpu.VMEM((experts + 8, features), f32),
            pltpu.VMEM((features, rows), bf16),
            pltpu.VMEM((features, rows), bf16),
            pltpu.VMEM((rank, rows), bf16),
            pltpu.VMEM((rank + 128, rows), bf16),
        ]
        + several(8)[1:]
        + several(4, 2)
        + several(4)
        + several(5)
        + [
            pltpu.VMEM((rows, heads * 128), bf16),
            pltpu.VMEM((rows, 128), f32),
            pltpu.VMEM((chunks, rows, features // chunks), bf16),
            pltpu.VMEM((chunks, rows, features // chunks), bf16),
            pltpu.VMEM((rows, rank + 128), bf16),
            pltpu.VMEM((rows, rank + 128), bf16),
            dma((6,)),
            dma((chunks,)),
            dma((chunks,)),
            dma((2,)),
            dma((5, 8)),
            dma((5, 4, 2)),
            dma((5, 4)),
            dma((5, 4)),
            dma((5, 4)),
            dma((5, 5)),
        ],
        compiler_params=pltpu.CompilerParams(
            collective_id=4, has_side_effects=True, vmem_limit_bytes=VMEM_LIMIT
        ),
        name="attention_backward",
    )(lengths, freqs, sums, hidden, grad_out, tokens, probs, *gains, router_t, *saved, *weights)


def add_window(dst, start, width, *srcs):
    rows = dst.shape[0]
    step = 32 if rows % 32 == 0 else 8
    cols = pl.ds(pl.multiple_of(start, 128), width)

    def body(i, _):
        here = pl.ds(pl.multiple_of(i * step, step), step)
        total = dst[here, cols].astype(jnp.float32)
        for src in srcs:
            total = total + src[here, :].astype(jnp.float32)
        dst[here, cols] = total.astype(dst.dtype)
        return 0

    lax.fori_loop(0, rows // step, body, 0)


def home_kernel(x_size, parts, share, whole, total, *refs):
    z_size, f32 = 4, jnp.float32
    rows = whole.shape[1] // parts
    piece = lambda p: pl.ds(p * rows, rows)
    own, c_buf, x_buf, z_buf, y_buf, f_buf = (refs[i * parts : (i + 1) * parts] for i in range(6))
    refs = refs[6 * parts :]
    l_sem, c_s, c_r, x_s, x_r, z_s, z_r, y_s, y_r, f_s, f_r = refs
    z, x, core = place_of(x_size)
    rank = lax.axis_index("tensor")
    at = functools.partial(index_of, x_size=x_size)
    half = z // 2
    inner = ((z + 3) // 4) * ((6 - z) // 4)
    order = [3 - 3 * half, 2 - half, 1 - z + 4 * half, z]
    width = [c.shape[3] for c in c_buf]
    window = [w - share for w in width]
    begin = pl.multiple_of(rank * share, 128)
    mine = lambda p: pl.multiple_of(rank * window[p], 128)
    theirs = lambda p: pl.multiple_of((1 - rank) * window[p], 128)

    slots = own[0].shape[0]
    blocks = [(w, v) for v in (1 - x, x) for w in order]
    load = lambda p, i: pltpu.make_async_copy(
        whole.at[at(blocks[i][0], blocks[i][1], core), piece(p)],
        own[p].at[i % slots],
        l_sem.at[p, i % slots],
    )
    beside = lambda p, w, v: remote(
        whole.at[at(w, v, 1 - core), piece(p)],
        c_buf[p].at[w, v],
        c_s.at[p, w, v],
        c_r.at[p, w, v],
        at(z, x, 1 - core),
    )
    twin = lambda p, w, v: pair_copy(
        c_buf[p].at[w, v, :, pl.ds(theirs(p), share)],
        y_buf[p].at[w, v],
        y_s.at[p, w, v],
        y_r.at[p, w, v],
    )
    across = lambda p, w: remote(
        c_buf[p].at[w, 1 - x, :, pl.ds(begin, window[p])],
        x_buf[p].at[w],
        x_s.at[p, w],
        x_r.at[p, w],
        at(z, 1 - x, core),
    )

    def along(p, w, slot, target):
        return remote(
            c_buf[p].at[w, x, :, pl.ds(begin, window[p])],
            z_buf[p].at[slot],
            z_s.at[p, w],
            z_r.at[p, slot],
            at(target, x, core),
        )

    final = lambda p: pair_copy(
        c_buf[p].at[z, x, :, pl.ds(begin, window[p])], f_buf[p], f_s.at[p], f_r.at[p]
    )

    for p in range(parts):
        for i in range(slots):
            load(p, i).start()
    greet(z, x, core, z_size, x_size, True)
    for p in range(parts):
        for w, v in blocks:
            beside(p, w, v).start()
    def on_chip(p, i):
        w, v = blocks[i]
        load(p, i).wait()
        beside(p, w, v).wait_recv()
        add_into(c_buf[p].at[w, v], own[p].at[i % slots])
        if i + slots < len(blocks):
            load(p, i + slots).start()
        twin(p, w, v).start()

    def go_across(p, i):
        w, v = blocks[i]
        twin(p, w, v).wait()
        add_window(c_buf[p].at[w, v], mine(p), share, y_buf[p].at[w, v])
        across(p, w).start()

    def go_along(p, k):
        w = order[k]
        twin(p, w, x).wait()
        add_window(c_buf[p].at[w, x], mine(p), share, y_buf[p].at[w, x])
        across(p, w).wait_recv()
        if k < 3:

            @pl.when(inner == 1)
            def _():
                along(p, w, w, z).wait_recv()
                add_window(c_buf[p].at[w, x], begin, window[p], x_buf[p].at[w], z_buf[p].at[w])

            @pl.when(inner == 0)
            def _():
                add_window(c_buf[p].at[w, x], begin, window[p], x_buf[p].at[w])

            @pl.when(w > z)
            def _():
                along(p, w, w, z + 1).start()

            @pl.when(w < z - 1)
            def _():
                along(p, w, w, z - 1).start()

            @pl.when(w == z - 1)
            def _():
                along(p, w, z_size, z - 1).start()

        else:
            add_window(c_buf[p].at[w, x], begin, window[p], x_buf[p].at[w])

            @pl.when(z > 0)
            def _():
                along(p, w, z, z).wait_recv()
                add_window(c_buf[p].at[w, x], begin, window[p], z_buf[p].at[z])

            @pl.when(z < z_size - 1)
            def _():
                along(p, w, z_size, z).wait_recv()
                add_window(c_buf[p].at[w, x], begin, window[p], z_buf[p].at[z_size])

            final(p).start()

    def begin_part(p, between):
        for i in range(5):
            on_chip(p, i)
            if i >= 1:
                go_across(p, i - 1)
            between(i)
        for i in range(5, 8):
            on_chip(p, i)

    begin_part(0, lambda i: None)
    for p in range(parts):
        if p + 1 < parts:

            def between(i):
                if i < 4:
                    go_along(p, i)

            begin_part(p + 1, between)
        else:
            for k in range(4):
                go_along(p, k)
    for p in range(parts):
        final(p).wait()
        common = window[p] - share
        near, far = c_buf[p].at[z, x], f_buf[p]
        total[piece(p), pl.ds(mine(p), share)] = near[:, pl.ds(mine(p), share)].astype(f32)
        total[piece(p), pl.ds(theirs(p), share)] = far[
            :, pl.ds(pl.multiple_of((1 - rank) * common, 128), share)
        ].astype(f32)
        total[piece(p), pl.ds(share, common)] = near[:, pl.ds(share, common)].astype(f32) + far[
            :, pl.ds(pl.multiple_of(rank * share, 128), common)
        ].astype(f32)
    for p in range(parts):
        for w in range(z_size):
            for v in range(x_size):
                beside(p, w, v).wait_send()
            across(p, w).wait_send()

            @pl.when(z != w)
            def _():
                along(p, w, w, z).wait_send()


def home_sums(array, collective_id, parts, share=768):
    bf16, f32, dma = jnp.bfloat16, jnp.float32, pltpu.SemaphoreType.DMA
    rows, width = array.shape[1:]
    block = lambda *lead, cut=0: [pltpu.VMEM(lead + (rows // parts, width - cut), bf16)] * parts
    return pl.pallas_call(
        functools.partial(home_kernel, 2, parts, share),
        out_shape=jax.ShapeDtypeStruct((rows, width), f32),
        in_specs=[pl.BlockSpec(memory_space=pl.ANY)],
        out_specs=pl.BlockSpec(memory_space=pltpu.VMEM),
        scratch_shapes=block(3)
        + block(4, 2)
        + block(4, cut=share)
        + block(5, cut=share)
        + block(4, 2, cut=width - share)
        + block(cut=share)
        + [dma((parts, 3))]
        + [dma((parts, 4, 2))] * 2
        + [dma((parts, 4))] * 3
        + [dma((parts, 5))]
        + [dma((parts, 4, 2))] * 2
        + [dma((parts,))] * 2,
        compiler_params=pltpu.CompilerParams(
            collective_id=collective_id, has_side_effects=True, vmem_limit_bytes=VMEM_LIMIT
        ),
        name="home_sums",
    )(array)


def sum_home(arrays, pair=False):
    sums = [lax.psum_scatter(a, "dp", scatter_dimension=0) for a in arrays]
    if pair:
        sums = [lax.psum(a.astype(jnp.float32), "tensor") for a in sums]
    return [a.astype(jnp.float32) for a in sums]


def product_sum(left, right, extras):
    product = contract_last(left, right).astype(jnp.bfloat16)
    return [lax.psum(a, "tensor").astype(jnp.float32) for a in [product] + extras]


def ffn_with_kernel(own_ffn, gates, everyone_grad, weights, shared, capacity, experts):
    part = shared[0].shape[1]
    hidden, features = weights[0].shape[1], own_ffn.shape[1]
    gate_t, up_t, down_t = (jnp.pad(w.T, ((0, 128 - part), (0, 0))) for w in shared)
    out_part, grad_part, rows, dy, he, dge, due, shared_grads, _ = ffn_tuned(
        own_ffn,
        gates,
        everyone_grad,
        *(w.T for w in weights),
        jnp.concatenate([gate_t, up_t], axis=0),
        down_t,
        capacity,
    )
    rows, dy = rows.reshape(-1, features), dy.reshape(-1, features)
    he, dge, due = (a.reshape(-1, a.shape[2]) for a in (he, dge, due))
    devices, rows_here = everyone_grad.shape[:2]
    return (
        out_part.reshape(devices * rows_here, -1),
        grad_part.reshape(devices, rows_here, -1),
        [rows, dy, he, dge, due],
        shared_grads.reshape(3, 128, features)[:, :part].reshape(3 * part, features),
    )


def ffn_plain(own_ffn, gates, everyone_grad, weights, shared, capacity, experts):
    own, devices = lax.axis_index("dp"), lax.axis_size("dp")
    rows_here, features = own_ffn.shape
    places = jnp.arange(rows_here, dtype=jnp.int32)
    expert_gate, expert_up, expert_down = weights
    part_gate, part_up, part_down = shared
    everyone_ffn = lax.all_gather(own_ffn, "dp", tiled=True)
    everyone_gates = lax.all_gather(gates, "dp")
    everyone_grad = everyone_grad.reshape(devices * rows_here, features)
    own_probs = lax.dynamic_slice_in_dim(everyone_gates, own, 1, 2).reshape(devices, rows_here)
    chooses = own_probs >= 0.0
    own_gates = jnp.where(chooses, own_probs, 0.0)
    upto = (places[:, None] <= places[None, :]).astype(jnp.bfloat16)
    slot = jnp.dot(chooses.astype(jnp.bfloat16), upto, preferred_element_type=jnp.float32) - 1.0
    slots = jnp.arange(capacity, dtype=jnp.float32)
    picked = chooses[:, None, :] & (slot[:, None, :] == slots[None, :, None])
    pick = picked.astype(jnp.bfloat16)
    slot_gates = jnp.sum(jnp.where(picked, own_gates[:, None, :], 0.0), axis=2).reshape(-1, 1)

    def pick_rows(values):
        blocks = values.reshape(devices, rows_here, features)
        return jnp.einsum(
            "jst,jtc->jsc", pick, blocks, preferred_element_type=jnp.float32
        ).astype(jnp.bfloat16).reshape(devices * capacity, features)

    def put_rows(values, hidden_parts, weights):
        blocks = values.astype(jnp.bfloat16).reshape(devices, capacity, features)
        left = jnp.concatenate(
            [pick.transpose(0, 2, 1)]
            + [h.reshape(devices, rows_here, h.shape[1]) for h in hidden_parts],
            axis=2,
        )
        right = jnp.concatenate(
            [blocks]
            + [
                jnp.broadcast_to(w.T[None], (devices, w.shape[1], features))
                for w in weights
            ],
            axis=1,
        )
        return (
            jnp.einsum("jtk,jkc->jtc", left, right, preferred_element_type=jnp.float32)
            .astype(jnp.bfloat16)
            .reshape(devices * rows_here, features)
        )

    expert_rows = pick_rows(everyone_ffn)
    grad_picked = pick_rows(everyone_grad)
    grad_rows = (slot_gates * grad_picked.astype(jnp.float32)).astype(jnp.bfloat16)

    gate_pre = jnp.dot(expert_rows, expert_gate, preferred_element_type=jnp.float32)
    up_pre = jnp.dot(expert_rows, expert_up, preferred_element_type=jnp.float32)
    gate_act, gate_slope = swish_parts(gate_pre)
    expert_hidden = (gate_act * up_pre).astype(jnp.bfloat16)
    expert_result = contract_last(expert_hidden, expert_down)
    slot_grads = jnp.sum(grad_picked.astype(jnp.float32) * expert_result, axis=1)
    grad_expert_down = contract_first(grad_rows, expert_hidden)[None]
    grad_expert_hidden = jnp.dot(grad_rows, expert_down, preferred_element_type=jnp.float32)
    grad_gate_pre = (grad_expert_hidden * up_pre * gate_slope).astype(jnp.bfloat16)
    grad_up_pre = (grad_expert_hidden * gate_act).astype(jnp.bfloat16)
    grad_expert_gate = contract_first(expert_rows, grad_gate_pre)[None]
    grad_expert_up = contract_first(expert_rows, grad_up_pre)[None]
    grad_rows_in = contract_last(grad_gate_pre, expert_gate) + contract_last(
        grad_up_pre, expert_up
    )

    shared_pre_gate = jnp.dot(everyone_ffn, part_gate, preferred_element_type=jnp.float32)
    shared_pre_up = jnp.dot(everyone_ffn, part_up, preferred_element_type=jnp.float32)
    shared_act, shared_slope = swish_parts(shared_pre_gate)
    shared_hidden = (shared_act * shared_pre_up).astype(jnp.bfloat16)
    grad_shared_hidden = jnp.dot(everyone_grad, part_down, preferred_element_type=jnp.float32)
    grad_shared_gate_pre = (grad_shared_hidden * shared_pre_up * shared_slope).astype(jnp.bfloat16)
    grad_shared_up_pre = (grad_shared_hidden * shared_act).astype(jnp.bfloat16)
    shared_grads = jnp.concatenate(
        [
            contract_first(grad_shared_gate_pre, everyone_ffn),
            contract_first(grad_shared_up_pre, everyone_ffn),
            contract_first(shared_hidden, everyone_grad),
        ],
        axis=0,
    ).astype(jnp.bfloat16)
    ffn_part = put_rows(slot_gates * expert_result, [shared_hidden], [part_down])
    pair_grads = jnp.sum(
        jnp.where(picked, slot_grads.reshape(devices, capacity, 1), 0.0), axis=1
    ).reshape(devices * rows_here, 1)
    pair_high = pair_grads.astype(jnp.bfloat16).astype(jnp.float32)
    column = jnp.arange(128, dtype=jnp.int32)[None, :]
    pair_columns = jnp.where(
        column == own,
        pair_high,
        jnp.where(column == own + experts, pair_grads - pair_high, 0.0),
    )
    grad_ffn_in = put_rows(
        grad_rows_in, [grad_shared_gate_pre, grad_shared_up_pre], [part_gate, part_up]
    )
    grad_part = jnp.concatenate([grad_ffn_in, pair_columns.astype(jnp.bfloat16)], axis=1)
    return (
        ffn_part.reshape(devices, rows_here, -1),
        grad_part.reshape(devices, rows_here, -1),
        grad_expert_gate,
        grad_expert_up,
        grad_expert_down,
        shared_grads,
    )


def shared_home(grads, part):
    devices = lax.axis_size("dp")
    share_rows = grads.shape[1] // devices
    grads = lax.all_to_all(
        grads.reshape(3 * part, devices, share_rows).transpose(1, 2, 0).astype(jnp.bfloat16),
        "dp",
        split_axis=0,
        concat_axis=0,
    ).astype(jnp.float32)
    return [
        grads[:, :, i * part : (i + 1) * part].transpose(1, 0, 2).reshape(share_rows, -1)
        for i in range(3)
    ]


def shards_tuned(
    tokens,
    lengths,
    routes,
    grad_out,
    g_attn,
    w_query,
    key_value_down_weight,
    latent_norm_gain,
    key_value_up_weight,
    w_out,
    g_ffn,
    router,
    shared_gate,
    shared_up,
    shared_down,
    expert_gate,
    expert_up,
    expert_down,
):
    rows_here, features = tokens.shape
    devices, ranks = lax.axis_size("dp"), lax.axis_size("tensor")
    own, rank = lax.axis_index("dp"), lax.axis_index("tensor")
    experts = router.shape[1]
    capacity = rows_here * TOPK * 4 // (3 * devices)
    half = (key_value_down_weight.shape[1] - LATENT_RANK) // 2
    freqs = (10000.0 ** (-np.arange(half) / half)).astype(np.float32)
    freqs = np.tile(freqs, 128 // half)[None, :]
    router_t = jnp.pad(router.T, ((0, 128 - experts), (0, 0)))
    gains = [g_attn[None, :], latent_norm_gain[None, :], g_ffn[None, :]]
    weights = [w_query, key_value_down_weight.T, key_value_up_weight, w_out]
    hidden, ffn_bf, dense_gates, probs, normed, *saved = forward_tuned(
        lengths, freqs, tokens, routes, *gains, router_t, *weights, grad_out
    )
    queries, kv, key_turned, latent_bf, latent, context, log_totals, everyone_grad = saved
    part = shared_gate.shape[1] // devices
    shared_parts = [
        lax.dynamic_slice_in_dim(w, own * part, part, 1)
        for w in (shared_gate, shared_up, shared_down)
    ]
    ffn_part, grad_ffn_part, expert_saved, shared_grads = ffn_with_kernel(
        ffn_bf,
        dense_gates,
        everyone_grad,
        [w[0] for w in (expert_gate, expert_up, expert_down)],
        shared_parts,
        capacity,
        experts,
    )
    shared_grads = shared_home(shared_grads, part)
    ffn_sum = lax.psum_scatter(ffn_part, "dp", scatter_dimension=0, tiled=True)
    sums = home_sums(grad_ffn_part, 3, 2)
    (
        grad_tokens,
        grad_w_out,
        grad_w_query,
        grad_w_kv_up,
        grad_w_kv_down,
        vectors,
    ) = backward_tuned(
        lengths,
        freqs,
        sums,
        [hidden, grad_out, tokens, probs],
        gains,
        router_t,
        [queries, kv, key_turned, latent, log_totals, normed, context, latent_bf],
        weights,
    )
    grad_tokens, ffn_sum, *expert_saved = lax.optimization_barrier(
        (grad_tokens, ffn_sum, *expert_saved)
    )
    ffn_twin = lax.ppermute(ffn_sum, "tensor", [(0, 1), (1, 0)])
    rows, dy, he, dge, due = expert_saved
    units = expert_gate.shape[2]
    expert_grads = [
        contract_first(rows, dge[:, :units])[None],
        contract_first(rows, due[:, :units])[None],
        contract_first(dy, he[:, :units])[None],
    ]
    output = (
        hidden + (ffn_sum.astype(jnp.float32) + ffn_twin.astype(jnp.float32))
    ).astype(jnp.bfloat16)
    share_rows = features // devices
    router_rows = share_rows // ranks
    grad_router = lax.dynamic_slice_in_dim(vectors[:experts], rank * router_rows, router_rows, 1).T
    latent_rows = LATENT_RANK // devices // ranks
    grad_g_kv = lax.dynamic_slice_in_dim(
        vectors[experts + 2 : experts + 2 + LATENT_RANK // 128].reshape(-1),
        (own * ranks + rank) * latent_rows,
        latent_rows,
        0,
    )
    return (
        output,
        grad_tokens,
        vectors[experts],
        grad_w_query,
        grad_w_kv_down.T,
        grad_g_kv,
        grad_w_kv_up,
        grad_w_out,
        vectors[experts + 1],
        grad_router,
        *shared_grads,
        *expert_grads,
    )


def shards(
    tokens,
    lengths,
    routes,
    grad_out,
    g_attn,
    w_query,
    key_value_down_weight,
    latent_norm_gain,
    key_value_up_weight,
    w_out,
    g_ffn,
    router,
    shared_gate,
    shared_up,
    shared_down,
    expert_gate,
    expert_up,
    expert_down,
):
    rows_here = tokens.shape[0]
    features = tokens.shape[1]
    heads_local = w_out.shape[1] // VALUE_HEAD_SIZE
    devices = lax.axis_size("dp")
    capacity = rows_here * TOPK * 4 // (3 * devices)
    experts = router.shape[1]
    highest = lax.Precision.HIGHEST
    softmax_scale = QK ** (-0.5)
    segment, token_position = doc_layout(lengths[0], rows_here)
    places = jnp.arange(rows_here, dtype=jnp.int32)
    allowed = (segment[:, None] == segment[None, :]) & (places[None, :] <= places[:, None])
    tokens_f = tokens.astype(jnp.float32)
    attn_normed, attn_unit, attn_factor = rms_normalize_pieces(tokens_f, g_attn)
    normed_bf = attn_normed.astype(jnp.bfloat16)
    query_full = jnp.dot(normed_bf, w_query, preferred_element_type=jnp.float32).reshape(
        rows_here, heads_local, QK
    )
    query_bf = jnp.concatenate(
        [
            query_full[..., :PLAIN_HEAD_SIZE],
            apply_rotation(query_full[..., PLAIN_HEAD_SIZE:], token_position),
        ],
        axis=-1,
    ).astype(jnp.bfloat16)
    latent_with_key = jnp.dot(normed_bf, key_value_down_weight, preferred_element_type=jnp.float32)
    key_turned_part = apply_rotation(latent_with_key[:, LATENT_RANK:], token_position).astype(
        jnp.bfloat16
    )
    latent_after_norm, latent_unit_scale, latent_norm_factor = rms_normalize_pieces(
        latent_with_key[:, :LATENT_RANK], latent_norm_gain
    )
    latent_bf = latent_after_norm.astype(jnp.bfloat16)
    key_value = (
        jnp.dot(latent_bf, key_value_up_weight, preferred_element_type=jnp.float32)
        .astype(jnp.bfloat16)
        .reshape(rows_here, heads_local, PLAIN_HEAD_SIZE + VALUE_HEAD_SIZE)
    )
    key_nope = key_value[..., :PLAIN_HEAD_SIZE]
    value = key_value[..., PLAIN_HEAD_SIZE:]

    def masked_scores():
        raw = jnp.einsum(
            "thd,shd->hts",
            query_bf[..., :PLAIN_HEAD_SIZE],
            key_nope,
            preferred_element_type=jnp.float32,
        )
        raw = raw + jnp.einsum(
            "thd,sd->hts",
            query_bf[..., PLAIN_HEAD_SIZE:],
            key_turned_part,
            preferred_element_type=jnp.float32,
        )
        return jnp.where(allowed[None], raw * softmax_scale, -jnp.inf)

    scores = masked_scores()
    top_score = jnp.max(scores, axis=-1, keepdims=True)
    expo = jnp.exp(scores - top_score)
    total = jnp.sum(expo, axis=-1, keepdims=True)
    log_total = top_score + jnp.log(total)
    attn_weights = (expo / total).astype(jnp.bfloat16)
    context = jnp.einsum("hts,shd->thd", attn_weights, value, preferred_element_type=jnp.float32)
    context = context.astype(jnp.bfloat16).reshape(rows_here, heads_local * VALUE_HEAD_SIZE)
    (attn,) = product_sum(context, w_out, [])
    hidden = tokens_f + attn
    ffn_normed, ffn_unit, ffn_factor = rms_normalize_pieces(hidden, g_ffn)
    ffn_bf = ffn_normed.astype(jnp.bfloat16)
    router_probs = jax.nn.softmax(jnp.dot(ffn_normed, router, precision=highest), axis=-1)
    own = lax.axis_index("dp")

    named = jnp.any(routes[:, :, None] == jnp.arange(128, dtype=jnp.int32)[None, None, :], axis=1)
    dense_gates = jnp.where(named, jnp.pad(router_probs, ((0, 0), (0, 128 - experts))), -1.0)
    everyone_grad = lax.all_gather(grad_out, "dp")
    part = shared_gate.shape[1] // devices
    shared_parts = [
        lax.dynamic_slice_in_dim(w, own * part, part, 1)
        for w in (shared_gate, shared_up, shared_down)
    ]
    (
        ffn_part,
        grad_ffn_part,
        grad_expert_gate,
        grad_expert_up,
        grad_expert_down,
        shared_grads,
    ) = ffn_plain(
        ffn_bf,
        dense_gates,
        everyone_grad,
        [w[0] for w in (expert_gate, expert_up, expert_down)],
        shared_parts,
        capacity,
        experts,
    )
    share_rows = features // devices
    grad_shared_gate, grad_shared_up, grad_shared_down = shared_home(shared_grads, part)

    grad_top = grad_out.astype(jnp.float32)
    ffn_total = lax.psum_scatter(
        ffn_part.reshape(devices * rows_here, features), "dp", scatter_dimension=0, tiled=True
    )
    ffn_total = lax.psum(ffn_total, "tensor").astype(jnp.float32)
    output = (hidden + ffn_total).astype(jnp.bfloat16)
    (grad_ffn_sum,) = sum_home([grad_ffn_part], True)
    dense_grad = (
        grad_ffn_sum[:, features : features + experts]
        + grad_ffn_sum[:, features + experts : features + 2 * experts]
    )
    grad_logits = router_probs * (
        dense_grad - jnp.sum(router_probs * dense_grad, axis=-1, keepdims=True)
    )
    grad_router_in = contract_last(grad_logits, router, highest)
    grad_router_part = contract_first(ffn_normed, grad_logits, highest)
    grad_ffn_total = grad_ffn_sum[:, :features] + grad_router_in
    grad_g_ffn = jnp.sum(grad_ffn_total * ffn_unit, axis=0)
    grad_hidden = grad_top + normalize_back(grad_ffn_total, ffn_unit, ffn_factor, g_ffn)
    grad_hidden_bf = grad_hidden.astype(jnp.bfloat16)
    grad_w_out = contract_first(grad_hidden_bf, context)
    grad_context = jnp.dot(grad_hidden_bf, w_out, preferred_element_type=jnp.float32).astype(
        jnp.bfloat16
    )
    grad_context = grad_context.reshape(rows_here, heads_local, VALUE_HEAD_SIZE)
    redone = jnp.exp(masked_scores() - log_total)
    redone_bf = redone.astype(jnp.bfloat16)
    grad_weights = jnp.einsum(
        "thd,shd->hts", grad_context, value, preferred_element_type=jnp.float32
    )
    grad_value = jnp.einsum(
        "hts,thd->shd", redone_bf, grad_context, preferred_element_type=jnp.float32
    )
    row_inner = jnp.sum(redone * grad_weights, axis=-1, keepdims=True)
    grad_raw = (redone * (grad_weights - row_inner) * softmax_scale).astype(jnp.bfloat16)
    grad_query_nope = jnp.einsum(
        "hts,shd->thd", grad_raw, key_nope, preferred_element_type=jnp.float32
    )
    grad_query_rot = jnp.einsum(
        "hts,sd->thd", grad_raw, key_turned_part, preferred_element_type=jnp.float32
    )
    grad_key_nope = jnp.einsum(
        "hts,thd->shd",
        grad_raw,
        query_bf[..., :PLAIN_HEAD_SIZE],
        preferred_element_type=jnp.float32,
    )
    grad_key_rot = jnp.einsum(
        "hts,thd->sd", grad_raw, query_bf[..., PLAIN_HEAD_SIZE:], preferred_element_type=jnp.float32
    )
    grad_query = jnp.concatenate(
        [grad_query_nope, apply_rotation(grad_query_rot, -token_position)], axis=-1
    )
    grad_query = grad_query.reshape(rows_here, heads_local * QK).astype(jnp.bfloat16)
    grad_w_query = contract_first(normed_bf, grad_query)
    grad_key_value = (
        jnp.concatenate([grad_key_nope, grad_value], axis=-1)
        .reshape(rows_here, heads_local * (PLAIN_HEAD_SIZE + VALUE_HEAD_SIZE))
        .astype(jnp.bfloat16)
    )
    grad_w_kv_up = contract_first(latent_bf, grad_key_value)
    grad_latent_normed = contract_last(grad_key_value, key_value_up_weight)
    grad_latent_part = jnp.concatenate(
        [grad_latent_normed, apply_rotation(grad_key_rot, -token_position)], axis=1
    ).astype(jnp.bfloat16)
    grad_in_summed, grad_latent_sum = product_sum(grad_query, w_query, [grad_latent_part])
    grad_latent_normed = grad_latent_sum[:, :LATENT_RANK]
    grad_g_kv = jnp.sum(grad_latent_normed * latent_unit_scale, axis=0)
    grad_latent = normalize_back(
        grad_latent_normed, latent_unit_scale, latent_norm_factor, latent_norm_gain
    )
    grad_down = jnp.concatenate([grad_latent, grad_latent_sum[:, LATENT_RANK:]], axis=1)
    grad_down_bf = grad_down.astype(jnp.bfloat16)
    share = grad_down.shape[1] // lax.axis_size("tensor")
    grad_columns = lax.dynamic_slice_in_dim(
        grad_down_bf, lax.axis_index("tensor") * share, share, 1
    )
    grad_w_kv_down = contract_first(normed_bf, grad_columns)
    grad_attn_in = grad_in_summed + contract_last(grad_down_bf, key_value_down_weight)
    grad_g_attn = jnp.sum(grad_attn_in * attn_unit, axis=0)
    grad_tokens = grad_hidden + normalize_back(grad_attn_in, attn_unit, attn_factor, g_attn)
    vectors = jnp.concatenate(
        [
            grad_router_part,
            grad_g_attn[:, None],
            grad_g_ffn[:, None],
            jnp.pad(
                grad_g_kv.reshape(devices, -1), ((0, 0), (0, share_rows - LATENT_RANK // devices))
            ).reshape(-1, 1),
            jnp.zeros((features, 128 - experts - 3), jnp.float32),
        ],
        axis=1,
    )
    blocks = [
        a.astype(jnp.bfloat16).reshape(devices, a.shape[0] // devices, a.shape[1])
        for a in (grad_w_query, grad_w_out, grad_w_kv_up, grad_w_kv_down)
    ]
    grad_w_query, grad_w_out, grad_w_kv_up, grad_w_kv_down, vectors = sum_home(
        blocks + [vectors.reshape(devices, share_rows, 128)]
    )
    rank, ranks = lax.axis_index("tensor"), lax.axis_size("tensor")
    router_rows = share_rows // ranks
    grad_router = lax.dynamic_slice_in_dim(vectors[:, :experts], rank * router_rows, router_rows, 0)
    latent_rows = LATENT_RANK // devices // ranks
    grad_g_kv = lax.dynamic_slice_in_dim(
        vectors[:, experts + 2], rank * latent_rows, latent_rows, 0
    )
    return (
        output,
        grad_tokens,
        vectors[:, experts],
        grad_w_query,
        grad_w_kv_down,
        grad_g_kv,
        grad_w_kv_up,
        grad_w_out,
        vectors[:, experts + 1],
        grad_router,
        grad_shared_gate,
        grad_shared_up,
        grad_shared_down,
        grad_expert_gate,
        grad_expert_up,
        grad_expert_down,
    )


def solution(mesh):
    in_specs = (
        P("dp", None),
        P("dp", None),
        P("dp", None),
        P("dp", None),
        P(),
        P(None, "tensor"),
        P(),
        P(),
        P(None, "tensor"),
        P(None, "tensor"),
        P(),
        P(),
        P(None, "tensor"),
        P(None, "tensor"),
        P(None, "tensor"),
        P("dp", None, "tensor"),
        P("dp", None, "tensor"),
        P("dp", None, "tensor"),
    )
    out_specs = (
        P("dp", None),
        P("dp", None),
        P("dp"),
        P("dp", "tensor"),
        P("dp", "tensor"),
        P(("dp", "tensor")),
        P("dp", "tensor"),
        P("dp", "tensor"),
        P("dp"),
        P(("dp", "tensor"), None),
        P("dp", "tensor"),
        P("dp", "tensor"),
        P("dp", "tensor"),
        P("dp", None, "tensor"),
        P("dp", None, "tensor"),
        P("dp", None, "tensor"),
    )
    tuned = mesh.shape["dp"] == 16 and mesh.shape["tensor"] == 2
    return jax.shard_map(
        shards_tuned if tuned else shards, mesh=mesh, in_specs=in_specs, out_specs=out_specs, check_vma=False)
```
